32 devices in a mesh: dp: 2 (over core), seq: 16 (over z, y, x).
Axes of the slice: x: 2, y: 2, z: 4, core: 2. Of those that a mesh axis runs over, the one named last changes fastest.
Arguments:
- inputs: bfloat16 [2, 9216, 512], P('dp', 'seq'), may hold values from -6 to 6
- doc_bounds: int32 [2, 2], P('dp'), may hold values from 1 to 3071, as said below
- pool_weight: bfloat16 [1536, 512], replicated, may hold values from -0.15625 to 0.15625
- pool_bias: float32 [512], replicated, may hold values from -1.75 to 1.75
- ln1_gain: float32 [512], replicated, may hold values from 0.5 to 1.5
- ln1_bias: float32 [512], replicated, may hold values from -1.75 to 1.75
- query_weight: bfloat16 [512, 512], replicated, may hold values from -0.25 to 0.25
- key_weight: bfloat16 [512, 512], replicated, may hold values from -0.25 to 0.25
- value_weight: bfloat16 [512, 512], replicated, may hold values from -0.25 to 0.25
- out_weight: bfloat16 [512, 512], replicated, may hold values from -6 to 6
- pos_weight: bfloat16 [512, 512], replicated, may hold values from -0.25 to 0.25
- content_bias: float32 [512], replicated, may hold values from -6 to 6
- pos_bias: float32 [512], replicated, may hold values from -6 to 6
- ln2_gain: float32 [512], replicated, may hold values from 0.5 to 1.5
- ln2_bias: float32 [512], replicated, may hold values from -1.75 to 1.75
- ffn_in: bfloat16 [512, 2048], replicated, may hold values from -0.25 to 0.25
- ffn_in_bias: float32 [2048], replicated, may hold values from -1.75 to 1.75
- ffn_out: bfloat16 [2048, 512], replicated, may hold values from -0.125 to 0.125
- ffn_out_bias: float32 [512], replicated, may hold values from -1.75 to 1.75
- up_weight: bfloat16 [512, 1536], replicated, may hold values from -0.25 to 0.25
- up_bias: float32 [1536], replicated, may hold values from -1.75 to 1.75
- cotangent: bfloat16 [2, 9216, 512], P('dp', 'seq'), may hold values from -6 to 6
Outputs:
- outputs: bfloat16 [2, 9216, 512], P('dp', 'seq')
- input_grad: bfloat16 [2, 9216, 512], P('dp', 'seq')
- grad_pool_weight: float32 [1536, 512], replicated
- grad_pool_bias: float32 [512], replicated
- grad_ln1_gain: float32 [512], replicated
- grad_ln1_bias: float32 [512], replicated
- grad_query_weight: float32 [512, 512], replicated
- grad_key_weight: float32 [512, 512], replicated
- grad_value_weight: float32 [512, 512], replicated
- grad_out_weight: float32 [512, 512], replicated
- grad_pos_weight: float32 [512, 512], replicated
- grad_content_bias: float32 [512], replicated
- grad_pos_bias: float32 [512], replicated
- grad_ln2_gain: float32 [512], replicated
- grad_ln2_bias: float32 [512], replicated
- grad_ffn_in: float32 [512, 2048], replicated
- grad_ffn_in_bias: float32 [2048], replicated
- grad_ffn_out: float32 [2048, 512], replicated
- grad_ffn_out_bias: float32 [512], replicated
- grad_up_weight: float32 [512, 1536], replicated
- grad_up_bias: float32 [1536], replicated
The draws below stay inside these ranges and needn't reach their ends.
Inputs may be any that keep to these rules, and one draw needn't show every extreme that they name: `doc_bounds`: each row holds three packed documents: the second begins inside the first 192 shortened positions and the third inside the last 192, so the second spans every block of the row.
All inputs are finite; a program needn't handle non-finite values.
Results may differ from the reference program's by a relative error of at most 0.015.
Values may be sent and summed in bfloat16 or wider, within the bound.
A program may use at most 320 MiB of HBM per device.

```python
import math
import jax
import jax.numpy as jnp
from jax import lax

D = 512
HEADS = 8
FF = 2048
TOK_DEV = 192
TOKENS = 3072
BYTES = 9216
ROWS = 2
N_SEQ = 16


def draw_doc_bounds(key, part):
    key = jax.random.fold_in(key, 7)
    first_key, second_key = jax.random.split(key)
    opening = jax.random.randint(first_key, (ROWS, 1), 1, TOK_DEV)
    closing = jax.random.randint(second_key, (ROWS, 1), TOKENS - TOK_DEV + 1, TOKENS)
    return jnp.concatenate([opening, closing], 1).astype(jnp.int32)


def block_levels(own_key, dims, shards, low, top_value):
    level, own = 1.0, jax.random.fold_in(own_key, 6)
    for position, parts in shards:
        draws = jnp.exp(jax.random.uniform(jax.random.fold_in(own, position), (parts,), jnp.float32, low / len(shards), top_value / len(shards)))
        level = level * jnp.repeat(draws, dims[position] // parts).reshape([-1 if axis == position else 1 for axis in range(len(dims))])
    return level


def scatter_about(rng, shape, spread, reach, cuts=(), kind=jnp.bfloat16):
    values = jax.random.normal(rng, shape, jnp.float32) * spread
    if len(cuts) > 0:
        values = block_levels(rng, shape, cuts, -0.22, 0.18) * values
    return jnp.clip(values, min=-reach, max=reach).astype(kind)


def setup_inputs(seed: int = 0) -> dict:
    seeds = jax.random.split(jax.random.key(seed), 23)
    inputs = scatter_about(seeds[0], (ROWS, BYTES, D), 1.0, 6.0, ((0, 2), (1, 16)))
    doc_bounds = draw_doc_bounds(jax.random.fold_in(seeds[22], 71), 0)
    pool_weight = scatter_about(seeds[2], (3 * D, D), (3 * D) ** -0.5, 0.15625)
    pool_bias = scatter_about(seeds[3], (D,), 0.3, 1.75, (), jnp.float32)
    ln1_gain = jnp.clip(1.0 + 0.1 * jax.random.normal(seeds[4], (D,), jnp.float32), 0.5, 1.5)
    ln1_bias = scatter_about(seeds[5], (D,), 0.3, 1.75, (), jnp.float32)
    query_weight = scatter_about(seeds[6], (D, D), D ** -0.5, 0.25)
    key_weight = scatter_about(seeds[7], (D, D), D ** -0.5, 0.25)
    value_weight = scatter_about(seeds[8], (D, D), D ** -0.5, 0.25)
    out_weight = scatter_about(seeds[9], (D, D), ((TOK_DEV * N_SEQ // (3 * D) + 1) ** 0.5), 6.0)
    pos_weight = scatter_about(seeds[10], (D, D), D ** -0.5, 0.25)
    content_bias = scatter_about(seeds[11], (D,), 1.0, 6.0, (), jnp.float32)
    pos_bias = scatter_about(seeds[12], (D,), 1.0, 6.0, (), jnp.float32)
    ln2_gain = jnp.clip(1.0 + 0.1 * jax.random.normal(seeds[13], (D,), jnp.float32), 0.5, 1.5)
    ln2_bias = scatter_about(seeds[14], (D,), 0.3, 1.75, (), jnp.float32)
    ffn_in = scatter_about(seeds[15], (D, FF), D ** -0.5, 0.25)
    ffn_in_bias = scatter_about(seeds[16], (FF,), 0.3, 1.75, (), jnp.float32)
    ffn_out = scatter_about(seeds[17], (FF, D), FF ** -0.5, 0.125)
    ffn_out_bias = scatter_about(seeds[18], (D,), 0.3, 1.75, (), jnp.float32)
    up_weight = scatter_about(seeds[19], (D, 3 * D), D ** -0.5, 0.25)
    up_bias = scatter_about(seeds[20], (3 * D,), 0.3, 1.75, (), jnp.float32)
    cotangent = scatter_about(seeds[21], (ROWS, BYTES, D), 1.0, 6.0, ((0, 2), (1, 16)))
    return dict(inputs=inputs, doc_bounds=doc_bounds, pool_weight=pool_weight, pool_bias=pool_bias, ln1_gain=ln1_gain, ln1_bias=ln1_bias, query_weight=query_weight, key_weight=key_weight, value_weight=value_weight, out_weight=out_weight, pos_weight=pos_weight, content_bias=content_bias, pos_bias=pos_bias, ln2_gain=ln2_gain, ln2_bias=ln2_bias, ffn_in=ffn_in, ffn_in_bias=ffn_in_bias, ffn_out=ffn_out, ffn_out_bias=ffn_out_bias, up_weight=up_weight, up_bias=up_bias, cotangent=cotangent)


@jax.custom_vjp
def low(v):
    return lax.optimization_barrier(v.astype(jnp.bfloat16)).astype(jnp.float32)

@jax.custom_vjp
def low_back(v):
    return v

def low_keep(v):
    return (low(v), None)

def low_pass(kept, grad):
    return (grad,)

def back_keep(v):
    return (v, None)

def back_low(kept, grad):
    return (low(grad),)
low.defvjp(low_keep, low_pass)
low_back.defvjp(back_keep, back_low)
epsilon = 1e-05
masked_score = -1e+30
highest = lax.Precision.HIGHEST

def matmul(left, right):
    return jnp.dot(left, right, precision=highest)

def layer_norm(hidden, gain, bias):
    average = lax.optimization_barrier(jnp.mean(hidden, -1, keepdims=True))
    centred = hidden - average
    inverse = lax.rsqrt(lax.optimization_barrier(jnp.mean(centred * centred, -1, keepdims=True)) + epsilon)
    return centred * inverse * gain + bias

def exact_gelu(value):
    return jax.nn.gelu(value, approximate=False)

def doc_index(positions, bounds):
    return (positions >= bounds[0]).astype(jnp.int32) + (positions >= bounds[1]).astype(jnp.int32)

def angles(positions, model_width):
    half_width = model_width // 2
    rates = 10000.0 ** (-2.0 * jnp.arange(half_width, dtype=jnp.float32) / model_width)
    phase = positions.astype(jnp.float32)[:, None] * rates[None, :]
    return (jnp.sin(phase), jnp.cos(phase))

def skew(full, width):
    lead = full.shape[:-2]
    count, span = (full.shape[-2], full.shape[-1])
    padded = jnp.pad(full, [(0, 0)] * len(lead) + [(0, 0), (0, 1)])
    flat = padded.reshape(lead + (count * (span + 1),))[..., count - 1:count - 1 + count * span]
    return flat.reshape(lead + (count, span))[..., :width]

def layer(params, row, bounds):
    pool_weight, pool_bias, ln1_gain, ln1_bias, query_weight, key_weight, value_weight, out_weight, pos_weight, content_bias, pos_bias, ln2_gain, ln2_bias, ffn_in, ffn_in_bias, ffn_out, ffn_out_bias, up_weight, up_bias = params
    model_width = row.shape[1]
    head_size = model_width // HEADS
    tokens = row.shape[0] // 3
    score_scale = head_size ** (-0.5)
    shifted = jnp.concatenate([jnp.zeros((2, model_width), jnp.float32), row[:-2]], 0)
    pooled = low_back(matmul(low(shifted.reshape(tokens, 3 * model_width)), pool_weight) + pool_bias)
    normed = low(layer_norm(pooled, ln1_gain, ln1_bias))
    query = low_back(matmul(normed, query_weight))
    key_rows = low(low_back(matmul(normed, key_weight))).reshape(tokens, HEADS, head_size)
    value_rows = low(low_back(matmul(normed, value_weight))).reshape(tokens, HEADS, head_size)
    query_u = low(query + content_bias).reshape(tokens, HEADS, head_size)
    query_v = low(query + pos_bias).reshape(tokens, HEADS, head_size)
    distances = tokens - 1 - jnp.arange(tokens, dtype=jnp.int32)
    sines, cosines = angles(distances, model_width)
    feats = low(jnp.concatenate([sines, cosines], -1))
    rel_rows = low(matmul(feats, pos_weight)).reshape(tokens, HEADS, head_size)
    rev_table = jnp.concatenate([rel_rows, jnp.zeros((tokens, HEADS, head_size), jnp.float32)], 0)
    places = jnp.arange(tokens, dtype=jnp.int32)
    docs = doc_index(places, bounds)
    block_len = math.gcd(tokens, 512)
    block_count = tokens // block_len

    def attend_block(element):
        block_u, block_v, block_places, block_docs, block_start = element
        raw = jnp.einsum('the,she->hts', block_u, key_rows, precision=highest)
        window = lax.dynamic_slice_in_dim(rev_table, tokens - block_len - block_start, block_len + tokens - 1, 0)
        raw = raw + skew(jnp.einsum('the,khe->htk', block_v, window, precision=highest), tokens)
        score = low_back(raw * score_scale)
        allowed = ((places[None, :] <= block_places[:, None]) & (docs[None, :] == block_docs[:, None]))[None, :, :]
        score = jnp.where(allowed, score, masked_score)
        top_score = lax.optimization_barrier(jnp.max(score, -1, keepdims=True))
        weight = jnp.where(allowed, jnp.exp(score - top_score), 0.0)
        total = lax.optimization_barrier(jnp.sum(weight, -1))
        summed = jnp.einsum('hts,she->hte', low(weight), value_rows, precision=highest)
        return jnp.transpose(summed / total[..., None], (1, 0, 2))
    attended = lax.map(jax.checkpoint(attend_block), (query_u.reshape(block_count, block_len, HEADS, head_size), query_v.reshape(block_count, block_len, HEADS, head_size), places.reshape(block_count, block_len), docs.reshape(block_count, block_len), jnp.arange(block_count, dtype=jnp.int32) * block_len))
    attended = low_back(attended.reshape(tokens, model_width))
    mixed = pooled + low_back(matmul(low(attended), out_weight))
    ffn_input = low(layer_norm(mixed, ln2_gain, ln2_bias))
    pre_act = low_back(matmul(ffn_input, ffn_in) + ffn_in_bias)
    activated = low(exact_gelu(pre_act))
    final = mixed + low_back(matmul(activated, ffn_out) + ffn_out_bias)
    upsampled = low_back(matmul(low(final), up_weight) + up_bias)
    return row + upsampled.reshape(3 * tokens, model_width)

def reference(inputs, doc_bounds, pool_weight, pool_bias, ln1_gain, ln1_bias, query_weight, key_weight, value_weight, out_weight, pos_weight, content_bias, pos_bias, ln2_gain, ln2_bias, ffn_in, ffn_in_bias, ffn_out, ffn_out_bias, up_weight, up_bias, cotangent):
    params = tuple((array.astype(jnp.float32) for array in (pool_weight, pool_bias, ln1_gain, ln1_bias, query_weight, key_weight, value_weight, out_weight, pos_weight, content_bias, pos_bias, ln2_gain, ln2_bias, ffn_in, ffn_in_bias, ffn_out, ffn_out_bias, up_weight, up_bias)))

    def per_row(totals, element):
        row, bounds, grad_row = element
        result, pullback = jax.vjp(lambda weights, data: layer(weights, data, bounds), params, row)
        weight_grads, row_grad = pullback(grad_row)
        totals = jax.tree.map(jnp.add, totals, weight_grads)
        return (totals, (result.astype(jnp.bfloat16), row_grad.astype(jnp.bfloat16)))
    zeros = jax.tree.map(jnp.zeros_like, params)
    totals, (outputs, input_grad) = lax.scan(per_row, zeros, (inputs.astype(jnp.float32), doc_bounds, cotangent.astype(jnp.float32)))
    return (outputs, input_grad, totals[0], totals[1], totals[2], totals[3], totals[4], totals[5], totals[6], totals[7], totals[8], totals[9], totals[10], totals[11], totals[12], totals[13], totals[14], totals[15], totals[16], totals[17], totals[18])
```

```python
import functools

import jax
import jax.numpy as jnp
import numpy as np
from jax import lax
from jax.experimental import pallas as pl
from jax.experimental.pallas import tpu as pltpu
from jax.sharding import PartitionSpec as P

HEADS = 8
ROWS = 2
HEAD = 64
PAIR = 2 * HEAD
MESH = pl.DeviceIdType.MESH
F32 = jnp.float32
BF16 = jnp.bfloat16

epsilon = 1e-05
masked_score = -1e30


def dot(left, right, dims=((1,), (0,))):
    return lax.dot_general(left, right, (dims, ((), ())), preferred_element_type=F32)


def passed_along(value, axis, steps):
    count = lax.axis_size(axis)
    first, last = (max(0, -steps), min(count, count - steps))
    return lax.ppermute(value, axis, [(source, source + steps) for source in range(first, last)])


def place_of(block, group):
    turn, spot = block // group, block % group
    return turn, jnp.where(turn % 2 == 0, spot, group - 1 - spot)


def block_of(turn, member, group):
    return turn * group + jnp.where(turn % 2 == 0, member, group - 1 - member)


def whereabouts(group):
    core, chip = lax.axis_index("dp"), lax.axis_index("seq")
    chips = group // 2
    unit = chip // chips
    member = (chip % chips) * 2 + core
    return core, chip, unit // HEADS, unit % HEADS, member


def chip_of(row, head, member, group):
    return (row * HEADS + head) * (group // 2) + member // 2, member % 2


def meet(n, group, to_units):
    core, chip, row, head, member = whereabouts(group)
    barrier = pltpu.get_barrier_semaphore()

    def greet(row_or_core, chip_at):
        away = jnp.logical_or(row_or_core != core, chip_at != chip)

        @pl.when(away)
        def _():
            pl.semaphore_signal(
                barrier, inc=1, device_id=(row_or_core, chip_at), device_id_type=MESH
            )

        return away.astype(jnp.int32)

    own_row = row == core
    if to_units:
        for s in range(n):
            greet(row, jnp.int32(s))
        mine = jnp.logical_and(chip // (HEADS * (group // 2)) == core, True)
        pl.semaphore_wait(barrier, HEADS * group - mine.astype(jnp.int32))
    else:
        for h in range(HEADS):
            for g in range(group):
                c, k = chip_of(core, h, g, group)
                greet(jnp.int32(k), c)
        pl.semaphore_wait(barrier, n - own_row.astype(jnp.int32))


def send(source, target, sems, core, chip):
    here_core, here_chip = lax.axis_index("dp"), lax.axis_index("seq")
    here = jnp.logical_and(core == here_core, chip == here_chip)

    @pl.when(here)
    def _():
        pltpu.make_async_copy(source, target, sems[1]).start()

    @pl.when(jnp.logical_not(here))
    def _():
        pltpu.make_async_remote_copy(
            source, target, sems[0], sems[1], device_id=(core, chip), device_id_type=MESH
        ).start()


def sent(source, sem, core, chip):
    here_core, here_chip = lax.axis_index("dp"), lax.axis_index("seq")
    here = jnp.logical_and(core == here_core, chip == here_chip)

    @pl.when(jnp.logical_not(here))
    def _():
        pltpu.make_async_copy(source, source, sem).wait()


def arrived(whole, sem):
    pltpu.make_async_copy(whole, whole, sem).wait()


def to_units_kernel(n, group, *refs):
    count = len(refs) - 2
    arrays, outs = refs[: count // 2], refs[count // 2 : count]
    send_sem, recv_sem = refs[count:]
    core, chip, row, head, member = whereabouts(group)
    turn, spot = place_of(chip, group)
    meet(n, group, True)
    jobs = []
    for h in range(HEADS):
        for index, (array, out) in enumerate(zip(arrays, outs)):
            sems = (send_sem.at[index], recv_sem.at[index])
            if index == 0:
                to_chip, to_core = chip_of(core, h, spot, group)
                jobs.append((array.at[h], out.at[turn], sems, to_core, to_chip))
            else:
                for g in range(group):
                    to_chip, to_core = chip_of(core, h, g, group)
                    jobs.append((array.at[h], out.at[chip], sems, jnp.int32(to_core), to_chip))
    for job in jobs:
        send(*job)
    for source, _, sems, to_core, to_chip in jobs:
        sent(source, sems[0], to_core, to_chip)
    for index, out in enumerate(outs):
        arrived(out, recv_sem.at[index])


def to_owners_kernel(n, group, *refs):
    count = len(refs) - 2
    arrays, outs = refs[: count // 2], refs[count // 2 : count]
    send_sem, recv_sem = refs[count:]
    core, chip, row, head, member = whereabouts(group)
    meet(n, group, False)
    jobs = []
    for turn in range(n // group):
        block = block_of(jnp.int32(turn), member, group)
        sems = (send_sem.at[0], recv_sem.at[0])
        jobs.append((arrays[0].at[turn], outs[0].at[head], sems, row, block))
    if len(arrays) > 1:
        for block in range(n):
            sems = (send_sem.at[1], recv_sem.at[1])
            jobs.append((arrays[1].at[block], outs[1].at[member, head], sems, row, jnp.int32(block)))
    for job in jobs:
        send(*job)
    for source, _, sems, to_core, to_chip in jobs:
        sent(source, sems[0], to_core, to_chip)
    for index, out in enumerate(outs):
        arrived(out, recv_sem.at[index])


def exchange(kernel, n, group, arrays, shapes, ident):
    vmem = pl.BlockSpec(memory_space=pltpu.VMEM)
    return pl.pallas_call(
        functools.partial(kernel, n, group),
        out_shape=[jax.ShapeDtypeStruct(shape, array.dtype) for shape, array in zip(shapes, arrays)],
        in_specs=[vmem] * len(arrays),
        out_specs=[vmem] * len(arrays),
        scratch_shapes=[
            pltpu.SemaphoreType.DMA((len(arrays),)),
            pltpu.SemaphoreType.DMA((len(arrays),)),
        ],
        compiler_params=pltpu.CompilerParams(
            collective_id=ident, has_side_effects=True, vmem_limit_bytes=48 * 2**20
        ),
    )(*arrays)


def unpacked(pair):
    return jnp.concatenate([pair[:, :HEAD], pair[:, HEAD:]], 0)


def packed(block):
    half = block.shape[0] // 2
    return jnp.concatenate([block[:half], block[half:]], 1)


def query_parts(q_pair, content_bias, pos_bias, pos_weight, turn_sin, turn_cos):
    query = unpacked(q_pair.astype(F32))
    query_u = (query + content_bias).astype(BF16)
    query_v = (query + pos_bias).astype(BF16)
    spread = dot(query_v, pos_weight, ((1,), (1,)))
    half = turn_sin.shape[1]
    lift, rest = spread[:, :half], spread[:, half:]
    on_sin = rest * turn_sin - lift * turn_cos
    on_cos = lift * turn_sin + rest * turn_cos
    turned = jnp.concatenate([on_sin, on_cos], 1)
    return query_u, query_v, turned


def attend_kernel(
    n, group, tile, q_ref, kv_ref, table_ref, sin_ref, cos_ref, weight_ref, cb_ref, pb_ref, bounds_ref,
    att_ref, low_ref, total_ref, keep_ref, score_ref, extra_ref,
):
    turn = pl.program_id(0)
    member = whereabouts(group)[4]
    block = block_of(turn, member, group)
    length = sin_ref.shape[0]
    tokens = n * length
    query_u, _, turned = query_parts(
        q_ref[...], cb_ref[...], pb_ref[...], weight_ref[...], sin_ref[...], cos_ref[...]
    )
    scale = HEAD**-0.5
    head_part = (query_u.astype(F32) * scale).astype(BF16)
    extra_ref[:, :HEAD] = head_part
    extra_ref[:, HEAD:PAIR] = jnp.zeros_like(head_part)
    extra_ref[:, PAIR:] = (turned * scale).astype(BF16)
    first = block * length
    tiles = (first + length + tile - 1) // tile
    low_bound, high_bound = bounds_ref[0], bounds_ref[1]
    places = first + lax.broadcasted_iota(jnp.int32, (length, 1), 0)
    opening = jnp.where(
        places >= high_bound, high_bound, jnp.where(places >= low_bound, low_bound, 0)
    )
    lanes = lax.broadcasted_iota(jnp.int32, (length, tile), 1)

    def score_step(step, top):
        start = pl.multiple_of(step * tile, tile)
        keys = kv_ref[pl.ds(start, tile), :]
        waves = table_ref[pl.ds(pl.multiple_of((n - 1 - block) * length + start, length), tile), :]
        score = dot(extra_ref[:, :PAIR], keys, ((1,), (1,))) + dot(
            extra_ref[:, PAIR:], waves, ((1,), (1,))
        )
        at = lanes + start
        allowed = jnp.logical_and(at <= places, at >= opening)
        score = jnp.where(allowed, score, masked_score)
        score_ref[:, pl.ds(start, tile)] = score
        for part in range(tile // 128):
            top = jnp.maximum(top, score[:, part * 128 : (part + 1) * 128])
        return top

    top = lax.fori_loop(0, tiles, score_step, jnp.full((length, 128), masked_score, F32))
    top = jnp.max(top, 1, keepdims=True)

    def value_step(step, state):
        total, summed = state
        start = pl.multiple_of(step * tile, tile)
        weight = jnp.exp(score_ref[:, pl.ds(start, tile)] - top)
        for part in range(tile // 128):
            total = total + weight[:, part * 128 : (part + 1) * 128]
        low = weight.astype(BF16)
        keep_ref[:, pl.ds(start, tile)] = low
        return total, summed + dot(low, kv_ref[pl.ds(start, tile), :])

    total, summed = lax.fori_loop(
        0, tiles, value_step, (jnp.zeros((length, 128), F32), jnp.zeros((length, PAIR), F32))
    )
    total = jnp.sum(total, 1, keepdims=True)
    attended = summed[:, HEAD:] / total
    att_ref[...] = attended
    total_ref[...] = jnp.broadcast_to(total, (length, 128))
    low_ref[...] = packed(attended).astype(BF16)


def back_kernel(
    n, group, tile, q_ref, kv_ref, table_ref, sin_ref, cos_ref, weight_ref, cb_ref, pb_ref,
    att_ref, total_ref, keep_ref, grad_ref,
    dq_ref, dkv_ref, dweight_ref, dcb_ref, dpb_ref, dkv_acc,
):
    turn = pl.program_id(0)
    member = whereabouts(group)[4]
    block = block_of(turn, member, group)
    length = sin_ref.shape[0]
    scale = HEAD**-0.5

    @pl.when(turn == 0)
    def _():
        dkv_acc[...] = jnp.zeros_like(dkv_acc)
        dweight_ref[...] = jnp.zeros_like(dweight_ref)
        dcb_ref[...] = jnp.zeros_like(dcb_ref)
        dpb_ref[...] = jnp.zeros_like(dpb_ref)

    query_u, query_v, _ = query_parts(
        q_ref[...], cb_ref[...], pb_ref[...], weight_ref[...], sin_ref[...], cos_ref[...]
    )
    head_part = (query_u.astype(F32) * scale).astype(BF16)
    grad = unpacked(grad_ref[...].astype(F32))
    inverse = 1.0 / total_ref[:, :1]
    delta = jnp.sum(grad * att_ref[...], 1, keepdims=True) * inverse
    grad_low = (grad * inverse).astype(BF16)
    nothing = jnp.zeros_like(grad_low)
    grad_wide = jnp.concatenate([nothing, grad_low], 1)
    query_wide = jnp.concatenate([head_part, nothing], 1)
    tiles = (block * length + length + tile - 1) // tile

    def step_over(step, state):
        near, far = state
        start = pl.multiple_of(step * tile, tile)
        keys = kv_ref[pl.ds(start, tile), :]
        waves = table_ref[pl.ds(pl.multiple_of((n - 1 - block) * length + start, length), tile), :]
        weight = keep_ref[:, pl.ds(start, tile)]
        grad_weight = dot(grad_wide, keys, ((1,), (1,)))
        grad_score = (weight.astype(F32) * (grad_weight - delta)).astype(BF16)
        near = near + dot(grad_score, keys)
        far = far + dot(grad_score, waves)
        dkv_acc[pl.ds(start, tile), :] += dot(grad_score, query_wide, ((0,), (0,))) + dot(
            weight, grad_wide, ((0,), (0,))
        )
        return near, far

    near, far = lax.fori_loop(
        0,
        tiles,
        step_over,
        (jnp.zeros((length, PAIR), F32), jnp.zeros((length, table_ref.shape[1]), F32)),
    )
    grad_u = near[:, :HEAD] * scale
    half = sin_ref.shape[1]
    turn_sin, turn_cos = sin_ref[...], cos_ref[...]
    on_sin, on_cos = far[:, :half] * scale, far[:, half:] * scale
    lift = on_cos * turn_sin - on_sin * turn_cos
    rest = on_cos * turn_cos + on_sin * turn_sin
    spread = jnp.concatenate([lift, rest], 1).astype(BF16)
    grad_v = dot(spread, weight_ref[...])
    dweight_ref[...] += dot(spread, query_v, ((0,), (0,)))
    dcb_ref[...] += jnp.sum(grad_u, 0, keepdims=True)
    dpb_ref[...] += jnp.sum(grad_v, 0, keepdims=True)
    dq_ref[...] = packed(grad_u + grad_v).astype(BF16)

    @pl.when(turn == pl.num_programs(0) - 1)
    def _():
        dkv_ref[...] = dkv_acc[...].astype(BF16)


def wave_tables(tokens, length, width):
    rates = 10000.0 ** (-2.0 * np.arange(width // 2, dtype=np.float64) / width)
    far = (np.arange(tokens + length, dtype=np.float64) - (tokens - length))[:, None] * rates
    near = np.arange(length, dtype=np.float64)[:, None] * rates
    table = np.concatenate([np.sin(far), np.cos(far)], 1)
    return (
        jnp.asarray(table, dtype=BF16),
        jnp.asarray(np.sin(near), dtype=F32),
        jnp.asarray(np.cos(near), dtype=F32),
    )


def whole_spec(shape):
    return pl.BlockSpec(shape, lambda turn: (0,) * len(shape))


def turn_spec(shape):
    return pl.BlockSpec((None,) + shape, lambda turn: (turn,) + (0,) * len(shape))


def layer_norm(hidden, gain, bias):
    average = jnp.mean(hidden, -1, keepdims=True)
    centred = hidden - average
    inverse = lax.rsqrt(jnp.mean(centred * centred, -1, keepdims=True) + epsilon)
    normed = centred * inverse
    return (normed * gain + bias, normed, inverse)


def norm_back(grad_out, normed, inverse, gain):
    scaled = grad_out * gain
    grad_in = inverse * (
        scaled
        - jnp.mean(scaled, -1, keepdims=True)
        - normed * jnp.mean(scaled * normed, -1, keepdims=True)
    )
    return (grad_in, jnp.sum(grad_out * normed, axis=0), jnp.sum(grad_out, axis=0))


def exact_gelu(value):
    return jax.nn.gelu(value, approximate=False)


def heads_packed(array):
    length = array.shape[0]
    split = array.reshape(2, length // 2, HEADS, HEAD)
    return jnp.transpose(split, (2, 1, 0, 3)).reshape(HEADS, length // 2, PAIR)


def heads_unpacked(array):
    half = array.shape[1]
    split = array.reshape(HEADS, half, 2, HEAD)
    return jnp.transpose(split, (2, 1, 0, 3)).reshape(2 * half, HEADS * HEAD)


def body(
    inputs, doc_bounds, pool_weight, pool_bias, ln1_gain, ln1_bias, query_weight, key_weight,
    value_weight, out_weight, pos_weight, content_bias, pos_bias, ln2_gain, ln2_bias, ffn_in,
    ffn_in_bias, ffn_out, ffn_out_bias, up_weight, up_bias, cotangent,
):
    _, bytes_here, width = inputs.shape
    length = bytes_here // 3
    n = lax.axis_size("seq")
    tokens = n * length
    group = 2 * n // (ROWS * HEADS)
    rounds = n // group
    tile = 2 * length
    row, head, member = whereabouts(group)[2:]

    all_bounds = lax.all_gather(doc_bounds, "dp", axis=0, tiled=True)
    bounds = lax.dynamic_slice(all_bounds, (row, 0), (1, 2))[0]
    table, turn_sin, turn_cos = wave_tables(tokens, length, width)
    head_weight = lax.dynamic_slice(pos_weight, (0, head * HEAD), (width, HEAD))
    head_cb = lax.dynamic_slice(content_bias, (head * HEAD,), (HEAD,))[None]
    head_pb = lax.dynamic_slice(pos_bias, (head * HEAD,), (HEAD,))[None]

    rim = passed_along(inputs[:, bytes_here - 2 :, :], "seq", 1)
    shifted = jnp.concatenate([rim, inputs[:, : bytes_here - 2, :]], 1)
    pooled_in = shifted.reshape(length, 3 * width)
    pooled = dot(pooled_in, pool_weight) + pool_bias
    normed_one, plain_one, inverse_one = layer_norm(pooled, ln1_gain, ln1_bias)
    attn_in = normed_one.astype(BF16)
    query = dot(attn_in, query_weight).astype(BF16)
    keys = dot(attn_in, key_weight).astype(BF16).reshape(length, HEADS, HEAD)
    values = dot(attn_in, value_weight).astype(BF16).reshape(length, HEADS, HEAD)
    q_out = heads_packed(query)
    kv_out = jnp.transpose(jnp.concatenate([keys, values], 2), (1, 0, 2))

    q_in, kv_in = exchange(
        to_units_kernel, n, group, (q_out, kv_out),
        ((rounds, length // 2, PAIR), (n, length, PAIR)), 0,
    )
    kv_in = kv_in.reshape(tokens, PAIR)

    common_specs = [
        turn_spec((length // 2, PAIR)),
        whole_spec((tokens, PAIR)),
        whole_spec(table.shape),
        whole_spec(turn_sin.shape),
        whole_spec(turn_cos.shape),
        whole_spec(head_weight.shape),
        whole_spec((1, HEAD)),
        whole_spec((1, HEAD)),
    ]
    common = (q_in, kv_in, table, turn_sin, turn_cos, head_weight, head_cb, head_pb)
    attended, att_low, total, keep = pl.pallas_call(
        functools.partial(attend_kernel, n, group, tile),
        grid=(rounds,),
        in_specs=common_specs + [pl.BlockSpec(memory_space=pltpu.SMEM)],
        out_specs=[
            turn_spec((length, HEAD)),
            turn_spec((length // 2, PAIR)),
            turn_spec((length, 128)),
            turn_spec((length, tokens)),
        ],
        out_shape=[
            jax.ShapeDtypeStruct((rounds, length, HEAD), F32),
            jax.ShapeDtypeStruct((rounds, length // 2, PAIR), BF16),
            jax.ShapeDtypeStruct((rounds, length, 128), F32),
            jax.ShapeDtypeStruct((rounds, length, tokens), BF16),
        ],
        scratch_shapes=[
            pltpu.VMEM((length, tokens), F32),
            pltpu.VMEM((length, PAIR + width), BF16),
        ],
        compiler_params=pltpu.CompilerParams(vmem_limit_bytes=56 * 2**20),
    )(*common, bounds)

    (att_back,) = exchange(
        to_owners_kernel, n, group, (att_low,), ((HEADS, length // 2, PAIR),), 1
    )
    attended_low = heads_unpacked(att_back)

    mixed = pooled + dot(attended_low, out_weight)
    normed_two, plain_two, inverse_two = layer_norm(mixed, ln2_gain, ln2_bias)
    ffn_input = normed_two.astype(BF16)
    pre_act = dot(ffn_input, ffn_in) + ffn_in_bias
    activated, gelu_pull = jax.vjp(exact_gelu, pre_act)
    act_low = activated.astype(BF16)
    final = mixed + dot(act_low, ffn_out) + ffn_out_bias
    final_low = final.astype(BF16)
    upsampled = dot(final_low, up_weight) + up_bias
    outputs = (inputs.astype(F32) + upsampled.reshape(1, bytes_here, width)).astype(BF16)
    grad_up = cotangent.reshape(length, 3 * width)
    over_rows = ((0,), (0,))
    over_columns = ((1,), (1,))
    grad_up_weight = dot(final_low, grad_up, over_rows)
    grad_up_bias = jnp.sum(grad_up.astype(F32), axis=0)
    grad_final = dot(grad_up, up_weight, over_columns)
    grad_branch = grad_final.astype(BF16)
    grad_ffn_out = dot(act_low, grad_branch, over_rows)
    grad_ffn_out_bias = jnp.sum(grad_branch.astype(F32), axis=0)
    grad_act = dot(grad_branch, ffn_out, over_columns)
    grad_pre = gelu_pull(grad_act)[0].astype(BF16)
    grad_ffn_in = dot(ffn_input, grad_pre, over_rows)
    grad_ffn_in_bias = jnp.sum(grad_pre.astype(F32), axis=0)
    grad_normed_two = dot(grad_pre, ffn_in, over_columns)
    grad_from_two, grad_ln2_gain, grad_ln2_bias = norm_back(
        grad_normed_two, plain_two, inverse_two, ln2_gain
    )
    grad_mixed = grad_final + grad_from_two
    grad_attn_branch = grad_mixed.astype(BF16)
    grad_out_weight = dot(attended_low, grad_attn_branch, over_rows)
    grad_attended = dot(grad_attn_branch, out_weight, over_columns).astype(BF16)

    early = lax.psum(
        tuple(
            grad.astype(BF16) for grad in (grad_ffn_in, grad_ffn_out, grad_up_weight, grad_out_weight)
        ),
        ("dp", "seq"),
    )

    (grad_in,) = exchange(
        to_units_kernel, n, group, (heads_packed(grad_attended),), ((rounds, length // 2, PAIR),), 2
    )
    dq_out, dkv_out, grad_head_weight, grad_head_cb, grad_head_pb = pl.pallas_call(
        functools.partial(back_kernel, n, group, tile),
        grid=(rounds,),
        in_specs=common_specs
        + [
            turn_spec((length, HEAD)),
            turn_spec((length, 128)),
            turn_spec((length, tokens)),
            turn_spec((length // 2, PAIR)),
        ],
        out_specs=[
            turn_spec((length // 2, PAIR)),
            whole_spec((tokens, PAIR)),
            whole_spec((width, HEAD)),
            whole_spec((1, HEAD)),
            whole_spec((1, HEAD)),
        ],
        out_shape=[
            jax.ShapeDtypeStruct((rounds, length // 2, PAIR), BF16),
            jax.ShapeDtypeStruct((tokens, PAIR), BF16),
            jax.ShapeDtypeStruct((width, HEAD), F32),
            jax.ShapeDtypeStruct((1, HEAD), F32),
            jax.ShapeDtypeStruct((1, HEAD), F32),
        ],
        scratch_shapes=[pltpu.VMEM((tokens, PAIR), F32)],
        compiler_params=pltpu.CompilerParams(vmem_limit_bytes=56 * 2**20),
    )(*common, attended, total, keep, grad_in)
    dq_back, dkv_back = exchange(
        to_owners_kernel, n, group, (dq_out, dkv_out.reshape(n, length, PAIR)),
        ((HEADS, length // 2, PAIR), (group, HEADS, length, PAIR)), 3,
    )
    grad_query = heads_unpacked(dq_back)
    dkv_back = jnp.transpose(jnp.sum(dkv_back.astype(F32), 0), (1, 0, 2)).astype(BF16)
    grad_key_low = dkv_back[:, :, :HEAD].reshape(length, width)
    grad_value_low = dkv_back[:, :, HEAD:].reshape(length, width)

    def at_head(part, shape):
        return lax.dynamic_update_slice(
            jnp.zeros(shape, F32), part.reshape(shape[:-1] + (HEAD,)), (0,) * (len(shape) - 1) + (head * HEAD,)
        )

    grad_pos_weight = at_head(grad_head_weight, (width, width))
    grad_content_bias = at_head(grad_head_cb, (width,))
    grad_pos_bias = at_head(grad_head_pb, (width,))
    grad_query_weight = dot(attn_in, grad_query, over_rows)
    grad_key_weight = dot(attn_in, grad_key_low, over_rows)
    grad_value_weight = dot(attn_in, grad_value_low, over_rows)
    grad_normed_one = (
        dot(grad_query, query_weight, over_columns)
        + dot(grad_key_low, key_weight, over_columns)
        + dot(grad_value_low, value_weight, over_columns)
    )
    grad_from_one, grad_ln1_gain, grad_ln1_bias = norm_back(
        grad_normed_one, plain_one, inverse_one, ln1_gain
    )
    grad_pooled = (grad_mixed + grad_from_one).astype(BF16)
    grad_pool_weight = dot(pooled_in, grad_pooled, over_rows)
    grad_pool_bias = jnp.sum(grad_pooled.astype(F32), axis=0)
    grad_shifted = dot(grad_pooled, pool_weight, over_columns).reshape(1, bytes_here, width)
    incoming = passed_along(grad_shifted[:, :2, :], "seq", -1)
    input_grad = (
        cotangent.astype(F32) + jnp.concatenate([grad_shifted[:, 2:, :], incoming], 1)
    ).astype(BF16)
    late = lax.psum(
        tuple(
            grad.astype(BF16)
            for grad in (
                grad_pool_weight, grad_query_weight, grad_key_weight, grad_value_weight, grad_pos_weight,
            )
        ),
        ("dp", "seq"),
    )
    small_parts = (
        grad_pool_bias, grad_ln1_gain, grad_ln1_bias, grad_content_bias, grad_pos_bias,
        grad_ln2_gain, grad_ln2_bias, grad_ffn_in_bias, grad_ffn_out_bias, grad_up_bias,
    )
    small = lax.psum(jnp.concatenate(small_parts), ("dp", "seq"))
    cuts = np.cumsum([part.shape[0] for part in small_parts])[:-1].tolist()
    (
        sum_pool_bias, sum_ln1_gain, sum_ln1_bias, sum_content, sum_pos,
        sum_ln2_gain, sum_ln2_bias, sum_in_bias, sum_out_bias, sum_up_bias,
    ) = jnp.split(small, cuts)
    sum_in, sum_out, sum_up, sum_mix = (grad.astype(F32) for grad in early)
    sum_pool, sum_q, sum_k, sum_v, sum_p = (grad.astype(F32) for grad in late)
    return (
        outputs, input_grad, sum_pool, sum_pool_bias, sum_ln1_gain, sum_ln1_bias, sum_q, sum_k, sum_v,
        sum_mix, sum_p, sum_content, sum_pos, sum_ln2_gain, sum_ln2_bias, sum_in, sum_in_bias,
        sum_out, sum_out_bias, sum_up, sum_up_bias,
    )


def solution(mesh):
    split = P("dp", "seq", None)
    return jax.shard_map(
        body,
        mesh=mesh,
        in_specs=(split, P("dp", None)) + (P(),) * 19 + (split,),
        out_specs=(split, split) + (P(),) * 19,
        check_vma=False,
    )
```

```python
import functools
import types

import jax
import jax.numpy as jnp
import numpy as np
from jax import lax
from jax.experimental import pallas as pl
from jax.experimental.pallas import tpu as pltpu
from jax.sharding import PartitionSpec as P

HEADS = 8
ROWS = 2
HEAD = 64
PAIR = 2 * HEAD
MESH = pl.DeviceIdType.MESH
F32 = jnp.float32
BF16 = jnp.bfloat16

epsilon = 1e-05
masked_score = -1e30


def dot(left, right, dims=((1,), (0,))):
    return lax.dot_general(left, right, (dims, ((), ())), preferred_element_type=F32)


def passed_along(value, axis, steps):
    count = lax.axis_size(axis)
    first, last = (max(0, -steps), min(count, count - steps))
    return lax.ppermute(value, axis, [(source, source + steps) for source in range(first, last)])


def place_of(block, group):
    turn, spot = block // group, block % group
    return turn, jnp.where(turn % 2 == 0, spot, group - 1 - spot)


def block_of(turn, member, group):
    return turn * group + jnp.where(turn % 2 == 0, member, group - 1 - member)


def whereabouts(group):
    core, chip = lax.axis_index("dp"), lax.axis_index("seq")
    chips = group // 2
    unit = chip // chips
    member = (chip % chips) * 2 + core
    return core, chip, unit // HEADS, unit % HEADS, member


def chip_of(row, head, member, group):
    return (row * HEADS + head) * (group // 2) + member // 2, member % 2


def meet(n, group, to_units):
    core, chip, row, head, member = whereabouts(group)
    barrier = pltpu.get_barrier_semaphore()

    def greet(row_or_core, chip_at):
        away = jnp.logical_or(row_or_core != core, chip_at != chip)

        @pl.when(away)
        def _():
            pl.semaphore_signal(
                barrier, inc=1, device_id=(row_or_core, chip_at), device_id_type=MESH
            )

        return away.astype(jnp.int32)

    own_row = row == core
    if to_units:
        for s in range(n):
            greet(row, jnp.int32(s))
        mine = jnp.logical_and(chip // (HEADS * (group // 2)) == core, True)
        pl.semaphore_wait(barrier, HEADS * group - mine.astype(jnp.int32))
    else:
        for h in range(HEADS):
            for g in range(group):
                c, k = chip_of(core, h, g, group)
                greet(jnp.int32(k), c)
        pl.semaphore_wait(barrier, n - own_row.astype(jnp.int32))


def send(source, target, sems, core, chip):
    here_core, here_chip = lax.axis_index("dp"), lax.axis_index("seq")
    here = jnp.logical_and(core == here_core, chip == here_chip)

    @pl.when(here)
    def _():
        pltpu.make_async_copy(source, target, sems[1]).start()

    @pl.when(jnp.logical_not(here))
    def _():
        pltpu.make_async_remote_copy(
            source, target, sems[0], sems[1], device_id=(core, chip), device_id_type=MESH
        ).start()


def sent(source, sem, core, chip):
    here_core, here_chip = lax.axis_index("dp"), lax.axis_index("seq")
    here = jnp.logical_and(core == here_core, chip == here_chip)

    @pl.when(jnp.logical_not(here))
    def _():
        pltpu.make_async_copy(source, source, sem).wait()


def arrived(whole, sem):
    pltpu.make_async_copy(whole, whole, sem).wait()


def to_units_kernel(n, group, *refs):
    count = len(refs) - 2
    arrays, outs = refs[: count // 2], refs[count // 2 : count]
    send_sem, recv_sem = refs[count:]
    core, chip, row, head, member = whereabouts(group)
    turn, spot = place_of(chip, group)
    meet(n, group, True)
    jobs = []
    for h in range(HEADS):
        for index, (array, out) in enumerate(zip(arrays, outs)):
            sems = (send_sem.at[index], recv_sem.at[index])
            if index == 0:
                to_chip, to_core = chip_of(core, h, spot, group)
                jobs.append((array.at[h], out.at[turn], sems, to_core, to_chip))
            else:
                for g in range(group):
                    to_chip, to_core = chip_of(core, h, g, group)
                    jobs.append((array.at[h], out.at[chip], sems, jnp.int32(to_core), to_chip))
    for job in jobs:
        send(*job)
    for source, _, sems, to_core, to_chip in jobs:
        sent(source, sems[0], to_core, to_chip)
    for index, out in enumerate(outs):
        arrived(out, recv_sem.at[index])


def to_owners_kernel(n, group, *refs):
    count = len(refs) - 2
    arrays, outs = refs[: count // 2], refs[count // 2 : count]
    send_sem, recv_sem = refs[count:]
    core, chip, row, head, member = whereabouts(group)
    meet(n, group, False)
    jobs = []
    for turn in range(n // group):
        block = block_of(jnp.int32(turn), member, group)
        sems = (send_sem.at[0], recv_sem.at[0])
        jobs.append((arrays[0].at[turn], outs[0].at[head], sems, row, block))
    if len(arrays) > 1:
        for block in range(n):
            sems = (send_sem.at[1], recv_sem.at[1])
            jobs.append((arrays[1].at[block], outs[1].at[member, head], sems, row, jnp.int32(block)))
    for job in jobs:
        send(*job)
    for source, _, sems, to_core, to_chip in jobs:
        sent(source, sems[0], to_core, to_chip)
    for index, out in enumerate(outs):
        arrived(out, recv_sem.at[index])


def exchange(kernel, n, group, arrays, shapes, ident):
    vmem = pl.BlockSpec(memory_space=pltpu.VMEM)
    return pl.pallas_call(
        functools.partial(kernel, n, group),
        out_shape=[jax.ShapeDtypeStruct(shape, array.dtype) for shape, array in zip(shapes, arrays)],
        in_specs=[vmem] * len(arrays),
        out_specs=[vmem] * len(arrays),
        scratch_shapes=[
            pltpu.SemaphoreType.DMA((len(arrays),)),
            pltpu.SemaphoreType.DMA((len(arrays),)),
        ],
        compiler_params=pltpu.CompilerParams(
            collective_id=ident, has_side_effects=True, vmem_limit_bytes=48 * 2**20
        ),
    )(*arrays)


def unpacked(pair):
    return jnp.concatenate([pair[:, :HEAD], pair[:, HEAD:]], 0)


def packed(block):
    half = block.shape[0] // 2
    return jnp.concatenate([block[:half], block[half:]], 1)


def query_parts(q_pair, content_bias, pos_bias, pos_weight, turn_sin, turn_cos):
    query = unpacked(q_pair.astype(F32))
    query_u = (query + content_bias).astype(BF16)
    query_v = (query + pos_bias).astype(BF16)
    spread = dot(query_v, pos_weight, ((1,), (1,)))
    half = turn_sin.shape[1]
    lift, rest = spread[:, :half], spread[:, half:]
    on_sin = rest * turn_sin - lift * turn_cos
    on_cos = lift * turn_sin + rest * turn_cos
    turned = jnp.concatenate([on_sin, on_cos], 1)
    return query_u, query_v, turned


def attend_kernel(
    n, group, tile, q_ref, kv_ref, table_ref, sin_ref, cos_ref, weight_ref, cb_ref, pb_ref, bounds_ref,
    att_ref, low_ref, total_ref, keep_ref, score_ref, extra_ref,
):
    turn = pl.program_id(0)
    member = whereabouts(group)[4]
    block = block_of(turn, member, group)
    length = sin_ref.shape[0]
    tokens = n * length
    query_u, _, turned = query_parts(
        q_ref[...], cb_ref[...], pb_ref[...], weight_ref[...], sin_ref[...], cos_ref[...]
    )
    scale = HEAD**-0.5
    head_part = (query_u.astype(F32) * scale).astype(BF16)
    extra_ref[:, :HEAD] = head_part
    extra_ref[:, HEAD:PAIR] = jnp.zeros_like(head_part)
    extra_ref[:, PAIR:] = (turned * scale).astype(BF16)
    first = block * length
    tiles = (first + length + tile - 1) // tile
    low_bound, high_bound = bounds_ref[0], bounds_ref[1]
    places = first + lax.broadcasted_iota(jnp.int32, (length, 1), 0)
    opening = jnp.where(
        places >= high_bound, high_bound, jnp.where(places >= low_bound, low_bound, 0)
    )
    lanes = lax.broadcasted_iota(jnp.int32, (length, tile), 1)

    def score_step(step, top):
        start = pl.multiple_of(step * tile, tile)
        keys = kv_ref[pl.ds(start, tile), :]
        waves = table_ref[pl.ds(pl.multiple_of((n - 1 - block) * length + start, length), tile), :]
        score = dot(extra_ref[:, :PAIR], keys, ((1,), (1,))) + dot(
            extra_ref[:, PAIR:], waves, ((1,), (1,))
        )
        at = lanes + start
        allowed = jnp.logical_and(at <= places, at >= opening)
        score = jnp.where(allowed, score, masked_score)
        score_ref[:, pl.ds(start, tile)] = score
        for part in range(tile // 128):
            top = jnp.maximum(top, score[:, part * 128 : (part + 1) * 128])
        return top

    top = lax.fori_loop(0, tiles, score_step, jnp.full((length, 128), masked_score, F32))
    top = jnp.max(top, 1, keepdims=True)

    def value_step(step, state):
        total, summed = state
        start = pl.multiple_of(step * tile, tile)
        weight = jnp.exp(score_ref[:, pl.ds(start, tile)] - top)
        for part in range(tile // 128):
            total = total + weight[:, part * 128 : (part + 1) * 128]
        low = weight.astype(BF16)
        keep_ref[:, pl.ds(start, tile)] = low
        return total, summed + dot(low, kv_ref[pl.ds(start, tile), :])

    total, summed = lax.fori_loop(
        0, tiles, value_step, (jnp.zeros((length, 128), F32), jnp.zeros((length, PAIR), F32))
    )
    total = jnp.sum(total, 1, keepdims=True)
    attended = summed[:, HEAD:] / total
    att_ref[...] = attended
    total_ref[...] = jnp.broadcast_to(total, (length, 128))
    low_ref[...] = packed(attended).astype(BF16)


def back_kernel(
    n, group, tile, q_ref, kv_ref, table_ref, sin_ref, cos_ref, weight_ref, cb_ref, pb_ref,
    att_ref, total_ref, keep_ref, grad_ref,
    dq_ref, dkv_ref, dweight_ref, dcb_ref, dpb_ref, dkv_acc,
):
    turn = pl.program_id(0)
    member = whereabouts(group)[4]
    block = block_of(turn, member, group)
    length = sin_ref.shape[0]
    scale = HEAD**-0.5

    @pl.when(turn == 0)
    def _():
        dkv_acc[...] = jnp.zeros_like(dkv_acc)
        dweight_ref[...] = jnp.zeros_like(dweight_ref)
        dcb_ref[...] = jnp.zeros_like(dcb_ref)
        dpb_ref[...] = jnp.zeros_like(dpb_ref)

    query_u, query_v, _ = query_parts(
        q_ref[...], cb_ref[...], pb_ref[...], weight_ref[...], sin_ref[...], cos_ref[...]
    )
    head_part = (query_u.astype(F32) * scale).astype(BF16)
    grad = unpacked(grad_ref[...].astype(F32))
    inverse = 1.0 / total_ref[:, :1]
    delta = jnp.sum(grad * att_ref[...], 1, keepdims=True) * inverse
    grad_low = (grad * inverse).astype(BF16)
    nothing = jnp.zeros_like(grad_low)
    grad_wide = jnp.concatenate([nothing, grad_low], 1)
    query_wide = jnp.concatenate([head_part, nothing], 1)
    tiles = (block * length + length + tile - 1) // tile

    def step_over(step, state):
        near, far = state
        start = pl.multiple_of(step * tile, tile)
        keys = kv_ref[pl.ds(start, tile), :]
        waves = table_ref[pl.ds(pl.multiple_of((n - 1 - block) * length + start, length), tile), :]
        weight = keep_ref[:, pl.ds(start, tile)]
        grad_weight = dot(grad_wide, keys, ((1,), (1,)))
        grad_score = (weight.astype(F32) * (grad_weight - delta)).astype(BF16)
        near = near + dot(grad_score, keys)
        far = far + dot(grad_score, waves)
        dkv_acc[pl.ds(start, tile), :] += dot(grad_score, query_wide, ((0,), (0,))) + dot(
            weight, grad_wide, ((0,), (0,))
        )
        return near, far

    near, far = lax.fori_loop(
        0,
        tiles,
        step_over,
        (jnp.zeros((length, PAIR), F32), jnp.zeros((length, table_ref.shape[1]), F32)),
    )
    grad_u = near[:, :HEAD] * scale
    half = sin_ref.shape[1]
    turn_sin, turn_cos = sin_ref[...], cos_ref[...]
    on_sin, on_cos = far[:, :half] * scale, far[:, half:] * scale
    lift = on_cos * turn_sin - on_sin * turn_cos
    rest = on_cos * turn_cos + on_sin * turn_sin
    spread = jnp.concatenate([lift, rest], 1).astype(BF16)
    grad_v = dot(spread, weight_ref[...])
    dweight_ref[...] += dot(spread, query_v, ((0,), (0,)))
    dcb_ref[...] += jnp.sum(grad_u, 0, keepdims=True)
    dpb_ref[...] += jnp.sum(grad_v, 0, keepdims=True)
    dq_ref[...] = packed(grad_u + grad_v).astype(BF16)

    @pl.when(turn == pl.num_programs(0) - 1)
    def _():
        dkv_ref[...] = dkv_acc[...].astype(BF16)


def wave_tables(tokens, length, width):
    rates = 10000.0 ** (-2.0 * np.arange(width // 2, dtype=np.float64) / width)
    far = (np.arange(tokens + length, dtype=np.float64) - (tokens - length))[:, None] * rates
    near = np.arange(length, dtype=np.float64)[:, None] * rates
    table = np.concatenate([np.sin(far), np.cos(far)], 1)
    return (
        jnp.asarray(table, dtype=BF16),
        jnp.asarray(np.sin(near), dtype=F32),
        jnp.asarray(np.cos(near), dtype=F32),
    )


def whole_spec(shape):
    return pl.BlockSpec(shape, lambda turn: (0,) * len(shape))


def turn_spec(shape):
    return pl.BlockSpec((None,) + shape, lambda turn: (turn,) + (0,) * len(shape))


def layer_norm(hidden, gain, bias):
    average = jnp.mean(hidden, -1, keepdims=True)
    centred = hidden - average
    inverse = lax.rsqrt(jnp.mean(centred * centred, -1, keepdims=True) + epsilon)
    normed = centred * inverse
    return (normed * gain + bias, normed, inverse)


def norm_back(grad_out, normed, inverse, gain):
    scaled = grad_out * gain
    grad_in = inverse * (
        scaled
        - jnp.mean(scaled, -1, keepdims=True)
        - normed * jnp.mean(scaled * normed, -1, keepdims=True)
    )
    return (grad_in, jnp.sum(grad_out * normed, axis=0), jnp.sum(grad_out, axis=0))


def exact_gelu(value):
    return jax.nn.gelu(value, approximate=False)


def heads_packed(array):
    length = array.shape[0]
    split = array.reshape(2, length // 2, HEADS, HEAD)
    return jnp.transpose(split, (2, 1, 0, 3)).reshape(HEADS, length // 2, PAIR)


def heads_unpacked(array):
    half = array.shape[1]
    split = array.reshape(HEADS, half, 2, HEAD)
    return jnp.transpose(split, (2, 1, 0, 3)).reshape(2 * half, HEADS * HEAD)


def body(
    inputs, doc_bounds, pool_weight, pool_bias, ln1_gain, ln1_bias, query_weight, key_weight,
    value_weight, out_weight, pos_weight, content_bias, pos_bias, ln2_gain, ln2_bias, ffn_in,
    ffn_in_bias, ffn_out, ffn_out_bias, up_weight, up_bias, cotangent,
):
    _, bytes_here, width = inputs.shape
    length = bytes_here // 3
    n = lax.axis_size("seq")
    tokens = n * length
    group = 2 * n // (ROWS * HEADS)
    rounds = n // group
    tile = 2 * length
    row, head, member = whereabouts(group)[2:]

    all_bounds = lax.all_gather(doc_bounds, "dp", axis=0, tiled=True)
    bounds = lax.dynamic_slice(all_bounds, (row, 0), (1, 2))[0]
    table, turn_sin, turn_cos = wave_tables(tokens, length, width)
    head_weight = lax.dynamic_slice(pos_weight, (0, head * HEAD), (width, HEAD))
    head_cb = lax.dynamic_slice(content_bias, (head * HEAD,), (HEAD,))[None]
    head_pb = lax.dynamic_slice(pos_bias, (head * HEAD,), (HEAD,))[None]

    rim = passed_along(inputs[:, bytes_here - 2 :, :], "seq", 1)
    shifted = jnp.concatenate([rim, inputs[:, : bytes_here - 2, :]], 1)
    pooled_in = shifted.reshape(length, 3 * width)
    pooled = dot(pooled_in, pool_weight) + pool_bias
    normed_one, plain_one, inverse_one = layer_norm(pooled, ln1_gain, ln1_bias)
    attn_in = normed_one.astype(BF16)
    query = dot(attn_in, query_weight).astype(BF16)
    keys = dot(attn_in, key_weight).astype(BF16).reshape(length, HEADS, HEAD)
    values = dot(attn_in, value_weight).astype(BF16).reshape(length, HEADS, HEAD)
    q_out = heads_packed(query)
    kv_out = jnp.transpose(jnp.concatenate([keys, values], 2), (1, 0, 2))

    q_in, kv_in = exchange(
        to_units_kernel, n, group, (q_out, kv_out),
        ((rounds, length // 2, PAIR), (n, length, PAIR)), 0,
    )
    kv_in = kv_in.reshape(tokens, PAIR)

    common_specs = [
        turn_spec((length // 2, PAIR)),
        whole_spec((tokens, PAIR)),
        whole_spec(table.shape),
        whole_spec(turn_sin.shape),
        whole_spec(turn_cos.shape),
        whole_spec(head_weight.shape),
        whole_spec((1, HEAD)),
        whole_spec((1, HEAD)),
    ]
    common = (q_in, kv_in, table, turn_sin, turn_cos, head_weight, head_cb, head_pb)
    attended, att_low, total, keep = pl.pallas_call(
        functools.partial(attend_kernel, n, group, tile),
        grid=(rounds,),
        in_specs=common_specs + [pl.BlockSpec(memory_space=pltpu.SMEM)],
        out_specs=[
            turn_spec((length, HEAD)),
            turn_spec((length // 2, PAIR)),
            turn_spec((length, 128)),
            turn_spec((length, tokens)),
        ],
        out_shape=[
            jax.ShapeDtypeStruct((rounds, length, HEAD), F32),
            jax.ShapeDtypeStruct((rounds, length // 2, PAIR), BF16),
            jax.ShapeDtypeStruct((rounds, length, 128), F32),
            jax.ShapeDtypeStruct((rounds, length, tokens), BF16),
        ],
        scratch_shapes=[
            pltpu.VMEM((length, tokens), F32),
            pltpu.VMEM((length, PAIR + width), BF16),
        ],
        compiler_params=pltpu.CompilerParams(vmem_limit_bytes=56 * 2**20),
    )(*common, bounds)

    (att_back,) = exchange(
        to_owners_kernel, n, group, (att_low,), ((HEADS, length // 2, PAIR),), 1
    )
    attended_low = heads_unpacked(att_back)

    mixed = pooled + dot(attended_low, out_weight)
    normed_two, plain_two, inverse_two = layer_norm(mixed, ln2_gain, ln2_bias)
    ffn_input = normed_two.astype(BF16)
    pre_act = dot(ffn_input, ffn_in) + ffn_in_bias
    activated, gelu_pull = jax.vjp(exact_gelu, pre_act)
    act_low = activated.astype(BF16)
    final = mixed + dot(act_low, ffn_out) + ffn_out_bias
    final_low = final.astype(BF16)
    upsampled = dot(final_low, up_weight) + up_bias
    outputs = (inputs.astype(F32) + upsampled.reshape(1, bytes_here, width)).astype(BF16)
    grad_up = cotangent.reshape(length, 3 * width)
    over_rows = ((0,), (0,))
    over_columns = ((1,), (1,))
    grad_up_weight = dot(final_low, grad_up, over_rows)
    grad_up_bias = jnp.sum(grad_up.astype(F32), axis=0)
    grad_final = dot(grad_up, up_weight, over_columns)
    grad_branch = grad_final.astype(BF16)
    grad_ffn_out = dot(act_low, grad_branch, over_rows)
    grad_ffn_out_bias = jnp.sum(grad_branch.astype(F32), axis=0)
    grad_act = dot(grad_branch, ffn_out, over_columns)
    grad_pre = gelu_pull(grad_act)[0].astype(BF16)
    grad_ffn_in = dot(ffn_input, grad_pre, over_rows)
    grad_ffn_in_bias = jnp.sum(grad_pre.astype(F32), axis=0)
    grad_normed_two = dot(grad_pre, ffn_in, over_columns)
    grad_from_two, grad_ln2_gain, grad_ln2_bias = norm_back(
        grad_normed_two, plain_two, inverse_two, ln2_gain
    )
    grad_mixed = grad_final + grad_from_two
    grad_attn_branch = grad_mixed.astype(BF16)
    grad_out_weight = dot(attended_low, grad_attn_branch, over_rows)
    grad_attended = dot(grad_attn_branch, out_weight, over_columns).astype(BF16)

    early = lax.psum(
        tuple(
            grad.astype(BF16) for grad in (grad_ffn_in, grad_ffn_out, grad_up_weight, grad_out_weight)
        ),
        ("dp", "seq"),
    )

    (grad_in,) = exchange(
        to_units_kernel, n, group, (heads_packed(grad_attended),), ((rounds, length // 2, PAIR),), 2
    )
    dq_out, dkv_out, grad_head_weight, grad_head_cb, grad_head_pb = pl.pallas_call(
        functools.partial(back_kernel, n, group, tile),
        grid=(rounds,),
        in_specs=common_specs
        + [
            turn_spec((length, HEAD)),
            turn_spec((length, 128)),
            turn_spec((length, tokens)),
            turn_spec((length // 2, PAIR)),
        ],
        out_specs=[
            turn_spec((length // 2, PAIR)),
            whole_spec((tokens, PAIR)),
            whole_spec((width, HEAD)),
            whole_spec((1, HEAD)),
            whole_spec((1, HEAD)),
        ],
        out_shape=[
            jax.ShapeDtypeStruct((rounds, length // 2, PAIR), BF16),
            jax.ShapeDtypeStruct((tokens, PAIR), BF16),
            jax.ShapeDtypeStruct((width, HEAD), F32),
            jax.ShapeDtypeStruct((1, HEAD), F32),
            jax.ShapeDtypeStruct((1, HEAD), F32),
        ],
        scratch_shapes=[pltpu.VMEM((tokens, PAIR), F32)],
        compiler_params=pltpu.CompilerParams(vmem_limit_bytes=56 * 2**20),
    )(*common, attended, total, keep, grad_in)
    dq_back, dkv_back = exchange(
        to_owners_kernel, n, group, (dq_out, dkv_out.reshape(n, length, PAIR)),
        ((HEADS, length // 2, PAIR), (group, HEADS, length, PAIR)), 3,
    )
    grad_query = heads_unpacked(dq_back)
    dkv_back = jnp.transpose(jnp.sum(dkv_back.astype(F32), 0), (1, 0, 2)).astype(BF16)
    grad_key_low = dkv_back[:, :, :HEAD].reshape(length, width)
    grad_value_low = dkv_back[:, :, HEAD:].reshape(length, width)

    def at_head(part, shape):
        return lax.dynamic_update_slice(
            jnp.zeros(shape, F32), part.reshape(shape[:-1] + (HEAD,)), (0,) * (len(shape) - 1) + (head * HEAD,)
        )

    grad_pos_weight = at_head(grad_head_weight, (width, width))
    grad_content_bias = at_head(grad_head_cb, (width,))
    grad_pos_bias = at_head(grad_head_pb, (width,))
    grad_query_weight = dot(attn_in, grad_query, over_rows)
    grad_key_weight = dot(attn_in, grad_key_low, over_rows)
    grad_value_weight = dot(attn_in, grad_value_low, over_rows)
    grad_normed_one = (
        dot(grad_query, query_weight, over_columns)
        + dot(grad_key_low, key_weight, over_columns)
        + dot(grad_value_low, value_weight, over_columns)
    )
    grad_from_one, grad_ln1_gain, grad_ln1_bias = norm_back(
        grad_normed_one, plain_one, inverse_one, ln1_gain
    )
    grad_pooled = (grad_mixed + grad_from_one).astype(BF16)
    grad_pool_weight = dot(pooled_in, grad_pooled, over_rows)
    grad_pool_bias = jnp.sum(grad_pooled.astype(F32), axis=0)
    grad_shifted = dot(grad_pooled, pool_weight, over_columns).reshape(1, bytes_here, width)
    incoming = passed_along(grad_shifted[:, :2, :], "seq", -1)
    input_grad = (
        cotangent.astype(F32) + jnp.concatenate([grad_shifted[:, 2:, :], incoming], 1)
    ).astype(BF16)
    late = lax.psum(
        tuple(
            grad.astype(BF16)
            for grad in (
                grad_pool_weight, grad_query_weight, grad_key_weight, grad_value_weight, grad_pos_weight,
            )
        ),
        ("dp", "seq"),
    )
    small_parts = (
        grad_pool_bias, grad_ln1_gain, grad_ln1_bias, grad_content_bias, grad_pos_bias,
        grad_ln2_gain, grad_ln2_bias, grad_ffn_in_bias, grad_ffn_out_bias, grad_up_bias,
    )
    small = lax.psum(jnp.concatenate(small_parts), ("dp", "seq"))
    cuts = np.cumsum([part.shape[0] for part in small_parts])[:-1].tolist()
    (
        sum_pool_bias, sum_ln1_gain, sum_ln1_bias, sum_content, sum_pos,
        sum_ln2_gain, sum_ln2_bias, sum_in_bias, sum_out_bias, sum_up_bias,
    ) = jnp.split(small, cuts)
    sum_in, sum_out, sum_up, sum_mix = (grad.astype(F32) for grad in early)
    sum_pool, sum_q, sum_k, sum_v, sum_p = (grad.astype(F32) for grad in late)
    return (
        outputs, input_grad, sum_pool, sum_pool_bias, sum_ln1_gain, sum_ln1_bias, sum_q, sum_k, sum_v,
        sum_mix, sum_p, sum_content, sum_pos, sum_ln2_gain, sum_ln2_bias, sum_in, sum_in_bias,
        sum_out, sum_out_bias, sum_up, sum_up_bias,
    )


EARLY_ROWS, LATE_ROWS = 6144, 3584
SMALL_ROWS = 16
FAR_SHARE = {EARLY_ROWS: 768, LATE_ROWS: 512}
OVER_ROWS = ((0,), (0,))
OVER_COLUMNS = ((1,), (1,))


class Reduction:
    def __init__(self, buffer, bufs, sems, free, small=None):
        self.buffer, self.sems, self.free = buffer, sems, free
        (self.from_core, self.near_one, self.near_two, self.near_z, self.far_z, self.far_one, self.far_two) = bufs
        self.small = small
        rows = buffer.shape[0]
        self.half = rows // 2
        self.far_size = FAR_SHARE[rows]
        self.near_size = self.half - self.far_size
        core, chip = lax.axis_index("dp"), lax.axis_index("seq")
        self.core, self.chip = core, chip
        self.z = chip // 4
        bit_x, bit_y = chip % 2, (chip // 2) % 2
        first_x = core == 0
        self.peer_x, self.peer_y = chip + 1 - 2 * bit_x, chip + 2 - 4 * bit_y
        self.bit_one = jnp.where(first_x, bit_x, bit_y)
        self.bit_two = jnp.where(first_x, bit_y, bit_x)
        step_one = jnp.where(first_x, 1, 2)
        step_two = 3 - step_one
        self.peer_one = chip + jnp.where(self.bit_one == 0, step_one, -step_one)
        self.peer_two = chip + jnp.where(self.bit_two == 0, step_two, -step_two)
        base = core * self.half
        near, far = self.near_size, self.far_size
        self.near_at = base
        self.near_one_at = base + self.bit_one * (near // 2)
        self.near_one_out = base + (1 - self.bit_one) * (near // 2)
        self.near_two_at = self.near_one_at + self.bit_two * (near // 4)
        self.near_two_out = self.near_one_at + (1 - self.bit_two) * (near // 4)
        self.near_z_at = self.near_two_at + self.z * (near // 16)
        self.far_at = base + near
        self.far_z_at = self.far_at + self.z * (far // 4)
        self.far_one_at = self.far_z_at + self.bit_one * (far // 8)
        self.far_one_out = self.far_z_at + (1 - self.bit_one) * (far // 8)
        self.far_two_at = self.far_one_at + self.bit_two * (far // 16)
        self.far_two_out = self.far_one_at + (1 - self.bit_two) * (far // 16)

    def rows(self, start, size):
        return self.buffer.at[pl.ds(pl.multiple_of(start, 16), size)]

    def copy(self, index, source, target, core, chip):
        return pltpu.make_async_remote_copy(
            source, target, self.sems.at[0, index], self.sems.at[1, index],
            device_id=(core, chip), device_id_type=MESH,
        )

    def go(self, index, source, target, core, chip):
        self.copy(index, source, target, core, chip).start()

    def done(self, index, source):
        copy = self.copy(index, source, source, self.core, self.peer_one)
        copy.wait_send()
        copy.wait_recv()


    def freed(self, index, *devices):
        for core, chip in devices:
            pl.semaphore_signal(self.free.at[index], inc=1, device_id=(core, chip), device_id_type=MESH)

    def z_peers(self):
        return [(self.core, self.z_chip(away)[1]) for away in range(3)]

    def is_free(self, index, count=1):
        pl.semaphore_wait(self.free.at[index], count)

    def add(self, start, size, parts):
        chunk = min(size, 256)
        while size % chunk:
            chunk -= 16

        def one(step, carry):
            at = pl.ds(pl.multiple_of(start + step * chunk, 16), chunk)
            here = pl.ds(pl.multiple_of(step * chunk, 16), chunk)
            total = self.buffer[at].astype(F32)
            for part in parts:
                total = total + part[here].astype(F32)
            self.buffer[at] = total.astype(BF16)
            return carry

        lax.fori_loop(0, size // chunk, one, 0)

    def z_chip(self, away):
        there = (self.z + 1 + away) % 4
        return there, self.chip + (there - self.z) * 4

    def small_go(self, stage, core, chip):
        if self.small is not None:
            own, taken = self.small
            self.go(18 + stage, own, taken.at[stage], core, chip)

    def small_done(self, stage):
        if self.small is not None:
            own, taken = self.small
            self.done(18 + stage, own)
            own[...] = own[...] + taken[stage]

    def small_z_go(self):
        if self.small is not None:
            own, taken = self.small
            taken[3 + self.z] = own[...]
            for away in range(3):
                peer = self.z_chip(away)[1]
                self.go(21 + away, own, taken.at[3 + self.z], self.core, peer)

    def small_z_done(self):
        if self.small is not None:
            own, taken = self.small
            for away in range(3):
                self.done(21 + away, own)
            own[...] = (taken[3] + taken[4]) + (taken[5] + taken[6])

    def step(self, number):
        near, far = self.near_size, self.far_size
        core, chip = self.core, self.chip
        if number == 0:
            self.go(0, self.rows((1 - core) * self.half, self.half), self.from_core, 1 - core, chip)
            self.small_go(0, 1 - core, chip)
        if number == 1:
            self.done(0, self.from_core)
            self.freed(0, (1 - core, chip))
            self.add(core * self.half, self.half, (self.from_core,))
            self.go(1, self.rows(self.near_one_out, near // 2), self.near_one, core, self.peer_one)
            for away in range(3):
                there, peer = self.z_chip(away)
                self.go(3 + away, self.rows(self.far_at + there * (far // 4), far // 4), self.far_z.at[away], core, peer)
            self.small_done(0)
            self.small_go(1, core, self.peer_x)
        if number == 2:
            self.done(1, self.near_one)
            self.freed(1, (core, self.peer_one))
            self.add(self.near_one_at, near // 2, (self.near_one,))
            self.go(2, self.rows(self.near_two_out, near // 4), self.near_two, core, self.peer_two)
            for away in range(3):
                self.done(3 + away, self.far_z.at[away])
            self.freed(4, *self.z_peers())
            self.add(self.far_z_at, far // 4, tuple(self.far_z.at[away] for away in range(3)))
            self.go(6, self.rows(self.far_one_out, far // 8), self.far_one, core, self.peer_one)
            self.small_done(1)
            self.small_go(2, core, self.peer_y)
        if number == 3:
            self.done(2, self.near_two)
            self.freed(2, (core, self.peer_two))
            self.add(self.near_two_at, near // 4, (self.near_two,))
            for away in range(3):
                there, peer = self.z_chip(away)
                self.go(
                    7 + away, self.rows(self.near_two_at + there * (near // 16), near // 16),
                    self.near_z.at[away], core, peer,
                )
            self.done(6, self.far_one)
            self.freed(5, (core, self.peer_one))
            self.add(self.far_one_at, far // 8, (self.far_one,))
            self.go(10, self.rows(self.far_two_out, far // 16), self.far_two, core, self.peer_two)
            self.small_done(2)
            self.small_z_go()
        if number == 4:
            for away in range(3):
                self.done(7 + away, self.near_z.at[away])
            self.freed(3, *self.z_peers())
            self.add(self.near_z_at, near // 16, tuple(self.near_z.at[away] for away in range(3)))
            own = self.rows(self.near_z_at, near // 16)
            self.is_free(3, 3)
            for away in range(3):
                self.go(11 + away, own, own, core, self.z_chip(away)[1])
            self.done(10, self.far_two)
            self.freed(6, (core, self.peer_two))
            self.add(self.far_two_at, far // 16, (self.far_two,))
            own = self.rows(self.far_two_at, far // 16)
            self.is_free(6)
            self.go(14, own, own, core, self.peer_two)
            self.small_z_done()
        if number == 5:
            for away in range(3):
                self.done(11 + away, self.rows(self.near_z_at, near // 16))
            own = self.rows(self.near_two_at, near // 4)
            self.is_free(2)
            self.go(15, own, own, core, self.peer_two)
            self.done(14, self.rows(self.far_two_at, far // 16))
            own = self.rows(self.far_one_at, far // 8)
            self.is_free(5)
            self.go(16, own, own, core, self.peer_one)
        if number == 6:
            self.done(15, self.rows(self.near_two_at, near // 4))
            own = self.rows(self.near_one_at, near // 2)
            self.is_free(1)
            self.go(17, own, own, core, self.peer_one)
            self.done(16, self.rows(self.far_one_at, far // 8))
            own = self.rows(self.far_z_at, far // 4)
            self.is_free(4, 3)
            for away in range(3):
                self.go(24 + away, own, own, core, self.z_chip(away)[1])
        if number == 7:
            self.done(17, self.rows(self.near_one_at, near // 2))
            own = self.rows(self.near_at, near)
            self.is_free(0)
            self.go(27, own, own, 1 - core, chip)
            for away in range(3):
                self.done(24 + away, self.rows(self.far_z_at, far // 4))
            own = self.rows(self.far_at, far)
            self.go(28, own, own, 1 - core, chip)
        if number == 8:
            self.done(27, self.rows(self.near_at, near))
            self.done(28, self.rows(self.far_at, far))


REDUCTION_SEMS = 29


def reduction_scratch(rows):
    far = FAR_SHARE[rows]
    near = rows // 2 - far
    return [
        pltpu.VMEM(shape + (512,), BF16)
        for shape in (
            (rows // 2,), (near // 2,), (near // 4,), (3, near // 16), (3, far // 4), (far // 8,), (far // 16,),
        )
    ]


def gelu_pair(value):
    falling = jnp.exp(value * value * -0.5)
    turn = 1.0 / (1.0 + 0.3275911 * 0.7071067811865476 * jnp.abs(value))
    series = turn * (
        0.254829592
        + turn * (-0.284496736 + turn * (1.421413741 + turn * (-1.453152027 + turn * 1.061405429)))
    )
    tail = 0.5 * series * falling
    share = jnp.where(value >= 0, 1.0 - tail, tail)
    return value * share, share + value * falling * 0.3989422804014327


def norm_parts(hidden):
    average = jnp.mean(hidden, -1, keepdims=True)
    centred = hidden - average
    inverse = lax.rsqrt(jnp.mean(centred * centred, -1, keepdims=True) + epsilon)
    return centred * inverse, inverse


def norm_grad(grad_out, normed, inverse, gain):
    scaled = grad_out * gain
    return inverse * (
        scaled
        - jnp.mean(scaled, -1, keepdims=True)
        - normed * jnp.mean(scaled * normed, -1, keepdims=True)
    )


def column_sum(value):
    return jnp.sum(value, 0, keepdims=True)


def layer_kernel(n, length, layout, *refs):
    taken = iter(refs)
    given, vectors, outs, scratch = ({name: next(taken) for name in part} for part in layout)
    r = types.SimpleNamespace(**vectors, **outs, **scratch)
    group = 2
    rounds = n // group
    tile = 2 * length
    half_len = length // 2
    width = 512
    scale = HEAD**-0.5
    core, chip, row, head, member = whereabouts(group)
    count = 2 * n
    me = core * n + chip

    loads = {}
    r.early_parts, r.late_parts = refs[-14:-7], refs[-7:]
    for index, (name, source) in enumerate(given.items()):
        loads[name] = pltpu.make_async_copy(source, scratch[name], r.load_sem.at[index])
        loads[name].start()

    def ready(*which):
        for ref in which:
            next(loads[name] for name in given if scratch[name] is ref).wait()

    barrier = pltpu.get_barrier_semaphore()

    def greet(step, carry):
        other = (me + step) % count
        pl.semaphore_signal(barrier, inc=1, device_id=(other // n, other % n), device_id_type=MESH)
        return carry

    lax.fori_loop(1, count, greet, 0)

    low_bound, high_bound = r.bounds[0, 0], r.bounds[0, 1]
    r.edges[core, :8] = jnp.full((8, 128), low_bound, jnp.int32)
    r.edges[core, 8:] = jnp.full((8, 128), high_bound, jnp.int32)
    ready(r.x3, r.pool_w)
    own = dot(r.x3[:, :width], r.pool_w[2 * width :])
    before = dot(r.x3[:, width:], r.pool_w[: 2 * width])
    pl.semaphore_wait(barrier, count - 1)

    def edge_copy():
        return pltpu.make_async_remote_copy(
            r.edges.at[core], r.edges.at[core], r.side_sem.at[0], r.side_sem.at[1],
            device_id=(1 - core, chip), device_id_type=MESH,
        )

    def rim_copy():
        return pltpu.make_async_remote_copy(
            r.x3.at[length - 16 :, width:], r.rim, r.side_sem.at[2], r.side_sem.at[3],
            device_id=(core, (chip + 1) % n), device_id_type=MESH,
        )

    edge_copy().start()

    @pl.when(chip < n - 1)
    def _():
        rim_copy().start()

    @pl.when(chip == 0)
    def _():
        r.rim[...] = jnp.zeros_like(r.rim)

    @pl.when(chip > 0)
    def _():
        rim_copy().wait_recv()

    rim_sum = dot(r.rim[...], r.pool_w[: 2 * width])
    at_row = lax.broadcasted_iota(jnp.int32, (length, width), 0)
    before = jnp.where(at_row == 0, rim_sum[15:16], pltpu.roll(before, 1, 0))
    pooled = own + before + r.pool_b[...]
    r.pooled[...] = pooled
    plain, _ = norm_parts(pooled)
    attn_in = (plain * r.ln1_g[...] + r.ln1_b[...]).astype(BF16)
    r.attn_in[...] = attn_in
    ready(r.q_w, r.k_w, r.v_w)
    query = dot(attn_in, r.q_w[...])
    keys = dot(attn_in, r.k_w[...])
    values = dot(attn_in, r.v_w[...])
    for h in range(HEADS):
        at = slice(h * HEAD, (h + 1) * HEAD)
        r.q_out[h] = packed(query[:, at]).astype(BF16)
        r.kv_out[h] = jnp.concatenate([keys[:, at], values[:, at]], 1).astype(BF16)
    turn_to, spot_to = place_of(chip, group)

    def q_jobs(array, out, sem, recv):
        jobs = []
        for h in range(HEADS):
            to_chip, to_core = chip_of(core, h, spot_to, group)
            jobs.append((array.at[h], out.at[turn_to], (sem, recv.at[turn_to]), to_core, to_chip))
        return jobs

    kv_jobs = []
    for h in range(HEADS):
        for g in range(group):
            to_chip, to_core = chip_of(core, h, g, group)
            kv_jobs.append(
                (r.kv_out.at[h], r.kv.at[chip], (r.send_sem.at[1], r.kv_sem.at[chip]), jnp.int32(to_core), to_chip)
            )
    first_jobs = q_jobs(r.q_out, r.q, r.send_sem.at[0], r.q_sem) + kv_jobs
    for job in first_jobs:
        send(*job)

    ready(r.ct3, r.up_w, r.ffn_out)
    grad_final = dot(r.ct3[...], r.up_w[...], OVER_COLUMNS)
    r.grad_final[...] = grad_final
    grad_branch = grad_final.astype(BF16)
    r.grad_branch[...] = grad_branch
    for part in range(4):
        at = slice(part * width, (part + 1) * width)
        r.grad_act[:, at] = dot(grad_branch, r.ffn_out[at], OVER_COLUMNS)
    small = r.small
    small[...] = jnp.zeros_like(small)
    small[11:12] = column_sum(grad_branch.astype(F32))
    for part in range(3):
        at = slice(part * width, (part + 1) * width)
        small[12 + part : 13 + part] = column_sum(r.ct3[:, at].astype(F32))

    ready(r.pos_w, r.table)
    odd = head % 2 == 1
    pair_at = pl.ds(pl.multiple_of((head // 2) * PAIR, PAIR), PAIR)

    def of_head(ref):
        both = ref[:, pair_at].astype(F32)
        return jnp.where(odd, both[:, HEAD:], both[:, :HEAD])

    r.head_w[...] = of_head(r.pos_w).astype(BF16)
    content_bias, pos_bias = of_head(r.content), of_head(r.pos)
    edge_copy().wait_send()
    edge_copy().wait_recv()
    low_edge = r.edges[row, 0:1, 0:1]
    high_edge = r.edges[row, 8:9, 0:1]
    half = width // 2
    lanes = lax.broadcasted_iota(jnp.int32, (length, tile), 1)

    def rows_of(array):
        return pl.ds(pl.multiple_of(array, length), tile)

    def attend(turn, carry):
        block = block_of(turn, member, group)
        arrived(r.q.at[turn], r.q_sem.at[turn])
        for other in range(group):
            arrived(r.kv.at[turn * group + other], r.kv_sem.at[turn * group + other])
        query_u, _, turned = query_parts(
            r.q[turn], content_bias, pos_bias, r.head_w[...], r.sines[...], r.cosines[...]
        )
        head_part = (query_u.astype(F32) * scale).astype(BF16)
        r.extra[:, :PAIR] = jnp.concatenate([head_part, jnp.zeros_like(head_part)], 1)
        r.extra[:, PAIR:] = (turned * scale).astype(BF16)
        places = block * length + lax.broadcasted_iota(jnp.int32, (length, 1), 0)
        opening = jnp.where(places >= high_edge, high_edge, jnp.where(places >= low_edge, low_edge, 0))

        def score_step(step, top):
            pair = r.kv[pl.ds(step * group, group)].reshape(tile, PAIR)
            waves = r.table[rows_of((n - 1 - block) * length + step * tile), :]
            score = dot(r.extra[:, :PAIR], pair, OVER_COLUMNS) + dot(r.extra[:, PAIR:], waves, OVER_COLUMNS)
            at = lanes + step * tile
            allowed = jnp.logical_and(at <= places, at >= opening)
            score = jnp.where(allowed, score, masked_score)
            r.score[step] = score
            for part in range(tile // 128):
                top = jnp.maximum(top, score[:, part * 128 : (part + 1) * 128])
            return top

        top = lax.fori_loop(0, turn + 1, score_step, jnp.full((length, 128), masked_score, F32))
        top = jnp.max(top, 1, keepdims=True)

        def value_step(step, state):
            total, summed = state
            weight = jnp.exp(r.score[step] - top)
            for part in range(tile // 128):
                total = total + weight[:, part * 128 : (part + 1) * 128]
            low = weight.astype(BF16)
            r.keep[turn * (turn + 1) // 2 + step] = low
            pair = r.kv[pl.ds(step * group, group)].reshape(tile, PAIR)
            return total, summed + dot(low, pair)

        total, summed = lax.fori_loop(
            0, turn + 1, value_step, (jnp.zeros((length, 128), F32), jnp.zeros((length, PAIR), F32))
        )
        inverse = 1.0 / jnp.sum(total, 1, keepdims=True)
        attended = summed[:, HEAD:] * inverse
        r.att[turn] = jnp.concatenate([jnp.broadcast_to(inverse, (length, HEAD)), attended], 1)
        r.att_out[turn] = packed(attended).astype(BF16)
        send(
            r.att_out.at[turn], r.att_in.at[head], (r.send_sem.at[2], r.att_sem.at[0]), row, block
        )
        return carry

    lax.fori_loop(0, rounds, attend, 0)
    for source, _, sems, to_core, to_chip in first_jobs:
        sent(source, sems[0], to_core, to_chip)

    def joined(get):
        parts = [get(h) for h in range(HEADS)]
        upper = jnp.concatenate([part[:, :HEAD] for part in parts], 1)
        lower = jnp.concatenate([part[:, HEAD:] for part in parts], 1)
        return jnp.concatenate([upper, lower], 0)

    arrived(r.att_in, r.att_sem.at[0])
    ready(r.out_w, r.ffn_in)
    att_low = joined(lambda h: r.att_in[h].astype(F32)).astype(BF16)
    r.att_low[...] = att_low
    mixed = r.pooled[...] + dot(att_low, r.out_w[...])
    r.mixed[...] = mixed
    plain_two, inverse_two = norm_parts(mixed)
    ffn_input = (plain_two * r.ln2_g[...] + r.ln2_b[...]).astype(BF16)
    r.ffn_input[...] = ffn_input
    grad_normed = jnp.zeros((length, width), F32)
    for part in range(4):
        at = slice(part * width, (part + 1) * width)
        pre_act = dot(ffn_input, r.ffn_in[:, at]) + r.ffn_in_b[:, at]
        act, slope = gelu_pair(pre_act)
        r.act_low[:, at] = act.astype(BF16)
        grad_pre = (r.grad_act[:, at] * slope).astype(BF16)
        r.grad_pre[:, at] = grad_pre
        small[7 + part : 8 + part] = column_sum(grad_pre.astype(F32))
        grad_normed = grad_normed + dot(grad_pre, r.ffn_in[:, at], OVER_COLUMNS)
    small[5:6] = column_sum(grad_normed * plain_two)
    small[6:7] = column_sum(grad_normed)
    grad_mixed = r.grad_final[...] + norm_grad(grad_normed, plain_two, inverse_two, r.ln2_g[...])
    r.grad_final[...] = grad_mixed
    grad_mixed_low = grad_mixed.astype(BF16)
    grad_att = dot(grad_mixed_low, r.out_w[...], OVER_COLUMNS)
    for h in range(HEADS):
        r.q_out[h] = packed(grad_att[:, h * HEAD : (h + 1) * HEAD]).astype(BF16)
    second_jobs = q_jobs(r.q_out, r.grad, r.send_sem.at[3], r.grad_sem)
    for job in second_jobs:
        send(*job)

    early, late = r.early, r.late
    for part in range(4):
        at = slice(part * width, (part + 1) * width)
        early[at] = dot(r.ffn_input[...], r.grad_pre[:, at], OVER_ROWS).astype(BF16)
        early[2048 + part * width : 2048 + (part + 1) * width] = dot(
            r.act_low[:, at], r.grad_branch[...], OVER_ROWS
        ).astype(BF16)
    early[5632:] = dot(r.att_low[...], grad_mixed_low, OVER_ROWS).astype(BF16)
    final_low = (r.mixed[...] + dot(r.act_low[...], r.ffn_out[...]) + r.ffn_out_b[...]).astype(BF16)
    for part in range(3):
        at = slice(part * width, (part + 1) * width)
        early[4096 + part * width : 4096 + (part + 1) * width] = dot(final_low, r.ct3[:, at], OVER_ROWS).astype(BF16)
    first_sum = Reduction(early, r.early_parts, r.early_sem, r.early_free)
    first_sum.step(0)
    for part in range(3):
        at = slice(part * width, (part + 1) * width)
        lifted = dot(final_low, r.up_w[:, at]) + r.up_b[:, at]
        r.out3[:, at] = (r.x3[:, at].astype(F32) + lifted).astype(BF16)

    r.dkv[...] = jnp.zeros_like(r.dkv)
    r.dhead[...] = jnp.zeros_like(r.dhead)
    r.dbias[...] = jnp.zeros_like(r.dbias)

    def back(index, carry):
        turn = rounds - 1 - index
        block = block_of(turn, member, group)
        arrived(r.grad.at[turn], r.grad_sem.at[turn])
        query = unpacked(r.q[turn].astype(F32))
        query_u = ((query + content_bias).astype(BF16).astype(F32) * scale).astype(BF16)
        query_v = (query + pos_bias).astype(BF16)
        grad = unpacked(r.grad[turn].astype(F32))
        inverse = r.att[turn][:, :HEAD]
        grad_part = grad * inverse
        delta = jnp.sum(grad_part * r.att[turn][:, HEAD:], 1, keepdims=True)
        nothing = jnp.zeros((length, HEAD), F32)
        r.extra[:, :PAIR] = jnp.concatenate([nothing, grad_part], 1).astype(BF16)
        r.extra[:, PAIR : 2 * PAIR] = jnp.concatenate([query_u.astype(F32), nothing], 1).astype(BF16)
        r.near[...] = jnp.zeros_like(r.near)
        r.far[...] = jnp.zeros_like(r.far)

        def step_over(step, inner):
            pair = r.kv[pl.ds(step * group, group)].reshape(tile, PAIR)
            waves = r.table[rows_of((n - 1 - block) * length + step * tile), :]
            weight = r.keep[turn * (turn + 1) // 2 + step]
            grad_weight = dot(r.extra[:, :PAIR], pair, OVER_COLUMNS)
            grad_score = (weight.astype(F32) * (grad_weight - delta)).astype(BF16)
            r.near[...] += dot(grad_score, pair)
            r.far[...] += dot(grad_score, waves)
            at = pl.ds(pl.multiple_of(step * tile, tile), tile)
            r.dkv[at] += dot(grad_score, r.extra[:, PAIR : 2 * PAIR], OVER_ROWS) + dot(
                weight, r.extra[:, :PAIR], OVER_ROWS
            )
            return inner

        lax.fori_loop(0, turn + 1, step_over, 0)
        at = pl.ds(pl.multiple_of(turn * tile, tile), tile)
        r.dkv_out[pl.ds(turn * group, group)] = r.dkv[at].astype(BF16).reshape(group, length, PAIR)
        for other in range(group):
            key_block = turn * group + other
            send(
                r.dkv_out.at[key_block], r.dkv_in.at[member, head],
                (r.send_sem.at[4], r.dkv_sem.at[0]), row, key_block,
            )
        grad_u = r.near[:, :HEAD] * scale
        turn_sin, turn_cos = r.sines[...], r.cosines[...]
        on_sin, on_cos = r.far[:, :half] * scale, r.far[:, half:] * scale
        lift = on_cos * turn_sin - on_sin * turn_cos
        rest = on_cos * turn_cos + on_sin * turn_sin
        spread = jnp.concatenate([lift, rest], 1).astype(BF16)
        grad_v = dot(spread, r.head_w[...])
        r.dhead[...] += dot(spread, query_v, OVER_ROWS)
        r.dbias[0:1] += column_sum(grad_u)
        r.dbias[1:2] += column_sum(grad_v)
        r.dq_out[turn] = packed(grad_u + grad_v).astype(BF16)
        send(r.dq_out.at[turn], r.dq_in.at[head], (r.send_sem.at[5], r.dq_sem.at[0]), row, block)
        for when, number in EARLY_STEPS:

            @pl.when(index == when)
            def _(number=number):
                first_sum.step(number)

        return carry

    lax.fori_loop(0, rounds, back, 0)
    first_left = [number for number in range(1, 9) if number not in [number for _, number in EARLY_STEPS]]

    late[2048 + 1024 :] = jnp.zeros((512, 512), BF16)
    dhead = r.dhead[...]
    nothing = jnp.zeros_like(dhead)
    late[3072:, pair_at] = jnp.where(
        odd, jnp.concatenate([nothing, dhead], 1), jnp.concatenate([dhead, nothing], 1)
    ).astype(BF16)
    nothing = jnp.zeros((2, HEAD), F32)
    dbias = r.dbias[...][:2]
    small[3:5, pair_at] = jnp.where(
        odd, jnp.concatenate([nothing, dbias], 1), jnp.concatenate([dbias, nothing], 1)
    )
    for source, _, sems, to_core, to_chip in second_jobs:
        sent(source, sems[0], to_core, to_chip)
    for turn in range(rounds):
        block = block_of(jnp.int32(turn), member, group)
        sent(r.att_out.at[turn], r.send_sem.at[2], row, block)
        sent(r.dq_out.at[turn], r.send_sem.at[5], row, block)
    for block in range(n):
        sent(r.dkv_out.at[block], r.send_sem.at[4], row, jnp.int32(block))
    arrived(r.dq_in, r.dq_sem.at[0])
    arrived(r.dkv_in, r.dkv_sem.at[0])
    grad_query = joined(lambda h: r.dq_in[h].astype(F32)).astype(BF16)
    both = [r.dkv_in[0, h].astype(F32) + r.dkv_in[1, h].astype(F32) for h in range(HEADS)]
    grad_keys = jnp.concatenate([part[:, :HEAD] for part in both], 1).astype(BF16)
    grad_values = jnp.concatenate([part[:, HEAD:] for part in both], 1).astype(BF16)
    attn_in = r.attn_in[...]
    late[1536:2048] = dot(attn_in, grad_query, OVER_ROWS).astype(BF16)
    late[2048:2560] = dot(attn_in, grad_keys, OVER_ROWS).astype(BF16)
    late[2560:3072] = dot(attn_in, grad_values, OVER_ROWS).astype(BF16)
    grad_normed = (
        dot(grad_query, r.q_w[...], OVER_COLUMNS)
        + dot(grad_keys, r.k_w[...], OVER_COLUMNS)
        + dot(grad_values, r.v_w[...], OVER_COLUMNS)
    )
    plain, inverse = norm_parts(r.pooled[...])
    small[1:2] = column_sum(grad_normed * plain)
    small[2:3] = column_sum(grad_normed)
    grad_pooled = (r.grad_final[...] + norm_grad(grad_normed, plain, inverse, r.ln1_g[...])).astype(BF16)
    r.grad_pooled[...] = grad_pooled
    grad_pooled_wide = grad_pooled.astype(F32)
    small[0:1] = column_sum(grad_pooled_wide)

    def back_rim_copy():
        return pltpu.make_async_remote_copy(
            r.grad_pooled.at[:16], r.back_rim, r.side_sem.at[4], r.side_sem.at[5],
            device_id=(core, (chip + n - 1) % n), device_id_type=MESH,
        )

    @pl.when(chip > 0)
    def _():
        back_rim_copy().start()

    late[1024:1536] = dot(r.x3[:, :width], grad_pooled, OVER_ROWS).astype(BF16)
    follow = pltpu.roll(grad_pooled_wide, length - 1, 0)
    within = jnp.where(at_row == length - 1, 0.0, follow).astype(BF16)
    at_rim = lax.broadcasted_iota(jnp.int32, (16, width), 0)
    rim_row = jnp.where(at_rim == 15, jnp.broadcast_to(grad_pooled_wide[:1], (16, width)), 0.0).astype(BF16)
    late[:1024] = (
        dot(r.x3[:, width:], within, OVER_ROWS) + dot(r.rim[...], rim_row, OVER_ROWS)
    ).astype(BF16)
    second_sum = Reduction(late, r.late_parts, r.late_sem, r.late_free, (small, r.small_in))
    second_sum.step(0)
    if first_left:
        first_sum.step(first_left.pop(0))

    @pl.when(chip == n - 1)
    def _():
        r.back_rim[...] = jnp.zeros_like(r.back_rim)

    @pl.when(chip < n - 1)
    def _():
        back_rim_copy().wait_recv()

    next_row = r.back_rim[...].astype(F32)[:1]
    follow = jnp.where(at_row == length - 1, next_row, follow).astype(BF16)
    first_part = r.ct3[:, :width].astype(F32) + dot(grad_pooled, r.pool_w[2 * width :], OVER_COLUMNS)
    r.grad3[:, :width] = first_part.astype(BF16)
    other_part = r.ct3[:, width:].astype(F32) + dot(follow, r.pool_w[: 2 * width], OVER_COLUMNS)
    r.grad3[:, width:] = other_part.astype(BF16)

    @pl.when(chip < n - 1)
    def _():
        rim_copy().wait_send()

    @pl.when(chip > 0)
    def _():
        back_rim_copy().wait_send()

    for number in range(1, 9):
        second_sum.step(number)
        if first_left:
            first_sum.step(first_left.pop(0))


EARLY_STEPS = ((0, 1), (3, 2), (5, 3), (7, 4))


def widen_kernel(early_ref, late_ref, *outs):
    at = pl.program_id(0)
    wide = jnp.where(at < EARLY_ROWS // 512, early_ref[...].astype(F32), late_ref[...].astype(F32))
    for out, (start, blocks) in zip(outs, WIDENED):

        @pl.when(jnp.logical_and(at >= start, at < start + blocks))
        def _(out=out):
            out[...] = wide


WIDENED = ((0, 4), (4, 4), (8, 3), (11, 1), (12, 3), (15, 1), (16, 1), (17, 1), (18, 1))
ACROSS = (True, False, True, False, False, False, False, False, False)


def widened(early, late):
    def out_spec(start, blocks, across):
        def place(at):
            block = jnp.clip(at - start, 0, blocks - 1)
            return (0, block) if across else (block, 0)

        return pl.BlockSpec((512, 512), place)

    first = EARLY_ROWS // 512
    return pl.pallas_call(
        widen_kernel,
        grid=(first + LATE_ROWS // 512,),
        in_specs=[
            pl.BlockSpec((512, 512), lambda at: (jnp.minimum(at, first - 1), 0)),
            pl.BlockSpec((512, 512), lambda at: (jnp.maximum(at - first, 0), 0)),
        ],
        out_specs=[out_spec(*cut, across) for cut, across in zip(WIDENED, ACROSS)],
        out_shape=[
            jax.ShapeDtypeStruct((512, 512 * blocks) if across else (512 * blocks, 512), F32)
            for (_, blocks), across in zip(WIDENED, ACROSS)
        ],
        compiler_params=pltpu.CompilerParams(vmem_limit_bytes=48 * 2**20),
    )(early, late)


def fused_body(
    inputs, doc_bounds, pool_weight, pool_bias, ln1_gain, ln1_bias, query_weight, key_weight,
    value_weight, out_weight, pos_weight, content_bias, pos_bias, ln2_gain, ln2_bias, ffn_in,
    ffn_in_bias, ffn_out, ffn_out_bias, up_weight, up_bias, cotangent,
):
    _, bytes_here, width = inputs.shape
    length = bytes_here // 3
    n = lax.axis_size("seq")
    tokens = n * length
    rounds = n // 2
    table, sines, cosines = wave_tables(tokens, length, width)
    given = dict(
        x3=inputs.reshape(length, 3 * width), pool_w=pool_weight, q_w=query_weight, k_w=key_weight, v_w=value_weight,
        ct3=cotangent.reshape(length, 3 * width), up_w=up_weight, ffn_out=ffn_out, pos_w=pos_weight, table=table,
        out_w=out_weight, ffn_in=ffn_in,
    )
    vectors = dict(
        pool_b=pool_bias, ln1_g=ln1_gain, ln1_b=ln1_bias, content=content_bias, pos=pos_bias, ln2_g=ln2_gain,
        ln2_b=ln2_bias, ffn_in_b=ffn_in_bias, ffn_out_b=ffn_out_bias, up_b=up_bias,
    )
    vectors = {name: vector[None] for name, vector in vectors.items()} | dict(sines=sines, cosines=cosines)
    vmem = pl.BlockSpec(memory_space=pltpu.VMEM)
    outs = dict(
        out3=((length, 3 * width), BF16), grad3=((length, 3 * width), BF16), early=((EARLY_ROWS, 512), BF16),
        late=((LATE_ROWS, 512), BF16), small=((SMALL_ROWS, 512), F32),
    )
    pair_half = (length // 2, PAIR)
    block, wide = (length, width), (length, 4 * width)
    dma, signal = pltpu.SemaphoreType.DMA, pltpu.SemaphoreType.REGULAR
    scratch = {name: pltpu.VMEM(array.shape, array.dtype) for name, array in given.items()}
    low = dict(
        rim=(16, 2 * width), back_rim=(16, width), attn_in=block, q_out=(HEADS,) + pair_half,
        kv_out=(HEADS, length, PAIR), q=(rounds,) + pair_half, kv=(n, length, PAIR), grad_branch=block,
        head_w=(width, HEAD), extra=(length, PAIR + width), keep=(rounds * (rounds + 1) // 2, length, 2 * length),
        att_out=(rounds,) + pair_half, att_in=(HEADS,) + pair_half, att_low=block, ffn_input=block, act_low=wide,
        grad_pre=wide, grad=(rounds,) + pair_half, dkv_out=(n, length, PAIR), dkv_in=(2, HEADS, length, PAIR),
        dq_out=(rounds,) + pair_half, dq_in=(HEADS,) + pair_half, grad_pooled=block,
    )
    full = dict(
        pooled=block, grad_final=block, grad_act=wide, score=(rounds, length, 2 * length), att=(rounds, length, PAIR),
        mixed=block, dkv=(tokens, PAIR), dhead=(width, HEAD), dbias=(8, HEAD), near=(length, PAIR), far=block,
        small_in=(7, SMALL_ROWS, 512),
    )
    scratch |= {name: pltpu.VMEM(shape, BF16) for name, shape in low.items()}
    scratch |= {name: pltpu.VMEM(shape, F32) for name, shape in full.items()}
    scratch |= dict(
        edges=pltpu.VMEM((2, 16, 128), jnp.int32), load_sem=dma((len(given),)), side_sem=dma((6,)), send_sem=dma((6,)),
        q_sem=dma((rounds,)), kv_sem=dma((n,)), att_sem=dma((1,)), grad_sem=dma((rounds,)), dkv_sem=dma((1,)),
        dq_sem=dma((1,)), early_sem=dma((2, REDUCTION_SEMS)), late_sem=dma((2, REDUCTION_SEMS)),
        early_free=signal((7,)), late_free=signal((7,)),
    )
    layout = (list(given), list(vectors) + ["bounds"], list(outs), list(scratch))
    out3, grad3, early, late, small = pl.pallas_call(
        functools.partial(layer_kernel, n, length, layout),
        in_specs=[pl.BlockSpec(memory_space=pl.ANY)] * len(given)
        + [vmem] * len(vectors)
        + [pl.BlockSpec(memory_space=pltpu.SMEM)],
        out_specs=[vmem] * len(outs),
        out_shape=[jax.ShapeDtypeStruct(*out) for out in outs.values()],
        scratch_shapes=list(scratch.values()) + reduction_scratch(EARLY_ROWS) + reduction_scratch(LATE_ROWS),
        compiler_params=pltpu.CompilerParams(
            collective_id=0, has_side_effects=True, vmem_limit_bytes=60 * 2**20
        ),
    )(*given.values(), *vectors.values(), doc_bounds)
    sum_in, sum_out, sum_up, sum_mix, sum_pool, sum_q, sum_k, sum_v, sum_p = widened(early, late)
    return (
        out3.reshape(inputs.shape), grad3.reshape(inputs.shape), sum_pool, small[0], small[1], small[2],
        sum_q, sum_k, sum_v, sum_mix, sum_p, small[3], small[4], small[5], small[6], sum_in,
        small[7:11].reshape(-1), sum_out, small[11], sum_up, small[12:15].reshape(-1),
    )


def solution(mesh):
    split = P("dp", "seq", None)
    fits = mesh.shape["seq"] == 16
    return jax.shard_map(
        fused_body if fits else body,
        mesh=mesh,
        in_specs=(split, P("dp", None)) + (P(),) * 19 + (split,),
        out_specs=(split, split) + (P(),) * 19,
        check_vma=False,
    )
```

```python
import functools
import types

import jax
import jax.numpy as jnp
import numpy as np
from jax import lax
from jax.experimental import pallas as pl
from jax.experimental.pallas import tpu as pltpu
from jax.sharding import PartitionSpec as P

HEADS = 8
ROWS = 2
HEAD = 64
PAIR = 2 * HEAD
MESH = pl.DeviceIdType.MESH
F32 = jnp.float32
BF16 = jnp.bfloat16

epsilon = 1e-05
masked_score = -1e30


def dot(left, right, dims=((1,), (0,))):
    return lax.dot_general(left, right, (dims, ((), ())), preferred_element_type=F32)


def passed_along(value, axis, steps):
    count = lax.axis_size(axis)
    first, last = (max(0, -steps), min(count, count - steps))
    return lax.ppermute(value, axis, [(source, source + steps) for source in range(first, last)])


def place_of(block, group):
    turn, spot = block // group, block % group
    return turn, jnp.where(turn % 2 == 0, spot, group - 1 - spot)


def block_of(turn, member, group):
    return turn * group + jnp.where(turn % 2 == 0, member, group - 1 - member)


def whereabouts(group):
    core, chip = lax.axis_index("dp"), lax.axis_index("seq")
    chips = group // 2
    unit = chip // chips
    member = (chip % chips) * 2 + core
    return core, chip, unit // HEADS, unit % HEADS, member


def chip_of(row, head, member, group):
    return (row * HEADS + head) * (group // 2) + member // 2, member % 2


def meet(n, group, to_units):
    core, chip, row, head, member = whereabouts(group)
    barrier = pltpu.get_barrier_semaphore()

    def greet(row_or_core, chip_at):
        away = jnp.logical_or(row_or_core != core, chip_at != chip)

        @pl.when(away)
        def _():
            pl.semaphore_signal(
                barrier, inc=1, device_id=(row_or_core, chip_at), device_id_type=MESH
            )

        return away.astype(jnp.int32)

    own_row = row == core
    if to_units:
        for s in range(n):
            greet(row, jnp.int32(s))
        mine = jnp.logical_and(chip // (HEADS * (group // 2)) == core, True)
        pl.semaphore_wait(barrier, HEADS * group - mine.astype(jnp.int32))
    else:
        for h in range(HEADS):
            for g in range(group):
                c, k = chip_of(core, h, g, group)
                greet(jnp.int32(k), c)
        pl.semaphore_wait(barrier, n - own_row.astype(jnp.int32))


def send(source, target, sems, core, chip):
    here_core, here_chip = lax.axis_index("dp"), lax.axis_index("seq")
    here = jnp.logical_and(core == here_core, chip == here_chip)

    @pl.when(here)
    def _():
        pltpu.make_async_copy(source, target, sems[1]).start()

    @pl.when(jnp.logical_not(here))
    def _():
        pltpu.make_async_remote_copy(
            source, target, sems[0], sems[1], device_id=(core, chip), device_id_type=MESH
        ).start()


def sent(source, sem, core, chip):
    here_core, here_chip = lax.axis_index("dp"), lax.axis_index("seq")
    here = jnp.logical_and(core == here_core, chip == here_chip)

    @pl.when(jnp.logical_not(here))
    def _():
        pltpu.make_async_copy(source, source, sem).wait()


def arrived(whole, sem):
    pltpu.make_async_copy(whole, whole, sem).wait()


def to_units_kernel(n, group, *refs):
    count = len(refs) - 2
    arrays, outs = refs[: count // 2], refs[count // 2 : count]
    send_sem, recv_sem = refs[count:]
    core, chip, row, head, member = whereabouts(group)
    turn, spot = place_of(chip, group)
    meet(n, group, True)
    jobs = []
    for h in range(HEADS):
        for index, (array, out) in enumerate(zip(arrays, outs)):
            sems = (send_sem.at[index], recv_sem.at[index])
            if index == 0:
                to_chip, to_core = chip_of(core, h, spot, group)
                jobs.append((array.at[h], out.at[turn], sems, to_core, to_chip))
            else:
                for g in range(group):
                    to_chip, to_core = chip_of(core, h, g, group)
                    jobs.append((array.at[h], out.at[chip], sems, jnp.int32(to_core), to_chip))
    for job in jobs:
        send(*job)
    for source, _, sems, to_core, to_chip in jobs:
        sent(source, sems[0], to_core, to_chip)
    for index, out in enumerate(outs):
        arrived(out, recv_sem.at[index])


def to_owners_kernel(n, group, *refs):
    count = len(refs) - 2
    arrays, outs = refs[: count // 2], refs[count // 2 : count]
    send_sem, recv_sem = refs[count:]
    core, chip, row, head, member = whereabouts(group)
    meet(n, group, False)
    jobs = []
    for turn in range(n // group):
        block = block_of(jnp.int32(turn), member, group)
        sems = (send_sem.at[0], recv_sem.at[0])
        jobs.append((arrays[0].at[turn], outs[0].at[head], sems, row, block))
    if len(arrays) > 1:
        for block in range(n):
            sems = (send_sem.at[1], recv_sem.at[1])
            jobs.append((arrays[1].at[block], outs[1].at[member, head], sems, row, jnp.int32(block)))
    for job in jobs:
        send(*job)
    for source, _, sems, to_core, to_chip in jobs:
        sent(source, sems[0], to_core, to_chip)
    for index, out in enumerate(outs):
        arrived(out, recv_sem.at[index])


def exchange(kernel, n, group, arrays, shapes, ident):
    vmem = pl.BlockSpec(memory_space=pltpu.VMEM)
    return pl.pallas_call(
        functools.partial(kernel, n, group),
        out_shape=[jax.ShapeDtypeStruct(shape, array.dtype) for shape, array in zip(shapes, arrays)],
        in_specs=[vmem] * len(arrays),
        out_specs=[vmem] * len(arrays),
        scratch_shapes=[
            pltpu.SemaphoreType.DMA((len(arrays),)),
            pltpu.SemaphoreType.DMA((len(arrays),)),
        ],
        compiler_params=pltpu.CompilerParams(
            collective_id=ident, has_side_effects=True, vmem_limit_bytes=48 * 2**20
        ),
    )(*arrays)


def unpacked(pair):
    return jnp.concatenate([pair[:, :HEAD], pair[:, HEAD:]], 0)


def packed(block):
    half = block.shape[0] // 2
    return jnp.concatenate([block[:half], block[half:]], 1)


def query_parts(q_pair, content_bias, pos_bias, pos_weight, turn_sin, turn_cos):
    query = unpacked(q_pair.astype(F32))
    query_u = (query + content_bias).astype(BF16)
    query_v = (query + pos_bias).astype(BF16)
    spread = dot(query_v, pos_weight, ((1,), (1,)))
    half = turn_sin.shape[1]
    lift, rest = spread[:, :half], spread[:, half:]
    on_sin = rest * turn_sin - lift * turn_cos
    on_cos = lift * turn_sin + rest * turn_cos
    turned = jnp.concatenate([on_sin, on_cos], 1)
    return query_u, query_v, turned


def attend_kernel(
    n, group, tile, q_ref, kv_ref, table_ref, sin_ref, cos_ref, weight_ref, cb_ref, pb_ref, bounds_ref,
    att_ref, low_ref, total_ref, keep_ref, score_ref, extra_ref,
):
    turn = pl.program_id(0)
    member = whereabouts(group)[4]
    block = block_of(turn, member, group)
    length = sin_ref.shape[0]
    tokens = n * length
    query_u, _, turned = query_parts(
        q_ref[...], cb_ref[...], pb_ref[...], weight_ref[...], sin_ref[...], cos_ref[...]
    )
    scale = HEAD**-0.5
    head_part = (query_u.astype(F32) * scale).astype(BF16)
    extra_ref[:, :HEAD] = head_part
    extra_ref[:, HEAD:PAIR] = jnp.zeros_like(head_part)
    extra_ref[:, PAIR:] = (turned * scale).astype(BF16)
    first = block * length
    tiles = (first + length + tile - 1) // tile
    low_bound, high_bound = bounds_ref[0], bounds_ref[1]
    places = first + lax.broadcasted_iota(jnp.int32, (length, 1), 0)
    opening = jnp.where(
        places >= high_bound, high_bound, jnp.where(places >= low_bound, low_bound, 0)
    )
    lanes = lax.broadcasted_iota(jnp.int32, (length, tile), 1)

    def score_step(step, top):
        start = pl.multiple_of(step * tile, tile)
        keys = kv_ref[pl.ds(start, tile), :]
        waves = table_ref[pl.ds(pl.multiple_of((n - 1 - block) * length + start, length), tile), :]
        score = dot(extra_ref[:, :PAIR], keys, ((1,), (1,))) + dot(
            extra_ref[:, PAIR:], waves, ((1,), (1,))
        )
        at = lanes + start
        allowed = jnp.logical_and(at <= places, at >= opening)
        score = jnp.where(allowed, score, masked_score)
        score_ref[:, pl.ds(start, tile)] = score
        for part in range(tile // 128):
            top = jnp.maximum(top, score[:, part * 128 : (part + 1) * 128])
        return top

    top = lax.fori_loop(0, tiles, score_step, jnp.full((length, 128), masked_score, F32))
    top = jnp.max(top, 1, keepdims=True)

    def value_step(step, state):
        total, summed = state
        start = pl.multiple_of(step * tile, tile)
        weight = jnp.exp(score_ref[:, pl.ds(start, tile)] - top)
        for part in range(tile // 128):
            total = total + weight[:, part * 128 : (part + 1) * 128]
        low = weight.astype(BF16)
        keep_ref[:, pl.ds(start, tile)] = low
        return total, summed + dot(low, kv_ref[pl.ds(start, tile), :])

    total, summed = lax.fori_loop(
        0, tiles, value_step, (jnp.zeros((length, 128), F32), jnp.zeros((length, PAIR), F32))
    )
    total = jnp.sum(total, 1, keepdims=True)
    attended = summed[:, HEAD:] / total
    att_ref[...] = attended
    total_ref[...] = jnp.broadcast_to(total, (length, 128))
    low_ref[...] = packed(attended).astype(BF16)


def back_kernel(
    n, group, tile, q_ref, kv_ref, table_ref, sin_ref, cos_ref, weight_ref, cb_ref, pb_ref,
    att_ref, total_ref, keep_ref, grad_ref,
    dq_ref, dkv_ref, dweight_ref, dcb_ref, dpb_ref, dkv_acc,
):
    turn = pl.program_id(0)
    member = whereabouts(group)[4]
    block = block_of(turn, member, group)
    length = sin_ref.shape[0]
    scale = HEAD**-0.5

    @pl.when(turn == 0)
    def _():
        dkv_acc[...] = jnp.zeros_like(dkv_acc)
        dweight_ref[...] = jnp.zeros_like(dweight_ref)
        dcb_ref[...] = jnp.zeros_like(dcb_ref)
        dpb_ref[...] = jnp.zeros_like(dpb_ref)

    query_u, query_v, _ = query_parts(
        q_ref[...], cb_ref[...], pb_ref[...], weight_ref[...], sin_ref[...], cos_ref[...]
    )
    head_part = (query_u.astype(F32) * scale).astype(BF16)
    grad = unpacked(grad_ref[...].astype(F32))
    inverse = 1.0 / total_ref[:, :1]
    delta = jnp.sum(grad * att_ref[...], 1, keepdims=True) * inverse
    grad_low = (grad * inverse).astype(BF16)
    nothing = jnp.zeros_like(grad_low)
    grad_wide = jnp.concatenate([nothing, grad_low], 1)
    query_wide = jnp.concatenate([head_part, nothing], 1)
    tiles = (block * length + length + tile - 1) // tile

    def step_over(step, state):
        near, far = state
        start = pl.multiple_of(step * tile, tile)
        keys = kv_ref[pl.ds(start, tile), :]
        waves = table_ref[pl.ds(pl.multiple_of((n - 1 - block) * length + start, length), tile), :]
        weight = keep_ref[:, pl.ds(start, tile)]
        grad_weight = dot(grad_wide, keys, ((1,), (1,)))
        grad_score = (weight.astype(F32) * (grad_weight - delta)).astype(BF16)
        near = near + dot(grad_score, keys)
        far = far + dot(grad_score, waves)
        dkv_acc[pl.ds(start, tile), :] += dot(grad_score, query_wide, ((0,), (0,))) + dot(
            weight, grad_wide, ((0,), (0,))
        )
        return near, far

    near, far = lax.fori_loop(
        0,
        tiles,
        step_over,
        (jnp.zeros((length, PAIR), F32), jnp.zeros((length, table_ref.shape[1]), F32)),
    )
    grad_u = near[:, :HEAD] * scale
    half = sin_ref.shape[1]
    turn_sin, turn_cos = sin_ref[...], cos_ref[...]
    on_sin, on_cos = far[:, :half] * scale, far[:, half:] * scale
    lift = on_cos * turn_sin - on_sin * turn_cos
    rest = on_cos * turn_cos + on_sin * turn_sin
    spread = jnp.concatenate([lift, rest], 1).astype(BF16)
    grad_v = dot(spread, weight_ref[...])
    dweight_ref[...] += dot(spread, query_v, ((0,), (0,)))
    dcb_ref[...] += jnp.sum(grad_u, 0, keepdims=True)
    dpb_ref[...] += jnp.sum(grad_v, 0, keepdims=True)
    dq_ref[...] = packed(grad_u + grad_v).astype(BF16)

    @pl.when(turn == pl.num_programs(0) - 1)
    def _():
        dkv_ref[...] = dkv_acc[...].astype(BF16)


def wave_tables(tokens, length, width):
    rates = 10000.0 ** (-2.0 * np.arange(width // 2, dtype=np.float64) / width)
    far = (np.arange(tokens + length, dtype=np.float64) - (tokens - length))[:, None] * rates
    near = np.arange(length, dtype=np.float64)[:, None] * rates
    table = np.concatenate([np.sin(far), np.cos(far)], 1)
    return (
        jnp.asarray(table, dtype=BF16),
        jnp.asarray(np.sin(near), dtype=F32),
        jnp.asarray(np.cos(near), dtype=F32),
    )


def whole_spec(shape):
    return pl.BlockSpec(shape, lambda turn: (0,) * len(shape))


def turn_spec(shape):
    return pl.BlockSpec((None,) + shape, lambda turn: (turn,) + (0,) * len(shape))


def layer_norm(hidden, gain, bias):
    average = jnp.mean(hidden, -1, keepdims=True)
    centred = hidden - average
    inverse = lax.rsqrt(jnp.mean(centred * centred, -1, keepdims=True) + epsilon)
    normed = centred * inverse
    return (normed * gain + bias, normed, inverse)


def norm_back(grad_out, normed, inverse, gain):
    scaled = grad_out * gain
    grad_in = inverse * (
        scaled
        - jnp.mean(scaled, -1, keepdims=True)
        - normed * jnp.mean(scaled * normed, -1, keepdims=True)
    )
    return (grad_in, jnp.sum(grad_out * normed, axis=0), jnp.sum(grad_out, axis=0))


def exact_gelu(value):
    return jax.nn.gelu(value, approximate=False)


def heads_packed(array):
    length = array.shape[0]
    split = array.reshape(2, length // 2, HEADS, HEAD)
    return jnp.transpose(split, (2, 1, 0, 3)).reshape(HEADS, length // 2, PAIR)


def heads_unpacked(array):
    half = array.shape[1]
    split = array.reshape(HEADS, half, 2, HEAD)
    return jnp.transpose(split, (2, 1, 0, 3)).reshape(2 * half, HEADS * HEAD)


def body(
    inputs, doc_bounds, pool_weight, pool_bias, ln1_gain, ln1_bias, query_weight, key_weight,
    value_weight, out_weight, pos_weight, content_bias, pos_bias, ln2_gain, ln2_bias, ffn_in,
    ffn_in_bias, ffn_out, ffn_out_bias, up_weight, up_bias, cotangent,
):
    _, bytes_here, width = inputs.shape
    length = bytes_here // 3
    n = lax.axis_size("seq")
    tokens = n * length
    group = 2 * n // (ROWS * HEADS)
    rounds = n // group
    tile = 2 * length
    row, head, member = whereabouts(group)[2:]

    all_bounds = lax.all_gather(doc_bounds, "dp", axis=0, tiled=True)
    bounds = lax.dynamic_slice(all_bounds, (row, 0), (1, 2))[0]
    table, turn_sin, turn_cos = wave_tables(tokens, length, width)
    head_weight = lax.dynamic_slice(pos_weight, (0, head * HEAD), (width, HEAD))
    head_cb = lax.dynamic_slice(content_bias, (head * HEAD,), (HEAD,))[None]
    head_pb = lax.dynamic_slice(pos_bias, (head * HEAD,), (HEAD,))[None]

    rim = passed_along(inputs[:, bytes_here - 2 :, :], "seq", 1)
    shifted = jnp.concatenate([rim, inputs[:, : bytes_here - 2, :]], 1)
    pooled_in = shifted.reshape(length, 3 * width)
    pooled = dot(pooled_in, pool_weight) + pool_bias
    normed_one, plain_one, inverse_one = layer_norm(pooled, ln1_gain, ln1_bias)
    attn_in = normed_one.astype(BF16)
    query = dot(attn_in, query_weight).astype(BF16)
    keys = dot(attn_in, key_weight).astype(BF16).reshape(length, HEADS, HEAD)
    values = dot(attn_in, value_weight).astype(BF16).reshape(length, HEADS, HEAD)
    q_out = heads_packed(query)
    kv_out = jnp.transpose(jnp.concatenate([keys, values], 2), (1, 0, 2))

    q_in, kv_in = exchange(
        to_units_kernel, n, group, (q_out, kv_out),
        ((rounds, length // 2, PAIR), (n, length, PAIR)), 0,
    )
    kv_in = kv_in.reshape(tokens, PAIR)

    common_specs = [
        turn_spec((length // 2, PAIR)),
        whole_spec((tokens, PAIR)),
        whole_spec(table.shape),
        whole_spec(turn_sin.shape),
        whole_spec(turn_cos.shape),
        whole_spec(head_weight.shape),
        whole_spec((1, HEAD)),
        whole_spec((1, HEAD)),
    ]
    common = (q_in, kv_in, table, turn_sin, turn_cos, head_weight, head_cb, head_pb)
    attended, att_low, total, keep = pl.pallas_call(
        functools.partial(attend_kernel, n, group, tile),
        grid=(rounds,),
        in_specs=common_specs + [pl.BlockSpec(memory_space=pltpu.SMEM)],
        out_specs=[
            turn_spec((length, HEAD)),
            turn_spec((length // 2, PAIR)),
            turn_spec((length, 128)),
            turn_spec((length, tokens)),
        ],
        out_shape=[
            jax.ShapeDtypeStruct((rounds, length, HEAD), F32),
            jax.ShapeDtypeStruct((rounds, length // 2, PAIR), BF16),
            jax.ShapeDtypeStruct((rounds, length, 128), F32),
            jax.ShapeDtypeStruct((rounds, length, tokens), BF16),
        ],
        scratch_shapes=[
            pltpu.VMEM((length, tokens), F32),
            pltpu.VMEM((length, PAIR + width), BF16),
        ],
        compiler_params=pltpu.CompilerParams(vmem_limit_bytes=56 * 2**20),
    )(*common, bounds)

    (att_back,) = exchange(
        to_owners_kernel, n, group, (att_low,), ((HEADS, length // 2, PAIR),), 1
    )
    attended_low = heads_unpacked(att_back)

    mixed = pooled + dot(attended_low, out_weight)
    normed_two, plain_two, inverse_two = layer_norm(mixed, ln2_gain, ln2_bias)
    ffn_input = normed_two.astype(BF16)
    pre_act = dot(ffn_input, ffn_in) + ffn_in_bias
    activated, gelu_pull = jax.vjp(exact_gelu, pre_act)
    act_low = activated.astype(BF16)
    final = mixed + dot(act_low, ffn_out) + ffn_out_bias
    final_low = final.astype(BF16)
    upsampled = dot(final_low, up_weight) + up_bias
    outputs = (inputs.astype(F32) + upsampled.reshape(1, bytes_here, width)).astype(BF16)
    grad_up = cotangent.reshape(length, 3 * width)
    over_rows = ((0,), (0,))
    over_columns = ((1,), (1,))
    grad_up_weight = dot(final_low, grad_up, over_rows)
    grad_up_bias = jnp.sum(grad_up.astype(F32), axis=0)
    grad_final = dot(grad_up, up_weight, over_columns)
    grad_branch = grad_final.astype(BF16)
    grad_ffn_out = dot(act_low, grad_branch, over_rows)
    grad_ffn_out_bias = jnp.sum(grad_branch.astype(F32), axis=0)
    grad_act = dot(grad_branch, ffn_out, over_columns)
    grad_pre = gelu_pull(grad_act)[0].astype(BF16)
    grad_ffn_in = dot(ffn_input, grad_pre, over_rows)
    grad_ffn_in_bias = jnp.sum(grad_pre.astype(F32), axis=0)
    grad_normed_two = dot(grad_pre, ffn_in, over_columns)
    grad_from_two, grad_ln2_gain, grad_ln2_bias = norm_back(
        grad_normed_two, plain_two, inverse_two, ln2_gain
    )
    grad_mixed = grad_final + grad_from_two
    grad_attn_branch = grad_mixed.astype(BF16)
    grad_out_weight = dot(attended_low, grad_attn_branch, over_rows)
    grad_attended = dot(grad_attn_branch, out_weight, over_columns).astype(BF16)

    early = lax.psum(
        tuple(
            grad.astype(BF16) for grad in (grad_ffn_in, grad_ffn_out, grad_up_weight, grad_out_weight)
        ),
        ("dp", "seq"),
    )

    (grad_in,) = exchange(
        to_units_kernel, n, group, (heads_packed(grad_attended),), ((rounds, length // 2, PAIR),), 2
    )
    dq_out, dkv_out, grad_head_weight, grad_head_cb, grad_head_pb = pl.pallas_call(
        functools.partial(back_kernel, n, group, tile),
        grid=(rounds,),
        in_specs=common_specs
        + [
            turn_spec((length, HEAD)),
            turn_spec((length, 128)),
            turn_spec((length, tokens)),
            turn_spec((length // 2, PAIR)),
        ],
        out_specs=[
            turn_spec((length // 2, PAIR)),
            whole_spec((tokens, PAIR)),
            whole_spec((width, HEAD)),
            whole_spec((1, HEAD)),
            whole_spec((1, HEAD)),
        ],
        out_shape=[
            jax.ShapeDtypeStruct((rounds, length // 2, PAIR), BF16),
            jax.ShapeDtypeStruct((tokens, PAIR), BF16),
            jax.ShapeDtypeStruct((width, HEAD), F32),
            jax.ShapeDtypeStruct((1, HEAD), F32),
            jax.ShapeDtypeStruct((1, HEAD), F32),
        ],
        scratch_shapes=[pltpu.VMEM((tokens, PAIR), F32)],
        compiler_params=pltpu.CompilerParams(vmem_limit_bytes=56 * 2**20),
    )(*common, attended, total, keep, grad_in)
    dq_back, dkv_back = exchange(
        to_owners_kernel, n, group, (dq_out, dkv_out.reshape(n, length, PAIR)),
        ((HEADS, length // 2, PAIR), (group, HEADS, length, PAIR)), 3,
    )
    grad_query = heads_unpacked(dq_back)
    dkv_back = jnp.transpose(jnp.sum(dkv_back.astype(F32), 0), (1, 0, 2)).astype(BF16)
    grad_key_low = dkv_back[:, :, :HEAD].reshape(length, width)
    grad_value_low = dkv_back[:, :, HEAD:].reshape(length, width)

    def at_head(part, shape):
        return lax.dynamic_update_slice(
            jnp.zeros(shape, F32), part.reshape(shape[:-1] + (HEAD,)), (0,) * (len(shape) - 1) + (head * HEAD,)
        )

    grad_pos_weight = at_head(grad_head_weight, (width, width))
    grad_content_bias = at_head(grad_head_cb, (width,))
    grad_pos_bias = at_head(grad_head_pb, (width,))
    grad_query_weight = dot(attn_in, grad_query, over_rows)
    grad_key_weight = dot(attn_in, grad_key_low, over_rows)
    grad_value_weight = dot(attn_in, grad_value_low, over_rows)
    grad_normed_one = (
        dot(grad_query, query_weight, over_columns)
        + dot(grad_key_low, key_weight, over_columns)
        + dot(grad_value_low, value_weight, over_columns)
    )
    grad_from_one, grad_ln1_gain, grad_ln1_bias = norm_back(
        grad_normed_one, plain_one, inverse_one, ln1_gain
    )
    grad_pooled = (grad_mixed + grad_from_one).astype(BF16)
    grad_pool_weight = dot(pooled_in, grad_pooled, over_rows)
    grad_pool_bias = jnp.sum(grad_pooled.astype(F32), axis=0)
    grad_shifted = dot(grad_pooled, pool_weight, over_columns).reshape(1, bytes_here, width)
    incoming = passed_along(grad_shifted[:, :2, :], "seq", -1)
    input_grad = (
        cotangent.astype(F32) + jnp.concatenate([grad_shifted[:, 2:, :], incoming], 1)
    ).astype(BF16)
    late = lax.psum(
        tuple(
            grad.astype(BF16)
            for grad in (
                grad_pool_weight, grad_query_weight, grad_key_weight, grad_value_weight, grad_pos_weight,
            )
        ),
        ("dp", "seq"),
    )
    small_parts = (
        grad_pool_bias, grad_ln1_gain, grad_ln1_bias, grad_content_bias, grad_pos_bias,
        grad_ln2_gain, grad_ln2_bias, grad_ffn_in_bias, grad_ffn_out_bias, grad_up_bias,
    )
    small = lax.psum(jnp.concatenate(small_parts), ("dp", "seq"))
    cuts = np.cumsum([part.shape[0] for part in small_parts])[:-1].tolist()
    (
        sum_pool_bias, sum_ln1_gain, sum_ln1_bias, sum_content, sum_pos,
        sum_ln2_gain, sum_ln2_bias, sum_in_bias, sum_out_bias, sum_up_bias,
    ) = jnp.split(small, cuts)
    sum_in, sum_out, sum_up, sum_mix = (grad.astype(F32) for grad in early)
    sum_pool, sum_q, sum_k, sum_v, sum_p = (grad.astype(F32) for grad in late)
    return (
        outputs, input_grad, sum_pool, sum_pool_bias, sum_ln1_gain, sum_ln1_bias, sum_q, sum_k, sum_v,
        sum_mix, sum_p, sum_content, sum_pos, sum_ln2_gain, sum_ln2_bias, sum_in, sum_in_bias,
        sum_out, sum_out_bias, sum_up, sum_up_bias,
    )


EARLY_ROWS, LATE_ROWS = 6144, 3584
EARLY_CHUNKS = ((0, 2048), (2048, 2048), (4096, 2048))
LATE_CHUNKS = ((0, 1536), (1536, 1536), (3072, 512))
SMALL_ROWS = 16
OVER_ROWS = ((0,), (0,))
OVER_COLUMNS = ((1,), (1,))


class Reduction:
    def __init__(self, buffer, start, rows, bufs, sems, free, small=None):
        self.buffer, self.sems, self.free, self.small = buffer, sems, free, small
        self.from_core, self.from_one, self.from_two, self.from_z = bufs
        core, chip = lax.axis_index("dp"), lax.axis_index("seq")
        self.core, self.chip, self.size = core, chip, rows // 2
        self.z = chip // 4
        bit_x, bit_y = chip % 2, (chip // 2) % 2
        first_x = core == 0
        self.peer_x, self.peer_y = chip + 1 - 2 * bit_x, chip + 2 - 4 * bit_y
        bit_one, bit_two = jnp.where(first_x, bit_x, bit_y), jnp.where(first_x, bit_y, bit_x)
        self.peer_one = jnp.where(first_x, self.peer_x, self.peer_y)
        self.peer_two = jnp.where(first_x, self.peer_y, self.peer_x)
        size = self.size
        self.at = start + core * size
        self.out = start + (1 - core) * size
        self.one_at = self.at + bit_one * (size // 2)
        self.one_out = self.at + (1 - bit_one) * (size // 2)
        self.two_at = self.one_at + bit_two * (size // 4)
        self.two_out = self.one_at + (1 - bit_two) * (size // 4)
        self.z_at = self.two_at + self.z * (size // 16)

    def rows(self, start, size):
        return self.buffer.at[pl.ds(pl.multiple_of(start, 16), size)]

    def copy(self, index, source, target, core, chip):
        return pltpu.make_async_remote_copy(
            source, target, self.sems.at[0, index], self.sems.at[1, index],
            device_id=(core, chip), device_id_type=MESH,
        )

    def go(self, index, source, target, core, chip):
        self.copy(index, source, target, core, chip).start()

    def done(self, index, source):
        copy = self.copy(index, source, source, self.core, self.peer_one)
        copy.wait_send()
        copy.wait_recv()

    def freed(self, index, *devices):
        for core, chip in devices:
            pl.semaphore_signal(self.free.at[index], inc=1, device_id=(core, chip), device_id_type=MESH)

    def is_free(self, index, count=1):
        pl.semaphore_wait(self.free.at[index], count)

    def z_chip(self, away):
        there = (self.z + 1 + away) % 4
        return there, self.chip + (there - self.z) * 4

    def z_peers(self):
        return [(self.core, self.z_chip(away)[1]) for away in range(3)]

    def add(self, start, size, parts):
        chunk = min(size, 128)
        while size % chunk:
            chunk -= 16

        def one(step, carry):
            at = pl.ds(pl.multiple_of(start + step * chunk, 16), chunk)
            here = pl.ds(pl.multiple_of(step * chunk, 16), chunk)
            total = self.buffer[at].astype(F32)
            for part in parts:
                total = total + part[here].astype(F32)
            self.buffer[at] = total.astype(BF16)
            return carry

        lax.fori_loop(0, size // chunk, one, 0)

    def small_go(self, stage, core, chip):
        if self.small is not None:
            own, taken = self.small
            self.go(12 + stage, own, taken.at[stage], core, chip)

    def small_done(self, stage):
        if self.small is not None:
            own, taken = self.small
            self.done(12 + stage, own)
            own[...] = own[...] + taken[stage]

    def small_z_go(self):
        if self.small is not None:
            own, taken = self.small
            taken[3 + self.z] = own[...]
            for away in range(3):
                self.go(15 + away, own, taken.at[3 + self.z], self.core, self.z_chip(away)[1])

    def small_z_done(self):
        if self.small is not None:
            own, taken = self.small
            for away in range(3):
                self.done(15 + away, own)
            own[...] = (taken[3] + taken[4]) + (taken[5] + taken[6])

    def step(self, number):
        size, core, chip = self.size, self.core, self.chip
        if number == 0:
            self.go(0, self.rows(self.out, size), self.from_core, 1 - core, chip)
            self.small_go(0, 1 - core, chip)
        if number == 1:
            self.done(0, self.from_core)
            self.freed(0, (1 - core, chip))
            self.add(self.one_out, size // 2, (self.part(self.from_core, self.one_out - self.at, size // 2),))
            self.go(1, self.rows(self.one_out, size // 2), self.from_one, core, self.peer_one)
            self.add(self.one_at, size // 2, (self.part(self.from_core, self.one_at - self.at, size // 2),))
            self.small_done(0)
            self.small_go(1, core, self.peer_x)
        if number == 2:
            self.done(1, self.from_one)
            self.freed(1, (core, self.peer_one))
            self.add(self.two_out, size // 4, (self.part(self.from_one, self.two_out - self.one_at, size // 4),))
            self.go(2, self.rows(self.two_out, size // 4), self.from_two, core, self.peer_two)
            self.add(self.two_at, size // 4, (self.part(self.from_one, self.two_at - self.one_at, size // 4),))
            self.small_done(1)
            self.small_go(2, core, self.peer_y)
        if number == 3:
            self.done(2, self.from_two)
            self.freed(2, (core, self.peer_two))
            self.add(self.two_at, size // 4, (self.from_two,))
            for away in range(3):
                there, peer = self.z_chip(away)
                self.go(3 + away, self.rows(self.two_at + there * (size // 16), size // 16), self.from_z.at[away], core, peer)
            self.small_done(2)
            self.small_z_go()
        if number == 4:
            for away in range(3):
                self.done(3 + away, self.from_z.at[away])
            self.freed(3, *self.z_peers())
            self.add(self.z_at, size // 16, tuple(self.from_z.at[away] for away in range(3)))
            own = self.rows(self.z_at, size // 16)
            self.is_free(3, 3)
            for away in range(3):
                self.go(6 + away, own, own, core, self.z_chip(away)[1])
            self.small_z_done()
        if number == 5:
            for away in range(3):
                self.done(6 + away, self.rows(self.z_at, size // 16))
            own = self.rows(self.two_at, size // 4)
            self.is_free(2)
            self.go(9, own, own, core, self.peer_two)
        if number == 6:
            self.done(9, self.rows(self.two_at, size // 4))
            own = self.rows(self.one_at, size // 2)
            self.is_free(1)
            self.go(10, own, own, core, self.peer_one)
        if number == 7:
            self.done(10, self.rows(self.one_at, size // 2))
            own = self.rows(self.at, size)
            self.is_free(0)
            self.go(11, own, own, 1 - core, chip)
        if number == 8:
            self.done(11, self.rows(self.at, size))

    def part(self, ref, start, size):
        return ref.at[pl.ds(pl.multiple_of(start, 16), size)]


REDUCTION_SEMS = 18


def reduction_scratch(rows):
    return [
        pltpu.VMEM(shape + (512,), BF16) for shape in ((rows // 2,), (rows // 4,), (rows // 8,), (3, rows // 32))
    ]


def gelu_pair(value):
    falling = jnp.exp(value * value * -0.5)
    turn = 1.0 / (1.0 + 0.3275911 * 0.7071067811865476 * jnp.abs(value))
    series = turn * (
        0.254829592
        + turn * (-0.284496736 + turn * (1.421413741 + turn * (-1.453152027 + turn * 1.061405429)))
    )
    tail = 0.5 * series * falling
    share = jnp.where(value >= 0, 1.0 - tail, tail)
    return value * share, share + value * falling * 0.3989422804014327


def norm_parts(hidden):
    average = jnp.mean(hidden, -1, keepdims=True)
    centred = hidden - average
    inverse = lax.rsqrt(jnp.mean(centred * centred, -1, keepdims=True) + epsilon)
    return centred * inverse, inverse


def norm_grad(grad_out, normed, inverse, gain):
    scaled = grad_out * gain
    return inverse * (
        scaled
        - jnp.mean(scaled, -1, keepdims=True)
        - normed * jnp.mean(scaled * normed, -1, keepdims=True)
    )


def column_sum(value):
    return jnp.sum(value, 0, keepdims=True)


def layer_kernel(n, length, layout, *refs):
    taken = iter(refs)
    given, vectors, outs, scratch = ({name: next(taken) for name in part} for part in layout)
    r = types.SimpleNamespace(**vectors, **outs, **scratch)
    group = 2
    rounds = n // group
    tile = 2 * length
    half_len = length // 2
    width = 512
    scale = HEAD**-0.5
    core, chip, row, head, member = whereabouts(group)
    count = 2 * n
    me = core * n + chip

    loads = {}
    count_early, count_late = len(EARLY_CHUNKS), len(LATE_CHUNKS)
    chunk_refs = refs[-4 * (count_early + count_late) :]

    def reduction(buffer, index, cut, small=None):
        bufs = chunk_refs[4 * index : 4 * index + 4]
        return Reduction(buffer, *cut, bufs, r.sum_sem.at[index], r.sum_free.at[index], small)

    for index, (name, source) in enumerate(given.items()):
        loads[name] = pltpu.make_async_copy(source, scratch[name], r.load_sem.at[index])
        loads[name].start()

    def ready(*which):
        for ref in which:
            next(loads[name] for name in given if scratch[name] is ref).wait()

    barrier = pltpu.get_barrier_semaphore()

    def greet(step, carry):
        other = (me + step) % count
        pl.semaphore_signal(barrier, inc=1, device_id=(other // n, other % n), device_id_type=MESH)
        return carry

    lax.fori_loop(1, count, greet, 0)

    low_bound, high_bound = r.bounds[0, 0], r.bounds[0, 1]
    r.edges[core, :8] = jnp.full((8, 128), low_bound, jnp.int32)
    r.edges[core, 8:] = jnp.full((8, 128), high_bound, jnp.int32)

    def tokens_of(source, target):
        for block in range(width // 128):
            r.mixing[block] = source[:, block * 128 : (block + 1) * 128].astype(F32)
            for part in range(3):
                every = r.mixing[block, pl.ds(part, length, stride=3), :]
                start = part * width + block * 128
                target[:, start : start + 128] = every.astype(BF16)

    ready(r.x_bytes, r.pool_w)
    tokens_of(r.x_bytes, r.x3)
    own = dot(r.x3[:, :width], r.pool_w[2 * width :])
    before = dot(r.x3[:, width:], r.pool_w[: 2 * width])
    pl.semaphore_wait(barrier, count - 1)

    def edge_copy():
        return pltpu.make_async_remote_copy(
            r.edges.at[core], r.edges.at[core], r.side_sem.at[0], r.side_sem.at[1],
            device_id=(1 - core, chip), device_id_type=MESH,
        )

    def rim_copy():
        return pltpu.make_async_remote_copy(
            r.x3.at[length - 16 :, width:], r.rim, r.side_sem.at[2], r.side_sem.at[3],
            device_id=(core, (chip + 1) % n), device_id_type=MESH,
        )

    edge_copy().start()

    @pl.when(chip < n - 1)
    def _():
        rim_copy().start()

    @pl.when(chip == 0)
    def _():
        r.rim[...] = jnp.zeros_like(r.rim)

    @pl.when(chip > 0)
    def _():
        rim_copy().wait_recv()

    rim_sum = dot(r.rim[...], r.pool_w[: 2 * width])
    at_row = lax.broadcasted_iota(jnp.int32, (length, width), 0)
    before = jnp.where(at_row == 0, rim_sum[15:16], pltpu.roll(before, 1, 0))
    pooled = own + before + r.pool_b[...]
    r.pooled[...] = pooled
    plain, _ = norm_parts(pooled)
    attn_in = (plain * r.ln1_g[...] + r.ln1_b[...]).astype(BF16)
    r.attn_in[...] = attn_in
    ready(r.q_w, r.k_w, r.v_w)
    query = dot(attn_in, r.q_w[...])
    keys = dot(attn_in, r.k_w[...])
    values = dot(attn_in, r.v_w[...])
    for h in range(HEADS):
        at = slice(h * HEAD, (h + 1) * HEAD)
        r.q_out[h] = packed(query[:, at]).astype(BF16)
        r.kv_out[h] = jnp.concatenate([keys[:, at], values[:, at]], 1).astype(BF16)
    turn_to, spot_to = place_of(chip, group)

    def q_jobs(array, out, sem, recv):
        jobs = []
        for h in range(HEADS):
            to_chip, to_core = chip_of(core, h, spot_to, group)
            jobs.append((array.at[h], out.at[turn_to], (sem, recv.at[turn_to]), to_core, to_chip))
        return jobs

    kv_jobs = []
    for h in range(HEADS):
        to_chip, _ = chip_of(core, h, 0, group)
        sems = (r.send_sem.at[1], r.kv_sem.at[chip])
        kv_jobs.append((r.kv_out.at[h], r.kv.at[chip], sems, chip % 2, to_chip))
    first_jobs = kv_jobs + q_jobs(r.q_out, r.q, r.send_sem.at[0], r.q_sem)
    for job in first_jobs:
        send(*job)

    ready(r.ct_bytes, r.up_w, r.ffn_out)
    tokens_of(r.ct_bytes, r.ct3)
    grad_final = dot(r.ct3[...], r.up_w[...], OVER_COLUMNS)
    r.grad_final[...] = grad_final
    grad_branch = grad_final.astype(BF16)
    r.grad_branch[...] = grad_branch
    for part in range(4):
        at = slice(part * width, (part + 1) * width)
        r.grad_act[:, at] = dot(grad_branch, r.ffn_out[at], OVER_COLUMNS)
    small = r.small
    small[...] = jnp.zeros_like(small)
    small[11:12] = column_sum(grad_branch.astype(F32))
    for part in range(3):
        at = slice(part * width, (part + 1) * width)
        small[12 + part : 13 + part] = column_sum(r.ct3[:, at].astype(F32))

    ready(r.pos_w, r.table)
    odd = head % 2 == 1
    pair_at = pl.ds(pl.multiple_of((head // 2) * PAIR, PAIR), PAIR)

    def of_head(ref):
        both = ref[:, pair_at].astype(F32)
        return jnp.where(odd, both[:, HEAD:], both[:, :HEAD])

    r.head_w[...] = of_head(r.pos_w).astype(BF16)
    content_bias, pos_bias = of_head(r.content), of_head(r.pos)
    edge_copy().wait_send()
    edge_copy().wait_recv()
    low_edge = r.edges[row, 0:1, 0:1]
    high_edge = r.edges[row, 8:9, 0:1]
    half = width // 2
    lanes = lax.broadcasted_iota(jnp.int32, (length, tile), 1)

    def rows_of(array):
        return pl.ds(pl.multiple_of(array, length), tile)

    def forward(turn):
        at = turn * group + core
        return pltpu.make_async_remote_copy(
            r.kv.at[at], r.kv.at[at], r.send_sem.at[6], r.kv_sem.at[at], device_id=(1 - core, chip), device_id_type=MESH
        )

    def pass_on(turn):
        at = turn * group + core
        arrived(r.kv.at[at], r.kv_sem.at[at])
        forward(turn).start()

    pass_on(0)

    def attend(turn, carry):
        block = block_of(turn, member, group)

        @pl.when(turn < rounds - 1)
        def _():
            pass_on(turn + 1)

        arrived(r.q.at[turn], r.q_sem.at[turn])
        other = turn * group + 1 - core
        arrived(r.kv.at[other], r.kv_sem.at[other])
        query_u, _, turned = query_parts(
            r.q[turn], content_bias, pos_bias, r.head_w[...], r.sines[...], r.cosines[...]
        )
        head_part = (query_u.astype(F32) * scale).astype(BF16)
        r.extra[:, :PAIR] = jnp.concatenate([head_part, jnp.zeros_like(head_part)], 1)
        r.extra[:, PAIR:] = (turned * scale).astype(BF16)
        places = block * length + lax.broadcasted_iota(jnp.int32, (length, 1), 0)
        opening = jnp.where(places >= high_edge, high_edge, jnp.where(places >= low_edge, low_edge, 0))

        def score_step(step, top):
            pair = r.kv[pl.ds(step * group, group)].reshape(tile, PAIR)
            waves = r.table[rows_of((n - 1 - block) * length + step * tile), :]
            score = dot(r.extra[:, :PAIR], pair, OVER_COLUMNS) + dot(r.extra[:, PAIR:], waves, OVER_COLUMNS)
            at = lanes + step * tile
            allowed = jnp.logical_and(at <= places, at >= opening)
            score = jnp.where(allowed, score, masked_score)
            r.score[step] = score
            for part in range(tile // 128):
                top = jnp.maximum(top, score[:, part * 128 : (part + 1) * 128])
            return top

        top = lax.fori_loop(0, turn + 1, score_step, jnp.full((length, 128), masked_score, F32))
        top = jnp.max(top, 1, keepdims=True)

        def value_step(step, state):
            total, summed = state
            weight = jnp.exp(r.score[step] - top)
            for part in range(tile // 128):
                total = total + weight[:, part * 128 : (part + 1) * 128]
            low = weight.astype(BF16)
            r.keep[turn * (turn + 1) // 2 + step] = low
            pair = r.kv[pl.ds(step * group, group)].reshape(tile, PAIR)
            return total, summed + dot(low, pair)

        total, summed = lax.fori_loop(
            0, turn + 1, value_step, (jnp.zeros((length, 128), F32), jnp.zeros((length, PAIR), F32))
        )
        inverse = 1.0 / jnp.sum(total, 1, keepdims=True)
        attended = summed[:, HEAD:] * inverse
        r.att[turn] = jnp.concatenate([jnp.broadcast_to(inverse, (length, HEAD)), attended], 1)
        r.att_out[turn] = packed(attended).astype(BF16)
        send(
            r.att_out.at[turn], r.att_in.at[head], (r.send_sem.at[2], r.att_sem.at[0]), row, block
        )
        return carry

    lax.fori_loop(0, rounds, attend, 0)
    for source, _, sems, to_core, to_chip in first_jobs:
        sent(source, sems[0], to_core, to_chip)
    for turn in range(rounds):
        forward(turn).wait_send()

    def joined(get):
        parts = [get(h) for h in range(HEADS)]
        upper = jnp.concatenate([part[:, :HEAD] for part in parts], 1)
        lower = jnp.concatenate([part[:, HEAD:] for part in parts], 1)
        return jnp.concatenate([upper, lower], 0)

    arrived(r.att_in, r.att_sem.at[0])
    ready(r.out_w, r.ffn_in)
    att_low = joined(lambda h: r.att_in[h].astype(F32)).astype(BF16)
    r.att_low[...] = att_low
    mixed = r.pooled[...] + dot(att_low, r.out_w[...])
    r.mixed[...] = mixed
    plain_two, inverse_two = norm_parts(mixed)
    ffn_input = (plain_two * r.ln2_g[...] + r.ln2_b[...]).astype(BF16)
    r.ffn_input[...] = ffn_input
    grad_normed = jnp.zeros((length, width), F32)
    for part in range(4):
        at = slice(part * width, (part + 1) * width)
        pre_act = dot(ffn_input, r.ffn_in[:, at]) + r.ffn_in_b[:, at]
        act, slope = gelu_pair(pre_act)
        r.act_low[:, at] = act.astype(BF16)
        grad_pre = (r.grad_act[:, at] * slope).astype(BF16)
        r.grad_pre[:, at] = grad_pre
        small[7 + part : 8 + part] = column_sum(grad_pre.astype(F32))
        grad_normed = grad_normed + dot(grad_pre, r.ffn_in[:, at], OVER_COLUMNS)
    small[5:6] = column_sum(grad_normed * plain_two)
    small[6:7] = column_sum(grad_normed)
    grad_mixed = r.grad_final[...] + norm_grad(grad_normed, plain_two, inverse_two, r.ln2_g[...])
    r.grad_final[...] = grad_mixed
    grad_mixed_low = grad_mixed.astype(BF16)
    grad_att = dot(grad_mixed_low, r.out_w[...], OVER_COLUMNS)
    for h in range(HEADS):
        r.q_out[h] = packed(grad_att[:, h * HEAD : (h + 1) * HEAD]).astype(BF16)
    second_jobs = q_jobs(r.q_out, r.grad, r.send_sem.at[3], r.grad_sem)
    for job in second_jobs:
        send(*job)

    early, late = r.early, r.late
    sums = [reduction(early, index, cut) for index, cut in enumerate(EARLY_CHUNKS)]
    for index, cut in enumerate(LATE_CHUNKS):
        small_pair = (small, r.small_in) if index == 0 else None
        sums.append(reduction(late, count_early + index, cut, small_pair))

    def steps_at(moment):
        for index, number in SCHEDULE.get(moment, ()):
            sums[index].step(number)

    for part in range(4):
        at = slice(part * width, (part + 1) * width)
        early[at] = dot(r.ffn_input[...], r.grad_pre[:, at], OVER_ROWS).astype(BF16)
    sums[0].step(0)
    for part in range(4):
        at = slice(part * width, (part + 1) * width)
        early[2048 + part * width : 2048 + (part + 1) * width] = dot(
            r.act_low[:, at], r.grad_branch[...], OVER_ROWS
        ).astype(BF16)
    sums[1].step(0)
    steps_at(-3)
    early[5632:] = dot(r.att_low[...], grad_mixed_low, OVER_ROWS).astype(BF16)
    final_low = (r.mixed[...] + dot(r.act_low[...], r.ffn_out[...]) + r.ffn_out_b[...]).astype(BF16)
    for part in range(3):
        at = slice(part * width, (part + 1) * width)
        early[4096 + part * width : 4096 + (part + 1) * width] = dot(final_low, r.ct3[:, at], OVER_ROWS).astype(BF16)
    sums[2].step(0)
    steps_at(-2)
    for part in range(3):
        at = slice(part * width, (part + 1) * width)
        lifted = dot(final_low, r.up_w[:, at]) + r.up_b[:, at]
        r.out3[:, at] = (r.x3[:, at].astype(F32) + lifted).astype(BF16)

    steps_at(-1)

    r.dkv[...] = jnp.zeros_like(r.dkv)
    r.dhead[...] = jnp.zeros_like(r.dhead)
    r.dbias[...] = jnp.zeros_like(r.dbias)

    def give_over(turn):
        return pltpu.make_async_remote_copy(
            r.dkv_out.at[turn * group + 1 - core], r.dkv_other.at[turn], r.send_sem.at[7], r.other_sem.at[turn],
            device_id=(1 - core, chip), device_id_type=MESH,
        )

    def hand_in(turn):
        at = turn * group + core
        give_over(turn).wait_recv()
        total = r.dkv[pl.ds(pl.multiple_of(at * length, length), length)] + r.dkv_other[turn].astype(F32)
        r.dkv_out[at] = total.astype(BF16)
        send(r.dkv_out.at[at], r.dkv_in.at[head], (r.send_sem.at[4], r.dkv_sem.at[0]), row, at)

    def back(index, carry):
        turn = rounds - 1 - index
        block = block_of(turn, member, group)
        arrived(r.grad.at[turn], r.grad_sem.at[turn])
        query = unpacked(r.q[turn].astype(F32))
        query_u = ((query + content_bias).astype(BF16).astype(F32) * scale).astype(BF16)
        query_v = (query + pos_bias).astype(BF16)
        grad = unpacked(r.grad[turn].astype(F32))
        inverse = r.att[turn][:, :HEAD]
        grad_part = grad * inverse
        delta = jnp.sum(grad_part * r.att[turn][:, HEAD:], 1, keepdims=True)
        nothing = jnp.zeros((length, HEAD), F32)
        r.extra[:, :PAIR] = jnp.concatenate([nothing, grad_part], 1).astype(BF16)
        r.extra[:, PAIR : 2 * PAIR] = jnp.concatenate([query_u.astype(F32), nothing], 1).astype(BF16)
        r.near[...] = jnp.zeros_like(r.near)
        r.far[...] = jnp.zeros_like(r.far)

        def step_over(step, inner):
            pair = r.kv[pl.ds(step * group, group)].reshape(tile, PAIR)
            waves = r.table[rows_of((n - 1 - block) * length + step * tile), :]
            weight = r.keep[turn * (turn + 1) // 2 + step]
            grad_weight = dot(r.extra[:, :PAIR], pair, OVER_COLUMNS)
            grad_score = (weight.astype(F32) * (grad_weight - delta)).astype(BF16)
            r.near[...] += dot(grad_score, pair)
            r.far[...] += dot(grad_score, waves)
            at = pl.ds(pl.multiple_of(step * tile, tile), tile)
            r.dkv[at] += dot(grad_score, r.extra[:, PAIR : 2 * PAIR], OVER_ROWS) + dot(
                weight, r.extra[:, :PAIR], OVER_ROWS
            )
            return inner

        lax.fori_loop(0, turn + 1, step_over, 0)
        give = turn * group + 1 - core
        r.dkv_out[give] = r.dkv[pl.ds(pl.multiple_of(give * length, length), length)].astype(BF16)
        give_over(turn).start()

        @pl.when(index > 0)
        def _():
            hand_in(turn + 1)

        grad_u = r.near[:, :HEAD] * scale
        turn_sin, turn_cos = r.sines[...], r.cosines[...]
        on_sin, on_cos = r.far[:, :half] * scale, r.far[:, half:] * scale
        lift = on_cos * turn_sin - on_sin * turn_cos
        rest = on_cos * turn_cos + on_sin * turn_sin
        spread = jnp.concatenate([lift, rest], 1).astype(BF16)
        grad_v = dot(spread, r.head_w[...])
        r.dhead[...] += dot(spread, query_v, OVER_ROWS)
        r.dbias[0:1] += column_sum(grad_u)
        r.dbias[1:2] += column_sum(grad_v)
        r.dq_out[turn] = packed(grad_u + grad_v).astype(BF16)
        send(r.dq_out.at[turn], r.dq_in.at[head], (r.send_sem.at[5], r.dq_sem.at[0]), row, block)
        for when in range(rounds):
            if when in SCHEDULE:

                @pl.when(index == when)
                def _(when=when):
                    steps_at(when)

        return carry

    lax.fori_loop(0, rounds, back, 0)
    hand_in(0)

    late[2048 + 1024 :] = jnp.zeros((512, 512), BF16)
    dhead = r.dhead[...]
    nothing = jnp.zeros_like(dhead)
    late[3072:, pair_at] = jnp.where(
        odd, jnp.concatenate([nothing, dhead], 1), jnp.concatenate([dhead, nothing], 1)
    ).astype(BF16)
    nothing = jnp.zeros((2, HEAD), F32)
    dbias = r.dbias[...][:2]
    small[3:5, pair_at] = jnp.where(
        odd, jnp.concatenate([nothing, dbias], 1), jnp.concatenate([dbias, nothing], 1)
    )
    sums[5].step(0)
    steps_at(8)
    for source, _, sems, to_core, to_chip in second_jobs:
        sent(source, sems[0], to_core, to_chip)
    for turn in range(rounds):
        block = block_of(jnp.int32(turn), member, group)
        sent(r.att_out.at[turn], r.send_sem.at[2], row, block)
        sent(r.dq_out.at[turn], r.send_sem.at[5], row, block)
    for turn in range(rounds):
        sent(r.dkv_out.at[turn * group + core], r.send_sem.at[4], row, turn * group + core)
        give_over(turn).wait_send()
    steps_at(9)
    arrived(r.dq_in, r.dq_sem.at[0])
    arrived(r.dkv_in, r.dkv_sem.at[0])
    grad_query = joined(lambda h: r.dq_in[h].astype(F32)).astype(BF16)
    both = [r.dkv_in[h].astype(F32) for h in range(HEADS)]
    grad_keys = jnp.concatenate([part[:, :HEAD] for part in both], 1).astype(BF16)
    grad_values = jnp.concatenate([part[:, HEAD:] for part in both], 1).astype(BF16)
    attn_in = r.attn_in[...]
    late[1536:2048] = dot(attn_in, grad_query, OVER_ROWS).astype(BF16)
    late[2048:2560] = dot(attn_in, grad_keys, OVER_ROWS).astype(BF16)
    late[2560:3072] = dot(attn_in, grad_values, OVER_ROWS).astype(BF16)
    sums[4].step(0)
    steps_at(10)
    grad_normed = (
        dot(grad_query, r.q_w[...], OVER_COLUMNS)
        + dot(grad_keys, r.k_w[...], OVER_COLUMNS)
        + dot(grad_values, r.v_w[...], OVER_COLUMNS)
    )
    plain, inverse = norm_parts(r.pooled[...])
    small[1:2] = column_sum(grad_normed * plain)
    small[2:3] = column_sum(grad_normed)
    grad_pooled = (r.grad_final[...] + norm_grad(grad_normed, plain, inverse, r.ln1_g[...])).astype(BF16)
    r.grad_pooled[...] = grad_pooled
    grad_pooled_wide = grad_pooled.astype(F32)
    small[0:1] = column_sum(grad_pooled_wide)

    def back_rim_copy():
        return pltpu.make_async_remote_copy(
            r.grad_pooled.at[:16], r.back_rim, r.side_sem.at[4], r.side_sem.at[5],
            device_id=(core, (chip + n - 1) % n), device_id_type=MESH,
        )

    @pl.when(chip > 0)
    def _():
        back_rim_copy().start()

    late[1024:1536] = dot(r.x3[:, :width], grad_pooled, OVER_ROWS).astype(BF16)
    follow = pltpu.roll(grad_pooled_wide, length - 1, 0)
    within = jnp.where(at_row == length - 1, 0.0, follow).astype(BF16)
    at_rim = lax.broadcasted_iota(jnp.int32, (16, width), 0)
    rim_row = jnp.where(at_rim == 15, jnp.broadcast_to(grad_pooled_wide[:1], (16, width)), 0.0).astype(BF16)
    late[:1024] = (
        dot(r.x3[:, width:], within, OVER_ROWS) + dot(r.rim[...], rim_row, OVER_ROWS)
    ).astype(BF16)
    sums[3].step(0)
    steps_at(11)

    @pl.when(chip == n - 1)
    def _():
        r.back_rim[...] = jnp.zeros_like(r.back_rim)

    @pl.when(chip < n - 1)
    def _():
        back_rim_copy().wait_recv()

    next_row = r.back_rim[...].astype(F32)[:1]
    follow = jnp.where(at_row == length - 1, next_row, follow).astype(BF16)
    first_part = r.ct3[:, :width].astype(F32) + dot(grad_pooled, r.pool_w[2 * width :], OVER_COLUMNS)
    r.grad3[:, :width] = first_part.astype(BF16)
    other_part = r.ct3[:, width:].astype(F32) + dot(follow, r.pool_w[: 2 * width], OVER_COLUMNS)
    r.grad3[:, width:] = other_part.astype(BF16)

    @pl.when(chip < n - 1)
    def _():
        rim_copy().wait_send()

    @pl.when(chip > 0)
    def _():
        back_rim_copy().wait_send()

    steps_at(12)


SCHEDULE = {
    -2: ((0, 1),),
    -1: ((1, 1),),
    0: ((0, 2), (2, 1)),
    1: ((0, 3), (1, 2)),
    2: ((1, 3), (2, 2)),
    3: ((0, 4),),
    4: ((2, 3), (1, 4)),
    5: ((0, 5), (2, 4)),
    7: ((1, 5), (0, 6)),
    8: ((2, 5), (5, 1)),
    9: ((1, 6),),
    10: ((0, 7), (5, 2), (2, 6)),
    11: ((4, 1), (1, 7), (5, 3)),
    12: (
        (3, 1), (4, 2), (2, 7), (5, 4), (3, 2), (4, 3), (5, 5), (3, 3), (4, 4), (5, 6), (3, 4), (4, 5), (5, 7),
        (3, 5), (4, 6), (3, 6), (4, 7), (3, 7), (0, 8), (1, 8), (2, 8), (5, 8), (4, 8), (3, 8),
    ),
}


WIDENED = (
    (0, 4, True), (2048, 4, False), (4096, 3, True), (5632, 1, False),
    (0, 3, False), (1536, 1, False), (2048, 1, False), (2560, 1, False), (3072, 1, False),
)
NARROW = ((0, 1), (1, 1), (2, 1), (3, 1), (4, 1), (5, 1), (6, 1), (7, 4), (11, 1), (12, 3))


def last_kernel(*refs):
    early, late, out3, grad3, small = refs[:5]
    wide_outs, narrow_outs, byte_outs = refs[5:14], refs[14:24], refs[24:26]
    staging, mixing, sems = refs[26:]
    copies = []
    for index, (out, (start, blocks, across)) in enumerate(zip(wide_outs, WIDENED)):
        source = early if index < 4 else late
        for block in range(blocks):
            slot = len(copies)

            def widen(step, carry, source=source, slot=slot, first=start + block * 512):
                here = pl.ds(pl.multiple_of(step * 64, 64), 64)
                staging[slot, here] = source[pl.ds(pl.multiple_of(first + step * 64, 64), 64)].astype(F32)
                return carry

            lax.fori_loop(0, 8, widen, 0)
            at = slice(block * 512, (block + 1) * 512)
            target = out.at[:, at] if across else out.at[at]
            copy = pltpu.make_async_copy(staging.at[slot], target, sems.at[slot])
            copy.start()
            copies.append(copy)
    for out, tokens in zip(byte_outs, (out3, grad3)):
        length, width = out.shape[0] // 3, out.shape[1]
        for block in range(width // 128):
            for part in range(3):
                start = part * width + block * 128
                mixing[block, pl.ds(part, length, stride=3), :] = tokens[:, start : start + 128].astype(F32)
            out[:, block * 128 : (block + 1) * 128] = mixing[block].astype(BF16)
    for out, (start, blocks) in zip(narrow_outs, NARROW):
        for block in range(blocks):
            out[:, block * 512 : (block + 1) * 512] = small[start + block : start + block + 1]
    for copy in copies:
        copy.wait()


def finished(early, late, out3, grad3, small):
    length, width = out3.shape[0], out3.shape[1] // 3
    vmem = pl.BlockSpec(memory_space=pltpu.VMEM)
    shapes = [(512, 512 * blocks) if across else (512 * blocks, 512) for _, blocks, across in WIDENED]
    narrow = [(1, 512 * blocks) for _, blocks in NARROW]
    count = sum(blocks for _, blocks, _ in WIDENED)
    outs = pl.pallas_call(
        last_kernel,
        in_specs=[vmem] * 5,
        out_specs=[pl.BlockSpec(memory_space=pl.ANY)] * len(shapes) + [vmem] * (len(narrow) + 2),
        out_shape=[jax.ShapeDtypeStruct(shape, F32) for shape in shapes + narrow]
        + [jax.ShapeDtypeStruct((3 * length, width), BF16)] * 2,
        scratch_shapes=[
            pltpu.VMEM((count, 512, 512), F32), pltpu.VMEM((width // 128, 3 * length, 128), F32),
            pltpu.SemaphoreType.DMA((count,)),
        ],
        compiler_params=pltpu.CompilerParams(vmem_limit_bytes=56 * 2**20),
    )(early, late, out3, grad3, small)
    return outs[: len(shapes)], [out[0] for out in outs[len(shapes) : -2]], outs[-2:]


def fused_body(
    inputs, doc_bounds, pool_weight, pool_bias, ln1_gain, ln1_bias, query_weight, key_weight,
    value_weight, out_weight, pos_weight, content_bias, pos_bias, ln2_gain, ln2_bias, ffn_in,
    ffn_in_bias, ffn_out, ffn_out_bias, up_weight, up_bias, cotangent,
):
    _, bytes_here, width = inputs.shape
    length = bytes_here // 3
    n = lax.axis_size("seq")
    tokens = n * length
    rounds = n // 2
    table, sines, cosines = wave_tables(tokens, length, width)
    given = dict(
        x_bytes=inputs[0], pool_w=pool_weight, q_w=query_weight, k_w=key_weight, v_w=value_weight,
        ct_bytes=cotangent[0], up_w=up_weight, ffn_out=ffn_out, pos_w=pos_weight, table=table,
        out_w=out_weight, ffn_in=ffn_in,
    )
    vectors = dict(
        pool_b=pool_bias, ln1_g=ln1_gain, ln1_b=ln1_bias, content=content_bias, pos=pos_bias, ln2_g=ln2_gain,
        ln2_b=ln2_bias, ffn_in_b=ffn_in_bias, ffn_out_b=ffn_out_bias, up_b=up_bias,
    )
    vectors = {name: vector[None] for name, vector in vectors.items()} | dict(sines=sines, cosines=cosines)
    vmem = pl.BlockSpec(memory_space=pltpu.VMEM)
    outs = dict(
        out3=((length, 3 * width), BF16), grad3=((length, 3 * width), BF16), early=((EARLY_ROWS, 512), BF16),
        late=((LATE_ROWS, 512), BF16), small=((SMALL_ROWS, 512), F32),
    )
    pair_half = (length // 2, PAIR)
    block, wide = (length, width), (length, 4 * width)
    dma, signal = pltpu.SemaphoreType.DMA, pltpu.SemaphoreType.REGULAR
    scratch = {name: pltpu.VMEM(array.shape, array.dtype) for name, array in given.items()}
    low = dict(
        x3=(length, 3 * width), ct3=(length, 3 * width), rim=(16, 2 * width), back_rim=(16, width), attn_in=block, q_out=(HEADS,) + pair_half,
        kv_out=(HEADS, length, PAIR), q=(rounds,) + pair_half, kv=(n, length, PAIR), grad_branch=block,
        head_w=(width, HEAD), extra=(length, PAIR + width), keep=(rounds * (rounds + 1) // 2, length, 2 * length),
        att_out=(rounds,) + pair_half, att_in=(HEADS,) + pair_half, att_low=block, ffn_input=block, act_low=wide,
        grad_pre=wide, grad=(rounds,) + pair_half, dkv_out=(n, length, PAIR), dkv_in=(HEADS, length, PAIR),
        dkv_other=(rounds, length, PAIR), dq_out=(rounds,) + pair_half, dq_in=(HEADS,) + pair_half, grad_pooled=block,
    )
    full = dict(
        mixing=(width // 128, 3 * length, 128), pooled=block, grad_final=block, grad_act=wide, score=(rounds, length, 2 * length), att=(rounds, length, PAIR),
        mixed=block, dkv=(tokens, PAIR), dhead=(width, HEAD), dbias=(8, HEAD), near=(length, PAIR), far=block,
        small_in=(7, SMALL_ROWS, 512),
    )
    scratch |= {name: pltpu.VMEM(shape, BF16) for name, shape in low.items()}
    scratch |= {name: pltpu.VMEM(shape, F32) for name, shape in full.items()}
    scratch |= dict(
        edges=pltpu.VMEM((2, 16, 128), jnp.int32), load_sem=dma((len(given),)), side_sem=dma((6,)), send_sem=dma((8,)), other_sem=dma((rounds,)),

        q_sem=dma((rounds,)), kv_sem=dma((n,)), att_sem=dma((1,)), grad_sem=dma((rounds,)), dkv_sem=dma((1,)),
        dq_sem=dma((1,)), sum_sem=dma((6, 2, REDUCTION_SEMS)), sum_free=signal((6, 4)),
    )
    layout = (list(given), list(vectors) + ["bounds"], list(outs), list(scratch))
    out3, grad3, early, late, small = pl.pallas_call(
        functools.partial(layer_kernel, n, length, layout),
        in_specs=[pl.BlockSpec(memory_space=pl.ANY)] * len(given)
        + [vmem] * len(vectors)
        + [pl.BlockSpec(memory_space=pltpu.SMEM)],
        out_specs=[vmem] * len(outs),
        out_shape=[jax.ShapeDtypeStruct(*out) for out in outs.values()],
        scratch_shapes=list(scratch.values())
        + sum((reduction_scratch(rows) for _, rows in EARLY_CHUNKS + LATE_CHUNKS), []),
        compiler_params=pltpu.CompilerParams(
            collective_id=0, has_side_effects=True, vmem_limit_bytes=60 * 2**20
        ),
    )(*given.values(), *vectors.values(), doc_bounds)
    wide, narrow, both = finished(early, late, out3, grad3, small)
    sum_in, sum_out, sum_up, sum_mix, sum_pool, sum_q, sum_k, sum_v, sum_p = wide
    pool_b, ln1_g, ln1_b, content, pos, ln2_g, ln2_b, in_b, out_b, up_b = narrow
    return (
        both[0][None], both[1][None], sum_pool, pool_b, ln1_g, ln1_b, sum_q, sum_k, sum_v, sum_mix, sum_p,
        content, pos, ln2_g, ln2_b, sum_in, in_b, sum_out, out_b, sum_up, up_b,
    )


def solution(mesh):
    split = P("dp", "seq", None)
    fits = mesh.shape["seq"] == 16
    return jax.shard_map(
        fused_body if fits else body,
        mesh=mesh,
        in_specs=(split, P("dp", None)) + (P(),) * 19 + (split,),
        out_specs=(split, split) + (P(),) * 19,
        check_vma=False,
    )
```

```python
import functools
import types

import jax
import jax.numpy as jnp
import numpy as np
from jax import lax
from jax.experimental import pallas as pl
from jax.experimental.pallas import tpu as pltpu
from jax.sharding import PartitionSpec as P

HEADS = 8
ROWS = 2
HEAD = 64
PAIR = 2 * HEAD
MESH = pl.DeviceIdType.MESH
F32 = jnp.float32
BF16 = jnp.bfloat16

epsilon = 1e-05
masked_score = -1e30


def dot(left, right, dims=((1,), (0,))):
    return lax.dot_general(left, right, (dims, ((), ())), preferred_element_type=F32)


def passed_along(value, axis, steps):
    count = lax.axis_size(axis)
    first, last = (max(0, -steps), min(count, count - steps))
    return lax.ppermute(value, axis, [(source, source + steps) for source in range(first, last)])


def place_of(block, group):
    turn, spot = block // group, block % group
    return turn, jnp.where(turn % 2 == 0, spot, group - 1 - spot)


def block_of(turn, member, group):
    return turn * group + jnp.where(turn % 2 == 0, member, group - 1 - member)


def whereabouts(group):
    core, chip = lax.axis_index("dp"), lax.axis_index("seq")
    chips = group // 2
    unit = chip // chips
    member = (chip % chips) * 2 + core
    return core, chip, unit // HEADS, unit % HEADS, member


def chip_of(row, head, member, group):
    return (row * HEADS + head) * (group // 2) + member // 2, member % 2


def meet(n, group, to_units):
    core, chip, row, head, member = whereabouts(group)
    barrier = pltpu.get_barrier_semaphore()

    def greet(row_or_core, chip_at):
        away = jnp.logical_or(row_or_core != core, chip_at != chip)

        @pl.when(away)
        def _():
            pl.semaphore_signal(
                barrier, inc=1, device_id=(row_or_core, chip_at), device_id_type=MESH
            )

        return away.astype(jnp.int32)

    own_row = row == core
    if to_units:
        for s in range(n):
            greet(row, jnp.int32(s))
        mine = jnp.logical_and(chip // (HEADS * (group // 2)) == core, True)
        pl.semaphore_wait(barrier, HEADS * group - mine.astype(jnp.int32))
    else:
        for h in range(HEADS):
            for g in range(group):
                c, k = chip_of(core, h, g, group)
                greet(jnp.int32(k), c)
        pl.semaphore_wait(barrier, n - own_row.astype(jnp.int32))


def send(source, target, sems, core, chip):
    here_core, here_chip = lax.axis_index("dp"), lax.axis_index("seq")
    here = jnp.logical_and(core == here_core, chip == here_chip)

    @pl.when(here)
    def _():
        pltpu.make_async_copy(source, target, sems[1]).start()

    @pl.when(jnp.logical_not(here))
    def _():
        pltpu.make_async_remote_copy(
            source, target, sems[0], sems[1], device_id=(core, chip), device_id_type=MESH
        ).start()


def sent(source, sem, core, chip):
    here_core, here_chip = lax.axis_index("dp"), lax.axis_index("seq")
    here = jnp.logical_and(core == here_core, chip == here_chip)

    @pl.when(jnp.logical_not(here))
    def _():
        pltpu.make_async_copy(source, source, sem).wait()


def arrived(whole, sem):
    pltpu.make_async_copy(whole, whole, sem).wait()


def to_units_kernel(n, group, *refs):
    count = len(refs) - 2
    arrays, outs = refs[: count // 2], refs[count // 2 : count]
    send_sem, recv_sem = refs[count:]
    core, chip, row, head, member = whereabouts(group)
    turn, spot = place_of(chip, group)
    meet(n, group, True)
    jobs = []
    for h in range(HEADS):
        for index, (array, out) in enumerate(zip(arrays, outs)):
            sems = (send_sem.at[index], recv_sem.at[index])
            if index == 0:
                to_chip, to_core = chip_of(core, h, spot, group)
                jobs.append((array.at[h], out.at[turn], sems, to_core, to_chip))
            else:
                for g in range(group):
                    to_chip, to_core = chip_of(core, h, g, group)
                    jobs.append((array.at[h], out.at[chip], sems, jnp.int32(to_core), to_chip))
    for job in jobs:
        send(*job)
    for source, _, sems, to_core, to_chip in jobs:
        sent(source, sems[0], to_core, to_chip)
    for index, out in enumerate(outs):
        arrived(out, recv_sem.at[index])


def to_owners_kernel(n, group, *refs):
    count = len(refs) - 2
    arrays, outs = refs[: count // 2], refs[count // 2 : count]
    send_sem, recv_sem = refs[count:]
    core, chip, row, head, member = whereabouts(group)
    meet(n, group, False)
    jobs = []
    for turn in range(n // group):
        block = block_of(jnp.int32(turn), member, group)
        sems = (send_sem.at[0], recv_sem.at[0])
        jobs.append((arrays[0].at[turn], outs[0].at[head], sems, row, block))
    if len(arrays) > 1:
        for block in range(n):
            sems = (send_sem.at[1], recv_sem.at[1])
            jobs.append((arrays[1].at[block], outs[1].at[member, head], sems, row, jnp.int32(block)))
    for job in jobs:
        send(*job)
    for source, _, sems, to_core, to_chip in jobs:
        sent(source, sems[0], to_core, to_chip)
    for index, out in enumerate(outs):
        arrived(out, recv_sem.at[index])


def exchange(kernel, n, group, arrays, shapes, ident):
    vmem = pl.BlockSpec(memory_space=pltpu.VMEM)
    return pl.pallas_call(
        functools.partial(kernel, n, group),
        out_shape=[jax.ShapeDtypeStruct(shape, array.dtype) for shape, array in zip(shapes, arrays)],
        in_specs=[vmem] * len(arrays),
        out_specs=[vmem] * len(arrays),
        scratch_shapes=[
            pltpu.SemaphoreType.DMA((len(arrays),)),
            pltpu.SemaphoreType.DMA((len(arrays),)),
        ],
        compiler_params=pltpu.CompilerParams(
            collective_id=ident, has_side_effects=True, vmem_limit_bytes=48 * 2**20
        ),
    )(*arrays)


def unpacked(pair):
    return jnp.concatenate([pair[:, :HEAD], pair[:, HEAD:]], 0)


def packed(block):
    half = block.shape[0] // 2
    return jnp.concatenate([block[:half], block[half:]], 1)


def query_parts(q_pair, content_bias, pos_bias, pos_weight, turn_sin, turn_cos):
    query = unpacked(q_pair.astype(F32))
    query_u = (query + content_bias).astype(BF16)
    query_v = (query + pos_bias).astype(BF16)
    spread = dot(query_v, pos_weight, ((1,), (1,)))
    half = turn_sin.shape[1]
    lift, rest = spread[:, :half], spread[:, half:]
    on_sin = rest * turn_sin - lift * turn_cos
    on_cos = lift * turn_sin + rest * turn_cos
    turned = jnp.concatenate([on_sin, on_cos], 1)
    return query_u, query_v, turned


def attend_kernel(
    n, group, tile, q_ref, kv_ref, table_ref, sin_ref, cos_ref, weight_ref, cb_ref, pb_ref, bounds_ref,
    att_ref, low_ref, total_ref, keep_ref, score_ref, extra_ref,
):
    turn = pl.program_id(0)
    member = whereabouts(group)[4]
    block = block_of(turn, member, group)
    length = sin_ref.shape[0]
    tokens = n * length
    query_u, _, turned = query_parts(
        q_ref[...], cb_ref[...], pb_ref[...], weight_ref[...], sin_ref[...], cos_ref[...]
    )
    scale = HEAD**-0.5
    head_part = (query_u.astype(F32) * scale).astype(BF16)
    extra_ref[:, :HEAD] = head_part
    extra_ref[:, HEAD:PAIR] = jnp.zeros_like(head_part)
    extra_ref[:, PAIR:] = (turned * scale).astype(BF16)
    first = block * length
    tiles = (first + length + tile - 1) // tile
    low_bound, high_bound = bounds_ref[0], bounds_ref[1]
    places = first + lax.broadcasted_iota(jnp.int32, (length, 1), 0)
    opening = jnp.where(
        places >= high_bound, high_bound, jnp.where(places >= low_bound, low_bound, 0)
    )
    lanes = lax.broadcasted_iota(jnp.int32, (length, tile), 1)

    def score_step(step, top):
        start = pl.multiple_of(step * tile, tile)
        keys = kv_ref[pl.ds(start, tile), :]
        waves = table_ref[pl.ds(pl.multiple_of((n - 1 - block) * length + start, length), tile), :]
        score = dot(extra_ref[:, :PAIR], keys, ((1,), (1,))) + dot(
            extra_ref[:, PAIR:], waves, ((1,), (1,))
        )
        at = lanes + start
        allowed = jnp.logical_and(at <= places, at >= opening)
        score = jnp.where(allowed, score, masked_score)
        score_ref[:, pl.ds(start, tile)] = score
        for part in range(tile // 128):
            top = jnp.maximum(top, score[:, part * 128 : (part + 1) * 128])
        return top

    top = lax.fori_loop(0, tiles, score_step, jnp.full((length, 128), masked_score, F32))
    top = jnp.max(top, 1, keepdims=True)

    def value_step(step, state):
        total, summed = state
        start = pl.multiple_of(step * tile, tile)
        weight = jnp.exp(score_ref[:, pl.ds(start, tile)] - top)
        for part in range(tile // 128):
            total = total + weight[:, part * 128 : (part + 1) * 128]
        low = weight.astype(BF16)
        keep_ref[:, pl.ds(start, tile)] = low
        return total, summed + dot(low, kv_ref[pl.ds(start, tile), :])

    total, summed = lax.fori_loop(
        0, tiles, value_step, (jnp.zeros((length, 128), F32), jnp.zeros((length, PAIR), F32))
    )
    total = jnp.sum(total, 1, keepdims=True)
    attended = summed[:, HEAD:] / total
    att_ref[...] = attended
    total_ref[...] = jnp.broadcast_to(total, (length, 128))
    low_ref[...] = packed(attended).astype(BF16)


def back_kernel(
    n, group, tile, q_ref, kv_ref, table_ref, sin_ref, cos_ref, weight_ref, cb_ref, pb_ref,
    att_ref, total_ref, keep_ref, grad_ref,
    dq_ref, dkv_ref, dweight_ref, dcb_ref, dpb_ref, dkv_acc,
):
    turn = pl.program_id(0)
    member = whereabouts(group)[4]
    block = block_of(turn, member, group)
    length = sin_ref.shape[0]
    scale = HEAD**-0.5

    @pl.when(turn == 0)
    def _():
        dkv_acc[...] = jnp.zeros_like(dkv_acc)
        dweight_ref[...] = jnp.zeros_like(dweight_ref)
        dcb_ref[...] = jnp.zeros_like(dcb_ref)
        dpb_ref[...] = jnp.zeros_like(dpb_ref)

    query_u, query_v, _ = query_parts(
        q_ref[...], cb_ref[...], pb_ref[...], weight_ref[...], sin_ref[...], cos_ref[...]
    )
    head_part = (query_u.astype(F32) * scale).astype(BF16)
    grad = unpacked(grad_ref[...].astype(F32))
    inverse = 1.0 / total_ref[:, :1]
    delta = jnp.sum(grad * att_ref[...], 1, keepdims=True) * inverse
    grad_low = (grad * inverse).astype(BF16)
    nothing = jnp.zeros_like(grad_low)
    grad_wide = jnp.concatenate([nothing, grad_low], 1)
    query_wide = jnp.concatenate([head_part, nothing], 1)
    tiles = (block * length + length + tile - 1) // tile

    def step_over(step, state):
        near, far = state
        start = pl.multiple_of(step * tile, tile)
        keys = kv_ref[pl.ds(start, tile), :]
        waves = table_ref[pl.ds(pl.multiple_of((n - 1 - block) * length + start, length), tile), :]
        weight = keep_ref[:, pl.ds(start, tile)]
        grad_weight = dot(grad_wide, keys, ((1,), (1,)))
        grad_score = (weight.astype(F32) * (grad_weight - delta)).astype(BF16)
        near = near + dot(grad_score, keys)
        far = far + dot(grad_score, waves)
        dkv_acc[pl.ds(start, tile), :] += dot(grad_score, query_wide, ((0,), (0,))) + dot(
            weight, grad_wide, ((0,), (0,))
        )
        return near, far

    near, far = lax.fori_loop(
        0,
        tiles,
        step_over,
        (jnp.zeros((length, PAIR), F32), jnp.zeros((length, table_ref.shape[1]), F32)),
    )
    grad_u = near[:, :HEAD] * scale
    half = sin_ref.shape[1]
    turn_sin, turn_cos = sin_ref[...], cos_ref[...]
    on_sin, on_cos = far[:, :half] * scale, far[:, half:] * scale
    lift = on_cos * turn_sin - on_sin * turn_cos
    rest = on_cos * turn_cos + on_sin * turn_sin
    spread = jnp.concatenate([lift, rest], 1).astype(BF16)
    grad_v = dot(spread, weight_ref[...])
    dweight_ref[...] += dot(spread, query_v, ((0,), (0,)))
    dcb_ref[...] += jnp.sum(grad_u, 0, keepdims=True)
    dpb_ref[...] += jnp.sum(grad_v, 0, keepdims=True)
    dq_ref[...] = packed(grad_u + grad_v).astype(BF16)

    @pl.when(turn == pl.num_programs(0) - 1)
    def _():
        dkv_ref[...] = dkv_acc[...].astype(BF16)


def wave_tables(tokens, length, width):
    rates = 10000.0 ** (-2.0 * np.arange(width // 2, dtype=np.float64) / width)
    far = (np.arange(tokens + length, dtype=np.float64) - (tokens - length))[:, None] * rates
    near = np.arange(length, dtype=np.float64)[:, None] * rates
    table = np.concatenate([np.sin(far), np.cos(far)], 1)
    return (
        jnp.asarray(table, dtype=BF16),
        jnp.asarray(np.sin(near), dtype=F32),
        jnp.asarray(np.cos(near), dtype=F32),
    )


def whole_spec(shape):
    return pl.BlockSpec(shape, lambda turn: (0,) * len(shape))


def turn_spec(shape):
    return pl.BlockSpec((None,) + shape, lambda turn: (turn,) + (0,) * len(shape))


def layer_norm(hidden, gain, bias):
    average = jnp.mean(hidden, -1, keepdims=True)
    centred = hidden - average
    inverse = lax.rsqrt(jnp.mean(centred * centred, -1, keepdims=True) + epsilon)
    normed = centred * inverse
    return (normed * gain + bias, normed, inverse)


def norm_back(grad_out, normed, inverse, gain):
    scaled = grad_out * gain
    grad_in = inverse * (
        scaled
        - jnp.mean(scaled, -1, keepdims=True)
        - normed * jnp.mean(scaled * normed, -1, keepdims=True)
    )
    return (grad_in, jnp.sum(grad_out * normed, axis=0), jnp.sum(grad_out, axis=0))


def exact_gelu(value):
    return jax.nn.gelu(value, approximate=False)


def heads_packed(array):
    length = array.shape[0]
    split = array.reshape(2, length // 2, HEADS, HEAD)
    return jnp.transpose(split, (2, 1, 0, 3)).reshape(HEADS, length // 2, PAIR)


def heads_unpacked(array):
    half = array.shape[1]
    split = array.reshape(HEADS, half, 2, HEAD)
    return jnp.transpose(split, (2, 1, 0, 3)).reshape(2 * half, HEADS * HEAD)


def body(
    inputs, doc_bounds, pool_weight, pool_bias, ln1_gain, ln1_bias, query_weight, key_weight,
    value_weight, out_weight, pos_weight, content_bias, pos_bias, ln2_gain, ln2_bias, ffn_in,
    ffn_in_bias, ffn_out, ffn_out_bias, up_weight, up_bias, cotangent,
):
    _, bytes_here, width = inputs.shape
    length = bytes_here // 3
    n = lax.axis_size("seq")
    tokens = n * length
    group = 2 * n // (ROWS * HEADS)
    rounds = n // group
    tile = 2 * length
    row, head, member = whereabouts(group)[2:]

    all_bounds = lax.all_gather(doc_bounds, "dp", axis=0, tiled=True)
    bounds = lax.dynamic_slice(all_bounds, (row, 0), (1, 2))[0]
    table, turn_sin, turn_cos = wave_tables(tokens, length, width)
    head_weight = lax.dynamic_slice(pos_weight, (0, head * HEAD), (width, HEAD))
    head_cb = lax.dynamic_slice(content_bias, (head * HEAD,), (HEAD,))[None]
    head_pb = lax.dynamic_slice(pos_bias, (head * HEAD,), (HEAD,))[None]

    rim = passed_along(inputs[:, bytes_here - 2 :, :], "seq", 1)
    shifted = jnp.concatenate([rim, inputs[:, : bytes_here - 2, :]], 1)
    pooled_in = shifted.reshape(length, 3 * width)
    pooled = dot(pooled_in, pool_weight) + pool_bias
    normed_one, plain_one, inverse_one = layer_norm(pooled, ln1_gain, ln1_bias)
    attn_in = normed_one.astype(BF16)
    query = dot(attn_in, query_weight).astype(BF16)
    keys = dot(attn_in, key_weight).astype(BF16).reshape(length, HEADS, HEAD)
    values = dot(attn_in, value_weight).astype(BF16).reshape(length, HEADS, HEAD)
    q_out = heads_packed(query)
    kv_out = jnp.transpose(jnp.concatenate([keys, values], 2), (1, 0, 2))

    q_in, kv_in = exchange(
        to_units_kernel, n, group, (q_out, kv_out),
        ((rounds, length // 2, PAIR), (n, length, PAIR)), 0,
    )
    kv_in = kv_in.reshape(tokens, PAIR)

    common_specs = [
        turn_spec((length // 2, PAIR)),
        whole_spec((tokens, PAIR)),
        whole_spec(table.shape),
        whole_spec(turn_sin.shape),
        whole_spec(turn_cos.shape),
        whole_spec(head_weight.shape),
        whole_spec((1, HEAD)),
        whole_spec((1, HEAD)),
    ]
    common = (q_in, kv_in, table, turn_sin, turn_cos, head_weight, head_cb, head_pb)
    attended, att_low, total, keep = pl.pallas_call(
        functools.partial(attend_kernel, n, group, tile),
        grid=(rounds,),
        in_specs=common_specs + [pl.BlockSpec(memory_space=pltpu.SMEM)],
        out_specs=[
            turn_spec((length, HEAD)),
            turn_spec((length // 2, PAIR)),
            turn_spec((length, 128)),
            turn_spec((length, tokens)),
        ],
        out_shape=[
            jax.ShapeDtypeStruct((rounds, length, HEAD), F32),
            jax.ShapeDtypeStruct((rounds, length // 2, PAIR), BF16),
            jax.ShapeDtypeStruct((rounds, length, 128), F32),
            jax.ShapeDtypeStruct((rounds, length, tokens), BF16),
        ],
        scratch_shapes=[
            pltpu.VMEM((length, tokens), F32),
            pltpu.VMEM((length, PAIR + width), BF16),
        ],
        compiler_params=pltpu.CompilerParams(vmem_limit_bytes=56 * 2**20),
    )(*common, bounds)

    (att_back,) = exchange(
        to_owners_kernel, n, group, (att_low,), ((HEADS, length // 2, PAIR),), 1
    )
    attended_low = heads_unpacked(att_back)

    mixed = pooled + dot(attended_low, out_weight)
    normed_two, plain_two, inverse_two = layer_norm(mixed, ln2_gain, ln2_bias)
    ffn_input = normed_two.astype(BF16)
    pre_act = dot(ffn_input, ffn_in) + ffn_in_bias
    activated, gelu_pull = jax.vjp(exact_gelu, pre_act)
    act_low = activated.astype(BF16)
    final = mixed + dot(act_low, ffn_out) + ffn_out_bias
    final_low = final.astype(BF16)
    upsampled = dot(final_low, up_weight) + up_bias
    outputs = (inputs.astype(F32) + upsampled.reshape(1, bytes_here, width)).astype(BF16)
    grad_up = cotangent.reshape(length, 3 * width)
    over_rows = ((0,), (0,))
    over_columns = ((1,), (1,))
    grad_up_weight = dot(final_low, grad_up, over_rows)
    grad_up_bias = jnp.sum(grad_up.astype(F32), axis=0)
    grad_final = dot(grad_up, up_weight, over_columns)
    grad_branch = grad_final.astype(BF16)
    grad_ffn_out = dot(act_low, grad_branch, over_rows)
    grad_ffn_out_bias = jnp.sum(grad_branch.astype(F32), axis=0)
    grad_act = dot(grad_branch, ffn_out, over_columns)
    grad_pre = gelu_pull(grad_act)[0].astype(BF16)
    grad_ffn_in = dot(ffn_input, grad_pre, over_rows)
    grad_ffn_in_bias = jnp.sum(grad_pre.astype(F32), axis=0)
    grad_normed_two = dot(grad_pre, ffn_in, over_columns)
    grad_from_two, grad_ln2_gain, grad_ln2_bias = norm_back(
        grad_normed_two, plain_two, inverse_two, ln2_gain
    )
    grad_mixed = grad_final + grad_from_two
    grad_attn_branch = grad_mixed.astype(BF16)
    grad_out_weight = dot(attended_low, grad_attn_branch, over_rows)
    grad_attended = dot(grad_attn_branch, out_weight, over_columns).astype(BF16)

    early = lax.psum(
        tuple(
            grad.astype(BF16) for grad in (grad_ffn_in, grad_ffn_out, grad_up_weight, grad_out_weight)
        ),
        ("dp", "seq"),
    )

    (grad_in,) = exchange(
        to_units_kernel, n, group, (heads_packed(grad_attended),), ((rounds, length // 2, PAIR),), 2
    )
    dq_out, dkv_out, grad_head_weight, grad_head_cb, grad_head_pb = pl.pallas_call(
        functools.partial(back_kernel, n, group, tile),
        grid=(rounds,),
        in_specs=common_specs
        + [
            turn_spec((length, HEAD)),
            turn_spec((length, 128)),
            turn_spec((length, tokens)),
            turn_spec((length // 2, PAIR)),
        ],
        out_specs=[
            turn_spec((length // 2, PAIR)),
            whole_spec((tokens, PAIR)),
            whole_spec((width, HEAD)),
            whole_spec((1, HEAD)),
            whole_spec((1, HEAD)),
        ],
        out_shape=[
            jax.ShapeDtypeStruct((rounds, length // 2, PAIR), BF16),
            jax.ShapeDtypeStruct((tokens, PAIR), BF16),
            jax.ShapeDtypeStruct((width, HEAD), F32),
            jax.ShapeDtypeStruct((1, HEAD), F32),
            jax.ShapeDtypeStruct((1, HEAD), F32),
        ],
        scratch_shapes=[pltpu.VMEM((tokens, PAIR), F32)],
        compiler_params=pltpu.CompilerParams(vmem_limit_bytes=56 * 2**20),
    )(*common, attended, total, keep, grad_in)
    dq_back, dkv_back = exchange(
        to_owners_kernel, n, group, (dq_out, dkv_out.reshape(n, length, PAIR)),
        ((HEADS, length // 2, PAIR), (group, HEADS, length, PAIR)), 3,
    )
    grad_query = heads_unpacked(dq_back)
    dkv_back = jnp.transpose(jnp.sum(dkv_back.astype(F32), 0), (1, 0, 2)).astype(BF16)
    grad_key_low = dkv_back[:, :, :HEAD].reshape(length, width)
    grad_value_low = dkv_back[:, :, HEAD:].reshape(length, width)

    def at_head(part, shape):
        return lax.dynamic_update_slice(
            jnp.zeros(shape, F32), part.reshape(shape[:-1] + (HEAD,)), (0,) * (len(shape) - 1) + (head * HEAD,)
        )

    grad_pos_weight = at_head(grad_head_weight, (width, width))
    grad_content_bias = at_head(grad_head_cb, (width,))
    grad_pos_bias = at_head(grad_head_pb, (width,))
    grad_query_weight = dot(attn_in, grad_query, over_rows)
    grad_key_weight = dot(attn_in, grad_key_low, over_rows)
    grad_value_weight = dot(attn_in, grad_value_low, over_rows)
    grad_normed_one = (
        dot(grad_query, query_weight, over_columns)
        + dot(grad_key_low, key_weight, over_columns)
        + dot(grad_value_low, value_weight, over_columns)
    )
    grad_from_one, grad_ln1_gain, grad_ln1_bias = norm_back(
        grad_normed_one, plain_one, inverse_one, ln1_gain
    )
    grad_pooled = (grad_mixed + grad_from_one).astype(BF16)
    grad_pool_weight = dot(pooled_in, grad_pooled, over_rows)
    grad_pool_bias = jnp.sum(grad_pooled.astype(F32), axis=0)
    grad_shifted = dot(grad_pooled, pool_weight, over_columns).reshape(1, bytes_here, width)
    incoming = passed_along(grad_shifted[:, :2, :], "seq", -1)
    input_grad = (
        cotangent.astype(F32) + jnp.concatenate([grad_shifted[:, 2:, :], incoming], 1)
    ).astype(BF16)
    late = lax.psum(
        tuple(
            grad.astype(BF16)
            for grad in (
                grad_pool_weight, grad_query_weight, grad_key_weight, grad_value_weight, grad_pos_weight,
            )
        ),
        ("dp", "seq"),
    )
    small_parts = (
        grad_pool_bias, grad_ln1_gain, grad_ln1_bias, grad_content_bias, grad_pos_bias,
        grad_ln2_gain, grad_ln2_bias, grad_ffn_in_bias, grad_ffn_out_bias, grad_up_bias,
    )
    small = lax.psum(jnp.concatenate(small_parts), ("dp", "seq"))
    cuts = np.cumsum([part.shape[0] for part in small_parts])[:-1].tolist()
    (
        sum_pool_bias, sum_ln1_gain, sum_ln1_bias, sum_content, sum_pos,
        sum_ln2_gain, sum_ln2_bias, sum_in_bias, sum_out_bias, sum_up_bias,
    ) = jnp.split(small, cuts)
    sum_in, sum_out, sum_up, sum_mix = (grad.astype(F32) for grad in early)
    sum_pool, sum_q, sum_k, sum_v, sum_p = (grad.astype(F32) for grad in late)
    return (
        outputs, input_grad, sum_pool, sum_pool_bias, sum_ln1_gain, sum_ln1_bias, sum_q, sum_k, sum_v,
        sum_mix, sum_p, sum_content, sum_pos, sum_ln2_gain, sum_ln2_bias, sum_in, sum_in_bias,
        sum_out, sum_out_bias, sum_up, sum_up_bias,
    )


EARLY_ROWS, LATE_ROWS = 6144, 3584
EARLY_CHUNKS = ((0, 2048, False), (2048, 2048, True), (4096, 2048, False))
LATE_CHUNKS = ((3072, 512, False), (1536, 1536, False), (0, 1024, True), (1024, 512, False))
SMALL_ROWS = 16
OVER_ROWS = ((0,), (0,))
OVER_COLUMNS = ((1,), (1,))


class Reduction:
    def __init__(self, buffer, start, rows, by_z, bufs, sems, free, small=None):
        self.buffer, self.sems, self.free, self.small = buffer, sems, free, small
        core, chip = lax.axis_index("dp"), lax.axis_index("seq")
        self.core, self.chip = core, chip
        x, y, z = chip % 2, (chip // 2) % 2, chip // 4
        first_x = core == 0
        self.peer_x, self.peer_y = (core, chip + 1 - 2 * x), (core, chip + 2 - 4 * y)
        self.z_peers = [(core, chip + ((z + away) % 4 - z) * 4) for away in (1, 2, 3)]
        self.z = z

        def pair(bit, peer_core, peer_chip):
            return (bit, [(1 - bit, peer_core, peer_chip)])

        one = pair(jnp.where(first_x, x, y), core, jnp.where(first_x, self.peer_x[1], self.peer_y[1]))
        two = pair(jnp.where(first_x, y, x), core, jnp.where(first_x, self.peer_y[1], self.peer_x[1]))
        stages = [pair(core, 1 - core, chip)]
        if by_z:
            low, high = z % 2, z // 2
            stages += [pair(low, core, chip + 4 - 8 * low), one, two, pair(high, core, chip + 8 - 16 * high)]
        else:
            stages += [one, two, (z, [((z + away) % 4, core, self.z_peers[away - 1][1]) for away in (1, 2, 3)])]
        self.stages = []
        at, size, first = start, rows, 0
        for buf, (own, others) in zip(bufs, stages):
            ways = len(others) + 1
            self.stages.append((at, size, size // ways, own, others, buf, first))
            at, size, first = at + own * (size // ways), size // ways, first + len(others)
        self.back = first
        self.last = 2 * len(stages)

    def rows(self, start, size):
        return self.buffer.at[pl.ds(pl.multiple_of(start, 16), size)]

    def copy(self, index, source, target, core, chip):
        return pltpu.make_async_remote_copy(
            source, target, self.sems.at[0, index], self.sems.at[1, index],
            device_id=(core, chip), device_id_type=MESH,
        )

    def done(self, index, source):
        copy = self.copy(index, source, source, 1 - self.core, self.chip)
        copy.wait_send()
        copy.wait_recv()

    def add(self, start, size, part_start, buf):
        chunk = min(size, 128)
        while size % chunk:
            chunk -= 16

        def one(step, carry):
            at = pl.ds(pl.multiple_of(start + step * chunk, 16), chunk)
            here = pl.ds(pl.multiple_of(part_start + step * chunk, 16), chunk)
            total = self.buffer[at].astype(F32)
            for part in range(buf.shape[0]):
                total = total + buf[part, here].astype(F32)
            self.buffer[at] = total.astype(BF16)
            return carry

        lax.fori_loop(0, size // chunk, one, 0)

    def send_parts(self, number):
        at, _, part, _, others, buf, first = self.stages[number]
        for place, (other, core, chip) in enumerate(others):
            self.copy(first + place, self.rows(at + other * part, part), buf.at[place], core, chip).start()

    def send_back(self, number):
        at, _, part, own, others, _, first = self.stages[number]
        pl.semaphore_wait(self.free.at[number], len(others))
        mine = self.rows(at + own * part, part)
        for place, (_, core, chip) in enumerate(others):
            self.copy(self.back + first + place, mine, mine, core, chip).start()

    def step(self, number):
        count = len(self.stages)
        if number == 0:
            self.send_parts(0)
        elif number <= count:
            at, _, part, own, others, buf, first = self.stages[number - 1]
            for place, (_, core, chip) in enumerate(others):
                self.done(first + place, buf.at[place])
            for _, core, chip in others:
                pl.semaphore_signal(self.free.at[number - 1], inc=1, device_id=(core, chip), device_id_type=MESH)
            kept = at + own * part
            if number < count:
                _, _, next_part, next_own, next_others, _, _ = self.stages[number]
                for other, _, _ in next_others:
                    self.add(kept + other * next_part, next_part, other * next_part, buf)
                self.send_parts(number)
                self.add(kept + next_own * next_part, next_part, next_own * next_part, buf)
            else:
                self.add(kept, part, 0, buf)
                self.send_back(count - 1)
        else:
            stage = 2 * count - number
            at, _, part, own, others, _, first = self.stages[stage]
            for place in range(len(others)):
                self.done(self.back + first + place, self.rows(at + own * part, part))
            if stage > 0:
                self.send_back(stage - 1)
        if self.small is not None:
            self.small_step(number)

    def small_step(self, number):
        own, taken = self.small
        first = 2 * self.back
        if number in (1, 2, 3):
            self.done(first + number - 1, own)
            own[...] = own[...] + taken[number - 1]
        if number < 3:
            core, chip = ((1 - self.core, self.chip), self.peer_x, self.peer_y)[number]
            self.copy(first + number, own, taken.at[number], core, chip).start()
        if number == 3:
            taken[3 + self.z] = own[...]
            for place, (core, chip) in enumerate(self.z_peers):
                self.copy(first + 3 + place, own, taken.at[3 + self.z], core, chip).start()
        if number == 4:
            for place in range(3):
                self.done(first + 3 + place, own)
            own[...] = (taken[3] + taken[4]) + (taken[5] + taken[6])


REDUCTION_SEMS = 18


def reduction_scratch(rows, by_z):
    shapes = [(1, rows // 2), (1, rows // 4), (1, rows // 8)]
    shapes += [(1, rows // 16), (1, rows // 32)] if by_z else [(3, rows // 32)]
    return [pltpu.VMEM(shape + (512,), BF16) for shape in shapes]


def gelu_pair(value):
    falling = jnp.exp(value * value * -0.5)
    turn = 1.0 / (1.0 + 0.3275911 * 0.7071067811865476 * jnp.abs(value))
    series = turn * (
        0.254829592
        + turn * (-0.284496736 + turn * (1.421413741 + turn * (-1.453152027 + turn * 1.061405429)))
    )
    tail = 0.5 * series * falling
    share = jnp.where(value >= 0, 1.0 - tail, tail)
    return value * share, share + value * falling * 0.3989422804014327


def norm_parts(hidden):
    average = jnp.mean(hidden, -1, keepdims=True)
    centred = hidden - average
    inverse = lax.rsqrt(jnp.mean(centred * centred, -1, keepdims=True) + epsilon)
    return centred * inverse, inverse


def norm_grad(grad_out, normed, inverse, gain):
    scaled = grad_out * gain
    return inverse * (
        scaled
        - jnp.mean(scaled, -1, keepdims=True)
        - normed * jnp.mean(scaled * normed, -1, keepdims=True)
    )


def column_sum(value):
    return jnp.sum(value, 0, keepdims=True)


def layer_kernel(n, length, layout, *refs):
    taken = iter(refs)
    given, vectors, outs, scratch = ({name: next(taken) for name in part} for part in layout)
    r = types.SimpleNamespace(**vectors, **outs, **scratch)
    group = 2
    rounds = n // group
    tile = 2 * length
    half_len = length // 2
    width = 512
    scale = HEAD**-0.5
    core, chip, row, head, member = whereabouts(group)
    count = 2 * n
    me = core * n + chip

    loads = {}
    chunk_refs = list(refs[len(refs) - sum(5 if cut[2] else 4 for cut in EARLY_CHUNKS + LATE_CHUNKS) :])

    def reduction(buffer, index, cut, small=None):
        bufs = [chunk_refs.pop(0) for _ in range(5 if cut[2] else 4)]
        return Reduction(buffer, *cut, bufs, r.sum_sem.at[index], r.sum_free.at[index], small)

    for index, (name, source) in enumerate(given.items()):
        loads[name] = pltpu.make_async_copy(source, scratch[name], r.load_sem.at[index])
        loads[name].start()

    def ready(*which):
        for ref in which:
            next(loads[name] for name in given if scratch[name] is ref).wait()

    barrier = pltpu.get_barrier_semaphore()

    def greet(step, carry):
        other = (me + step) % count
        pl.semaphore_signal(barrier, inc=1, device_id=(other // n, other % n), device_id_type=MESH)
        return carry

    lax.fori_loop(1, count, greet, 0)

    low_bound, high_bound = r.bounds[0, 0], r.bounds[0, 1]
    r.edges[core, :8] = jnp.full((8, 128), low_bound, jnp.int32)
    r.edges[core, 8:] = jnp.full((8, 128), high_bound, jnp.int32)

    def tokens_of(source, target):
        for block in range(width // 128):
            r.mixing[block] = source[:, block * 128 : (block + 1) * 128].astype(F32)
            for part in range(3):
                every = r.mixing[block, pl.ds(part, length, stride=3), :]
                start = part * width + block * 128
                target[:, start : start + 128] = every.astype(BF16)

    ready(r.x_bytes, r.pool_w)
    tokens_of(r.x_bytes, r.x3)
    own = dot(r.x3[:, :width], r.pool_w[2 * width :])
    before = dot(r.x3[:, width:], r.pool_w[: 2 * width])
    pl.semaphore_wait(barrier, count - 1)

    def edge_copy():
        return pltpu.make_async_remote_copy(
            r.edges.at[core], r.edges.at[core], r.side_sem.at[0], r.side_sem.at[1],
            device_id=(1 - core, chip), device_id_type=MESH,
        )

    def rim_copy():
        return pltpu.make_async_remote_copy(
            r.x3.at[length - 16 :, width:], r.rim, r.side_sem.at[2], r.side_sem.at[3],
            device_id=(core, (chip + 1) % n), device_id_type=MESH,
        )

    edge_copy().start()

    @pl.when(chip < n - 1)
    def _():
        rim_copy().start()

    @pl.when(chip == 0)
    def _():
        r.rim[...] = jnp.zeros_like(r.rim)

    @pl.when(chip > 0)
    def _():
        rim_copy().wait_recv()

    rim_sum = dot(r.rim[...], r.pool_w[: 2 * width])
    at_row = lax.broadcasted_iota(jnp.int32, (length, width), 0)
    before = jnp.where(at_row == 0, rim_sum[15:16], pltpu.roll(before, 1, 0))
    pooled = own + before + r.pool_b[...]
    r.pooled[...] = pooled
    plain, _ = norm_parts(pooled)
    attn_in = (plain * r.ln1_g[...] + r.ln1_b[...]).astype(BF16)
    r.attn_in[...] = attn_in
    ready(r.q_w, r.k_w, r.v_w)
    query = dot(attn_in, r.q_w[...])
    keys = dot(attn_in, r.k_w[...])
    values = dot(attn_in, r.v_w[...])
    for h in range(HEADS):
        at = slice(h * HEAD, (h + 1) * HEAD)
        r.q_out[h] = packed(query[:, at]).astype(BF16)
        r.kv_out[h] = jnp.concatenate([keys[:, at], values[:, at]], 1).astype(BF16)
    turn_to, spot_to = place_of(chip, group)

    def q_jobs(array, out, sem, recv):
        jobs = []
        for h in range(HEADS):
            to_chip, to_core = chip_of(core, h, spot_to, group)
            jobs.append((array.at[h], out.at[turn_to], (sem, recv.at[turn_to]), to_core, to_chip))
        return jobs

    kv_jobs = []
    for h in range(HEADS):
        to_chip, _ = chip_of(core, h, 0, group)
        sems = (r.send_sem.at[1], r.kv_sem.at[chip])
        kv_jobs.append((r.kv_out.at[h], r.kv.at[chip], sems, chip % 2, to_chip))
    first_jobs = kv_jobs + q_jobs(r.q_out, r.q, r.send_sem.at[0], r.q_sem)
    for job in first_jobs:
        send(*job)

    ready(r.ct_bytes, r.up_w, r.ffn_out)
    tokens_of(r.ct_bytes, r.ct3)
    grad_final = dot(r.ct3[...], r.up_w[...], OVER_COLUMNS)
    r.grad_final[...] = grad_final
    grad_branch = grad_final.astype(BF16)
    r.grad_branch[...] = grad_branch
    for part in range(4):
        at = slice(part * width, (part + 1) * width)
        r.grad_act[:, at] = dot(grad_branch, r.ffn_out[at], OVER_COLUMNS)
    small = r.small
    small[...] = jnp.zeros_like(small)
    small[11:12] = column_sum(grad_branch.astype(F32))
    for part in range(3):
        at = slice(part * width, (part + 1) * width)
        small[12 + part : 13 + part] = column_sum(r.ct3[:, at].astype(F32))

    ready(r.pos_w, r.table)
    odd = head % 2 == 1
    pair_at = pl.ds(pl.multiple_of((head // 2) * PAIR, PAIR), PAIR)

    def of_head(ref):
        both = ref[:, pair_at].astype(F32)
        return jnp.where(odd, both[:, HEAD:], both[:, :HEAD])

    r.head_w[...] = of_head(r.pos_w).astype(BF16)
    content_bias, pos_bias = of_head(r.content), of_head(r.pos)
    edge_copy().wait_send()
    edge_copy().wait_recv()
    low_edge = r.edges[row, 0:1, 0:1]
    high_edge = r.edges[row, 8:9, 0:1]
    half = width // 2
    lanes = lax.broadcasted_iota(jnp.int32, (length, tile), 1)

    def rows_of(array):
        return pl.ds(pl.multiple_of(array, length), tile)

    def forward(turn):
        at = turn * group + core
        return pltpu.make_async_remote_copy(
            r.kv.at[at], r.kv.at[at], r.send_sem.at[6], r.kv_sem.at[at], device_id=(1 - core, chip), device_id_type=MESH
        )

    def pass_on(turn):
        at = turn * group + core
        arrived(r.kv.at[at], r.kv_sem.at[at])
        forward(turn).start()

    pass_on(0)

    def attend(turn, carry):
        block = block_of(turn, member, group)

        @pl.when(turn < rounds - 1)
        def _():
            pass_on(turn + 1)

        arrived(r.q.at[turn], r.q_sem.at[turn])
        other = turn * group + 1 - core
        arrived(r.kv.at[other], r.kv_sem.at[other])
        query_u, _, turned = query_parts(
            r.q[turn], content_bias, pos_bias, r.head_w[...], r.sines[...], r.cosines[...]
        )
        head_part = (query_u.astype(F32) * scale).astype(BF16)
        r.extra[:, :PAIR] = jnp.concatenate([head_part, jnp.zeros_like(head_part)], 1)
        r.extra[:, PAIR:] = (turned * scale).astype(BF16)
        places = block * length + lax.broadcasted_iota(jnp.int32, (length, 1), 0)
        opening = jnp.where(places >= high_edge, high_edge, jnp.where(places >= low_edge, low_edge, 0))

        def score_step(step, top):
            pair = r.kv[pl.ds(step * group, group)].reshape(tile, PAIR)
            waves = r.table[rows_of((n - 1 - block) * length + step * tile), :]
            score = dot(r.extra[:, :PAIR], pair, OVER_COLUMNS) + dot(r.extra[:, PAIR:], waves, OVER_COLUMNS)
            at = lanes + step * tile
            allowed = jnp.logical_and(at <= places, at >= opening)
            score = jnp.where(allowed, score, masked_score)
            r.score[step] = score
            for part in range(tile // 128):
                top = jnp.maximum(top, score[:, part * 128 : (part + 1) * 128])
            return top

        top = lax.fori_loop(0, turn + 1, score_step, jnp.full((length, 128), masked_score, F32))
        top = jnp.max(top, 1, keepdims=True)

        def value_step(step, state):
            total, summed = state
            weight = jnp.exp(r.score[step] - top)
            for part in range(tile // 128):
                total = total + weight[:, part * 128 : (part + 1) * 128]
            low = weight.astype(BF16)
            r.keep[turn * (turn + 1) // 2 + step] = low
            pair = r.kv[pl.ds(step * group, group)].reshape(tile, PAIR)
            return total, summed + dot(low, pair)

        total, summed = lax.fori_loop(
            0, turn + 1, value_step, (jnp.zeros((length, 128), F32), jnp.zeros((length, PAIR), F32))
        )
        inverse = 1.0 / jnp.sum(total, 1, keepdims=True)
        attended = summed[:, HEAD:] * inverse
        r.att[turn] = jnp.concatenate([jnp.broadcast_to(inverse, (length, HEAD)), attended], 1)
        r.att_out[turn] = packed(attended).astype(BF16)
        send(
            r.att_out.at[turn], r.att_in.at[head], (r.send_sem.at[2], r.att_sem.at[0]), row, block
        )
        return carry

    lax.fori_loop(0, rounds, attend, 0)
    for source, _, sems, to_core, to_chip in first_jobs:
        sent(source, sems[0], to_core, to_chip)
    for turn in range(rounds):
        forward(turn).wait_send()

    def joined(get):
        parts = [get(h) for h in range(HEADS)]
        upper = jnp.concatenate([part[:, :HEAD] for part in parts], 1)
        lower = jnp.concatenate([part[:, HEAD:] for part in parts], 1)
        return jnp.concatenate([upper, lower], 0)

    arrived(r.att_in, r.att_sem.at[0])
    ready(r.out_w, r.ffn_in)
    att_low = joined(lambda h: r.att_in[h].astype(F32)).astype(BF16)
    r.att_low[...] = att_low
    mixed = r.pooled[...] + dot(att_low, r.out_w[...])
    r.mixed[...] = mixed
    plain_two, inverse_two = norm_parts(mixed)
    ffn_input = (plain_two * r.ln2_g[...] + r.ln2_b[...]).astype(BF16)
    r.ffn_input[...] = ffn_input
    grad_normed = jnp.zeros((length, width), F32)
    for part in range(4):
        at = slice(part * width, (part + 1) * width)
        pre_act = dot(ffn_input, r.ffn_in[:, at]) + r.ffn_in_b[:, at]
        act, slope = gelu_pair(pre_act)
        r.act_low[:, at] = act.astype(BF16)
        grad_pre = (r.grad_act[:, at] * slope).astype(BF16)
        r.grad_pre[:, at] = grad_pre
        small[7 + part : 8 + part] = column_sum(grad_pre.astype(F32))
        grad_normed = grad_normed + dot(grad_pre, r.ffn_in[:, at], OVER_COLUMNS)
    small[5:6] = column_sum(grad_normed * plain_two)
    small[6:7] = column_sum(grad_normed)
    grad_mixed = r.grad_final[...] + norm_grad(grad_normed, plain_two, inverse_two, r.ln2_g[...])
    r.grad_final[...] = grad_mixed
    grad_mixed_low = grad_mixed.astype(BF16)
    grad_att = dot(grad_mixed_low, r.out_w[...], OVER_COLUMNS)
    for h in range(HEADS):
        r.q_out[h] = packed(grad_att[:, h * HEAD : (h + 1) * HEAD]).astype(BF16)
    second_jobs = q_jobs(r.q_out, r.grad, r.send_sem.at[3], r.grad_sem)
    for job in second_jobs:
        send(*job)

    early, late = r.early, r.late
    count_early, count_late = len(EARLY_CHUNKS), len(LATE_CHUNKS)
    sums = [reduction(early, index, cut) for index, cut in enumerate(EARLY_CHUNKS)]
    for index, cut in enumerate(LATE_CHUNKS):
        small_pair = (small, r.small_in) if index == count_late - 1 else None
        sums.append(reduction(late, count_early + index, cut, small_pair))

    def steps_at(moment):
        for index, number in SCHEDULE.get(moment, ()):
            sums[index].step(number)

    for part in range(4):
        at = slice(part * width, (part + 1) * width)
        early[at] = dot(r.ffn_input[...], r.grad_pre[:, at], OVER_ROWS).astype(BF16)
    sums[0].step(0)
    steps_at(-4)
    for part in range(4):
        at = slice(part * width, (part + 1) * width)
        early[2048 + part * width : 2048 + (part + 1) * width] = dot(
            r.act_low[:, at], r.grad_branch[...], OVER_ROWS
        ).astype(BF16)
    sums[1].step(0)
    steps_at(-3)
    early[5632:] = dot(r.att_low[...], grad_mixed_low, OVER_ROWS).astype(BF16)
    final_low = (r.mixed[...] + dot(r.act_low[...], r.ffn_out[...]) + r.ffn_out_b[...]).astype(BF16)
    for part in range(3):
        at = slice(part * width, (part + 1) * width)
        early[4096 + part * width : 4096 + (part + 1) * width] = dot(final_low, r.ct3[:, at], OVER_ROWS).astype(BF16)
    sums[2].step(0)
    steps_at(-2)
    for part in range(3):
        at = slice(part * width, (part + 1) * width)
        lifted = dot(final_low, r.up_w[:, at]) + r.up_b[:, at]
        r.out3[:, at] = (r.x3[:, at].astype(F32) + lifted).astype(BF16)

    steps_at(-1)

    r.dkv[...] = jnp.zeros_like(r.dkv)
    r.dhead[...] = jnp.zeros_like(r.dhead)
    r.dbias[...] = jnp.zeros_like(r.dbias)

    def give_over(turn):
        return pltpu.make_async_remote_copy(
            r.dkv_out.at[turn * group + 1 - core], r.dkv_other.at[turn], r.send_sem.at[7], r.other_sem.at[turn],
            device_id=(1 - core, chip), device_id_type=MESH,
        )

    def hand_in(turn):
        at = turn * group + core
        give_over(turn).wait_recv()
        total = r.dkv[pl.ds(pl.multiple_of(at * length, length), length)] + r.dkv_other[turn].astype(F32)
        r.dkv_out[at] = total.astype(BF16)
        send(r.dkv_out.at[at], r.dkv_in.at[head], (r.send_sem.at[4], r.dkv_sem.at[0]), row, at)

    def back(index, carry):
        turn = rounds - 1 - index
        block = block_of(turn, member, group)
        arrived(r.grad.at[turn], r.grad_sem.at[turn])
        query = unpacked(r.q[turn].astype(F32))
        query_u = ((query + content_bias).astype(BF16).astype(F32) * scale).astype(BF16)
        query_v = (query + pos_bias).astype(BF16)
        grad = unpacked(r.grad[turn].astype(F32))
        inverse = r.att[turn][:, :HEAD]
        grad_part = grad * inverse
        delta = jnp.sum(grad_part * r.att[turn][:, HEAD:], 1, keepdims=True)
        nothing = jnp.zeros((length, HEAD), F32)
        r.extra[:, :PAIR] = jnp.concatenate([nothing, grad_part], 1).astype(BF16)
        r.extra[:, PAIR : 2 * PAIR] = jnp.concatenate([query_u.astype(F32), nothing], 1).astype(BF16)
        r.near[...] = jnp.zeros_like(r.near)
        r.far[...] = jnp.zeros_like(r.far)

        def step_over(step, inner):
            pair = r.kv[pl.ds(step * group, group)].reshape(tile, PAIR)
            waves = r.table[rows_of((n - 1 - block) * length + step * tile), :]
            weight = r.keep[turn * (turn + 1) // 2 + step]
            grad_weight = dot(r.extra[:, :PAIR], pair, OVER_COLUMNS)
            grad_score = (weight.astype(F32) * (grad_weight - delta)).astype(BF16)
            r.near[...] += dot(grad_score, pair)
            r.far[...] += dot(grad_score, waves)
            at = pl.ds(pl.multiple_of(step * tile, tile), tile)
            r.dkv[at] += dot(grad_score, r.extra[:, PAIR : 2 * PAIR], OVER_ROWS) + dot(
                weight, r.extra[:, :PAIR], OVER_ROWS
            )
            return inner

        lax.fori_loop(0, turn + 1, step_over, 0)
        give = turn * group + 1 - core
        r.dkv_out[give] = r.dkv[pl.ds(pl.multiple_of(give * length, length), length)].astype(BF16)
        give_over(turn).start()

        @pl.when(index > 0)
        def _():
            hand_in(turn + 1)

        grad_u = r.near[:, :HEAD] * scale
        turn_sin, turn_cos = r.sines[...], r.cosines[...]
        on_sin, on_cos = r.far[:, :half] * scale, r.far[:, half:] * scale
        lift = on_cos * turn_sin - on_sin * turn_cos
        rest = on_cos * turn_cos + on_sin * turn_sin
        spread = jnp.concatenate([lift, rest], 1).astype(BF16)
        grad_v = dot(spread, r.head_w[...])
        r.dhead[...] += dot(spread, query_v, OVER_ROWS)
        r.dbias[0:1] += column_sum(grad_u)
        r.dbias[1:2] += column_sum(grad_v)
        r.dq_out[turn] = packed(grad_u + grad_v).astype(BF16)
        send(r.dq_out.at[turn], r.dq_in.at[head], (r.send_sem.at[5], r.dq_sem.at[0]), row, block)
        for when in range(rounds):
            if when in SCHEDULE:

                @pl.when(index == when)
                def _(when=when):
                    steps_at(when)

        return carry

    lax.fori_loop(0, rounds, back, 0)
    hand_in(0)

    late[2048 + 1024 :] = jnp.zeros((512, 512), BF16)
    dhead = r.dhead[...]
    nothing = jnp.zeros_like(dhead)
    late[3072:, pair_at] = jnp.where(
        odd, jnp.concatenate([nothing, dhead], 1), jnp.concatenate([dhead, nothing], 1)
    ).astype(BF16)
    nothing = jnp.zeros((2, HEAD), F32)
    dbias = r.dbias[...][:2]
    small[3:5, pair_at] = jnp.where(
        odd, jnp.concatenate([nothing, dbias], 1), jnp.concatenate([dbias, nothing], 1)
    )
    sums[3].step(0)
    steps_at(8)
    for source, _, sems, to_core, to_chip in second_jobs:
        sent(source, sems[0], to_core, to_chip)
    for turn in range(rounds):
        block = block_of(jnp.int32(turn), member, group)
        sent(r.att_out.at[turn], r.send_sem.at[2], row, block)
        sent(r.dq_out.at[turn], r.send_sem.at[5], row, block)
    for turn in range(rounds):
        sent(r.dkv_out.at[turn * group + core], r.send_sem.at[4], row, turn * group + core)
        give_over(turn).wait_send()
    arrived(r.dq_in, r.dq_sem.at[0])
    arrived(r.dkv_in, r.dkv_sem.at[0])
    grad_query = joined(lambda h: r.dq_in[h].astype(F32)).astype(BF16)
    both = [r.dkv_in[h].astype(F32) for h in range(HEADS)]
    grad_keys = jnp.concatenate([part[:, :HEAD] for part in both], 1).astype(BF16)
    grad_values = jnp.concatenate([part[:, HEAD:] for part in both], 1).astype(BF16)
    steps_at(9)
    attn_in = r.attn_in[...]
    late[1536:2048] = dot(attn_in, grad_query, OVER_ROWS).astype(BF16)
    late[2048:2560] = dot(attn_in, grad_keys, OVER_ROWS).astype(BF16)
    late[2560:3072] = dot(attn_in, grad_values, OVER_ROWS).astype(BF16)
    sums[4].step(0)
    steps_at(10)
    grad_normed = (
        dot(grad_query, r.q_w[...], OVER_COLUMNS)
        + dot(grad_keys, r.k_w[...], OVER_COLUMNS)
        + dot(grad_values, r.v_w[...], OVER_COLUMNS)
    )
    plain, inverse = norm_parts(r.pooled[...])
    small[1:2] = column_sum(grad_normed * plain)
    small[2:3] = column_sum(grad_normed)
    grad_pooled = (r.grad_final[...] + norm_grad(grad_normed, plain, inverse, r.ln1_g[...])).astype(BF16)
    r.grad_pooled[...] = grad_pooled
    grad_pooled_wide = grad_pooled.astype(F32)
    steps_at(11)
    small[0:1] = column_sum(grad_pooled_wide)

    def back_rim_copy():
        return pltpu.make_async_remote_copy(
            r.grad_pooled.at[:16], r.back_rim, r.side_sem.at[4], r.side_sem.at[5],
            device_id=(core, (chip + n - 1) % n), device_id_type=MESH,
        )

    @pl.when(chip > 0)
    def _():
        back_rim_copy().start()

    late[1024:1536] = dot(r.x3[:, :width], grad_pooled, OVER_ROWS).astype(BF16)
    follow = pltpu.roll(grad_pooled_wide, length - 1, 0)
    within = jnp.where(at_row == length - 1, 0.0, follow).astype(BF16)
    at_rim = lax.broadcasted_iota(jnp.int32, (16, width), 0)
    rim_row = jnp.where(at_rim == 15, jnp.broadcast_to(grad_pooled_wide[:1], (16, width)), 0.0).astype(BF16)
    late[:1024] = (
        dot(r.x3[:, width:], within, OVER_ROWS) + dot(r.rim[...], rim_row, OVER_ROWS)
    ).astype(BF16)
    for later in sums[5:]:
        later.step(0)
    steps_at(12)

    @pl.when(chip == n - 1)
    def _():
        r.back_rim[...] = jnp.zeros_like(r.back_rim)

    @pl.when(chip < n - 1)
    def _():
        back_rim_copy().wait_recv()

    next_row = r.back_rim[...].astype(F32)[:1]
    follow = jnp.where(at_row == length - 1, next_row, follow).astype(BF16)
    first_part = r.ct3[:, :width].astype(F32) + dot(grad_pooled, r.pool_w[2 * width :], OVER_COLUMNS)
    r.grad3[:, :width] = first_part.astype(BF16)
    other_part = r.ct3[:, width:].astype(F32) + dot(follow, r.pool_w[: 2 * width], OVER_COLUMNS)
    r.grad3[:, width:] = other_part.astype(BF16)

    @pl.when(chip < n - 1)
    def _():
        rim_copy().wait_send()

    @pl.when(chip > 0)
    def _():
        back_rim_copy().wait_send()

    steps_at(13)


SCHEDULE = {
    -2: ((0, 1),),
    -1: ((1, 1),),
    0: ((2, 1), (0, 2),),
    2: ((0, 3), (1, 2),),
    6: ((2, 2),),
    8: ((3, 1), (0, 4), (1, 3),),
    10: ((2, 3),),
    11: ((4, 1),),
    12: ((1, 4), (5, 1), (0, 5),),
    13: (
        (3, 2), (4, 2), (2, 4), (1, 5), (6, 1), (0, 6), (5, 2), (1, 6), (4, 3), (6, 2), (3, 3), (5, 3), (2, 5),
        (6, 3), (3, 4), (1, 7), (5, 4), (4, 4), (0, 7), (2, 6), (6, 4), (5, 5), (3, 5), (1, 8), (0, 8), (3, 6),
        (5, 6), (4, 5), (2, 7), (5, 7), (3, 7), (4, 6), (3, 8), (5, 8), (1, 9), (6, 5), (2, 8), (1, 10), (6, 6),
        (4, 7), (5, 9), (6, 7), (5, 10), (4, 8), (6, 8),
    ),
}


WIDENED = (
    (0, 4, True), (2048, 4, False), (4096, 3, True), (5632, 1, False),
    (0, 3, False), (1536, 1, False), (2048, 1, False), (2560, 1, False), (3072, 1, False),
)
NARROW = ((0, 1), (1, 1), (2, 1), (3, 1), (4, 1), (5, 1), (6, 1), (7, 4), (11, 1), (12, 3))


def last_kernel(*refs):
    early, late, out3, grad3, small = refs[:5]
    wide_outs, narrow_outs, byte_outs = refs[5:14], refs[14:24], refs[24:26]
    staging, mixing, sems = refs[26:]
    copies = []
    for index, (out, (start, blocks, across)) in enumerate(zip(wide_outs, WIDENED)):
        source = early if index < 4 else late
        for block in range(blocks):
            slot = len(copies)

            def widen(step, carry, source=source, slot=slot, first=start + block * 512):
                here = pl.ds(pl.multiple_of(step * 64, 64), 64)
                staging[slot, here] = source[pl.ds(pl.multiple_of(first + step * 64, 64), 64)].astype(F32)
                return carry

            lax.fori_loop(0, 8, widen, 0)
            at = slice(block * 512, (block + 1) * 512)
            target = out.at[:, at] if across else out.at[at]
            copy = pltpu.make_async_copy(staging.at[slot], target, sems.at[slot])
            copy.start()
            copies.append(copy)
    for out, tokens in zip(byte_outs, (out3, grad3)):
        length, width = out.shape[0] // 3, out.shape[1]
        for block in range(width // 128):
            for part in range(3):
                start = part * width + block * 128
                mixing[block, pl.ds(part, length, stride=3), :] = tokens[:, start : start + 128].astype(F32)
            out[:, block * 128 : (block + 1) * 128] = mixing[block].astype(BF16)
    for out, (start, blocks) in zip(narrow_outs, NARROW):
        for block in range(blocks):
            out[:, block * 512 : (block + 1) * 512] = small[start + block : start + block + 1]
    for copy in copies:
        copy.wait()


def finished(early, late, out3, grad3, small):
    length, width = out3.shape[0], out3.shape[1] // 3
    vmem = pl.BlockSpec(memory_space=pltpu.VMEM)
    shapes = [(512, 512 * blocks) if across else (512 * blocks, 512) for _, blocks, across in WIDENED]
    narrow = [(1, 512 * blocks) for _, blocks in NARROW]
    count = sum(blocks for _, blocks, _ in WIDENED)
    outs = pl.pallas_call(
        last_kernel,
        in_specs=[vmem] * 5,
        out_specs=[pl.BlockSpec(memory_space=pl.ANY)] * len(shapes) + [vmem] * (len(narrow) + 2),
        out_shape=[jax.ShapeDtypeStruct(shape, F32) for shape in shapes + narrow]
        + [jax.ShapeDtypeStruct((3 * length, width), BF16)] * 2,
        scratch_shapes=[
            pltpu.VMEM((count, 512, 512), F32), pltpu.VMEM((width // 128, 3 * length, 128), F32),
            pltpu.SemaphoreType.DMA((count,)),
        ],
        compiler_params=pltpu.CompilerParams(vmem_limit_bytes=56 * 2**20),
    )(early, late, out3, grad3, small)
    return outs[: len(shapes)], [out[0] for out in outs[len(shapes) : -2]], outs[-2:]


def fused_body(
    inputs, doc_bounds, pool_weight, pool_bias, ln1_gain, ln1_bias, query_weight, key_weight,
    value_weight, out_weight, pos_weight, content_bias, pos_bias, ln2_gain, ln2_bias, ffn_in,
    ffn_in_bias, ffn_out, ffn_out_bias, up_weight, up_bias, cotangent,
):
    _, bytes_here, width = inputs.shape
    length = bytes_here // 3
    n = lax.axis_size("seq")
    tokens = n * length
    rounds = n // 2
    table, sines, cosines = wave_tables(tokens, length, width)
    given = dict(
        x_bytes=inputs[0], pool_w=pool_weight, q_w=query_weight, k_w=key_weight, v_w=value_weight,
        ct_bytes=cotangent[0], up_w=up_weight, ffn_out=ffn_out, pos_w=pos_weight, table=table,
        out_w=out_weight, ffn_in=ffn_in,
    )
    vectors = dict(
        pool_b=pool_bias, ln1_g=ln1_gain, ln1_b=ln1_bias, content=content_bias, pos=pos_bias, ln2_g=ln2_gain,
        ln2_b=ln2_bias, ffn_in_b=ffn_in_bias, ffn_out_b=ffn_out_bias, up_b=up_bias,
    )
    vectors = {name: vector[None] for name, vector in vectors.items()} | dict(sines=sines, cosines=cosines)
    vmem = pl.BlockSpec(memory_space=pltpu.VMEM)
    outs = dict(
        out3=((length, 3 * width), BF16), grad3=((length, 3 * width), BF16), early=((EARLY_ROWS, 512), BF16),
        late=((LATE_ROWS, 512), BF16), small=((SMALL_ROWS, 512), F32),
    )
    pair_half = (length // 2, PAIR)
    block, wide = (length, width), (length, 4 * width)
    dma, signal = pltpu.SemaphoreType.DMA, pltpu.SemaphoreType.REGULAR
    scratch = {name: pltpu.VMEM(array.shape, array.dtype) for name, array in given.items()}
    low = dict(
        x3=(length, 3 * width), ct3=(length, 3 * width), rim=(16, 2 * width), back_rim=(16, width), attn_in=block, q_out=(HEADS,) + pair_half,
        kv_out=(HEADS, length, PAIR), q=(rounds,) + pair_half, kv=(n, length, PAIR), grad_branch=block,
        head_w=(width, HEAD), extra=(length, PAIR + width), keep=(rounds * (rounds + 1) // 2, length, 2 * length),
        att_out=(rounds,) + pair_half, att_in=(HEADS,) + pair_half, att_low=block, ffn_input=block, act_low=wide,
        grad_pre=wide, grad=(rounds,) + pair_half, dkv_out=(n, length, PAIR), dkv_in=(HEADS, length, PAIR),
        dkv_other=(rounds, length, PAIR), dq_out=(rounds,) + pair_half, dq_in=(HEADS,) + pair_half, grad_pooled=block,
    )
    full = dict(
        mixing=(width // 128, 3 * length, 128), pooled=block, grad_final=block, grad_act=wide, score=(rounds, length, 2 * length), att=(rounds, length, PAIR),
        mixed=block, dkv=(tokens, PAIR), dhead=(width, HEAD), dbias=(8, HEAD), near=(length, PAIR), far=block,
        small_in=(7, SMALL_ROWS, 512),
    )
    scratch |= {name: pltpu.VMEM(shape, BF16) for name, shape in low.items()}
    scratch |= {name: pltpu.VMEM(shape, F32) for name, shape in full.items()}
    scratch |= dict(
        edges=pltpu.VMEM((2, 16, 128), jnp.int32), load_sem=dma((len(given),)), side_sem=dma((6,)), send_sem=dma((8,)), other_sem=dma((rounds,)),

        q_sem=dma((rounds,)), kv_sem=dma((n,)), att_sem=dma((1,)), grad_sem=dma((rounds,)), dkv_sem=dma((1,)),
        dq_sem=dma((1,)), sum_sem=dma((len(EARLY_CHUNKS + LATE_CHUNKS), 2, REDUCTION_SEMS)),
        sum_free=signal((len(EARLY_CHUNKS + LATE_CHUNKS), 5)),
    )
    layout = (list(given), list(vectors) + ["bounds"], list(outs), list(scratch))
    out3, grad3, early, late, small = pl.pallas_call(
        functools.partial(layer_kernel, n, length, layout),
        in_specs=[pl.BlockSpec(memory_space=pl.ANY)] * len(given)
        + [vmem] * len(vectors)
        + [pl.BlockSpec(memory_space=pltpu.SMEM)],
        out_specs=[vmem] * len(outs),
        out_shape=[jax.ShapeDtypeStruct(*out) for out in outs.values()],
        scratch_shapes=list(scratch.values())
        + sum((reduction_scratch(*cut[1:]) for cut in EARLY_CHUNKS + LATE_CHUNKS), []),
        compiler_params=pltpu.CompilerParams(
            collective_id=0, has_side_effects=True, vmem_limit_bytes=60 * 2**20
        ),
    )(*given.values(), *vectors.values(), doc_bounds)
    wide, narrow, both = finished(early, late, out3, grad3, small)
    sum_in, sum_out, sum_up, sum_mix, sum_pool, sum_q, sum_k, sum_v, sum_p = wide
    pool_b, ln1_g, ln1_b, content, pos, ln2_g, ln2_b, in_b, out_b, up_b = narrow
    return (
        both[0][None], both[1][None], sum_pool, pool_b, ln1_g, ln1_b, sum_q, sum_k, sum_v, sum_mix, sum_p,
        content, pos, ln2_g, ln2_b, sum_in, in_b, sum_out, out_b, sum_up, up_b,
    )


def solution(mesh):
    split = P("dp", "seq", None)
    fits = mesh.shape["seq"] == 16
    return jax.shard_map(
        fused_body if fits else body,
        mesh=mesh,
        in_specs=(split, P("dp", None)) + (P(),) * 19 + (split,),
        out_specs=(split, split) + (P(),) * 19,
        check_vma=False,
    )
```

```python
import functools
import types

import jax
import jax.numpy as jnp
import numpy as np
from jax import lax
from jax.experimental import pallas as pl
from jax.experimental.pallas import tpu as pltpu
from jax.sharding import PartitionSpec as P

HEADS = 8
ROWS = 2
HEAD = 64
PAIR = 2 * HEAD
MESH = pl.DeviceIdType.MESH
F32 = jnp.float32
BF16 = jnp.bfloat16

epsilon = 1e-05
masked_score = -1e30


def dot(left, right, dims=((1,), (0,))):
    return lax.dot_general(left, right, (dims, ((), ())), preferred_element_type=F32)


def passed_along(value, axis, steps):
    count = lax.axis_size(axis)
    first, last = (max(0, -steps), min(count, count - steps))
    return lax.ppermute(value, axis, [(source, source + steps) for source in range(first, last)])


def place_of(block, group):
    turn, spot = block // group, block % group
    return turn, jnp.where(turn % 2 == 0, spot, group - 1 - spot)


def block_of(turn, member, group):
    return turn * group + jnp.where(turn % 2 == 0, member, group - 1 - member)


def whereabouts(group):
    core, chip = lax.axis_index("dp"), lax.axis_index("seq")
    chips = group // 2
    unit = chip // chips
    member = (chip % chips) * 2 + core
    return core, chip, unit // HEADS, unit % HEADS, member


def chip_of(row, head, member, group):
    return (row * HEADS + head) * (group // 2) + member // 2, member % 2


def meet(n, group, to_units):
    core, chip, row, head, member = whereabouts(group)
    barrier = pltpu.get_barrier_semaphore()

    def greet(row_or_core, chip_at):
        away = jnp.logical_or(row_or_core != core, chip_at != chip)

        @pl.when(away)
        def _():
            pl.semaphore_signal(
                barrier, inc=1, device_id=(row_or_core, chip_at), device_id_type=MESH
            )

        return away.astype(jnp.int32)

    own_row = row == core
    if to_units:
        for s in range(n):
            greet(row, jnp.int32(s))
        mine = jnp.logical_and(chip // (HEADS * (group // 2)) == core, True)
        pl.semaphore_wait(barrier, HEADS * group - mine.astype(jnp.int32))
    else:
        for h in range(HEADS):
            for g in range(group):
                c, k = chip_of(core, h, g, group)
                greet(jnp.int32(k), c)
        pl.semaphore_wait(barrier, n - own_row.astype(jnp.int32))


def send(source, target, sems, core, chip):
    here_core, here_chip = lax.axis_index("dp"), lax.axis_index("seq")
    here = jnp.logical_and(core == here_core, chip == here_chip)

    @pl.when(here)
    def _():
        pltpu.make_async_copy(source, target, sems[1]).start()

    @pl.when(jnp.logical_not(here))
    def _():
        pltpu.make_async_remote_copy(
            source, target, sems[0], sems[1], device_id=(core, chip), device_id_type=MESH
        ).start()


def sent(source, sem, core, chip):
    here_core, here_chip = lax.axis_index("dp"), lax.axis_index("seq")
    here = jnp.logical_and(core == here_core, chip == here_chip)

    @pl.when(jnp.logical_not(here))
    def _():
        pltpu.make_async_copy(source, source, sem).wait()


def arrived(whole, sem):
    pltpu.make_async_copy(whole, whole, sem).wait()


def to_units_kernel(n, group, *refs):
    count = len(refs) - 2
    arrays, outs = refs[: count // 2], refs[count // 2 : count]
    send_sem, recv_sem = refs[count:]
    core, chip, row, head, member = whereabouts(group)
    turn, spot = place_of(chip, group)
    meet(n, group, True)
    jobs = []
    for h in range(HEADS):
        for index, (array, out) in enumerate(zip(arrays, outs)):
            sems = (send_sem.at[index], recv_sem.at[index])
            if index == 0:
                to_chip, to_core = chip_of(core, h, spot, group)
                jobs.append((array.at[h], out.at[turn], sems, to_core, to_chip))
            else:
                for g in range(group):
                    to_chip, to_core = chip_of(core, h, g, group)
                    jobs.append((array.at[h], out.at[chip], sems, jnp.int32(to_core), to_chip))
    for job in jobs:
        send(*job)
    for source, _, sems, to_core, to_chip in jobs:
        sent(source, sems[0], to_core, to_chip)
    for index, out in enumerate(outs):
        arrived(out, recv_sem.at[index])


def to_owners_kernel(n, group, *refs):
    count = len(refs) - 2
    arrays, outs = refs[: count // 2], refs[count // 2 : count]
    send_sem, recv_sem = refs[count:]
    core, chip, row, head, member = whereabouts(group)
    meet(n, group, False)
    jobs = []
    for turn in range(n // group):
        block = block_of(jnp.int32(turn), member, group)
        sems = (send_sem.at[0], recv_sem.at[0])
        jobs.append((arrays[0].at[turn], outs[0].at[head], sems, row, block))
    if len(arrays) > 1:
        for block in range(n):
            sems = (send_sem.at[1], recv_sem.at[1])
            jobs.append((arrays[1].at[block], outs[1].at[member, head], sems, row, jnp.int32(block)))
    for job in jobs:
        send(*job)
    for source, _, sems, to_core, to_chip in jobs:
        sent(source, sems[0], to_core, to_chip)
    for index, out in enumerate(outs):
        arrived(out, recv_sem.at[index])


def exchange(kernel, n, group, arrays, shapes, ident):
    vmem = pl.BlockSpec(memory_space=pltpu.VMEM)
    return pl.pallas_call(
        functools.partial(kernel, n, group),
        out_shape=[jax.ShapeDtypeStruct(shape, array.dtype) for shape, array in zip(shapes, arrays)],
        in_specs=[vmem] * len(arrays),
        out_specs=[vmem] * len(arrays),
        scratch_shapes=[
            pltpu.SemaphoreType.DMA((len(arrays),)),
            pltpu.SemaphoreType.DMA((len(arrays),)),
        ],
        compiler_params=pltpu.CompilerParams(
            collective_id=ident, has_side_effects=True, vmem_limit_bytes=48 * 2**20
        ),
    )(*arrays)


def unpacked(pair):
    return jnp.concatenate([pair[:, :HEAD], pair[:, HEAD:]], 0)


def packed(block):
    half = block.shape[0] // 2
    return jnp.concatenate([block[:half], block[half:]], 1)


def query_parts(q_pair, content_bias, pos_bias, pos_weight, turn_sin, turn_cos):
    query = unpacked(q_pair.astype(F32))
    query_u = (query + content_bias).astype(BF16)
    query_v = (query + pos_bias).astype(BF16)
    spread = dot(query_v, pos_weight, ((1,), (1,)))
    half = turn_sin.shape[1]
    lift, rest = spread[:, :half], spread[:, half:]
    on_sin = rest * turn_sin - lift * turn_cos
    on_cos = lift * turn_sin + rest * turn_cos
    turned = jnp.concatenate([on_sin, on_cos], 1)
    return query_u, query_v, turned


def attend_kernel(
    n, group, tile, q_ref, kv_ref, table_ref, sin_ref, cos_ref, weight_ref, cb_ref, pb_ref, bounds_ref,
    att_ref, low_ref, total_ref, keep_ref, score_ref, extra_ref,
):
    turn = pl.program_id(0)
    member = whereabouts(group)[4]
    block = block_of(turn, member, group)
    length = sin_ref.shape[0]
    tokens = n * length
    query_u, _, turned = query_parts(
        q_ref[...], cb_ref[...], pb_ref[...], weight_ref[...], sin_ref[...], cos_ref[...]
    )
    scale = HEAD**-0.5
    head_part = (query_u.astype(F32) * scale).astype(BF16)
    extra_ref[:, :HEAD] = head_part
    extra_ref[:, HEAD:PAIR] = jnp.zeros_like(head_part)
    extra_ref[:, PAIR:] = (turned * scale).astype(BF16)
    first = block * length
    tiles = (first + length + tile - 1) // tile
    low_bound, high_bound = bounds_ref[0], bounds_ref[1]
    places = first + lax.broadcasted_iota(jnp.int32, (length, 1), 0)
    opening = jnp.where(
        places >= high_bound, high_bound, jnp.where(places >= low_bound, low_bound, 0)
    )
    lanes = lax.broadcasted_iota(jnp.int32, (length, tile), 1)

    def score_step(step, top):
        start = pl.multiple_of(step * tile, tile)
        keys = kv_ref[pl.ds(start, tile), :]
        waves = table_ref[pl.ds(pl.multiple_of((n - 1 - block) * length + start, length), tile), :]
        score = dot(extra_ref[:, :PAIR], keys, ((1,), (1,))) + dot(
            extra_ref[:, PAIR:], waves, ((1,), (1,))
        )
        at = lanes + start
        allowed = jnp.logical_and(at <= places, at >= opening)
        score = jnp.where(allowed, score, masked_score)
        score_ref[:, pl.ds(start, tile)] = score
        for part in range(tile // 128):
            top = jnp.maximum(top, score[:, part * 128 : (part + 1) * 128])
        return top

    top = lax.fori_loop(0, tiles, score_step, jnp.full((length, 128), masked_score, F32))
    top = jnp.max(top, 1, keepdims=True)

    def value_step(step, state):
        total, summed = state
        start = pl.multiple_of(step * tile, tile)
        weight = jnp.exp(score_ref[:, pl.ds(start, tile)] - top)
        for part in range(tile // 128):
            total = total + weight[:, part * 128 : (part + 1) * 128]
        low = weight.astype(BF16)
        keep_ref[:, pl.ds(start, tile)] = low
        return total, summed + dot(low, kv_ref[pl.ds(start, tile), :])

    total, summed = lax.fori_loop(
        0, tiles, value_step, (jnp.zeros((length, 128), F32), jnp.zeros((length, PAIR), F32))
    )
    total = jnp.sum(total, 1, keepdims=True)
    attended = summed[:, HEAD:] / total
    att_ref[...] = attended
    total_ref[...] = jnp.broadcast_to(total, (length, 128))
    low_ref[...] = packed(attended).astype(BF16)


def back_kernel(
    n, group, tile, q_ref, kv_ref, table_ref, sin_ref, cos_ref, weight_ref, cb_ref, pb_ref,
    att_ref, total_ref, keep_ref, grad_ref,
    dq_ref, dkv_ref, dweight_ref, dcb_ref, dpb_ref, dkv_acc,
):
    turn = pl.program_id(0)
    member = whereabouts(group)[4]
    block = block_of(turn, member, group)
    length = sin_ref.shape[0]
    scale = HEAD**-0.5

    @pl.when(turn == 0)
    def _():
        dkv_acc[...] = jnp.zeros_like(dkv_acc)
        dweight_ref[...] = jnp.zeros_like(dweight_ref)
        dcb_ref[...] = jnp.zeros_like(dcb_ref)
        dpb_ref[...] = jnp.zeros_like(dpb_ref)

    query_u, query_v, _ = query_parts(
        q_ref[...], cb_ref[...], pb_ref[...], weight_ref[...], sin_ref[...], cos_ref[...]
    )
    head_part = (query_u.astype(F32) * scale).astype(BF16)
    grad = unpacked(grad_ref[...].astype(F32))
    inverse = 1.0 / total_ref[:, :1]
    delta = jnp.sum(grad * att_ref[...], 1, keepdims=True) * inverse
    grad_low = (grad * inverse).astype(BF16)
    nothing = jnp.zeros_like(grad_low)
    grad_wide = jnp.concatenate([nothing, grad_low], 1)
    query_wide = jnp.concatenate([head_part, nothing], 1)
    tiles = (block * length + length + tile - 1) // tile

    def step_over(step, state):
        near, far = state
        start = pl.multiple_of(step * tile, tile)
        keys = kv_ref[pl.ds(start, tile), :]
        waves = table_ref[pl.ds(pl.multiple_of((n - 1 - block) * length + start, length), tile), :]
        weight = keep_ref[:, pl.ds(start, tile)]
        grad_weight = dot(grad_wide, keys, ((1,), (1,)))
        grad_score = (weight.astype(F32) * (grad_weight - delta)).astype(BF16)
        near = near + dot(grad_score, keys)
        far = far + dot(grad_score, waves)
        dkv_acc[pl.ds(start, tile), :] += dot(grad_score, query_wide, ((0,), (0,))) + dot(
            weight, grad_wide, ((0,), (0,))
        )
        return near, far

    near, far = lax.fori_loop(
        0,
        tiles,
        step_over,
        (jnp.zeros((length, PAIR), F32), jnp.zeros((length, table_ref.shape[1]), F32)),
    )
    grad_u = near[:, :HEAD] * scale
    half = sin_ref.shape[1]
    turn_sin, turn_cos = sin_ref[...], cos_ref[...]
    on_sin, on_cos = far[:, :half] * scale, far[:, half:] * scale
    lift = on_cos * turn_sin - on_sin * turn_cos
    rest = on_cos * turn_cos + on_sin * turn_sin
    spread = jnp.concatenate([lift, rest], 1).astype(BF16)
    grad_v = dot(spread, weight_ref[...])
    dweight_ref[...] += dot(spread, query_v, ((0,), (0,)))
    dcb_ref[...] += jnp.sum(grad_u, 0, keepdims=True)
    dpb_ref[...] += jnp.sum(grad_v, 0, keepdims=True)
    dq_ref[...] = packed(grad_u + grad_v).astype(BF16)

    @pl.when(turn == pl.num_programs(0) - 1)
    def _():
        dkv_ref[...] = dkv_acc[...].astype(BF16)


def wave_tables(tokens, length, width, more=0):
    rates = 10000.0 ** (-2.0 * np.arange(width // 2, dtype=np.float64) / width)
    far = (np.arange(tokens + max(length, more), dtype=np.float64) - (tokens - length))[:, None] * rates
    near = np.arange(length, dtype=np.float64)[:, None] * rates
    table = np.concatenate([np.sin(far), np.cos(far)], 1)
    return (
        jnp.asarray(table, dtype=BF16),
        jnp.asarray(np.sin(near), dtype=F32),
        jnp.asarray(np.cos(near), dtype=F32),
    )


def whole_spec(shape):
    return pl.BlockSpec(shape, lambda turn: (0,) * len(shape))


def turn_spec(shape):
    return pl.BlockSpec((None,) + shape, lambda turn: (turn,) + (0,) * len(shape))


def layer_norm(hidden, gain, bias):
    average = jnp.mean(hidden, -1, keepdims=True)
    centred = hidden - average
    inverse = lax.rsqrt(jnp.mean(centred * centred, -1, keepdims=True) + epsilon)
    normed = centred * inverse
    return (normed * gain + bias, normed, inverse)


def norm_back(grad_out, normed, inverse, gain):
    scaled = grad_out * gain
    grad_in = inverse * (
        scaled
        - jnp.mean(scaled, -1, keepdims=True)
        - normed * jnp.mean(scaled * normed, -1, keepdims=True)
    )
    return (grad_in, jnp.sum(grad_out * normed, axis=0), jnp.sum(grad_out, axis=0))


def exact_gelu(value):
    return jax.nn.gelu(value, approximate=False)


def heads_packed(array):
    length = array.shape[0]
    split = array.reshape(2, length // 2, HEADS, HEAD)
    return jnp.transpose(split, (2, 1, 0, 3)).reshape(HEADS, length // 2, PAIR)


def heads_unpacked(array):
    half = array.shape[1]
    split = array.reshape(HEADS, half, 2, HEAD)
    return jnp.transpose(split, (2, 1, 0, 3)).reshape(2 * half, HEADS * HEAD)


def body(
    inputs, doc_bounds, pool_weight, pool_bias, ln1_gain, ln1_bias, query_weight, key_weight,
    value_weight, out_weight, pos_weight, content_bias, pos_bias, ln2_gain, ln2_bias, ffn_in,
    ffn_in_bias, ffn_out, ffn_out_bias, up_weight, up_bias, cotangent,
):
    _, bytes_here, width = inputs.shape
    length = bytes_here // 3
    n = lax.axis_size("seq")
    tokens = n * length
    group = 2 * n // (ROWS * HEADS)
    rounds = n // group
    tile = 2 * length
    row, head, member = whereabouts(group)[2:]

    all_bounds = lax.all_gather(doc_bounds, "dp", axis=0, tiled=True)
    bounds = lax.dynamic_slice(all_bounds, (row, 0), (1, 2))[0]
    table, turn_sin, turn_cos = wave_tables(tokens, length, width)
    head_weight = lax.dynamic_slice(pos_weight, (0, head * HEAD), (width, HEAD))
    head_cb = lax.dynamic_slice(content_bias, (head * HEAD,), (HEAD,))[None]
    head_pb = lax.dynamic_slice(pos_bias, (head * HEAD,), (HEAD,))[None]

    rim = passed_along(inputs[:, bytes_here - 2 :, :], "seq", 1)
    shifted = jnp.concatenate([rim, inputs[:, : bytes_here - 2, :]], 1)
    pooled_in = shifted.reshape(length, 3 * width)
    pooled = dot(pooled_in, pool_weight) + pool_bias
    normed_one, plain_one, inverse_one = layer_norm(pooled, ln1_gain, ln1_bias)
    attn_in = normed_one.astype(BF16)
    query = dot(attn_in, query_weight).astype(BF16)
    keys = dot(attn_in, key_weight).astype(BF16).reshape(length, HEADS, HEAD)
    values = dot(attn_in, value_weight).astype(BF16).reshape(length, HEADS, HEAD)
    q_out = heads_packed(query)
    kv_out = jnp.transpose(jnp.concatenate([keys, values], 2), (1, 0, 2))

    q_in, kv_in = exchange(
        to_units_kernel, n, group, (q_out, kv_out),
        ((rounds, length // 2, PAIR), (n, length, PAIR)), 0,
    )
    kv_in = kv_in.reshape(tokens, PAIR)

    common_specs = [
        turn_spec((length // 2, PAIR)),
        whole_spec((tokens, PAIR)),
        whole_spec(table.shape),
        whole_spec(turn_sin.shape),
        whole_spec(turn_cos.shape),
        whole_spec(head_weight.shape),
        whole_spec((1, HEAD)),
        whole_spec((1, HEAD)),
    ]
    common = (q_in, kv_in, table, turn_sin, turn_cos, head_weight, head_cb, head_pb)
    attended, att_low, total, keep = pl.pallas_call(
        functools.partial(attend_kernel, n, group, tile),
        grid=(rounds,),
        in_specs=common_specs + [pl.BlockSpec(memory_space=pltpu.SMEM)],
        out_specs=[
            turn_spec((length, HEAD)),
            turn_spec((length // 2, PAIR)),
            turn_spec((length, 128)),
            turn_spec((length, tokens)),
        ],
        out_shape=[
            jax.ShapeDtypeStruct((rounds, length, HEAD), F32),
            jax.ShapeDtypeStruct((rounds, length // 2, PAIR), BF16),
            jax.ShapeDtypeStruct((rounds, length, 128), F32),
            jax.ShapeDtypeStruct((rounds, length, tokens), BF16),
        ],
        scratch_shapes=[
            pltpu.VMEM((length, tokens), F32),
            pltpu.VMEM((length, PAIR + width), BF16),
        ],
        compiler_params=pltpu.CompilerParams(vmem_limit_bytes=56 * 2**20),
    )(*common, bounds)

    (att_back,) = exchange(
        to_owners_kernel, n, group, (att_low,), ((HEADS, length // 2, PAIR),), 1
    )
    attended_low = heads_unpacked(att_back)

    mixed = pooled + dot(attended_low, out_weight)
    normed_two, plain_two, inverse_two = layer_norm(mixed, ln2_gain, ln2_bias)
    ffn_input = normed_two.astype(BF16)
    pre_act = dot(ffn_input, ffn_in) + ffn_in_bias
    activated, gelu_pull = jax.vjp(exact_gelu, pre_act)
    act_low = activated.astype(BF16)
    final = mixed + dot(act_low, ffn_out) + ffn_out_bias
    final_low = final.astype(BF16)
    upsampled = dot(final_low, up_weight) + up_bias
    outputs = (inputs.astype(F32) + upsampled.reshape(1, bytes_here, width)).astype(BF16)
    grad_up = cotangent.reshape(length, 3 * width)
    over_rows = ((0,), (0,))
    over_columns = ((1,), (1,))
    grad_up_weight = dot(final_low, grad_up, over_rows)
    grad_up_bias = jnp.sum(grad_up.astype(F32), axis=0)
    grad_final = dot(grad_up, up_weight, over_columns)
    grad_branch = grad_final.astype(BF16)
    grad_ffn_out = dot(act_low, grad_branch, over_rows)
    grad_ffn_out_bias = jnp.sum(grad_branch.astype(F32), axis=0)
    grad_act = dot(grad_branch, ffn_out, over_columns)
    grad_pre = gelu_pull(grad_act)[0].astype(BF16)
    grad_ffn_in = dot(ffn_input, grad_pre, over_rows)
    grad_ffn_in_bias = jnp.sum(grad_pre.astype(F32), axis=0)
    grad_normed_two = dot(grad_pre, ffn_in, over_columns)
    grad_from_two, grad_ln2_gain, grad_ln2_bias = norm_back(
        grad_normed_two, plain_two, inverse_two, ln2_gain
    )
    grad_mixed = grad_final + grad_from_two
    grad_attn_branch = grad_mixed.astype(BF16)
    grad_out_weight = dot(attended_low, grad_attn_branch, over_rows)
    grad_attended = dot(grad_attn_branch, out_weight, over_columns).astype(BF16)

    early = lax.psum(
        tuple(
            grad.astype(BF16) for grad in (grad_ffn_in, grad_ffn_out, grad_up_weight, grad_out_weight)
        ),
        ("dp", "seq"),
    )

    (grad_in,) = exchange(
        to_units_kernel, n, group, (heads_packed(grad_attended),), ((rounds, length // 2, PAIR),), 2
    )
    dq_out, dkv_out, grad_head_weight, grad_head_cb, grad_head_pb = pl.pallas_call(
        functools.partial(back_kernel, n, group, tile),
        grid=(rounds,),
        in_specs=common_specs
        + [
            turn_spec((length, HEAD)),
            turn_spec((length, 128)),
            turn_spec((length, tokens)),
            turn_spec((length // 2, PAIR)),
        ],
        out_specs=[
            turn_spec((length // 2, PAIR)),
            whole_spec((tokens, PAIR)),
            whole_spec((width, HEAD)),
            whole_spec((1, HEAD)),
            whole_spec((1, HEAD)),
        ],
        out_shape=[
            jax.ShapeDtypeStruct((rounds, length // 2, PAIR), BF16),
            jax.ShapeDtypeStruct((tokens, PAIR), BF16),
            jax.ShapeDtypeStruct((width, HEAD), F32),
            jax.ShapeDtypeStruct((1, HEAD), F32),
            jax.ShapeDtypeStruct((1, HEAD), F32),
        ],
        scratch_shapes=[pltpu.VMEM((tokens, PAIR), F32)],
        compiler_params=pltpu.CompilerParams(vmem_limit_bytes=56 * 2**20),
    )(*common, attended, total, keep, grad_in)
    dq_back, dkv_back = exchange(
        to_owners_kernel, n, group, (dq_out, dkv_out.reshape(n, length, PAIR)),
        ((HEADS, length // 2, PAIR), (group, HEADS, length, PAIR)), 3,
    )
    grad_query = heads_unpacked(dq_back)
    dkv_back = jnp.transpose(jnp.sum(dkv_back.astype(F32), 0), (1, 0, 2)).astype(BF16)
    grad_key_low = dkv_back[:, :, :HEAD].reshape(length, width)
    grad_value_low = dkv_back[:, :, HEAD:].reshape(length, width)

    def at_head(part, shape):
        return lax.dynamic_update_slice(
            jnp.zeros(shape, F32), part.reshape(shape[:-1] + (HEAD,)), (0,) * (len(shape) - 1) + (head * HEAD,)
        )

    grad_pos_weight = at_head(grad_head_weight, (width, width))
    grad_content_bias = at_head(grad_head_cb, (width,))
    grad_pos_bias = at_head(grad_head_pb, (width,))
    grad_query_weight = dot(attn_in, grad_query, over_rows)
    grad_key_weight = dot(attn_in, grad_key_low, over_rows)
    grad_value_weight = dot(attn_in, grad_value_low, over_rows)
    grad_normed_one = (
        dot(grad_query, query_weight, over_columns)
        + dot(grad_key_low, key_weight, over_columns)
        + dot(grad_value_low, value_weight, over_columns)
    )
    grad_from_one, grad_ln1_gain, grad_ln1_bias = norm_back(
        grad_normed_one, plain_one, inverse_one, ln1_gain
    )
    grad_pooled = (grad_mixed + grad_from_one).astype(BF16)
    grad_pool_weight = dot(pooled_in, grad_pooled, over_rows)
    grad_pool_bias = jnp.sum(grad_pooled.astype(F32), axis=0)
    grad_shifted = dot(grad_pooled, pool_weight, over_columns).reshape(1, bytes_here, width)
    incoming = passed_along(grad_shifted[:, :2, :], "seq", -1)
    input_grad = (
        cotangent.astype(F32) + jnp.concatenate([grad_shifted[:, 2:, :], incoming], 1)
    ).astype(BF16)
    late = lax.psum(
        tuple(
            grad.astype(BF16)
            for grad in (
                grad_pool_weight, grad_query_weight, grad_key_weight, grad_value_weight, grad_pos_weight,
            )
        ),
        ("dp", "seq"),
    )
    small_parts = (
        grad_pool_bias, grad_ln1_gain, grad_ln1_bias, grad_content_bias, grad_pos_bias,
        grad_ln2_gain, grad_ln2_bias, grad_ffn_in_bias, grad_ffn_out_bias, grad_up_bias,
    )
    small = lax.psum(jnp.concatenate(small_parts), ("dp", "seq"))
    cuts = np.cumsum([part.shape[0] for part in small_parts])[:-1].tolist()
    (
        sum_pool_bias, sum_ln1_gain, sum_ln1_bias, sum_content, sum_pos,
        sum_ln2_gain, sum_ln2_bias, sum_in_bias, sum_out_bias, sum_up_bias,
    ) = jnp.split(small, cuts)
    sum_in, sum_out, sum_up, sum_mix = (grad.astype(F32) for grad in early)
    sum_pool, sum_q, sum_k, sum_v, sum_p = (grad.astype(F32) for grad in late)
    return (
        outputs, input_grad, sum_pool, sum_pool_bias, sum_ln1_gain, sum_ln1_bias, sum_q, sum_k, sum_v,
        sum_mix, sum_p, sum_content, sum_pos, sum_ln2_gain, sum_ln2_bias, sum_in, sum_in_bias,
        sum_out, sum_out_bias, sum_up, sum_up_bias,
    )


EARLY_ROWS, LATE_ROWS = 6144, 3584
EARLY_CHUNKS = ((0, 2048, False), (2048, 2048, True), (4096, 2048, False))
LATE_CHUNKS = ((3072, 512, False), (1536, 1024, False), (2560, 512, True), (0, 1024, False), (1024, 512, True))
QKV_SUMS, POOL_SUMS = slice(4, 6), slice(6, None)
SMALL_ROWS = 16
TILE = 512
OVER_ROWS = ((0,), (0,))
OVER_COLUMNS = ((1,), (1,))


class Reduction:
    def __init__(self, buffer, start, rows, by_z, bufs, sems, free, small=None):
        self.buffer, self.sems, self.free, self.small = buffer, sems, free, small
        core, chip = lax.axis_index("dp"), lax.axis_index("seq")
        self.core, self.chip = core, chip
        x, y, z = chip % 2, (chip // 2) % 2, chip // 4
        first_x = core == 0
        self.peer_x, self.peer_y = (core, chip + 1 - 2 * x), (core, chip + 2 - 4 * y)
        self.z_peers = [(core, chip + ((z + away) % 4 - z) * 4) for away in (1, 2, 3)]
        self.z = z

        def pair(bit, peer_core, peer_chip):
            return (bit, [(1 - bit, peer_core, peer_chip)])

        one = pair(jnp.where(first_x, x, y), core, jnp.where(first_x, self.peer_x[1], self.peer_y[1]))
        two = pair(jnp.where(first_x, y, x), core, jnp.where(first_x, self.peer_y[1], self.peer_x[1]))
        stages = [pair(core, 1 - core, chip)]
        if by_z:
            low, high = z % 2, z // 2
            stages += [pair(low, core, chip + 4 - 8 * low), one, two, pair(high, core, chip + 8 - 16 * high)]
        else:
            stages += [one, two, (z, [((z + away) % 4, core, self.z_peers[away - 1][1]) for away in (1, 2, 3)])]
        self.stages = []
        at, size, first = start, rows, 0
        for buf, (own, others) in zip(bufs, stages):
            ways = len(others) + 1
            self.stages.append((at, size, size // ways, own, others, buf, first))
            at, size, first = at + own * (size // ways), size // ways, first + len(others)
        self.back = first
        self.last = 2 * len(stages)

    def rows(self, start, size):
        return self.buffer.at[pl.ds(pl.multiple_of(start, 16), size)]

    def copy(self, index, source, target, core, chip):
        return pltpu.make_async_remote_copy(
            source, target, self.sems.at[0, index], self.sems.at[1, index],
            device_id=(core, chip), device_id_type=MESH,
        )

    def done(self, index, source):
        copy = self.copy(index, source, source, 1 - self.core, self.chip)
        copy.wait_send()
        copy.wait_recv()

    def add(self, start, size, part_start, buf):
        chunk = min(size, 128)
        while size % chunk:
            chunk -= 16

        def one(step, carry):
            at = pl.ds(pl.multiple_of(start + step * chunk, 16), chunk)
            here = pl.ds(pl.multiple_of(part_start + step * chunk, 16), chunk)
            total = self.buffer[at].astype(F32)
            for part in range(buf.shape[0]):
                total = total + buf[part, here].astype(F32)
            self.buffer[at] = total.astype(BF16)
            return carry

        lax.fori_loop(0, size // chunk, one, 0)

    def send_parts(self, number):
        at, _, part, _, others, buf, first = self.stages[number]
        for place, (other, core, chip) in enumerate(others):
            self.copy(first + place, self.rows(at + other * part, part), buf.at[place], core, chip).start()

    def send_back(self, number):
        at, _, part, own, others, _, first = self.stages[number]
        pl.semaphore_wait(self.free.at[number], len(others))
        mine = self.rows(at + own * part, part)
        for place, (_, core, chip) in enumerate(others):
            self.copy(self.back + first + place, mine, mine, core, chip).start()

    def step(self, number):
        count = len(self.stages)
        if number == 0:
            self.send_parts(0)
        elif number <= count:
            at, _, part, own, others, buf, first = self.stages[number - 1]
            for place, (_, core, chip) in enumerate(others):
                self.done(first + place, buf.at[place])
            for _, core, chip in others:
                pl.semaphore_signal(self.free.at[number - 1], inc=1, device_id=(core, chip), device_id_type=MESH)
            kept = at + own * part
            if number < count:
                _, _, next_part, next_own, next_others, _, _ = self.stages[number]
                for other, _, _ in next_others:
                    self.add(kept + other * next_part, next_part, other * next_part, buf)
                self.send_parts(number)
                self.add(kept + next_own * next_part, next_part, next_own * next_part, buf)
            else:
                self.add(kept, part, 0, buf)
                self.send_back(count - 1)
        else:
            stage = 2 * count - number
            at, _, part, own, others, _, first = self.stages[stage]
            for place in range(len(others)):
                self.done(self.back + first + place, self.rows(at + own * part, part))
            if stage > 0:
                self.send_back(stage - 1)
        if self.small is not None:
            self.small_step(number)

    def small_step(self, number):
        own, taken = self.small
        first = 2 * self.back
        if number in (1, 2, 3):
            self.done(first + number - 1, own)
            own[...] = own[...] + taken[number - 1]
        if number < 3:
            core, chip = ((1 - self.core, self.chip), self.peer_x, self.peer_y)[number]
            self.copy(first + number, own, taken.at[number], core, chip).start()
        if number == 3:
            taken[3 + self.z] = own[...]
            for place, (core, chip) in enumerate(self.z_peers):
                self.copy(first + 3 + place, own, taken.at[3 + self.z], core, chip).start()
        if number == 4:
            for place in range(3):
                self.done(first + 3 + place, own)
            own[...] = (taken[3] + taken[4]) + (taken[5] + taken[6])


REDUCTION_SEMS = 18


def reduction_scratch(rows, by_z):
    shapes = [(1, rows // 2), (1, rows // 4), (1, rows // 8)]
    shapes += [(1, rows // 16), (1, rows // 32)] if by_z else [(3, rows // 32)]
    return [pltpu.VMEM(shape + (512,), BF16) for shape in shapes]


def gelu_pair(value):
    falling = jnp.exp(value * value * -0.5)
    turn = 1.0 / (1.0 + 0.3275911 * 0.7071067811865476 * jnp.abs(value))
    series = turn * (
        0.254829592
        + turn * (-0.284496736 + turn * (1.421413741 + turn * (-1.453152027 + turn * 1.061405429)))
    )
    tail = 0.5 * series * falling
    share = jnp.where(value >= 0, 1.0 - tail, tail)
    return value * share, share + value * falling * 0.3989422804014327


def norm_parts(hidden):
    average = jnp.mean(hidden, -1, keepdims=True)
    centred = hidden - average
    inverse = lax.rsqrt(jnp.mean(centred * centred, -1, keepdims=True) + epsilon)
    return centred * inverse, inverse


def norm_grad(grad_out, normed, inverse, gain):
    scaled = grad_out * gain
    return inverse * (
        scaled
        - jnp.mean(scaled, -1, keepdims=True)
        - normed * jnp.mean(scaled * normed, -1, keepdims=True)
    )


def column_sum(value):
    return jnp.sum(value, 0, keepdims=True)


def most_tiles(turn, length):
    return ((2 * turn + 2) * length + TILE - 1) // TILE


def layer_kernel(n, length, layout, *refs):
    taken = iter(refs)
    given, vectors, outs, scratch = ({name: next(taken) for name in part} for part in layout)
    r = types.SimpleNamespace(**vectors, **outs, **scratch)
    group = 2
    rounds = n // group
    tile = TILE
    width = 512
    scale = HEAD**-0.5
    core, chip, row, head, member = whereabouts(group)
    count = 2 * n
    me = core * n + chip

    loads = {}
    chunk_refs = list(refs[len(refs) - sum(5 if cut[2] else 4 for cut in EARLY_CHUNKS + LATE_CHUNKS) :])

    def reduction(buffer, index, cut, small=None):
        bufs = [chunk_refs.pop(0) for _ in range(5 if cut[2] else 4)]
        return Reduction(buffer, *cut, bufs, r.sum_sem.at[index], r.sum_free.at[index], small)

    for index, (name, source) in enumerate(given.items()):
        loads[name] = pltpu.make_async_copy(source, scratch[name], r.load_sem.at[index])
        loads[name].start()

    def ready(*which):
        for ref in which:
            next(loads[name] for name in given if scratch[name] is ref).wait()

    barrier = pltpu.get_barrier_semaphore()

    def greet(step, carry):
        other = (me + step) % count
        pl.semaphore_signal(barrier, inc=1, device_id=(other // n, other % n), device_id_type=MESH)
        return carry

    lax.fori_loop(1, count, greet, 0)

    low_bound, high_bound = r.bounds[0, 0], r.bounds[0, 1]
    r.edges[core, :8] = jnp.full((8, 128), low_bound, jnp.int32)
    r.edges[core, 8:] = jnp.full((8, 128), high_bound, jnp.int32)

    def tokens_of(source, target):
        for block in range(width // 128):
            r.mixing[block] = source[:, block * 128 : (block + 1) * 128].astype(F32)
            for part in range(3):
                every = r.mixing[block, pl.ds(part, length, stride=3), :]
                start = part * width + block * 128
                target[:, start : start + 128] = every.astype(BF16)

    ready(r.x_bytes, r.pool_w)
    tokens_of(r.x_bytes, r.x3)
    own = dot(r.x3[:, :width], r.pool_w[2 * width :])
    before = dot(r.x3[:, width:], r.pool_w[: 2 * width])
    pl.semaphore_wait(barrier, count - 1)

    def edge_copy():
        return pltpu.make_async_remote_copy(
            r.edges.at[core], r.edges.at[core], r.side_sem.at[0], r.side_sem.at[1],
            device_id=(1 - core, chip), device_id_type=MESH,
        )

    def rim_copy():
        return pltpu.make_async_remote_copy(
            r.x3.at[length - 16 :, width:], r.rim, r.side_sem.at[2], r.side_sem.at[3],
            device_id=(core, (chip + 1) % n), device_id_type=MESH,
        )

    edge_copy().start()

    @pl.when(chip < n - 1)
    def _():
        rim_copy().start()

    @pl.when(chip == 0)
    def _():
        r.rim[...] = jnp.zeros_like(r.rim)

    @pl.when(chip > 0)
    def _():
        rim_copy().wait_recv()

    rim_sum = dot(r.rim[...], r.pool_w[: 2 * width])
    at_row = lax.broadcasted_iota(jnp.int32, (length, width), 0)
    before = jnp.where(at_row == 0, rim_sum[15:16], pltpu.roll(before, 1, 0))
    pooled = own + before + r.pool_b[...]
    r.pooled[...] = pooled
    plain, _ = norm_parts(pooled)
    attn_in = (plain * r.ln1_g[...] + r.ln1_b[...]).astype(BF16)
    r.attn_in[...] = attn_in
    ready(r.q_w, r.k_w, r.v_w)
    query = dot(attn_in, r.q_w[...])
    keys = dot(attn_in, r.k_w[...])
    values = dot(attn_in, r.v_w[...])
    for h in range(HEADS):
        at = slice(h * HEAD, (h + 1) * HEAD)
        r.q_out[h] = packed(query[:, at]).astype(BF16)
        r.kv_out[h] = jnp.concatenate([keys[:, at], values[:, at]], 1).astype(BF16)
    turn_to, spot_to = place_of(chip, group)

    def q_jobs(array, out, sem, recv):
        jobs = []
        for h in range(HEADS):
            to_chip, to_core = chip_of(core, h, spot_to, group)
            jobs.append((array.at[h], out.at[turn_to], (sem, recv.at[turn_to]), to_core, to_chip))
        return jobs

    def rows_in(block):
        return pl.ds(pl.multiple_of(block * length, length), length)

    kv_jobs = []
    for h in range(HEADS):
        to_chip, _ = chip_of(core, h, 0, group)
        sems = (r.send_sem.at[1], r.kv_sem.at[chip])
        kv_jobs.append((r.kv_out.at[h], r.kv.at[rows_in(chip)], sems, chip % 2, to_chip))
    first_jobs = kv_jobs + q_jobs(r.q_out, r.q, r.send_sem.at[0], r.q_sem)
    for job in first_jobs:
        send(*job)

    ready(r.ct_bytes, r.up_w, r.ffn_out)
    tokens_of(r.ct_bytes, r.ct3)
    grad_final = dot(r.ct3[...], r.up_w[...], OVER_COLUMNS)
    r.grad_final[...] = grad_final
    grad_branch = grad_final.astype(BF16)
    r.grad_branch[...] = grad_branch
    for part in range(4):
        at = slice(part * width, (part + 1) * width)
        r.grad_act[:, at] = dot(grad_branch, r.ffn_out[at], OVER_COLUMNS)
    small = r.small
    small[...] = jnp.zeros_like(small)
    small[11:12] = column_sum(grad_branch.astype(F32))
    for part in range(3):
        at = slice(part * width, (part + 1) * width)
        small[12 + part : 13 + part] = column_sum(r.ct3[:, at].astype(F32))

    ready(r.pos_w, r.table)
    odd = head % 2 == 1
    pair_at = pl.ds(pl.multiple_of((head // 2) * PAIR, PAIR), PAIR)

    def of_head(ref):
        both = ref[:, pair_at].astype(F32)
        return jnp.where(odd, both[:, HEAD:], both[:, :HEAD])

    r.head_w[...] = of_head(r.pos_w).astype(BF16)
    content_bias, pos_bias = of_head(r.content), of_head(r.pos)
    edge_copy().wait_send()
    edge_copy().wait_recv()
    low_edge = r.edges[row, 0:1, 0:1]
    high_edge = r.edges[row, 8:9, 0:1]
    half = width // 2
    lanes = lax.broadcasted_iota(jnp.int32, (length, tile), 1)

    def rows_of(start):
        return pl.ds(pl.multiple_of(start, 64), tile)

    def tiles_to(block):
        return ((block + 1) * length + tile - 1) // tile

    def kept_at(turn):
        return sum(jnp.where(turn > before, most_tiles(before, length), 0) for before in range(rounds - 1))

    def forward(turn):
        at = turn * group + core
        return pltpu.make_async_remote_copy(
            r.kv.at[rows_in(at)], r.kv.at[rows_in(at)], r.send_sem.at[6], r.kv_sem.at[at], device_id=(1 - core, chip), device_id_type=MESH
        )

    def pass_on(turn):
        at = turn * group + core
        arrived(r.kv.at[rows_in(at)], r.kv_sem.at[at])
        forward(turn).start()

    pass_on(0)
    pass_on(1)
    arrived(r.kv.at[rows_in(1 - core)], r.kv_sem.at[1 - core])

    def attend(turn, carry):
        block = block_of(turn, member, group)

        @pl.when(turn < rounds - 2)
        def _():
            pass_on(turn + 2)

        @pl.when(turn < rounds - 1)
        def _():
            other = (turn + 1) * group + 1 - core
            arrived(r.kv.at[rows_in(other)], r.kv_sem.at[other])

        arrived(r.q.at[turn], r.q_sem.at[turn])
        query_u, _, turned = query_parts(
            r.q[turn], content_bias, pos_bias, r.head_w[...], r.sines[...], r.cosines[...]
        )
        head_part = (query_u.astype(F32) * scale).astype(BF16)
        r.extra[:, :PAIR] = jnp.concatenate([head_part, jnp.zeros_like(head_part)], 1)
        r.extra[:, PAIR:] = (turned * scale).astype(BF16)
        places = block * length + lax.broadcasted_iota(jnp.int32, (length, 1), 0)
        opening = jnp.where(places >= high_edge, high_edge, jnp.where(places >= low_edge, low_edge, 0))

        def score_step(step, top):
            pair = r.kv[rows_of(step * tile), :]
            waves = r.table[rows_of((n - 1 - block) * length + step * tile), :]
            score = dot(r.extra[:, :PAIR], pair, OVER_COLUMNS) + dot(r.extra[:, PAIR:], waves, OVER_COLUMNS)
            at = lanes + step * tile
            allowed = jnp.logical_and(at <= places, at >= opening)
            score = jnp.where(allowed, score, masked_score)
            r.score[step] = score
            for part in range(tile // 128):
                top = jnp.maximum(top, score[:, part * 128 : (part + 1) * 128])
            return top

        kept, tiles = kept_at(turn), tiles_to(block)
        top = lax.fori_loop(0, tiles, score_step, jnp.full((length, 128), masked_score, F32))
        top = jnp.max(top, 1, keepdims=True)

        def value_step(step, state):
            total, summed = state
            weight = jnp.exp(r.score[step] - top)
            for part in range(tile // 128):
                total = total + weight[:, part * 128 : (part + 1) * 128]
            low = weight.astype(BF16)
            r.keep[kept + step] = low
            pair = r.kv[rows_of(step * tile), :]
            return total, summed + dot(low, pair)

        total, summed = lax.fori_loop(
            0, tiles, value_step, (jnp.zeros((length, 128), F32), jnp.zeros((length, PAIR), F32))
        )
        inverse = 1.0 / jnp.sum(total, 1, keepdims=True)
        attended = summed[:, HEAD:] * inverse
        r.att[turn] = jnp.concatenate([jnp.broadcast_to(inverse, (length, HEAD)), attended], 1)
        r.att_out[turn] = packed(attended).astype(BF16)
        send(
            r.att_out.at[turn], r.att_in.at[head], (r.send_sem.at[2], r.att_sem.at[0]), row, block
        )
        return carry

    lax.fori_loop(0, rounds, attend, 0)
    for source, _, sems, to_core, to_chip in first_jobs:
        sent(source, sems[0], to_core, to_chip)
    for turn in range(rounds):
        forward(turn).wait_send()

    def joined(get):
        parts = [get(h) for h in range(HEADS)]
        upper = jnp.concatenate([part[:, :HEAD] for part in parts], 1)
        lower = jnp.concatenate([part[:, HEAD:] for part in parts], 1)
        return jnp.concatenate([upper, lower], 0)

    arrived(r.att_in, r.att_sem.at[0])
    ready(r.out_w, r.ffn_in)
    att_low = joined(lambda h: r.att_in[h].astype(F32)).astype(BF16)
    r.att_low[...] = att_low
    mixed = r.pooled[...] + dot(att_low, r.out_w[...])
    r.mixed[...] = mixed
    plain_two, inverse_two = norm_parts(mixed)
    ffn_input = (plain_two * r.ln2_g[...] + r.ln2_b[...]).astype(BF16)
    r.ffn_input[...] = ffn_input
    grad_normed = jnp.zeros((length, width), F32)
    for part in range(4):
        at = slice(part * width, (part + 1) * width)
        pre_act = dot(ffn_input, r.ffn_in[:, at]) + r.ffn_in_b[:, at]
        act, slope = gelu_pair(pre_act)
        r.act_low[:, at] = act.astype(BF16)
        grad_pre = (r.grad_act[:, at] * slope).astype(BF16)
        r.grad_pre[:, at] = grad_pre
        small[7 + part : 8 + part] = column_sum(grad_pre.astype(F32))
        grad_normed = grad_normed + dot(grad_pre, r.ffn_in[:, at], OVER_COLUMNS)
    small[5:6] = column_sum(grad_normed * plain_two)
    small[6:7] = column_sum(grad_normed)
    grad_mixed = r.grad_final[...] + norm_grad(grad_normed, plain_two, inverse_two, r.ln2_g[...])
    r.grad_final[...] = grad_mixed
    grad_mixed_low = grad_mixed.astype(BF16)
    grad_att = dot(grad_mixed_low, r.out_w[...], OVER_COLUMNS)
    for h in range(HEADS):
        r.q_out[h] = packed(grad_att[:, h * HEAD : (h + 1) * HEAD]).astype(BF16)
    second_jobs = q_jobs(r.q_out, r.grad, r.send_sem.at[3], r.grad_sem)
    for job in second_jobs:
        send(*job)

    early, late = r.early, r.late
    count_early, count_late = len(EARLY_CHUNKS), len(LATE_CHUNKS)
    sums = [reduction(early, index, cut) for index, cut in enumerate(EARLY_CHUNKS)]
    for index, cut in enumerate(LATE_CHUNKS):
        small_pair = (small, r.small_in) if index == count_late - 1 else None
        sums.append(reduction(late, count_early + index, cut, small_pair))

    def leave(index):
        cut = (EARLY_CHUNKS + LATE_CHUNKS)[index]
        buffer, target = (early, r.early_o) if index < count_early else (late, r.late_o)
        at = pl.ds(cut[0], cut[1])
        return pltpu.make_async_copy(buffer.at[at], target.at[at], r.leave_sem.at[index])

    def steps_at(moment):
        for index, number in SCHEDULE.get(moment, ()):
            sums[index].step(number)
            if number == sums[index].last:
                leave(index).start()

    for part in range(4):
        at = slice(part * width, (part + 1) * width)
        early[at] = dot(r.ffn_input[...], r.grad_pre[:, at], OVER_ROWS).astype(BF16)
    sums[0].step(0)
    steps_at(-4)
    for part in range(4):
        at = slice(part * width, (part + 1) * width)
        early[2048 + part * width : 2048 + (part + 1) * width] = dot(
            r.act_low[:, at], r.grad_branch[...], OVER_ROWS
        ).astype(BF16)
    sums[1].step(0)
    steps_at(-3)
    early[5632:] = dot(r.att_low[...], grad_mixed_low, OVER_ROWS).astype(BF16)
    final_low = (r.mixed[...] + dot(r.act_low[...], r.ffn_out[...]) + r.ffn_out_b[...]).astype(BF16)
    for part in range(3):
        at = slice(part * width, (part + 1) * width)
        early[4096 + part * width : 4096 + (part + 1) * width] = dot(final_low, r.ct3[:, at], OVER_ROWS).astype(BF16)
    sums[2].step(0)
    steps_at(-2)
    for part in range(3):
        at = slice(part * width, (part + 1) * width)
        lifted = dot(final_low, r.up_w[:, at]) + r.up_b[:, at]
        r.out3[:, at] = (r.x3[:, at].astype(F32) + lifted).astype(BF16)

    steps_at(-1)

    r.dkv[...] = jnp.zeros_like(r.dkv)
    r.dhead[...] = jnp.zeros_like(r.dhead)
    r.dbias[...] = jnp.zeros_like(r.dbias)

    def give_over(turn):
        return pltpu.make_async_remote_copy(
            r.dkv_out.at[turn * group + 1 - core], r.dkv_other.at[turn], r.send_sem.at[7], r.other_sem.at[turn],
            device_id=(1 - core, chip), device_id_type=MESH,
        )

    def hand_in(turn):
        at = turn * group + core
        give_over(turn).wait_recv()
        total = r.dkv[pl.ds(pl.multiple_of(at * length, length), length)] + r.dkv_other[turn].astype(F32)
        r.dkv_out[at] = total.astype(BF16)
        send(r.dkv_out.at[at], r.dkv_in.at[head], (r.send_sem.at[4], r.dkv_sem.at[0]), row, at)

    def back(index, carry):
        turn = rounds - 1 - index
        block = block_of(turn, member, group)
        arrived(r.grad.at[turn], r.grad_sem.at[turn])
        query = unpacked(r.q[turn].astype(F32))
        query_u = ((query + content_bias).astype(BF16).astype(F32) * scale).astype(BF16)
        query_v = (query + pos_bias).astype(BF16)
        grad = unpacked(r.grad[turn].astype(F32))
        inverse = r.att[turn][:, :HEAD]
        grad_part = grad * inverse
        delta = jnp.sum(grad_part * r.att[turn][:, HEAD:], 1, keepdims=True)
        nothing = jnp.zeros((length, HEAD), F32)
        r.extra[:, :PAIR] = jnp.concatenate([nothing, grad_part], 1).astype(BF16)
        r.extra[:, PAIR : 2 * PAIR] = jnp.concatenate([query_u.astype(F32), nothing], 1).astype(BF16)
        r.near[...] = jnp.zeros_like(r.near)
        r.far[...] = jnp.zeros_like(r.far)

        def step_over(step, inner):
            pair = r.kv[rows_of(step * tile), :]
            waves = r.table[rows_of((n - 1 - block) * length + step * tile), :]
            weight = r.keep[kept + step]
            grad_weight = dot(r.extra[:, :PAIR], pair, OVER_COLUMNS)
            grad_score = (weight.astype(F32) * (grad_weight - delta)).astype(BF16)
            r.near[...] += dot(grad_score, pair)
            r.far[...] += dot(grad_score, waves)
            at = pl.ds(pl.multiple_of(step * tile, tile), tile)
            r.dkv[at] += dot(grad_score, r.extra[:, PAIR : 2 * PAIR], OVER_ROWS) + dot(
                weight, r.extra[:, :PAIR], OVER_ROWS
            )
            return inner

        kept = kept_at(turn)
        lax.fori_loop(0, tiles_to(block), step_over, 0)
        give = turn * group + 1 - core
        r.dkv_out[give] = r.dkv[pl.ds(pl.multiple_of(give * length, length), length)].astype(BF16)
        give_over(turn).start()

        @pl.when(index > 0)
        def _():
            hand_in(turn + 1)

        grad_u = r.near[:, :HEAD] * scale
        turn_sin, turn_cos = r.sines[...], r.cosines[...]
        on_sin, on_cos = r.far[:, :half] * scale, r.far[:, half:] * scale
        lift = on_cos * turn_sin - on_sin * turn_cos
        rest = on_cos * turn_cos + on_sin * turn_sin
        spread = jnp.concatenate([lift, rest], 1).astype(BF16)
        grad_v = dot(spread, r.head_w[...])
        r.dhead[...] += dot(spread, query_v, OVER_ROWS)
        r.dbias[0:1] += column_sum(grad_u)
        r.dbias[1:2] += column_sum(grad_v)
        r.dq_out[turn] = packed(grad_u + grad_v).astype(BF16)
        send(r.dq_out.at[turn], r.dq_in.at[head], (r.send_sem.at[5], r.dq_sem.at[0]), row, block)
        for when in range(rounds):
            if when in SCHEDULE:

                @pl.when(index == when)
                def _(when=when):
                    steps_at(when)

        return carry

    lax.fori_loop(0, rounds, back, 0)
    hand_in(0)

    late[2048 + 1024 :] = jnp.zeros((512, 512), BF16)
    dhead = r.dhead[...]
    nothing = jnp.zeros_like(dhead)
    late[3072:, pair_at] = jnp.where(
        odd, jnp.concatenate([nothing, dhead], 1), jnp.concatenate([dhead, nothing], 1)
    ).astype(BF16)
    nothing = jnp.zeros((2, HEAD), F32)
    dbias = r.dbias[...][:2]
    small[3:5, pair_at] = jnp.where(
        odd, jnp.concatenate([nothing, dbias], 1), jnp.concatenate([dbias, nothing], 1)
    )
    sums[3].step(0)
    steps_at(8)
    for source, _, sems, to_core, to_chip in second_jobs:
        sent(source, sems[0], to_core, to_chip)
    for turn in range(rounds):
        block = block_of(jnp.int32(turn), member, group)
        sent(r.att_out.at[turn], r.send_sem.at[2], row, block)
        sent(r.dq_out.at[turn], r.send_sem.at[5], row, block)
    for turn in range(rounds):
        sent(r.dkv_out.at[turn * group + core], r.send_sem.at[4], row, turn * group + core)
        give_over(turn).wait_send()
    arrived(r.dq_in, r.dq_sem.at[0])
    arrived(r.dkv_in, r.dkv_sem.at[0])
    grad_query = joined(lambda h: r.dq_in[h].astype(F32)).astype(BF16)
    both = [r.dkv_in[h].astype(F32) for h in range(HEADS)]
    grad_keys = jnp.concatenate([part[:, :HEAD] for part in both], 1).astype(BF16)
    grad_values = jnp.concatenate([part[:, HEAD:] for part in both], 1).astype(BF16)
    steps_at(9)
    attn_in = r.attn_in[...]
    grad_normed = (
        dot(grad_query, r.q_w[...], OVER_COLUMNS)
        + dot(grad_keys, r.k_w[...], OVER_COLUMNS)
        + dot(grad_values, r.v_w[...], OVER_COLUMNS)
    )
    plain, inverse = norm_parts(r.pooled[...])
    small[1:2] = column_sum(grad_normed * plain)
    small[2:3] = column_sum(grad_normed)
    grad_pooled = (r.grad_final[...] + norm_grad(grad_normed, plain, inverse, r.ln1_g[...])).astype(BF16)
    r.grad_pooled[...] = grad_pooled
    grad_pooled_wide = grad_pooled.astype(F32)
    steps_at(10)
    small[0:1] = column_sum(grad_pooled_wide)

    def back_rim_copy():
        return pltpu.make_async_remote_copy(
            r.grad_pooled.at[:16], r.back_rim, r.side_sem.at[4], r.side_sem.at[5],
            device_id=(core, (chip + n - 1) % n), device_id_type=MESH,
        )

    @pl.when(chip > 0)
    def _():
        back_rim_copy().start()

    late[1024:1536] = dot(r.x3[:, :width], grad_pooled, OVER_ROWS).astype(BF16)
    follow = pltpu.roll(grad_pooled_wide, length - 1, 0)
    within = jnp.where(at_row == length - 1, 0.0, follow).astype(BF16)
    at_rim = lax.broadcasted_iota(jnp.int32, (16, width), 0)
    rim_row = jnp.where(at_rim == 15, jnp.broadcast_to(grad_pooled_wide[:1], (16, width)), 0.0).astype(BF16)
    late[:1024] = (
        dot(r.x3[:, width:], within, OVER_ROWS) + dot(r.rim[...], rim_row, OVER_ROWS)
    ).astype(BF16)
    for later in sums[POOL_SUMS]:
        later.step(0)
    steps_at(11)
    late[1536:2048] = dot(attn_in, grad_query, OVER_ROWS).astype(BF16)
    late[2048:2560] = dot(attn_in, grad_keys, OVER_ROWS).astype(BF16)
    late[2560:3072] = dot(attn_in, grad_values, OVER_ROWS).astype(BF16)
    for later in sums[QKV_SUMS]:
        later.step(0)
    steps_at(12)

    @pl.when(chip == n - 1)
    def _():
        r.back_rim[...] = jnp.zeros_like(r.back_rim)

    @pl.when(chip < n - 1)
    def _():
        back_rim_copy().wait_recv()

    next_row = r.back_rim[...].astype(F32)[:1]
    follow = jnp.where(at_row == length - 1, next_row, follow).astype(BF16)
    first_part = r.ct3[:, :width].astype(F32) + dot(grad_pooled, r.pool_w[2 * width :], OVER_COLUMNS)
    r.grad3[:, :width] = first_part.astype(BF16)
    other_part = r.ct3[:, width:].astype(F32) + dot(follow, r.pool_w[: 2 * width], OVER_COLUMNS)
    r.grad3[:, width:] = other_part.astype(BF16)

    @pl.when(chip < n - 1)
    def _():
        rim_copy().wait_send()

    @pl.when(chip > 0)
    def _():
        back_rim_copy().wait_send()

    steps_at(13)
    for index in range(len(sums)):
        leave(index).wait()


SCHEDULE = {
    -2: ((1, 1),),
    -1: ((0, 1),),
    1: ((0, 2),),
    2: ((1, 2), (2, 1), (0, 3),),
    8: ((2, 2), (1, 3), (0, 4), (3, 1),),
    10: ((1, 4),),
    11: ((2, 3),),
    12: ((3, 2), (0, 5), (7, 1), (4, 1), (3, 3), (1, 5), (5, 1), (6, 1),),
    13: (
        (7, 2), (2, 4), (4, 2), (1, 6), (6, 2), (3, 4), (5, 2), (7, 3), (0, 6), (4, 3), (1, 7), (5, 3), (6, 3),
        (2, 5), (3, 5), (5, 4), (7, 4), (4, 4), (5, 5), (6, 4), (7, 5), (1, 8), (3, 6), (2, 6), (5, 6), (7, 6),
        (4, 5), (0, 7), (7, 7), (3, 7), (6, 5), (0, 8), (5, 7), (3, 8), (7, 8), (4, 6), (6, 6), (5, 8), (1, 9),
        (2, 7), (7, 9), (4, 7), (5, 9), (1, 10), (6, 7), (7, 10), (4, 8), (2, 8), (5, 10), (6, 8),
    ),
}


WIDENED = (
    (0, 4, True), (2048, 4, False), (4096, 3, True), (5632, 1, False),
    (0, 3, False), (1536, 1, False), (2048, 1, False), (2560, 1, False), (3072, 1, False),
)
NARROW = ((0, 1), (1, 1), (2, 1), (3, 1), (4, 1), (5, 1), (6, 1), (7, 4), (11, 1), (12, 3))


def last_kernel(*refs):
    early, late, out3, grad3, small = refs[:5]
    wide_outs, narrow_outs, byte_outs = refs[5:14], refs[14:24], refs[24:26]
    loaded, staging, mixing, load_sems, sems = refs[26:]
    blocks = []
    for index, (out, (start, count, across)) in enumerate(zip(wide_outs, WIDENED)):
        for block in range(count):
            first = start + block * 512
            at = slice(block * 512, (block + 1) * 512)
            source = (early if index < 4 else late).at[first : first + 512]
            blocks.append((source, out.at[:, at] if across else out.at[at]))
    loads = [
        pltpu.make_async_copy(source, loaded.at[slot], load_sems.at[slot]) for slot, (source, _) in enumerate(blocks)
    ]
    stores = [
        pltpu.make_async_copy(staging.at[slot], target, sems.at[slot]) for slot, (_, target) in enumerate(blocks)
    ]
    for load in loads:
        load.start()
    for out, tokens in zip(byte_outs, (out3, grad3)):
        length, width = out.shape[0] // 3, out.shape[1]
        for block in range(width // 128):
            for part in range(3):
                start = part * width + block * 128
                mixing[block, pl.ds(part, length, stride=3), :] = tokens[:, start : start + 128].astype(F32)
            out[:, block * 128 : (block + 1) * 128] = mixing[block].astype(BF16)
    for slot in range(len(blocks)):
        loads[slot].wait()

        def widen(step, carry, slot=slot):
            here = pl.ds(pl.multiple_of(step * 64, 64), 64)
            staging[slot, here] = loaded[slot, here].astype(F32)
            return carry

        lax.fori_loop(0, 8, widen, 0)
        stores[slot].start()
    for out, (start, count) in zip(narrow_outs, NARROW):
        for block in range(count):
            out[:, block * 512 : (block + 1) * 512] = small[start + block : start + block + 1]
    for store in stores:
        store.wait()


def finished(early, late, out3, grad3, small):
    length, width = out3.shape[0], out3.shape[1] // 3
    vmem = pl.BlockSpec(memory_space=pltpu.VMEM)
    shapes = [(512, 512 * blocks) if across else (512 * blocks, 512) for _, blocks, across in WIDENED]
    narrow = [(1, 512 * blocks) for _, blocks in NARROW]
    count = sum(blocks for _, blocks, _ in WIDENED)
    outs = pl.pallas_call(
        last_kernel,
        in_specs=[pl.BlockSpec(memory_space=pl.ANY)] * 2 + [vmem] * 3,
        out_specs=[pl.BlockSpec(memory_space=pl.ANY)] * len(shapes) + [vmem] * (len(narrow) + 2),
        out_shape=[jax.ShapeDtypeStruct(shape, F32) for shape in shapes + narrow]
        + [jax.ShapeDtypeStruct((3 * length, width), BF16)] * 2,
        scratch_shapes=[
            pltpu.VMEM((count, 512, 512), BF16), pltpu.VMEM((count, 512, 512), F32), pltpu.VMEM((width // 128, 3 * length, 128), F32),
            pltpu.SemaphoreType.DMA((count,)), pltpu.SemaphoreType.DMA((count,)),
        ],
        compiler_params=pltpu.CompilerParams(vmem_limit_bytes=56 * 2**20),
    )(early, late, out3, grad3, small)
    return outs[: len(shapes)], [out[0] for out in outs[len(shapes) : -2]], outs[-2:]


def fused_body(
    inputs, doc_bounds, pool_weight, pool_bias, ln1_gain, ln1_bias, query_weight, key_weight,
    value_weight, out_weight, pos_weight, content_bias, pos_bias, ln2_gain, ln2_bias, ffn_in,
    ffn_in_bias, ffn_out, ffn_out_bias, up_weight, up_bias, cotangent,
):
    _, bytes_here, width = inputs.shape
    length = bytes_here // 3
    n = lax.axis_size("seq")
    tokens = n * length
    rounds = n // 2
    table, sines, cosines = wave_tables(tokens, length, width, TILE)
    given = dict(
        x_bytes=inputs[0], pool_w=pool_weight, q_w=query_weight, k_w=key_weight, v_w=value_weight,
        ct_bytes=cotangent[0], up_w=up_weight, ffn_out=ffn_out, pos_w=pos_weight, table=table,
        out_w=out_weight, ffn_in=ffn_in,
    )
    vectors = dict(
        pool_b=pool_bias, ln1_g=ln1_gain, ln1_b=ln1_bias, content=content_bias, pos=pos_bias, ln2_g=ln2_gain,
        ln2_b=ln2_bias, ffn_in_b=ffn_in_bias, ffn_out_b=ffn_out_bias, up_b=up_bias,
    )
    vectors = {name: vector[None] for name, vector in vectors.items()} | dict(sines=sines, cosines=cosines)
    vmem = pl.BlockSpec(memory_space=pltpu.VMEM)
    outs = dict(
        out3=((length, 3 * width), BF16), grad3=((length, 3 * width), BF16), small=((SMALL_ROWS, 512), F32),
        early_o=((EARLY_ROWS, 512), BF16), late_o=((LATE_ROWS, 512), BF16),
    )
    pair_half = (length // 2, PAIR)
    block, wide = (length, width), (length, 4 * width)
    dma, signal = pltpu.SemaphoreType.DMA, pltpu.SemaphoreType.REGULAR
    scratch = {name: pltpu.VMEM(array.shape, array.dtype) for name, array in given.items()}
    low = dict(
        x3=(length, 3 * width), ct3=(length, 3 * width), rim=(16, 2 * width), back_rim=(16, width), attn_in=block, q_out=(HEADS,) + pair_half,
        kv_out=(HEADS, length, PAIR), q=(rounds,) + pair_half, kv=(tokens, PAIR), grad_branch=block,
        head_w=(width, HEAD), extra=(length, PAIR + width), keep=(sum(most_tiles(turn, length) for turn in range(rounds)), length, TILE),
        att_out=(rounds,) + pair_half, att_in=(HEADS,) + pair_half, att_low=block, ffn_input=block, act_low=wide,
        grad_pre=wide, grad=(rounds,) + pair_half, dkv_out=(n, length, PAIR), dkv_in=(HEADS, length, PAIR),
        dkv_other=(rounds, length, PAIR), dq_out=(rounds,) + pair_half, dq_in=(HEADS,) + pair_half, grad_pooled=block, early=(EARLY_ROWS, 512), late=(LATE_ROWS, 512),
    )
    full = dict(
        mixing=(width // 128, 3 * length, 128), pooled=block, grad_final=block, grad_act=wide, score=(tokens // TILE, length, TILE), att=(rounds, length, PAIR),
        mixed=block, dkv=(tokens, PAIR), dhead=(width, HEAD), dbias=(8, HEAD), near=(length, PAIR), far=block,
        small_in=(7, SMALL_ROWS, 512),
    )
    scratch |= {name: pltpu.VMEM(shape, BF16) for name, shape in low.items()}
    scratch |= {name: pltpu.VMEM(shape, F32) for name, shape in full.items()}
    scratch |= dict(
        edges=pltpu.VMEM((2, 16, 128), jnp.int32), load_sem=dma((len(given),)), side_sem=dma((6,)), send_sem=dma((8,)), other_sem=dma((rounds,)),

        q_sem=dma((rounds,)), kv_sem=dma((n,)), att_sem=dma((1,)), grad_sem=dma((rounds,)), dkv_sem=dma((1,)),
        dq_sem=dma((1,)), sum_sem=dma((len(EARLY_CHUNKS + LATE_CHUNKS), 2, REDUCTION_SEMS)),
        sum_free=signal((len(EARLY_CHUNKS + LATE_CHUNKS), 5)), leave_sem=dma((len(EARLY_CHUNKS + LATE_CHUNKS),)),
    )
    layout = (list(given), list(vectors) + ["bounds"], list(outs), list(scratch))
    out3, grad3, small, early, late = pl.pallas_call(
        functools.partial(layer_kernel, n, length, layout),
        in_specs=[pl.BlockSpec(memory_space=pl.ANY)] * len(given)
        + [vmem] * len(vectors)
        + [pl.BlockSpec(memory_space=pltpu.SMEM)],
        out_specs=[vmem] * 3 + [pl.BlockSpec(memory_space=pl.ANY)] * 2,
        out_shape=[jax.ShapeDtypeStruct(*out) for out in outs.values()],
        scratch_shapes=list(scratch.values())
        + sum((reduction_scratch(*cut[1:]) for cut in EARLY_CHUNKS + LATE_CHUNKS), []),
        compiler_params=pltpu.CompilerParams(
            collective_id=0, has_side_effects=True, vmem_limit_bytes=62 * 2**20
        ),
    )(*given.values(), *vectors.values(), doc_bounds)
    wide, narrow, both = finished(early, late, out3, grad3, small)
    sum_in, sum_out, sum_up, sum_mix, sum_pool, sum_q, sum_k, sum_v, sum_p = wide
    pool_b, ln1_g, ln1_b, content, pos, ln2_g, ln2_b, in_b, out_b, up_b = narrow
    return (
        both[0][None], both[1][None], sum_pool, pool_b, ln1_g, ln1_b, sum_q, sum_k, sum_v, sum_mix, sum_p,
        content, pos, ln2_g, ln2_b, sum_in, in_b, sum_out, out_b, sum_up, up_b,
    )


def solution(mesh):
    split = P("dp", "seq", None)
    fits = mesh.shape["seq"] == 16
    return jax.shard_map(
        fused_body if fits else body,
        mesh=mesh,
        in_specs=(split, P("dp", None)) + (P(),) * 19 + (split,),
        out_specs=(split, split) + (P(),) * 19,
        check_vma=False,
    )
```

```python
import functools
import types

import jax
import jax.numpy as jnp
import numpy as np
from jax import lax
from jax.experimental import pallas as pl
from jax.experimental.pallas import tpu as pltpu
from jax.sharding import PartitionSpec as P

HEADS = 8
ROWS = 2
HEAD = 64
PAIR = 2 * HEAD
MESH = pl.DeviceIdType.MESH
F32 = jnp.float32
BF16 = jnp.bfloat16

epsilon = 1e-05
masked_score = -1e30


def dot(left, right, dims=((1,), (0,))):
    return lax.dot_general(left, right, (dims, ((), ())), preferred_element_type=F32)


def passed_along(value, axis, steps):
    count = lax.axis_size(axis)
    first, last = (max(0, -steps), min(count, count - steps))
    return lax.ppermute(value, axis, [(source, source + steps) for source in range(first, last)])


def place_of(block, group):
    turn, spot = block // group, block % group
    return turn, jnp.where(turn % 2 == 0, spot, group - 1 - spot)


def block_of(turn, member, group):
    return turn * group + jnp.where(turn % 2 == 0, member, group - 1 - member)


def whereabouts(group):
    core, chip = lax.axis_index("dp"), lax.axis_index("seq")
    chips = group // 2
    unit = chip // chips
    member = (chip % chips) * 2 + core
    return core, chip, unit // HEADS, unit % HEADS, member


def chip_of(row, head, member, group):
    return (row * HEADS + head) * (group // 2) + member // 2, member % 2


def meet(n, group, to_units):
    core, chip, row, head, member = whereabouts(group)
    barrier = pltpu.get_barrier_semaphore()

    def greet(row_or_core, chip_at):
        away = jnp.logical_or(row_or_core != core, chip_at != chip)

        @pl.when(away)
        def _():
            pl.semaphore_signal(
                barrier, inc=1, device_id=(row_or_core, chip_at), device_id_type=MESH
            )

        return away.astype(jnp.int32)

    own_row = row == core
    if to_units:
        for s in range(n):
            greet(row, jnp.int32(s))
        mine = jnp.logical_and(chip // (HEADS * (group // 2)) == core, True)
        pl.semaphore_wait(barrier, HEADS * group - mine.astype(jnp.int32))
    else:
        for h in range(HEADS):
            for g in range(group):
                c, k = chip_of(core, h, g, group)
                greet(jnp.int32(k), c)
        pl.semaphore_wait(barrier, n - own_row.astype(jnp.int32))


def send(source, target, sems, core, chip):
    here_core, here_chip = lax.axis_index("dp"), lax.axis_index("seq")
    here = jnp.logical_and(core == here_core, chip == here_chip)

    @pl.when(here)
    def _():
        pltpu.make_async_copy(source, target, sems[1]).start()

    @pl.when(jnp.logical_not(here))
    def _():
        pltpu.make_async_remote_copy(
            source, target, sems[0], sems[1], device_id=(core, chip), device_id_type=MESH
        ).start()


def sent(source, sem, core, chip):
    here_core, here_chip = lax.axis_index("dp"), lax.axis_index("seq")
    here = jnp.logical_and(core == here_core, chip == here_chip)

    @pl.when(jnp.logical_not(here))
    def _():
        pltpu.make_async_copy(source, source, sem).wait()


def arrived(whole, sem):
    pltpu.make_async_copy(whole, whole, sem).wait()


def to_units_kernel(n, group, *refs):
    count = len(refs) - 2
    arrays, outs = refs[: count // 2], refs[count // 2 : count]
    send_sem, recv_sem = refs[count:]
    core, chip, row, head, member = whereabouts(group)
    turn, spot = place_of(chip, group)
    meet(n, group, True)
    jobs = []
    for h in range(HEADS):
        for index, (array, out) in enumerate(zip(arrays, outs)):
            sems = (send_sem.at[index], recv_sem.at[index])
            if index == 0:
                to_chip, to_core = chip_of(core, h, spot, group)
                jobs.append((array.at[h], out.at[turn], sems, to_core, to_chip))
            else:
                for g in range(group):
                    to_chip, to_core = chip_of(core, h, g, group)
                    jobs.append((array.at[h], out.at[chip], sems, jnp.int32(to_core), to_chip))
    for job in jobs:
        send(*job)
    for source, _, sems, to_core, to_chip in jobs:
        sent(source, sems[0], to_core, to_chip)
    for index, out in enumerate(outs):
        arrived(out, recv_sem.at[index])


def to_owners_kernel(n, group, *refs):
    count = len(refs) - 2
    arrays, outs = refs[: count // 2], refs[count // 2 : count]
    send_sem, recv_sem = refs[count:]
    core, chip, row, head, member = whereabouts(group)
    meet(n, group, False)
    jobs = []
    for turn in range(n // group):
        block = block_of(jnp.int32(turn), member, group)
        sems = (send_sem.at[0], recv_sem.at[0])
        jobs.append((arrays[0].at[turn], outs[0].at[head], sems, row, block))
    if len(arrays) > 1:
        for block in range(n):
            sems = (send_sem.at[1], recv_sem.at[1])
            jobs.append((arrays[1].at[block], outs[1].at[member, head], sems, row, jnp.int32(block)))
    for job in jobs:
        send(*job)
    for source, _, sems, to_core, to_chip in jobs:
        sent(source, sems[0], to_core, to_chip)
    for index, out in enumerate(outs):
        arrived(out, recv_sem.at[index])


def exchange(kernel, n, group, arrays, shapes, ident):
    vmem = pl.BlockSpec(memory_space=pltpu.VMEM)
    return pl.pallas_call(
        functools.partial(kernel, n, group),
        out_shape=[jax.ShapeDtypeStruct(shape, array.dtype) for shape, array in zip(shapes, arrays)],
        in_specs=[vmem] * len(arrays),
        out_specs=[vmem] * len(arrays),
        scratch_shapes=[
            pltpu.SemaphoreType.DMA((len(arrays),)),
            pltpu.SemaphoreType.DMA((len(arrays),)),
        ],
        compiler_params=pltpu.CompilerParams(
            collective_id=ident, has_side_effects=True, vmem_limit_bytes=48 * 2**20
        ),
    )(*arrays)


def unpacked(pair):
    return jnp.concatenate([pair[:, :HEAD], pair[:, HEAD:]], 0)


def packed(block):
    half = block.shape[0] // 2
    return jnp.concatenate([block[:half], block[half:]], 1)


def query_parts(q_pair, content_bias, pos_bias, pos_weight, turn_sin, turn_cos):
    query = unpacked(q_pair.astype(F32))
    query_u = (query + content_bias).astype(BF16)
    query_v = (query + pos_bias).astype(BF16)
    spread = dot(query_v, pos_weight, ((1,), (1,)))
    half = turn_sin.shape[1]
    lift, rest = spread[:, :half], spread[:, half:]
    on_sin = rest * turn_sin - lift * turn_cos
    on_cos = lift * turn_sin + rest * turn_cos
    turned = jnp.concatenate([on_sin, on_cos], 1)
    return query_u, query_v, turned


def attend_kernel(
    n, group, tile, q_ref, kv_ref, table_ref, sin_ref, cos_ref, weight_ref, cb_ref, pb_ref, bounds_ref,
    att_ref, low_ref, total_ref, keep_ref, score_ref, extra_ref,
):
    turn = pl.program_id(0)
    member = whereabouts(group)[4]
    block = block_of(turn, member, group)
    length = sin_ref.shape[0]
    tokens = n * length
    query_u, _, turned = query_parts(
        q_ref[...], cb_ref[...], pb_ref[...], weight_ref[...], sin_ref[...], cos_ref[...]
    )
    scale = HEAD**-0.5
    head_part = (query_u.astype(F32) * scale).astype(BF16)
    extra_ref[:, :HEAD] = head_part
    extra_ref[:, HEAD:PAIR] = jnp.zeros_like(head_part)
    extra_ref[:, PAIR:] = (turned * scale).astype(BF16)
    first = block * length
    tiles = (first + length + tile - 1) // tile
    low_bound, high_bound = bounds_ref[0], bounds_ref[1]
    places = first + lax.broadcasted_iota(jnp.int32, (length, 1), 0)
    opening = jnp.where(
        places >= high_bound, high_bound, jnp.where(places >= low_bound, low_bound, 0)
    )
    lanes = lax.broadcasted_iota(jnp.int32, (length, tile), 1)

    def score_step(step, top):
        start = pl.multiple_of(step * tile, tile)
        keys = kv_ref[pl.ds(start, tile), :]
        waves = table_ref[pl.ds(pl.multiple_of((n - 1 - block) * length + start, length), tile), :]
        score = dot(extra_ref[:, :PAIR], keys, ((1,), (1,))) + dot(
            extra_ref[:, PAIR:], waves, ((1,), (1,))
        )
        at = lanes + start
        allowed = jnp.logical_and(at <= places, at >= opening)
        score = jnp.where(allowed, score, masked_score)
        score_ref[:, pl.ds(start, tile)] = score
        for part in range(tile // 128):
            top = jnp.maximum(top, score[:, part * 128 : (part + 1) * 128])
        return top

    top = lax.fori_loop(0, tiles, score_step, jnp.full((length, 128), masked_score, F32))
    top = jnp.max(top, 1, keepdims=True)

    def value_step(step, state):
        total, summed = state
        start = pl.multiple_of(step * tile, tile)
        weight = jnp.exp(score_ref[:, pl.ds(start, tile)] - top)
        for part in range(tile // 128):
            total = total + weight[:, part * 128 : (part + 1) * 128]
        low = weight.astype(BF16)
        keep_ref[:, pl.ds(start, tile)] = low
        return total, summed + dot(low, kv_ref[pl.ds(start, tile), :])

    total, summed = lax.fori_loop(
        0, tiles, value_step, (jnp.zeros((length, 128), F32), jnp.zeros((length, PAIR), F32))
    )
    total = jnp.sum(total, 1, keepdims=True)
    attended = summed[:, HEAD:] / total
    att_ref[...] = attended
    total_ref[...] = jnp.broadcast_to(total, (length, 128))
    low_ref[...] = packed(attended).astype(BF16)


def back_kernel(
    n, group, tile, q_ref, kv_ref, table_ref, sin_ref, cos_ref, weight_ref, cb_ref, pb_ref,
    att_ref, total_ref, keep_ref, grad_ref,
    dq_ref, dkv_ref, dweight_ref, dcb_ref, dpb_ref, dkv_acc,
):
    turn = pl.program_id(0)
    member = whereabouts(group)[4]
    block = block_of(turn, member, group)
    length = sin_ref.shape[0]
    scale = HEAD**-0.5

    @pl.when(turn == 0)
    def _():
        dkv_acc[...] = jnp.zeros_like(dkv_acc)
        dweight_ref[...] = jnp.zeros_like(dweight_ref)
        dcb_ref[...] = jnp.zeros_like(dcb_ref)
        dpb_ref[...] = jnp.zeros_like(dpb_ref)

    query_u, query_v, _ = query_parts(
        q_ref[...], cb_ref[...], pb_ref[...], weight_ref[...], sin_ref[...], cos_ref[...]
    )
    head_part = (query_u.astype(F32) * scale).astype(BF16)
    grad = unpacked(grad_ref[...].astype(F32))
    inverse = 1.0 / total_ref[:, :1]
    delta = jnp.sum(grad * att_ref[...], 1, keepdims=True) * inverse
    grad_low = (grad * inverse).astype(BF16)
    nothing = jnp.zeros_like(grad_low)
    grad_wide = jnp.concatenate([nothing, grad_low], 1)
    query_wide = jnp.concatenate([head_part, nothing], 1)
    tiles = (block * length + length + tile - 1) // tile

    def step_over(step, state):
        near, far = state
        start = pl.multiple_of(step * tile, tile)
        keys = kv_ref[pl.ds(start, tile), :]
        waves = table_ref[pl.ds(pl.multiple_of((n - 1 - block) * length + start, length), tile), :]
        weight = keep_ref[:, pl.ds(start, tile)]
        grad_weight = dot(grad_wide, keys, ((1,), (1,)))
        grad_score = (weight.astype(F32) * (grad_weight - delta)).astype(BF16)
        near = near + dot(grad_score, keys)
        far = far + dot(grad_score, waves)
        dkv_acc[pl.ds(start, tile), :] += dot(grad_score, query_wide, ((0,), (0,))) + dot(
            weight, grad_wide, ((0,), (0,))
        )
        return near, far

    near, far = lax.fori_loop(
        0,
        tiles,
        step_over,
        (jnp.zeros((length, PAIR), F32), jnp.zeros((length, table_ref.shape[1]), F32)),
    )
    grad_u = near[:, :HEAD] * scale
    half = sin_ref.shape[1]
    turn_sin, turn_cos = sin_ref[...], cos_ref[...]
    on_sin, on_cos = far[:, :half] * scale, far[:, half:] * scale
    lift = on_cos * turn_sin - on_sin * turn_cos
    rest = on_cos * turn_cos + on_sin * turn_sin
    spread = jnp.concatenate([lift, rest], 1).astype(BF16)
    grad_v = dot(spread, weight_ref[...])
    dweight_ref[...] += dot(spread, query_v, ((0,), (0,)))
    dcb_ref[...] += jnp.sum(grad_u, 0, keepdims=True)
    dpb_ref[...] += jnp.sum(grad_v, 0, keepdims=True)
    dq_ref[...] = packed(grad_u + grad_v).astype(BF16)

    @pl.when(turn == pl.num_programs(0) - 1)
    def _():
        dkv_ref[...] = dkv_acc[...].astype(BF16)


def wave_tables(tokens, length, width, more=0):
    rates = 10000.0 ** (-2.0 * np.arange(width // 2, dtype=np.float64) / width)
    far = (np.arange(tokens + max(length, more), dtype=np.float64) - (tokens - length))[:, None] * rates
    near = np.arange(length, dtype=np.float64)[:, None] * rates
    table = np.concatenate([np.sin(far), np.cos(far)], 1)
    return (
        jnp.asarray(table, dtype=BF16),
        jnp.asarray(np.sin(near), dtype=F32),
        jnp.asarray(np.cos(near), dtype=F32),
    )


def whole_spec(shape):
    return pl.BlockSpec(shape, lambda turn: (0,) * len(shape))


def turn_spec(shape):
    return pl.BlockSpec((None,) + shape, lambda turn: (turn,) + (0,) * len(shape))


def layer_norm(hidden, gain, bias):
    average = jnp.mean(hidden, -1, keepdims=True)
    centred = hidden - average
    inverse = lax.rsqrt(jnp.mean(centred * centred, -1, keepdims=True) + epsilon)
    normed = centred * inverse
    return (normed * gain + bias, normed, inverse)


def norm_back(grad_out, normed, inverse, gain):
    scaled = grad_out * gain
    grad_in = inverse * (
        scaled
        - jnp.mean(scaled, -1, keepdims=True)
        - normed * jnp.mean(scaled * normed, -1, keepdims=True)
    )
    return (grad_in, jnp.sum(grad_out * normed, axis=0), jnp.sum(grad_out, axis=0))


def exact_gelu(value):
    return jax.nn.gelu(value, approximate=False)


def heads_packed(array):
    length = array.shape[0]
    split = array.reshape(2, length // 2, HEADS, HEAD)
    return jnp.transpose(split, (2, 1, 0, 3)).reshape(HEADS, length // 2, PAIR)


def heads_unpacked(array):
    half = array.shape[1]
    split = array.reshape(HEADS, half, 2, HEAD)
    return jnp.transpose(split, (2, 1, 0, 3)).reshape(2 * half, HEADS * HEAD)


def body(
    inputs, doc_bounds, pool_weight, pool_bias, ln1_gain, ln1_bias, query_weight, key_weight,
    value_weight, out_weight, pos_weight, content_bias, pos_bias, ln2_gain, ln2_bias, ffn_in,
    ffn_in_bias, ffn_out, ffn_out_bias, up_weight, up_bias, cotangent,
):
    _, bytes_here, width = inputs.shape
    length = bytes_here // 3
    n = lax.axis_size("seq")
    tokens = n * length
    group = 2 * n // (ROWS * HEADS)
    rounds = n // group
    tile = 2 * length
    row, head, member = whereabouts(group)[2:]

    all_bounds = lax.all_gather(doc_bounds, "dp", axis=0, tiled=True)
    bounds = lax.dynamic_slice(all_bounds, (row, 0), (1, 2))[0]
    table, turn_sin, turn_cos = wave_tables(tokens, length, width)
    head_weight = lax.dynamic_slice(pos_weight, (0, head * HEAD), (width, HEAD))
    head_cb = lax.dynamic_slice(content_bias, (head * HEAD,), (HEAD,))[None]
    head_pb = lax.dynamic_slice(pos_bias, (head * HEAD,), (HEAD,))[None]

    rim = passed_along(inputs[:, bytes_here - 2 :, :], "seq", 1)
    shifted = jnp.concatenate([rim, inputs[:, : bytes_here - 2, :]], 1)
    pooled_in = shifted.reshape(length, 3 * width)
    pooled = dot(pooled_in, pool_weight) + pool_bias
    normed_one, plain_one, inverse_one = layer_norm(pooled, ln1_gain, ln1_bias)
    attn_in = normed_one.astype(BF16)
    query = dot(attn_in, query_weight).astype(BF16)
    keys = dot(attn_in, key_weight).astype(BF16).reshape(length, HEADS, HEAD)
    values = dot(attn_in, value_weight).astype(BF16).reshape(length, HEADS, HEAD)
    q_out = heads_packed(query)
    kv_out = jnp.transpose(jnp.concatenate([keys, values], 2), (1, 0, 2))

    q_in, kv_in = exchange(
        to_units_kernel, n, group, (q_out, kv_out),
        ((rounds, length // 2, PAIR), (n, length, PAIR)), 0,
    )
    kv_in = kv_in.reshape(tokens, PAIR)

    common_specs = [
        turn_spec((length // 2, PAIR)),
        whole_spec((tokens, PAIR)),
        whole_spec(table.shape),
        whole_spec(turn_sin.shape),
        whole_spec(turn_cos.shape),
        whole_spec(head_weight.shape),
        whole_spec((1, HEAD)),
        whole_spec((1, HEAD)),
    ]
    common = (q_in, kv_in, table, turn_sin, turn_cos, head_weight, head_cb, head_pb)
    attended, att_low, total, keep = pl.pallas_call(
        functools.partial(attend_kernel, n, group, tile),
        grid=(rounds,),
        in_specs=common_specs + [pl.BlockSpec(memory_space=pltpu.SMEM)],
        out_specs=[
            turn_spec((length, HEAD)),
            turn_spec((length // 2, PAIR)),
            turn_spec((length, 128)),
            turn_spec((length, tokens)),
        ],
        out_shape=[
            jax.ShapeDtypeStruct((rounds, length, HEAD), F32),
            jax.ShapeDtypeStruct((rounds, length // 2, PAIR), BF16),
            jax.ShapeDtypeStruct((rounds, length, 128), F32),
            jax.ShapeDtypeStruct((rounds, length, tokens), BF16),
        ],
        scratch_shapes=[
            pltpu.VMEM((length, tokens), F32),
            pltpu.VMEM((length, PAIR + width), BF16),
        ],
        compiler_params=pltpu.CompilerParams(vmem_limit_bytes=56 * 2**20),
    )(*common, bounds)

    (att_back,) = exchange(
        to_owners_kernel, n, group, (att_low,), ((HEADS, length // 2, PAIR),), 1
    )
    attended_low = heads_unpacked(att_back)

    mixed = pooled + dot(attended_low, out_weight)
    normed_two, plain_two, inverse_two = layer_norm(mixed, ln2_gain, ln2_bias)
    ffn_input = normed_two.astype(BF16)
    pre_act = dot(ffn_input, ffn_in) + ffn_in_bias
    activated, gelu_pull = jax.vjp(exact_gelu, pre_act)
    act_low = activated.astype(BF16)
    final = mixed + dot(act_low, ffn_out) + ffn_out_bias
    final_low = final.astype(BF16)
    upsampled = dot(final_low, up_weight) + up_bias
    outputs = (inputs.astype(F32) + upsampled.reshape(1, bytes_here, width)).astype(BF16)
    grad_up = cotangent.reshape(length, 3 * width)
    over_rows = ((0,), (0,))
    over_columns = ((1,), (1,))
    grad_up_weight = dot(final_low, grad_up, over_rows)
    grad_up_bias = jnp.sum(grad_up.astype(F32), axis=0)
    grad_final = dot(grad_up, up_weight, over_columns)
    grad_branch = grad_final.astype(BF16)
    grad_ffn_out = dot(act_low, grad_branch, over_rows)
    grad_ffn_out_bias = jnp.sum(grad_branch.astype(F32), axis=0)
    grad_act = dot(grad_branch, ffn_out, over_columns)
    grad_pre = gelu_pull(grad_act)[0].astype(BF16)
    grad_ffn_in = dot(ffn_input, grad_pre, over_rows)
    grad_ffn_in_bias = jnp.sum(grad_pre.astype(F32), axis=0)
    grad_normed_two = dot(grad_pre, ffn_in, over_columns)
    grad_from_two, grad_ln2_gain, grad_ln2_bias = norm_back(
        grad_normed_two, plain_two, inverse_two, ln2_gain
    )
    grad_mixed = grad_final + grad_from_two
    grad_attn_branch = grad_mixed.astype(BF16)
    grad_out_weight = dot(attended_low, grad_attn_branch, over_rows)
    grad_attended = dot(grad_attn_branch, out_weight, over_columns).astype(BF16)

    early = lax.psum(
        tuple(
            grad.astype(BF16) for grad in (grad_ffn_in, grad_ffn_out, grad_up_weight, grad_out_weight)
        ),
        ("dp", "seq"),
    )

    (grad_in,) = exchange(
        to_units_kernel, n, group, (heads_packed(grad_attended),), ((rounds, length // 2, PAIR),), 2
    )
    dq_out, dkv_out, grad_head_weight, grad_head_cb, grad_head_pb = pl.pallas_call(
        functools.partial(back_kernel, n, group, tile),
        grid=(rounds,),
        in_specs=common_specs
        + [
            turn_spec((length, HEAD)),
            turn_spec((length, 128)),
            turn_spec((length, tokens)),
            turn_spec((length // 2, PAIR)),
        ],
        out_specs=[
            turn_spec((length // 2, PAIR)),
            whole_spec((tokens, PAIR)),
            whole_spec((width, HEAD)),
            whole_spec((1, HEAD)),
            whole_spec((1, HEAD)),
        ],
        out_shape=[
            jax.ShapeDtypeStruct((rounds, length // 2, PAIR), BF16),
            jax.ShapeDtypeStruct((tokens, PAIR), BF16),
            jax.ShapeDtypeStruct((width, HEAD), F32),
            jax.ShapeDtypeStruct((1, HEAD), F32),
            jax.ShapeDtypeStruct((1, HEAD), F32),
        ],
        scratch_shapes=[pltpu.VMEM((tokens, PAIR), F32)],
        compiler_params=pltpu.CompilerParams(vmem_limit_bytes=56 * 2**20),
    )(*common, attended, total, keep, grad_in)
    dq_back, dkv_back = exchange(
        to_owners_kernel, n, group, (dq_out, dkv_out.reshape(n, length, PAIR)),
        ((HEADS, length // 2, PAIR), (group, HEADS, length, PAIR)), 3,
    )
    grad_query = heads_unpacked(dq_back)
    dkv_back = jnp.transpose(jnp.sum(dkv_back.astype(F32), 0), (1, 0, 2)).astype(BF16)
    grad_key_low = dkv_back[:, :, :HEAD].reshape(length, width)
    grad_value_low = dkv_back[:, :, HEAD:].reshape(length, width)

    def at_head(part, shape):
        return lax.dynamic_update_slice(
            jnp.zeros(shape, F32), part.reshape(shape[:-1] + (HEAD,)), (0,) * (len(shape) - 1) + (head * HEAD,)
        )

    grad_pos_weight = at_head(grad_head_weight, (width, width))
    grad_content_bias = at_head(grad_head_cb, (width,))
    grad_pos_bias = at_head(grad_head_pb, (width,))
    grad_query_weight = dot(attn_in, grad_query, over_rows)
    grad_key_weight = dot(attn_in, grad_key_low, over_rows)
    grad_value_weight = dot(attn_in, grad_value_low, over_rows)
    grad_normed_one = (
        dot(grad_query, query_weight, over_columns)
        + dot(grad_key_low, key_weight, over_columns)
        + dot(grad_value_low, value_weight, over_columns)
    )
    grad_from_one, grad_ln1_gain, grad_ln1_bias = norm_back(
        grad_normed_one, plain_one, inverse_one, ln1_gain
    )
    grad_pooled = (grad_mixed + grad_from_one).astype(BF16)
    grad_pool_weight = dot(pooled_in, grad_pooled, over_rows)
    grad_pool_bias = jnp.sum(grad_pooled.astype(F32), axis=0)
    grad_shifted = dot(grad_pooled, pool_weight, over_columns).reshape(1, bytes_here, width)
    incoming = passed_along(grad_shifted[:, :2, :], "seq", -1)
    input_grad = (
        cotangent.astype(F32) + jnp.concatenate([grad_shifted[:, 2:, :], incoming], 1)
    ).astype(BF16)
    late = lax.psum(
        tuple(
            grad.astype(BF16)
            for grad in (
                grad_pool_weight, grad_query_weight, grad_key_weight, grad_value_weight, grad_pos_weight,
            )
        ),
        ("dp", "seq"),
    )
    small_parts = (
        grad_pool_bias, grad_ln1_gain, grad_ln1_bias, grad_content_bias, grad_pos_bias,
        grad_ln2_gain, grad_ln2_bias, grad_ffn_in_bias, grad_ffn_out_bias, grad_up_bias,
    )
    small = lax.psum(jnp.concatenate(small_parts), ("dp", "seq"))
    cuts = np.cumsum([part.shape[0] for part in small_parts])[:-1].tolist()
    (
        sum_pool_bias, sum_ln1_gain, sum_ln1_bias, sum_content, sum_pos,
        sum_ln2_gain, sum_ln2_bias, sum_in_bias, sum_out_bias, sum_up_bias,
    ) = jnp.split(small, cuts)
    sum_in, sum_out, sum_up, sum_mix = (grad.astype(F32) for grad in early)
    sum_pool, sum_q, sum_k, sum_v, sum_p = (grad.astype(F32) for grad in late)
    return (
        outputs, input_grad, sum_pool, sum_pool_bias, sum_ln1_gain, sum_ln1_bias, sum_q, sum_k, sum_v,
        sum_mix, sum_p, sum_content, sum_pos, sum_ln2_gain, sum_ln2_bias, sum_in, sum_in_bias,
        sum_out, sum_out_bias, sum_up, sum_up_bias,
    )


EARLY_ROWS, LATE_ROWS = 6144, 3584
EARLY_CHUNKS = ((0, 2048, False), (2048, 2048, True), (4096, 2048, False))
LATE_CHUNKS = ((3072, 512, False), (1536, 1024, False), (2560, 512, True), (0, 1024, False), (1024, 512, True))
QKV_SUMS, POOL_SUMS = slice(4, 6), slice(6, None)
SMALL_ROWS = 16
TILE = 512
OVER_ROWS = ((0,), (0,))
OVER_COLUMNS = ((1,), (1,))


class Reduction:
    def __init__(self, buffer, start, rows, by_z, bufs, sems, free, small=None):
        self.buffer, self.sems, self.free, self.small = buffer, sems, free, small
        core, chip = lax.axis_index("dp"), lax.axis_index("seq")
        self.core, self.chip = core, chip
        x, y, z = chip % 2, (chip // 2) % 2, chip // 4
        first_x = core == 0
        self.peer_x, self.peer_y = (core, chip + 1 - 2 * x), (core, chip + 2 - 4 * y)
        self.z_peers = [(core, chip + ((z + away) % 4 - z) * 4) for away in (1, 2, 3)]
        self.z = z

        def pair(bit, peer_core, peer_chip):
            return (bit, [(1 - bit, peer_core, peer_chip)])

        one = pair(jnp.where(first_x, x, y), core, jnp.where(first_x, self.peer_x[1], self.peer_y[1]))
        two = pair(jnp.where(first_x, y, x), core, jnp.where(first_x, self.peer_y[1], self.peer_x[1]))
        stages = [pair(core, 1 - core, chip)]
        if by_z:
            low, high = z % 2, z // 2
            stages += [pair(low, core, chip + 4 - 8 * low), one, two, pair(high, core, chip + 8 - 16 * high)]
        else:
            stages += [one, two, (z, [((z + away) % 4, core, self.z_peers[away - 1][1]) for away in (1, 2, 3)])]
        self.stages = []
        at, size, first = start, rows, 0
        for buf, (own, others) in zip(bufs, stages):
            ways = len(others) + 1
            self.stages.append((at, size, size // ways, own, others, buf, first))
            at, size, first = at + own * (size // ways), size // ways, first + len(others)
        self.back = first
        self.last = 2 * len(stages)

    def rows(self, start, size):
        return self.buffer.at[pl.ds(pl.multiple_of(start, 16), size)]

    def copy(self, index, source, target, core, chip):
        return pltpu.make_async_remote_copy(
            source, target, self.sems.at[0, index], self.sems.at[1, index],
            device_id=(core, chip), device_id_type=MESH,
        )

    def done(self, index, source):
        copy = self.copy(index, source, source, 1 - self.core, self.chip)
        copy.wait_send()
        copy.wait_recv()

    def add(self, start, size, part_start, buf):
        chunk = min(size, 128)
        while size % chunk:
            chunk -= 16

        def one(step, carry):
            at = pl.ds(pl.multiple_of(start + step * chunk, 16), chunk)
            here = pl.ds(pl.multiple_of(part_start + step * chunk, 16), chunk)
            total = self.buffer[at].astype(F32)
            for part in range(buf.shape[0]):
                total = total + buf[part, here].astype(F32)
            self.buffer[at] = total.astype(BF16)
            return carry

        lax.fori_loop(0, size // chunk, one, 0)

    def send_parts(self, number):
        at, _, part, _, others, buf, first = self.stages[number]
        for place, (other, core, chip) in enumerate(others):
            self.copy(first + place, self.rows(at + other * part, part), buf.at[place], core, chip).start()

    def send_back(self, number):
        at, _, part, own, others, _, first = self.stages[number]
        pl.semaphore_wait(self.free.at[number], len(others))
        mine = self.rows(at + own * part, part)
        for place, (_, core, chip) in enumerate(others):
            self.copy(self.back + first + place, mine, mine, core, chip).start()

    def step(self, number):
        count = len(self.stages)
        if number == 0:
            self.send_parts(0)
        elif number <= count:
            at, _, part, own, others, buf, first = self.stages[number - 1]
            for place, (_, core, chip) in enumerate(others):
                self.done(first + place, buf.at[place])
            for _, core, chip in others:
                pl.semaphore_signal(self.free.at[number - 1], inc=1, device_id=(core, chip), device_id_type=MESH)
            kept = at + own * part
            if number < count:
                _, _, next_part, next_own, next_others, _, _ = self.stages[number]
                for other, _, _ in next_others:
                    self.add(kept + other * next_part, next_part, other * next_part, buf)
                self.send_parts(number)
                self.add(kept + next_own * next_part, next_part, next_own * next_part, buf)
            else:
                self.add(kept, part, 0, buf)
                self.send_back(count - 1)
        else:
            stage = 2 * count - number
            at, _, part, own, others, _, first = self.stages[stage]
            for place in range(len(others)):
                self.done(self.back + first + place, self.rows(at + own * part, part))
            if stage > 0:
                self.send_back(stage - 1)
        if self.small is not None:
            self.small_step(number)

    def small_step(self, number):
        own, taken = self.small
        first = 2 * self.back
        if number in (1, 2, 3):
            self.done(first + number - 1, own)
            own[...] = own[...] + taken[number - 1]
        if number < 3:
            core, chip = ((1 - self.core, self.chip), self.peer_x, self.peer_y)[number]
            self.copy(first + number, own, taken.at[number], core, chip).start()
        if number == 3:
            taken[3 + self.z] = own[...]
            for place, (core, chip) in enumerate(self.z_peers):
                self.copy(first + 3 + place, own, taken.at[3 + self.z], core, chip).start()
        if number == 4:
            for place in range(3):
                self.done(first + 3 + place, own)
            own[...] = (taken[3] + taken[4]) + (taken[5] + taken[6])


REDUCTION_SEMS = 18


def reduction_scratch(rows, by_z):
    shapes = [(1, rows // 2), (1, rows // 4), (1, rows // 8)]
    shapes += [(1, rows // 16), (1, rows // 32)] if by_z else [(3, rows // 32)]
    return [pltpu.VMEM(shape + (512,), BF16) for shape in shapes]


def gelu_pair(value):
    falling = jnp.exp(value * value * -0.5)
    turn = 1.0 / (1.0 + 0.3275911 * 0.7071067811865476 * jnp.abs(value))
    series = turn * (
        0.254829592
        + turn * (-0.284496736 + turn * (1.421413741 + turn * (-1.453152027 + turn * 1.061405429)))
    )
    tail = 0.5 * series * falling
    share = jnp.where(value >= 0, 1.0 - tail, tail)
    return value * share, share + value * falling * 0.3989422804014327


def norm_parts(hidden):
    average = jnp.mean(hidden, -1, keepdims=True)
    centred = hidden - average
    inverse = lax.rsqrt(jnp.mean(centred * centred, -1, keepdims=True) + epsilon)
    return centred * inverse, inverse


def norm_grad(grad_out, normed, inverse, gain):
    scaled = grad_out * gain
    return inverse * (
        scaled
        - jnp.mean(scaled, -1, keepdims=True)
        - normed * jnp.mean(scaled * normed, -1, keepdims=True)
    )


def column_sum(value):
    return jnp.sum(value, 0, keepdims=True)


def most_tiles(turn, length):
    return ((2 * turn + 2) * length + TILE - 1) // TILE


def layer_kernel(n, length, layout, *refs):
    taken = iter(refs)
    given, vectors, outs, scratch = ({name: next(taken) for name in part} for part in layout)
    r = types.SimpleNamespace(**vectors, **outs, **scratch)
    group = 2
    rounds = n // group
    tile = TILE
    width = 512
    scale = HEAD**-0.5
    core, chip, row, head, member = whereabouts(group)
    count = 2 * n
    me = core * n + chip

    loads = {}
    chunk_refs = list(refs[len(refs) - sum(5 if cut[2] else 4 for cut in EARLY_CHUNKS + LATE_CHUNKS) :])

    def reduction(buffer, index, cut, small=None):
        bufs = [chunk_refs.pop(0) for _ in range(5 if cut[2] else 4)]
        return Reduction(buffer, *cut, bufs, r.sum_sem.at[index], r.sum_free.at[index], small)

    for index, (name, source) in enumerate(given.items()):
        loads[name] = pltpu.make_async_copy(source, scratch[name], r.load_sem.at[index])
        loads[name].start()

    def ready(*which):
        for ref in which:
            next(loads[name] for name in given if scratch[name] is ref).wait()

    r.up_b[...] = r.up_flat[...].reshape(1, 3 * width)

    barrier = pltpu.get_barrier_semaphore()

    def greet(step, carry):
        other = (me + step) % count
        pl.semaphore_signal(barrier, inc=1, device_id=(other // n, other % n), device_id_type=MESH)
        return carry

    lax.fori_loop(1, count, greet, 0)

    low_bound, high_bound = r.bounds[0, 0], r.bounds[0, 1]
    r.edges[core, :8] = jnp.full((8, 128), low_bound, jnp.int32)
    r.edges[core, 8:] = jnp.full((8, 128), high_bound, jnp.int32)

    def tokens_of(source, target):
        for block in range(width // 128):
            r.mixing[block] = source[:, block * 128 : (block + 1) * 128].astype(F32)
            for part in range(3):
                every = r.mixing[block, pl.ds(part, length, stride=3), :]
                start = part * width + block * 128
                target[:, start : start + 128] = every.astype(BF16)

    ready(r.x_bytes, r.pool_w)
    tokens_of(r.x_bytes, r.x3)
    own = dot(r.x3[:, :width], r.pool_w[2 * width :])
    before = dot(r.x3[:, width:], r.pool_w[: 2 * width])
    pl.semaphore_wait(barrier, count - 1)

    def edge_copy():
        return pltpu.make_async_remote_copy(
            r.edges.at[core], r.edges.at[core], r.side_sem.at[0], r.side_sem.at[1],
            device_id=(1 - core, chip), device_id_type=MESH,
        )

    def rim_copy():
        return pltpu.make_async_remote_copy(
            r.x3.at[length - 16 :, width:], r.rim, r.side_sem.at[2], r.side_sem.at[3],
            device_id=(core, (chip + 1) % n), device_id_type=MESH,
        )

    edge_copy().start()

    @pl.when(chip < n - 1)
    def _():
        rim_copy().start()

    @pl.when(chip == 0)
    def _():
        r.rim[...] = jnp.zeros_like(r.rim)

    @pl.when(chip > 0)
    def _():
        rim_copy().wait_recv()

    rim_sum = dot(r.rim[...], r.pool_w[: 2 * width])
    at_row = lax.broadcasted_iota(jnp.int32, (length, width), 0)
    before = jnp.where(at_row == 0, rim_sum[15:16], pltpu.roll(before, 1, 0))
    pooled = own + before + r.pool_b[...]
    r.pooled[...] = pooled
    plain, _ = norm_parts(pooled)
    attn_in = (plain * r.ln1_g[...] + r.ln1_b[...]).astype(BF16)
    r.attn_in[...] = attn_in
    ready(r.q_w, r.k_w, r.v_w)
    query = dot(attn_in, r.q_w[...])
    keys = dot(attn_in, r.k_w[...])
    values = dot(attn_in, r.v_w[...])
    for h in range(HEADS):
        at = slice(h * HEAD, (h + 1) * HEAD)
        r.q_out[h] = packed(query[:, at]).astype(BF16)
        r.kv_out[h] = jnp.concatenate([keys[:, at], values[:, at]], 1).astype(BF16)
    turn_to, spot_to = place_of(chip, group)

    def q_jobs(array, out, sem, recv):
        jobs = []
        for h in range(HEADS):
            to_chip, to_core = chip_of(core, h, spot_to, group)
            jobs.append((array.at[h], out.at[turn_to], (sem, recv.at[turn_to]), to_core, to_chip))
        return jobs

    def rows_in(block):
        return pl.ds(pl.multiple_of(block * length, length), length)

    kv_jobs = []
    for h in range(HEADS):
        to_chip, _ = chip_of(core, h, 0, group)
        sems = (r.send_sem.at[1], r.kv_sem.at[chip])
        kv_jobs.append((r.kv_out.at[h], r.kv.at[rows_in(chip)], sems, chip % 2, to_chip))
    first_jobs = kv_jobs + q_jobs(r.q_out, r.q, r.send_sem.at[0], r.q_sem)
    for job in first_jobs:
        send(*job)

    ready(r.ct_bytes, r.up_w, r.ffn_out)
    tokens_of(r.ct_bytes, r.ct3)
    grad_final = dot(r.ct3[...], r.up_w[...], OVER_COLUMNS)
    r.grad_final[...] = grad_final
    grad_branch = grad_final.astype(BF16)
    r.grad_branch[...] = grad_branch
    for part in range(4):
        at = slice(part * width, (part + 1) * width)
        r.grad_act[:, at] = dot(grad_branch, r.ffn_out[at], OVER_COLUMNS)
    small = r.small
    small[...] = jnp.zeros_like(small)
    small[11:12] = column_sum(grad_branch.astype(F32))
    for part in range(3):
        at = slice(part * width, (part + 1) * width)
        small[12 + part : 13 + part] = column_sum(r.ct3[:, at].astype(F32))

    ready(r.pos_w, r.table)
    odd = head % 2 == 1
    pair_at = pl.ds(pl.multiple_of((head // 2) * PAIR, PAIR), PAIR)

    def of_head(ref):
        both = ref[:, pair_at].astype(F32)
        return jnp.where(odd, both[:, HEAD:], both[:, :HEAD])

    r.head_w[...] = of_head(r.pos_w).astype(BF16)
    content_bias, pos_bias = of_head(r.content), of_head(r.pos)
    edge_copy().wait_send()
    edge_copy().wait_recv()
    low_edge = r.edges[row, 0:1, 0:1]
    high_edge = r.edges[row, 8:9, 0:1]
    half = width // 2
    lanes = lax.broadcasted_iota(jnp.int32, (length, tile), 1)

    def rows_of(start):
        return pl.ds(pl.multiple_of(start, 64), tile)

    def tiles_to(block):
        return ((block + 1) * length + tile - 1) // tile

    def kept_at(turn):
        return sum(jnp.where(turn > before, most_tiles(before, length), 0) for before in range(rounds - 1))

    def forward(turn):
        at = turn * group + core
        return pltpu.make_async_remote_copy(
            r.kv.at[rows_in(at)], r.kv.at[rows_in(at)], r.send_sem.at[6], r.kv_sem.at[at], device_id=(1 - core, chip), device_id_type=MESH
        )

    def pass_on(turn):
        at = turn * group + core
        arrived(r.kv.at[rows_in(at)], r.kv_sem.at[at])
        forward(turn).start()

    pass_on(0)
    pass_on(1)
    arrived(r.kv.at[rows_in(1 - core)], r.kv_sem.at[1 - core])

    def attend(turn, carry):
        block = block_of(turn, member, group)

        @pl.when(turn < rounds - 2)
        def _():
            pass_on(turn + 2)

        @pl.when(turn < rounds - 1)
        def _():
            other = (turn + 1) * group + 1 - core
            arrived(r.kv.at[rows_in(other)], r.kv_sem.at[other])

        arrived(r.q.at[turn], r.q_sem.at[turn])
        query_u, _, turned = query_parts(
            r.q[turn], content_bias, pos_bias, r.head_w[...], r.sines[...], r.cosines[...]
        )
        head_part = (query_u.astype(F32) * scale).astype(BF16)
        r.extra[:, :PAIR] = jnp.concatenate([head_part, jnp.zeros_like(head_part)], 1)
        r.extra[:, PAIR:] = (turned * scale).astype(BF16)
        places = block * length + lax.broadcasted_iota(jnp.int32, (length, 1), 0)
        opening = jnp.where(places >= high_edge, high_edge, jnp.where(places >= low_edge, low_edge, 0))

        def score_step(step, top):
            pair = r.kv[rows_of(step * tile), :]
            waves = r.table[rows_of((n - 1 - block) * length + step * tile), :]
            score = dot(r.extra[:, :PAIR], pair, OVER_COLUMNS) + dot(r.extra[:, PAIR:], waves, OVER_COLUMNS)
            at = lanes + step * tile
            allowed = jnp.logical_and(at <= places, at >= opening)
            score = jnp.where(allowed, score, masked_score)
            r.score[step] = score
            for part in range(tile // 128):
                top = jnp.maximum(top, score[:, part * 128 : (part + 1) * 128])
            return top

        kept, tiles = kept_at(turn), tiles_to(block)
        top = lax.fori_loop(0, tiles, score_step, jnp.full((length, 128), masked_score, F32))
        top = jnp.max(top, 1, keepdims=True)

        def value_step(step, state):
            total, summed = state
            weight = jnp.exp(r.score[step] - top)
            for part in range(tile // 128):
                total = total + weight[:, part * 128 : (part + 1) * 128]
            low = weight.astype(BF16)
            r.keep[kept + step] = low
            pair = r.kv[rows_of(step * tile), :]
            return total, summed + dot(low, pair)

        total, summed = lax.fori_loop(
            0, tiles, value_step, (jnp.zeros((length, 128), F32), jnp.zeros((length, PAIR), F32))
        )
        inverse = 1.0 / jnp.sum(total, 1, keepdims=True)
        attended = summed[:, HEAD:] * inverse
        r.att[turn] = jnp.concatenate([jnp.broadcast_to(inverse, (length, HEAD)), attended], 1)
        r.att_out[turn] = packed(attended).astype(BF16)
        send(
            r.att_out.at[turn], r.att_in.at[head], (r.send_sem.at[2], r.att_sem.at[0]), row, block
        )
        return carry

    lax.fori_loop(0, rounds, attend, 0)
    for source, _, sems, to_core, to_chip in first_jobs:
        sent(source, sems[0], to_core, to_chip)
    for turn in range(rounds):
        forward(turn).wait_send()

    def joined(get):
        parts = [get(h) for h in range(HEADS)]
        upper = jnp.concatenate([part[:, :HEAD] for part in parts], 1)
        lower = jnp.concatenate([part[:, HEAD:] for part in parts], 1)
        return jnp.concatenate([upper, lower], 0)

    arrived(r.att_in, r.att_sem.at[0])
    ready(r.out_w, r.ffn_in)
    att_low = joined(lambda h: r.att_in[h].astype(F32)).astype(BF16)
    r.att_low[...] = att_low
    mixed = r.pooled[...] + dot(att_low, r.out_w[...])
    r.mixed[...] = mixed
    plain_two, inverse_two = norm_parts(mixed)
    ffn_input = (plain_two * r.ln2_g[...] + r.ln2_b[...]).astype(BF16)
    r.ffn_input[...] = ffn_input
    grad_normed = jnp.zeros((length, width), F32)
    for part in range(4):
        at = slice(part * width, (part + 1) * width)
        pre_act = dot(ffn_input, r.ffn_in[:, at]) + r.ffn_in_b[:, at]
        act, slope = gelu_pair(pre_act)
        r.act_low[:, at] = act.astype(BF16)
        grad_pre = (r.grad_act[:, at] * slope).astype(BF16)
        r.grad_pre[:, at] = grad_pre
        small[7 + part : 8 + part] = column_sum(grad_pre.astype(F32))
        grad_normed = grad_normed + dot(grad_pre, r.ffn_in[:, at], OVER_COLUMNS)
    small[5:6] = column_sum(grad_normed * plain_two)
    small[6:7] = column_sum(grad_normed)
    grad_mixed = r.grad_final[...] + norm_grad(grad_normed, plain_two, inverse_two, r.ln2_g[...])
    r.grad_final[...] = grad_mixed
    grad_mixed_low = grad_mixed.astype(BF16)
    grad_att = dot(grad_mixed_low, r.out_w[...], OVER_COLUMNS)
    for h in range(HEADS):
        r.q_out[h] = packed(grad_att[:, h * HEAD : (h + 1) * HEAD]).astype(BF16)
    second_jobs = q_jobs(r.q_out, r.grad, r.send_sem.at[3], r.grad_sem)
    for job in second_jobs:
        send(*job)

    early, late = r.early, r.late
    count_early, count_late = len(EARLY_CHUNKS), len(LATE_CHUNKS)
    sums = [reduction(early, index, cut) for index, cut in enumerate(EARLY_CHUNKS)]
    for index, cut in enumerate(LATE_CHUNKS):
        small_pair = (small, r.small_in) if index == count_late - 1 else None
        sums.append(reduction(late, count_early + index, cut, small_pair))

    def leave(index):
        cut = (EARLY_CHUNKS + LATE_CHUNKS)[index]
        buffer, target = (early, r.early_o) if index < count_early else (late, r.late_o)
        at = pl.ds(cut[0], cut[1])
        return pltpu.make_async_copy(buffer.at[at], target.at[at], r.leave_sem.at[index])

    def steps_at(moment):
        for index, number in SCHEDULE.get(moment, ()):
            sums[index].step(number)
            if number == sums[index].last:
                leave(index).start()

    for part in range(4):
        at = slice(part * width, (part + 1) * width)
        early[at] = dot(r.ffn_input[...], r.grad_pre[:, at], OVER_ROWS).astype(BF16)
    sums[0].step(0)
    steps_at(-4)
    for part in range(4):
        at = slice(part * width, (part + 1) * width)
        early[2048 + part * width : 2048 + (part + 1) * width] = dot(
            r.act_low[:, at], r.grad_branch[...], OVER_ROWS
        ).astype(BF16)
    sums[1].step(0)
    steps_at(-3)
    early[5632:] = dot(r.att_low[...], grad_mixed_low, OVER_ROWS).astype(BF16)
    final_low = (r.mixed[...] + dot(r.act_low[...], r.ffn_out[...]) + r.ffn_out_b[...]).astype(BF16)
    for part in range(3):
        at = slice(part * width, (part + 1) * width)
        early[4096 + part * width : 4096 + (part + 1) * width] = dot(final_low, r.ct3[:, at], OVER_ROWS).astype(BF16)
    sums[2].step(0)
    steps_at(-2)
    for part in range(3):
        at = slice(part * width, (part + 1) * width)
        lifted = dot(final_low, r.up_w[:, at]) + r.up_b[:, at]
        r.out3[:, at] = (r.x3[:, at].astype(F32) + lifted).astype(BF16)

    steps_at(-1)

    r.dkv[...] = jnp.zeros_like(r.dkv)
    r.dhead[...] = jnp.zeros_like(r.dhead)
    r.dbias[...] = jnp.zeros_like(r.dbias)

    def give_over(turn):
        return pltpu.make_async_remote_copy(
            r.dkv_out.at[turn * group + 1 - core], r.dkv_other.at[turn], r.send_sem.at[7], r.other_sem.at[turn],
            device_id=(1 - core, chip), device_id_type=MESH,
        )

    def hand_in(turn):
        at = turn * group + core
        give_over(turn).wait_recv()
        total = r.dkv[pl.ds(pl.multiple_of(at * length, length), length)] + r.dkv_other[turn].astype(F32)
        r.dkv_out[at] = total.astype(BF16)
        send(r.dkv_out.at[at], r.dkv_in.at[head], (r.send_sem.at[4], r.dkv_sem.at[0]), row, at)

    def back(index, carry):
        turn = rounds - 1 - index
        block = block_of(turn, member, group)
        arrived(r.grad.at[turn], r.grad_sem.at[turn])
        query = unpacked(r.q[turn].astype(F32))
        query_u = ((query + content_bias).astype(BF16).astype(F32) * scale).astype(BF16)
        query_v = (query + pos_bias).astype(BF16)
        grad = unpacked(r.grad[turn].astype(F32))
        inverse = r.att[turn][:, :HEAD]
        grad_part = grad * inverse
        delta = jnp.sum(grad_part * r.att[turn][:, HEAD:], 1, keepdims=True)
        nothing = jnp.zeros((length, HEAD), F32)
        r.extra[:, :PAIR] = jnp.concatenate([nothing, grad_part], 1).astype(BF16)
        r.extra[:, PAIR : 2 * PAIR] = jnp.concatenate([query_u.astype(F32), nothing], 1).astype(BF16)
        r.near[...] = jnp.zeros_like(r.near)
        r.far[...] = jnp.zeros_like(r.far)

        def step_over(step, inner):
            pair = r.kv[rows_of(step * tile), :]
            waves = r.table[rows_of((n - 1 - block) * length + step * tile), :]
            weight = r.keep[kept + step]
            grad_weight = dot(r.extra[:, :PAIR], pair, OVER_COLUMNS)
            grad_score = (weight.astype(F32) * (grad_weight - delta)).astype(BF16)
            r.near[...] += dot(grad_score, pair)
            r.far[...] += dot(grad_score, waves)
            at = pl.ds(pl.multiple_of(step * tile, tile), tile)
            r.dkv[at] += dot(grad_score, r.extra[:, PAIR : 2 * PAIR], OVER_ROWS) + dot(
                weight, r.extra[:, :PAIR], OVER_ROWS
            )
            return inner

        kept = kept_at(turn)
        lax.fori_loop(0, tiles_to(block), step_over, 0)
        give = turn * group + 1 - core
        r.dkv_out[give] = r.dkv[pl.ds(pl.multiple_of(give * length, length), length)].astype(BF16)
        give_over(turn).start()

        @pl.when(index > 0)
        def _():
            hand_in(turn + 1)

        grad_u = r.near[:, :HEAD] * scale
        turn_sin, turn_cos = r.sines[...], r.cosines[...]
        on_sin, on_cos = r.far[:, :half] * scale, r.far[:, half:] * scale
        lift = on_cos * turn_sin - on_sin * turn_cos
        rest = on_cos * turn_cos + on_sin * turn_sin
        spread = jnp.concatenate([lift, rest], 1).astype(BF16)
        grad_v = dot(spread, r.head_w[...])
        r.dhead[...] += dot(spread, query_v, OVER_ROWS)
        r.dbias[0:1] += column_sum(grad_u)
        r.dbias[1:2] += column_sum(grad_v)
        r.dq_out[turn] = packed(grad_u + grad_v).astype(BF16)
        send(r.dq_out.at[turn], r.dq_in.at[head], (r.send_sem.at[5], r.dq_sem.at[0]), row, block)
        for when in range(rounds):
            if when in SCHEDULE:

                @pl.when(index == when)
                def _(when=when):
                    steps_at(when)

        return carry

    lax.fori_loop(0, rounds, back, 0)
    hand_in(0)

    late[2048 + 1024 :] = jnp.zeros((512, 512), BF16)
    dhead = r.dhead[...]
    nothing = jnp.zeros_like(dhead)
    late[3072:, pair_at] = jnp.where(
        odd, jnp.concatenate([nothing, dhead], 1), jnp.concatenate([dhead, nothing], 1)
    ).astype(BF16)
    nothing = jnp.zeros((2, HEAD), F32)
    dbias = r.dbias[...][:2]
    small[3:5, pair_at] = jnp.where(
        odd, jnp.concatenate([nothing, dbias], 1), jnp.concatenate([dbias, nothing], 1)
    )
    sums[3].step(0)
    steps_at(8)
    for source, _, sems, to_core, to_chip in second_jobs:
        sent(source, sems[0], to_core, to_chip)
    for turn in range(rounds):
        block = block_of(jnp.int32(turn), member, group)
        sent(r.att_out.at[turn], r.send_sem.at[2], row, block)
        sent(r.dq_out.at[turn], r.send_sem.at[5], row, block)
    for turn in range(rounds):
        sent(r.dkv_out.at[turn * group + core], r.send_sem.at[4], row, turn * group + core)
        give_over(turn).wait_send()
    arrived(r.dq_in, r.dq_sem.at[0])
    arrived(r.dkv_in, r.dkv_sem.at[0])
    grad_query = joined(lambda h: r.dq_in[h].astype(F32)).astype(BF16)
    both = [r.dkv_in[h].astype(F32) for h in range(HEADS)]
    grad_keys = jnp.concatenate([part[:, :HEAD] for part in both], 1).astype(BF16)
    grad_values = jnp.concatenate([part[:, HEAD:] for part in both], 1).astype(BF16)
    steps_at(9)
    attn_in = r.attn_in[...]
    grad_normed = (
        dot(grad_query, r.q_w[...], OVER_COLUMNS)
        + dot(grad_keys, r.k_w[...], OVER_COLUMNS)
        + dot(grad_values, r.v_w[...], OVER_COLUMNS)
    )
    plain, inverse = norm_parts(r.pooled[...])
    small[1:2] = column_sum(grad_normed * plain)
    small[2:3] = column_sum(grad_normed)
    grad_pooled = (r.grad_final[...] + norm_grad(grad_normed, plain, inverse, r.ln1_g[...])).astype(BF16)
    r.grad_pooled[...] = grad_pooled
    grad_pooled_wide = grad_pooled.astype(F32)
    steps_at(10)
    small[0:1] = column_sum(grad_pooled_wide)

    def back_rim_copy():
        return pltpu.make_async_remote_copy(
            r.grad_pooled.at[:16], r.back_rim, r.side_sem.at[4], r.side_sem.at[5],
            device_id=(core, (chip + n - 1) % n), device_id_type=MESH,
        )

    @pl.when(chip > 0)
    def _():
        back_rim_copy().start()

    late[1024:1536] = dot(r.x3[:, :width], grad_pooled, OVER_ROWS).astype(BF16)
    follow = pltpu.roll(grad_pooled_wide, length - 1, 0)
    within = jnp.where(at_row == length - 1, 0.0, follow).astype(BF16)
    at_rim = lax.broadcasted_iota(jnp.int32, (16, width), 0)
    rim_row = jnp.where(at_rim == 15, jnp.broadcast_to(grad_pooled_wide[:1], (16, width)), 0.0).astype(BF16)
    late[:1024] = (
        dot(r.x3[:, width:], within, OVER_ROWS) + dot(r.rim[...], rim_row, OVER_ROWS)
    ).astype(BF16)
    for later in sums[POOL_SUMS]:
        later.step(0)
    steps_at(11)
    late[1536:2048] = dot(attn_in, grad_query, OVER_ROWS).astype(BF16)
    late[2048:2560] = dot(attn_in, grad_keys, OVER_ROWS).astype(BF16)
    late[2560:3072] = dot(attn_in, grad_values, OVER_ROWS).astype(BF16)
    for later in sums[QKV_SUMS]:
        later.step(0)
    steps_at(12)

    @pl.when(chip == n - 1)
    def _():
        r.back_rim[...] = jnp.zeros_like(r.back_rim)

    @pl.when(chip < n - 1)
    def _():
        back_rim_copy().wait_recv()

    next_row = r.back_rim[...].astype(F32)[:1]
    follow = jnp.where(at_row == length - 1, next_row, follow).astype(BF16)
    first_part = r.ct3[:, :width].astype(F32) + dot(grad_pooled, r.pool_w[2 * width :], OVER_COLUMNS)
    r.grad3[:, :width] = first_part.astype(BF16)
    other_part = r.ct3[:, width:].astype(F32) + dot(follow, r.pool_w[: 2 * width], OVER_COLUMNS)
    r.grad3[:, width:] = other_part.astype(BF16)

    @pl.when(chip < n - 1)
    def _():
        rim_copy().wait_send()

    @pl.when(chip > 0)
    def _():
        back_rim_copy().wait_send()

    steps_at(13)
    for index in range(len(sums)):
        leave(index).wait()


SCHEDULE = {
    -2: ((1, 1),),
    -1: ((0, 1),),
    1: ((0, 2),),
    2: ((1, 2), (2, 1), (0, 3),),
    8: ((2, 2), (1, 3), (0, 4), (3, 1),),
    10: ((1, 4),),
    11: ((2, 3),),
    12: ((3, 2), (0, 5), (7, 1), (4, 1), (3, 3), (1, 5), (5, 1), (6, 1),),
    13: (
        (7, 2), (2, 4), (4, 2), (1, 6), (6, 2), (3, 4), (5, 2), (7, 3), (0, 6), (4, 3), (1, 7), (5, 3), (6, 3),
        (2, 5), (3, 5), (5, 4), (7, 4), (4, 4), (5, 5), (6, 4), (7, 5), (1, 8), (3, 6), (2, 6), (5, 6), (7, 6),
        (4, 5), (0, 7), (7, 7), (3, 7), (6, 5), (0, 8), (5, 7), (3, 8), (7, 8), (4, 6), (6, 6), (5, 8), (1, 9),
        (2, 7), (7, 9), (4, 7), (5, 9), (1, 10), (6, 7), (7, 10), (4, 8), (2, 8), (5, 10), (6, 8),
    ),
}


WIDENED = (
    (0, 4, True), (2048, 4, False), (4096, 3, True), (5632, 1, False),
    (0, 3, False), (1536, 1, False), (2048, 1, False), (2560, 1, False), (3072, 1, False),
)
NARROW = ((0, 1), (1, 1), (2, 1), (3, 1), (4, 1), (5, 1), (6, 1), (7, 4), (11, 1), (12, 3))


def last_kernel(*refs):
    early, late, out3, grad3, small = refs[:5]
    wide_outs, narrow_outs, byte_outs = refs[5:14], refs[14:24], refs[24:26]
    loaded, staging, mixing, bytes_low, load_sems, sems = refs[26:]
    blocks = []
    for index, (out, (start, count, across)) in enumerate(zip(wide_outs, WIDENED)):
        for block in range(count):
            first = start + block * 512
            at = slice(block * 512, (block + 1) * 512)
            source = (early if index < 4 else late).at[first : first + 512]
            blocks.append((source, out.at[:, at] if across else out.at[at]))
    loads = [
        pltpu.make_async_copy(source, loaded.at[slot], load_sems.at[slot]) for slot, (source, _) in enumerate(blocks)
    ]
    stores = [
        pltpu.make_async_copy(staging.at[slot], target, sems.at[slot]) for slot, (_, target) in enumerate(blocks)
    ]
    for load in loads:
        load.start()
    for out, (start, count) in zip(narrow_outs, NARROW):
        if count == 3:
            out[...] = jnp.concatenate([small[start + block : start + block + 1] for block in range(count)], 1).reshape(-1)
        else:
            for block in range(count):
                out[:, block * 512 : (block + 1) * 512] = small[start + block : start + block + 1]

    def widen(slot):
        loads[slot].wait()

        def rows(step, carry):
            here = pl.ds(pl.multiple_of(step * 128, 128), 128)
            staging[slot, here] = loaded[slot, here].astype(F32)
            return carry

        lax.fori_loop(0, 4, rows, 0)
        stores[slot].start()

    some = len(blocks) // 2
    for slot in range(some):
        widen(slot)
    for index, (out, tokens) in enumerate(zip(byte_outs, (out3, grad3))):
        length, width = out.shape[0] // 3, out.shape[1]
        for block in range(width // 128):
            for part in range(3):
                start = part * width + block * 128
                mixing[block, pl.ds(part, length, stride=3), :] = tokens[:, start : start + 128].astype(F32)
            bytes_low[index, :, block * 128 : (block + 1) * 128] = mixing[block].astype(BF16)
        store = pltpu.make_async_copy(bytes_low.at[index], out, sems.at[len(blocks) + index])
        store.start()
        stores.append(store)
    for slot in range(some, len(blocks)):
        widen(slot)
    for store in stores:
        store.wait()


def finished(early, late, out3, grad3, small):
    length, width = out3.shape[0], out3.shape[1] // 3
    vmem = pl.BlockSpec(memory_space=pltpu.VMEM)
    shapes = [(512, 512 * blocks) if across else (512 * blocks, 512) for _, blocks, across in WIDENED]
    narrow = [(512 * blocks,) if blocks == 3 else (1, 512 * blocks) for _, blocks in NARROW]
    count = sum(blocks for _, blocks, _ in WIDENED)
    outs = pl.pallas_call(
        last_kernel,
        in_specs=[pl.BlockSpec(memory_space=pl.ANY)] * 2 + [vmem] * 3,
        out_specs=[pl.BlockSpec(memory_space=pl.ANY)] * len(shapes)
        + [vmem] * len(narrow)
        + [pl.BlockSpec(memory_space=pl.ANY)] * 2,
        out_shape=[jax.ShapeDtypeStruct(shape, F32) for shape in shapes + narrow]
        + [jax.ShapeDtypeStruct((3 * length, width), BF16)] * 2,
        scratch_shapes=[
            pltpu.VMEM((count, 512, 512), BF16), pltpu.VMEM((count, 512, 512), F32), pltpu.VMEM((width // 128, 3 * length, 128), F32),
            pltpu.VMEM((2, 3 * length, width), BF16), pltpu.SemaphoreType.DMA((count,)), pltpu.SemaphoreType.DMA((count + 2,)),
        ],
        compiler_params=pltpu.CompilerParams(vmem_limit_bytes=56 * 2**20),
    )(early, late, out3, grad3, small)
    return outs[: len(shapes)], [out if out.ndim == 1 else out[0] for out in outs[len(shapes) : -2]], outs[-2:]


def fused_body(
    inputs, doc_bounds, pool_weight, pool_bias, ln1_gain, ln1_bias, query_weight, key_weight,
    value_weight, out_weight, pos_weight, content_bias, pos_bias, ln2_gain, ln2_bias, ffn_in,
    ffn_in_bias, ffn_out, ffn_out_bias, up_weight, up_bias, cotangent,
):
    _, bytes_here, width = inputs.shape
    length = bytes_here // 3
    n = lax.axis_size("seq")
    tokens = n * length
    rounds = n // 2
    table, sines, cosines = wave_tables(tokens, length, width, TILE)
    given = dict(
        x_bytes=inputs[0], pool_w=pool_weight, q_w=query_weight, k_w=key_weight, v_w=value_weight,
        ct_bytes=cotangent[0], up_w=up_weight, ffn_out=ffn_out, pos_w=pos_weight, table=table,
        out_w=out_weight, ffn_in=ffn_in,
    )
    vectors = dict(
        pool_b=pool_bias, ln1_g=ln1_gain, ln1_b=ln1_bias, content=content_bias, pos=pos_bias, ln2_g=ln2_gain,
        ln2_b=ln2_bias, ffn_in_b=ffn_in_bias, ffn_out_b=ffn_out_bias,
    )
    vectors = {name: vector[None] for name, vector in vectors.items()} | dict(up_flat=up_bias, sines=sines, cosines=cosines)
    vmem = pl.BlockSpec(memory_space=pltpu.VMEM)
    outs = dict(
        out3=((length, 3 * width), BF16), grad3=((length, 3 * width), BF16), small=((SMALL_ROWS, 512), F32),
        early_o=((EARLY_ROWS, 512), BF16), late_o=((LATE_ROWS, 512), BF16),
    )
    pair_half = (length // 2, PAIR)
    block, wide = (length, width), (length, 4 * width)
    dma, signal = pltpu.SemaphoreType.DMA, pltpu.SemaphoreType.REGULAR
    scratch = {name: pltpu.VMEM(array.shape, array.dtype) for name, array in given.items()}
    low = dict(
        x3=(length, 3 * width), ct3=(length, 3 * width), rim=(16, 2 * width), back_rim=(16, width), attn_in=block, q_out=(HEADS,) + pair_half,
        kv_out=(HEADS, length, PAIR), q=(rounds,) + pair_half, kv=(tokens, PAIR), grad_branch=block,
        head_w=(width, HEAD), extra=(length, PAIR + width), keep=(sum(most_tiles(turn, length) for turn in range(rounds)), length, TILE),
        att_out=(rounds,) + pair_half, att_in=(HEADS,) + pair_half, att_low=block, ffn_input=block, act_low=wide,
        grad_pre=wide, grad=(rounds,) + pair_half, dkv_out=(n, length, PAIR), dkv_in=(HEADS, length, PAIR),
        dkv_other=(rounds, length, PAIR), dq_out=(rounds,) + pair_half, dq_in=(HEADS,) + pair_half, grad_pooled=block, early=(EARLY_ROWS, 512), late=(LATE_ROWS, 512),
    )
    full = dict(
        mixing=(width // 128, 3 * length, 128), pooled=block, grad_final=block, grad_act=wide, score=(tokens // TILE, length, TILE), att=(rounds, length, PAIR),
        mixed=block, dkv=(tokens, PAIR), dhead=(width, HEAD), dbias=(8, HEAD), near=(length, PAIR), far=block,
        small_in=(7, SMALL_ROWS, 512), up_b=(1, 3 * width),
    )
    scratch |= {name: pltpu.VMEM(shape, BF16) for name, shape in low.items()}
    scratch |= {name: pltpu.VMEM(shape, F32) for name, shape in full.items()}
    scratch |= dict(
        edges=pltpu.VMEM((2, 16, 128), jnp.int32), load_sem=dma((len(given),)), side_sem=dma((6,)), send_sem=dma((8,)), other_sem=dma((rounds,)),

        q_sem=dma((rounds,)), kv_sem=dma((n,)), att_sem=dma((1,)), grad_sem=dma((rounds,)), dkv_sem=dma((1,)),
        dq_sem=dma((1,)), sum_sem=dma((len(EARLY_CHUNKS + LATE_CHUNKS), 2, REDUCTION_SEMS)),
        sum_free=signal((len(EARLY_CHUNKS + LATE_CHUNKS), 5)), leave_sem=dma((len(EARLY_CHUNKS + LATE_CHUNKS),)),
    )
    layout = (list(given), list(vectors) + ["bounds"], list(outs), list(scratch))
    out3, grad3, small, early, late = pl.pallas_call(
        functools.partial(layer_kernel, n, length, layout),
        in_specs=[pl.BlockSpec(memory_space=pl.ANY)] * len(given)
        + [vmem] * len(vectors)
        + [pl.BlockSpec(memory_space=pltpu.SMEM)],
        out_specs=[vmem] * 3 + [pl.BlockSpec(memory_space=pl.ANY)] * 2,
        out_shape=[jax.ShapeDtypeStruct(*out) for out in outs.values()],
        scratch_shapes=list(scratch.values())
        + sum((reduction_scratch(*cut[1:]) for cut in EARLY_CHUNKS + LATE_CHUNKS), []),
        compiler_params=pltpu.CompilerParams(
            collective_id=0, has_side_effects=True, vmem_limit_bytes=62 * 2**20
        ),
    )(*given.values(), *vectors.values(), doc_bounds)
    wide, narrow, both = finished(early, late, out3, grad3, small)
    sum_in, sum_out, sum_up, sum_mix, sum_pool, sum_q, sum_k, sum_v, sum_p = wide
    pool_b, ln1_g, ln1_b, content, pos, ln2_g, ln2_b, in_b, out_b, up_b = narrow
    return (
        both[0][None], both[1][None], sum_pool, pool_b, ln1_g, ln1_b, sum_q, sum_k, sum_v, sum_mix, sum_p,
        content, pos, ln2_g, ln2_b, sum_in, in_b, sum_out, out_b, sum_up, up_b,
    )


def solution(mesh):
    split = P("dp", "seq", None)
    fits = mesh.shape["seq"] == 16
    return jax.shard_map(
        fused_body if fits else body,
        mesh=mesh,
        in_specs=(split, P("dp", None)) + (P(),) * 19 + (split,),
        out_specs=(split, split) + (P(),) * 19,
        check_vma=False,
    )
```

```python
import functools
import types

import jax
import jax.numpy as jnp
import numpy as np
from jax import lax
from jax.experimental import pallas as pl
from jax.experimental.pallas import tpu as pltpu
from jax.sharding import PartitionSpec as P

HEADS = 8
ROWS = 2
HEAD = 64
PAIR = 2 * HEAD
MESH = pl.DeviceIdType.MESH
F32 = jnp.float32
BF16 = jnp.bfloat16

epsilon = 1e-05
masked_score = -1e30


def dot(left, right, dims=((1,), (0,))):
    return lax.dot_general(left, right, (dims, ((), ())), preferred_element_type=F32)


def passed_along(value, axis, steps):
    count = lax.axis_size(axis)
    first, last = (max(0, -steps), min(count, count - steps))
    return lax.ppermute(value, axis, [(source, source + steps) for source in range(first, last)])


def place_of(block, group):
    turn, spot = block // group, block % group
    return turn, jnp.where((turn + turn // 4) % 2 == 0, spot, group - 1 - spot)


def block_of(turn, member, group):
    return turn * group + jnp.where((turn + turn // 4) % 2 == 0, member, group - 1 - member)


def whereabouts(group):
    core, chip = lax.axis_index("dp"), lax.axis_index("seq")
    chips = group // 2
    unit = chip // chips
    member = (chip % chips) * 2 + core
    return core, chip, unit // HEADS, unit % HEADS, member


def chip_of(row, head, member, group):
    return (row * HEADS + head) * (group // 2) + member // 2, member % 2


def meet(n, group, to_units):
    core, chip, row, head, member = whereabouts(group)
    barrier = pltpu.get_barrier_semaphore()

    def greet(row_or_core, chip_at):
        away = jnp.logical_or(row_or_core != core, chip_at != chip)

        @pl.when(away)
        def _():
            pl.semaphore_signal(
                barrier, inc=1, device_id=(row_or_core, chip_at), device_id_type=MESH
            )

        return away.astype(jnp.int32)

    own_row = row == core
    if to_units:
        for s in range(n):
            greet(row, jnp.int32(s))
        mine = jnp.logical_and(chip // (HEADS * (group // 2)) == core, True)
        pl.semaphore_wait(barrier, HEADS * group - mine.astype(jnp.int32))
    else:
        for h in range(HEADS):
            for g in range(group):
                c, k = chip_of(core, h, g, group)
                greet(jnp.int32(k), c)
        pl.semaphore_wait(barrier, n - own_row.astype(jnp.int32))


def send(source, target, sems, core, chip):
    here_core, here_chip = lax.axis_index("dp"), lax.axis_index("seq")
    here = jnp.logical_and(core == here_core, chip == here_chip)

    @pl.when(here)
    def _():
        pltpu.make_async_copy(source, target, sems[1]).start()

    @pl.when(jnp.logical_not(here))
    def _():
        pltpu.make_async_remote_copy(
            source, target, sems[0], sems[1], device_id=(core, chip), device_id_type=MESH
        ).start()


def sent(source, sem, core, chip):
    here_core, here_chip = lax.axis_index("dp"), lax.axis_index("seq")
    here = jnp.logical_and(core == here_core, chip == here_chip)

    @pl.when(jnp.logical_not(here))
    def _():
        pltpu.make_async_copy(source, source, sem).wait()


def arrived(whole, sem):
    pltpu.make_async_copy(whole, whole, sem).wait()


def to_units_kernel(n, group, *refs):
    count = len(refs) - 2
    arrays, outs = refs[: count // 2], refs[count // 2 : count]
    send_sem, recv_sem = refs[count:]
    core, chip, row, head, member = whereabouts(group)
    turn, spot = place_of(chip, group)
    meet(n, group, True)
    jobs = []
    for h in range(HEADS):
        for index, (array, out) in enumerate(zip(arrays, outs)):
            sems = (send_sem.at[index], recv_sem.at[index])
            if index == 0:
                to_chip, to_core = chip_of(core, h, spot, group)
                jobs.append((array.at[h], out.at[turn], sems, to_core, to_chip))
            else:
                for g in range(group):
                    to_chip, to_core = chip_of(core, h, g, group)
                    jobs.append((array.at[h], out.at[chip], sems, jnp.int32(to_core), to_chip))
    for job in jobs:
        send(*job)
    for source, _, sems, to_core, to_chip in jobs:
        sent(source, sems[0], to_core, to_chip)
    for index, out in enumerate(outs):
        arrived(out, recv_sem.at[index])


def to_owners_kernel(n, group, *refs):
    count = len(refs) - 2
    arrays, outs = refs[: count // 2], refs[count // 2 : count]
    send_sem, recv_sem = refs[count:]
    core, chip, row, head, member = whereabouts(group)
    meet(n, group, False)
    jobs = []
    for turn in range(n // group):
        block = block_of(jnp.int32(turn), member, group)
        sems = (send_sem.at[0], recv_sem.at[0])
        jobs.append((arrays[0].at[turn], outs[0].at[head], sems, row, block))
    if len(arrays) > 1:
        for block in range(n):
            sems = (send_sem.at[1], recv_sem.at[1])
            jobs.append((arrays[1].at[block], outs[1].at[member, head], sems, row, jnp.int32(block)))
    for job in jobs:
        send(*job)
    for source, _, sems, to_core, to_chip in jobs:
        sent(source, sems[0], to_core, to_chip)
    for index, out in enumerate(outs):
        arrived(out, recv_sem.at[index])


def exchange(kernel, n, group, arrays, shapes, ident):
    vmem = pl.BlockSpec(memory_space=pltpu.VMEM)
    return pl.pallas_call(
        functools.partial(kernel, n, group),
        out_shape=[jax.ShapeDtypeStruct(shape, array.dtype) for shape, array in zip(shapes, arrays)],
        in_specs=[vmem] * len(arrays),
        out_specs=[vmem] * len(arrays),
        scratch_shapes=[
            pltpu.SemaphoreType.DMA((len(arrays),)),
            pltpu.SemaphoreType.DMA((len(arrays),)),
        ],
        compiler_params=pltpu.CompilerParams(
            collective_id=ident, has_side_effects=True, vmem_limit_bytes=48 * 2**20
        ),
    )(*arrays)


def unpacked(pair):
    return jnp.concatenate([pair[:, :HEAD], pair[:, HEAD:]], 0)


def packed(block):
    half = block.shape[0] // 2
    return jnp.concatenate([block[:half], block[half:]], 1)


def query_parts(q_pair, content_bias, pos_bias, pos_weight, turn_sin, turn_cos):
    query = unpacked(q_pair.astype(F32))
    query_u = (query + content_bias).astype(BF16)
    query_v = (query + pos_bias).astype(BF16)
    spread = dot(query_v, pos_weight, ((1,), (1,)))
    half = turn_sin.shape[1]
    lift, rest = spread[:, :half], spread[:, half:]
    on_sin = rest * turn_sin - lift * turn_cos
    on_cos = lift * turn_sin + rest * turn_cos
    turned = jnp.concatenate([on_sin, on_cos], 1)
    return query_u, query_v, turned


def attend_kernel(
    n, group, tile, q_ref, kv_ref, table_ref, sin_ref, cos_ref, weight_ref, cb_ref, pb_ref, bounds_ref,
    att_ref, low_ref, total_ref, keep_ref, score_ref, extra_ref,
):
    turn = pl.program_id(0)
    member = whereabouts(group)[4]
    block = block_of(turn, member, group)
    length = sin_ref.shape[0]
    tokens = n * length
    query_u, _, turned = query_parts(
        q_ref[...], cb_ref[...], pb_ref[...], weight_ref[...], sin_ref[...], cos_ref[...]
    )
    scale = HEAD**-0.5
    head_part = (query_u.astype(F32) * scale).astype(BF16)
    extra_ref[:, :HEAD] = head_part
    extra_ref[:, HEAD:PAIR] = jnp.zeros_like(head_part)
    extra_ref[:, PAIR:] = (turned * scale).astype(BF16)
    first = block * length
    tiles = (first + length + tile - 1) // tile
    low_bound, high_bound = bounds_ref[0], bounds_ref[1]
    places = first + lax.broadcasted_iota(jnp.int32, (length, 1), 0)
    opening = jnp.where(
        places >= high_bound, high_bound, jnp.where(places >= low_bound, low_bound, 0)
    )
    lanes = lax.broadcasted_iota(jnp.int32, (length, tile), 1)

    def score_step(step, top):
        start = pl.multiple_of(step * tile, tile)
        keys = kv_ref[pl.ds(start, tile), :]
        waves = table_ref[pl.ds(pl.multiple_of((n - 1 - block) * length + start, length), tile), :]
        score = dot(extra_ref[:, :PAIR], keys, ((1,), (1,))) + dot(
            extra_ref[:, PAIR:], waves, ((1,), (1,))
        )
        at = lanes + start
        allowed = jnp.logical_and(at <= places, at >= opening)
        score = jnp.where(allowed, score, masked_score)
        score_ref[:, pl.ds(start, tile)] = score
        for part in range(tile // 128):
            top = jnp.maximum(top, score[:, part * 128 : (part + 1) * 128])
        return top

    top = lax.fori_loop(0, tiles, score_step, jnp.full((length, 128), masked_score, F32))
    top = jnp.max(top, 1, keepdims=True)

    def value_step(step, state):
        total, summed = state
        start = pl.multiple_of(step * tile, tile)
        weight = jnp.exp(score_ref[:, pl.ds(start, tile)] - top)
        for part in range(tile // 128):
            total = total + weight[:, part * 128 : (part + 1) * 128]
        low = weight.astype(BF16)
        keep_ref[:, pl.ds(start, tile)] = low
        return total, summed + dot(low, kv_ref[pl.ds(start, tile), :])

    total, summed = lax.fori_loop(
        0, tiles, value_step, (jnp.zeros((length, 128), F32), jnp.zeros((length, PAIR), F32))
    )
    total = jnp.sum(total, 1, keepdims=True)
    attended = summed[:, HEAD:] / total
    att_ref[...] = attended
    total_ref[...] = jnp.broadcast_to(total, (length, 128))
    low_ref[...] = packed(attended).astype(BF16)


def back_kernel(
    n, group, tile, q_ref, kv_ref, table_ref, sin_ref, cos_ref, weight_ref, cb_ref, pb_ref,
    att_ref, total_ref, keep_ref, grad_ref,
    dq_ref, dkv_ref, dweight_ref, dcb_ref, dpb_ref, dkv_acc,
):
    turn = pl.program_id(0)
    member = whereabouts(group)[4]
    block = block_of(turn, member, group)
    length = sin_ref.shape[0]
    scale = HEAD**-0.5

    @pl.when(turn == 0)
    def _():
        dkv_acc[...] = jnp.zeros_like(dkv_acc)
        dweight_ref[...] = jnp.zeros_like(dweight_ref)
        dcb_ref[...] = jnp.zeros_like(dcb_ref)
        dpb_ref[...] = jnp.zeros_like(dpb_ref)

    query_u, query_v, _ = query_parts(
        q_ref[...], cb_ref[...], pb_ref[...], weight_ref[...], sin_ref[...], cos_ref[...]
    )
    head_part = (query_u.astype(F32) * scale).astype(BF16)
    grad = unpacked(grad_ref[...].astype(F32))
    inverse = 1.0 / total_ref[:, :1]
    delta = jnp.sum(grad * att_ref[...], 1, keepdims=True) * inverse
    grad_low = (grad * inverse).astype(BF16)
    nothing = jnp.zeros_like(grad_low)
    grad_wide = jnp.concatenate([nothing, grad_low], 1)
    query_wide = jnp.concatenate([head_part, nothing], 1)
    tiles = (block * length + length + tile - 1) // tile

    def step_over(step, state):
        near, far = state
        start = pl.multiple_of(step * tile, tile)
        keys = kv_ref[pl.ds(start, tile), :]
        waves = table_ref[pl.ds(pl.multiple_of((n - 1 - block) * length + start, length), tile), :]
        weight = keep_ref[:, pl.ds(start, tile)]
        grad_weight = dot(grad_wide, keys, ((1,), (1,)))
        grad_score = (weight.astype(F32) * (grad_weight - delta)).astype(BF16)
        near = near + dot(grad_score, keys)
        far = far + dot(grad_score, waves)
        dkv_acc[pl.ds(start, tile), :] += dot(grad_score, query_wide, ((0,), (0,))) + dot(
            weight, grad_wide, ((0,), (0,))
        )
        return near, far

    near, far = lax.fori_loop(
        0,
        tiles,
        step_over,
        (jnp.zeros((length, PAIR), F32), jnp.zeros((length, table_ref.shape[1]), F32)),
    )
    grad_u = near[:, :HEAD] * scale
    half = sin_ref.shape[1]
    turn_sin, turn_cos = sin_ref[...], cos_ref[...]
    on_sin, on_cos = far[:, :half] * scale, far[:, half:] * scale
    lift = on_cos * turn_sin - on_sin * turn_cos
    rest = on_cos * turn_cos + on_sin * turn_sin
    spread = jnp.concatenate([lift, rest], 1).astype(BF16)
    grad_v = dot(spread, weight_ref[...])
    dweight_ref[...] += dot(spread, query_v, ((0,), (0,)))
    dcb_ref[...] += jnp.sum(grad_u, 0, keepdims=True)
    dpb_ref[...] += jnp.sum(grad_v, 0, keepdims=True)
    dq_ref[...] = packed(grad_u + grad_v).astype(BF16)

    @pl.when(turn == pl.num_programs(0) - 1)
    def _():
        dkv_ref[...] = dkv_acc[...].astype(BF16)


def wave_tables(tokens, length, width, more=0):
    rates = 10000.0 ** (-2.0 * np.arange(width // 2, dtype=np.float64) / width)
    far = (np.arange(tokens + max(length, more), dtype=np.float64) - (tokens - length))[:, None] * rates
    near = np.arange(length, dtype=np.float64)[:, None] * rates
    table = np.concatenate([np.sin(far), np.cos(far)], 1)
    return (
        jnp.asarray(table, dtype=BF16),
        jnp.asarray(np.sin(near), dtype=F32),
        jnp.asarray(np.cos(near), dtype=F32),
    )


def whole_spec(shape):
    return pl.BlockSpec(shape, lambda turn: (0,) * len(shape))


def turn_spec(shape):
    return pl.BlockSpec((None,) + shape, lambda turn: (turn,) + (0,) * len(shape))


def layer_norm(hidden, gain, bias):
    average = jnp.mean(hidden, -1, keepdims=True)
    centred = hidden - average
    inverse = lax.rsqrt(jnp.mean(centred * centred, -1, keepdims=True) + epsilon)
    normed = centred * inverse
    return (normed * gain + bias, normed, inverse)


def norm_back(grad_out, normed, inverse, gain):
    scaled = grad_out * gain
    grad_in = inverse * (
        scaled
        - jnp.mean(scaled, -1, keepdims=True)
        - normed * jnp.mean(scaled * normed, -1, keepdims=True)
    )
    return (grad_in, jnp.sum(grad_out * normed, axis=0), jnp.sum(grad_out, axis=0))


def exact_gelu(value):
    return jax.nn.gelu(value, approximate=False)


def heads_packed(array):
    length = array.shape[0]
    split = array.reshape(2, length // 2, HEADS, HEAD)
    return jnp.transpose(split, (2, 1, 0, 3)).reshape(HEADS, length // 2, PAIR)


def heads_unpacked(array):
    half = array.shape[1]
    split = array.reshape(HEADS, half, 2, HEAD)
    return jnp.transpose(split, (2, 1, 0, 3)).reshape(2 * half, HEADS * HEAD)


def body(
    inputs, doc_bounds, pool_weight, pool_bias, ln1_gain, ln1_bias, query_weight, key_weight,
    value_weight, out_weight, pos_weight, content_bias, pos_bias, ln2_gain, ln2_bias, ffn_in,
    ffn_in_bias, ffn_out, ffn_out_bias, up_weight, up_bias, cotangent,
):
    _, bytes_here, width = inputs.shape
    length = bytes_here // 3
    n = lax.axis_size("seq")
    tokens = n * length
    group = 2 * n // (ROWS * HEADS)
    rounds = n // group
    tile = 2 * length
    row, head, member = whereabouts(group)[2:]

    all_bounds = lax.all_gather(doc_bounds, "dp", axis=0, tiled=True)
    bounds = lax.dynamic_slice(all_bounds, (row, 0), (1, 2))[0]
    table, turn_sin, turn_cos = wave_tables(tokens, length, width)
    head_weight = lax.dynamic_slice(pos_weight, (0, head * HEAD), (width, HEAD))
    head_cb = lax.dynamic_slice(content_bias, (head * HEAD,), (HEAD,))[None]
    head_pb = lax.dynamic_slice(pos_bias, (head * HEAD,), (HEAD,))[None]

    rim = passed_along(inputs[:, bytes_here - 2 :, :], "seq", 1)
    shifted = jnp.concatenate([rim, inputs[:, : bytes_here - 2, :]], 1)
    pooled_in = shifted.reshape(length, 3 * width)
    pooled = dot(pooled_in, pool_weight) + pool_bias
    normed_one, plain_one, inverse_one = layer_norm(pooled, ln1_gain, ln1_bias)
    attn_in = normed_one.astype(BF16)
    query = dot(attn_in, query_weight).astype(BF16)
    keys = dot(attn_in, key_weight).astype(BF16).reshape(length, HEADS, HEAD)
    values = dot(attn_in, value_weight).astype(BF16).reshape(length, HEADS, HEAD)
    q_out = heads_packed(query)
    kv_out = jnp.transpose(jnp.concatenate([keys, values], 2), (1, 0, 2))

    q_in, kv_in = exchange(
        to_units_kernel, n, group, (q_out, kv_out),
        ((rounds, length // 2, PAIR), (n, length, PAIR)), 0,
    )
    kv_in = kv_in.reshape(tokens, PAIR)

    common_specs = [
        turn_spec((length // 2, PAIR)),
        whole_spec((tokens, PAIR)),
        whole_spec(table.shape),
        whole_spec(turn_sin.shape),
        whole_spec(turn_cos.shape),
        whole_spec(head_weight.shape),
        whole_spec((1, HEAD)),
        whole_spec((1, HEAD)),
    ]
    common = (q_in, kv_in, table, turn_sin, turn_cos, head_weight, head_cb, head_pb)
    attended, att_low, total, keep = pl.pallas_call(
        functools.partial(attend_kernel, n, group, tile),
        grid=(rounds,),
        in_specs=common_specs + [pl.BlockSpec(memory_space=pltpu.SMEM)],
        out_specs=[
            turn_spec((length, HEAD)),
            turn_spec((length // 2, PAIR)),
            turn_spec((length, 128)),
            turn_spec((length, tokens)),
        ],
        out_shape=[
            jax.ShapeDtypeStruct((rounds, length, HEAD), F32),
            jax.ShapeDtypeStruct((rounds, length // 2, PAIR), BF16),
            jax.ShapeDtypeStruct((rounds, length, 128), F32),
            jax.ShapeDtypeStruct((rounds, length, tokens), BF16),
        ],
        scratch_shapes=[
            pltpu.VMEM((length, tokens), F32),
            pltpu.VMEM((length, PAIR + width), BF16),
        ],
        compiler_params=pltpu.CompilerParams(vmem_limit_bytes=56 * 2**20),
    )(*common, bounds)

    (att_back,) = exchange(
        to_owners_kernel, n, group, (att_low,), ((HEADS, length // 2, PAIR),), 1
    )
    attended_low = heads_unpacked(att_back)

    mixed = pooled + dot(attended_low, out_weight)
    normed_two, plain_two, inverse_two = layer_norm(mixed, ln2_gain, ln2_bias)
    ffn_input = normed_two.astype(BF16)
    pre_act = dot(ffn_input, ffn_in) + ffn_in_bias
    activated, gelu_pull = jax.vjp(exact_gelu, pre_act)
    act_low = activated.astype(BF16)
    final = mixed + dot(act_low, ffn_out) + ffn_out_bias
    final_low = final.astype(BF16)
    upsampled = dot(final_low, up_weight) + up_bias
    outputs = (inputs.astype(F32) + upsampled.reshape(1, bytes_here, width)).astype(BF16)
    grad_up = cotangent.reshape(length, 3 * width)
    over_rows = ((0,), (0,))
    over_columns = ((1,), (1,))
    grad_up_weight = dot(final_low, grad_up, over_rows)
    grad_up_bias = jnp.sum(grad_up.astype(F32), axis=0)
    grad_final = dot(grad_up, up_weight, over_columns)
    grad_branch = grad_final.astype(BF16)
    grad_ffn_out = dot(act_low, grad_branch, over_rows)
    grad_ffn_out_bias = jnp.sum(grad_branch.astype(F32), axis=0)
    grad_act = dot(grad_branch, ffn_out, over_columns)
    grad_pre = gelu_pull(grad_act)[0].astype(BF16)
    grad_ffn_in = dot(ffn_input, grad_pre, over_rows)
    grad_ffn_in_bias = jnp.sum(grad_pre.astype(F32), axis=0)
    grad_normed_two = dot(grad_pre, ffn_in, over_columns)
    grad_from_two, grad_ln2_gain, grad_ln2_bias = norm_back(
        grad_normed_two, plain_two, inverse_two, ln2_gain
    )
    grad_mixed = grad_final + grad_from_two
    grad_attn_branch = grad_mixed.astype(BF16)
    grad_out_weight = dot(attended_low, grad_attn_branch, over_rows)
    grad_attended = dot(grad_attn_branch, out_weight, over_columns).astype(BF16)

    early = lax.psum(
        tuple(
            grad.astype(BF16) for grad in (grad_ffn_in, grad_ffn_out, grad_up_weight, grad_out_weight)
        ),
        ("dp", "seq"),
    )

    (grad_in,) = exchange(
        to_units_kernel, n, group, (heads_packed(grad_attended),), ((rounds, length // 2, PAIR),), 2
    )
    dq_out, dkv_out, grad_head_weight, grad_head_cb, grad_head_pb = pl.pallas_call(
        functools.partial(back_kernel, n, group, tile),
        grid=(rounds,),
        in_specs=common_specs
        + [
            turn_spec((length, HEAD)),
            turn_spec((length, 128)),
            turn_spec((length, tokens)),
            turn_spec((length // 2, PAIR)),
        ],
        out_specs=[
            turn_spec((length // 2, PAIR)),
            whole_spec((tokens, PAIR)),
            whole_spec((width, HEAD)),
            whole_spec((1, HEAD)),
            whole_spec((1, HEAD)),
        ],
        out_shape=[
            jax.ShapeDtypeStruct((rounds, length // 2, PAIR), BF16),
            jax.ShapeDtypeStruct((tokens, PAIR), BF16),
            jax.ShapeDtypeStruct((width, HEAD), F32),
            jax.ShapeDtypeStruct((1, HEAD), F32),
            jax.ShapeDtypeStruct((1, HEAD), F32),
        ],
        scratch_shapes=[pltpu.VMEM((tokens, PAIR), F32)],
        compiler_params=pltpu.CompilerParams(vmem_limit_bytes=56 * 2**20),
    )(*common, attended, total, keep, grad_in)
    dq_back, dkv_back = exchange(
        to_owners_kernel, n, group, (dq_out, dkv_out.reshape(n, length, PAIR)),
        ((HEADS, length // 2, PAIR), (group, HEADS, length, PAIR)), 3,
    )
    grad_query = heads_unpacked(dq_back)
    dkv_back = jnp.transpose(jnp.sum(dkv_back.astype(F32), 0), (1, 0, 2)).astype(BF16)
    grad_key_low = dkv_back[:, :, :HEAD].reshape(length, width)
    grad_value_low = dkv_back[:, :, HEAD:].reshape(length, width)

    def at_head(part, shape):
        return lax.dynamic_update_slice(
            jnp.zeros(shape, F32), part.reshape(shape[:-1] + (HEAD,)), (0,) * (len(shape) - 1) + (head * HEAD,)
        )

    grad_pos_weight = at_head(grad_head_weight, (width, width))
    grad_content_bias = at_head(grad_head_cb, (width,))
    grad_pos_bias = at_head(grad_head_pb, (width,))
    grad_query_weight = dot(attn_in, grad_query, over_rows)
    grad_key_weight = dot(attn_in, grad_key_low, over_rows)
    grad_value_weight = dot(attn_in, grad_value_low, over_rows)
    grad_normed_one = (
        dot(grad_query, query_weight, over_columns)
        + dot(grad_key_low, key_weight, over_columns)
        + dot(grad_value_low, value_weight, over_columns)
    )
    grad_from_one, grad_ln1_gain, grad_ln1_bias = norm_back(
        grad_normed_one, plain_one, inverse_one, ln1_gain
    )
    grad_pooled = (grad_mixed + grad_from_one).astype(BF16)
    grad_pool_weight = dot(pooled_in, grad_pooled, over_rows)
    grad_pool_bias = jnp.sum(grad_pooled.astype(F32), axis=0)
    grad_shifted = dot(grad_pooled, pool_weight, over_columns).reshape(1, bytes_here, width)
    incoming = passed_along(grad_shifted[:, :2, :], "seq", -1)
    input_grad = (
        cotangent.astype(F32) + jnp.concatenate([grad_shifted[:, 2:, :], incoming], 1)
    ).astype(BF16)
    late = lax.psum(
        tuple(
            grad.astype(BF16)
            for grad in (
                grad_pool_weight, grad_query_weight, grad_key_weight, grad_value_weight, grad_pos_weight,
            )
        ),
        ("dp", "seq"),
    )
    small_parts = (
        grad_pool_bias, grad_ln1_gain, grad_ln1_bias, grad_content_bias, grad_pos_bias,
        grad_ln2_gain, grad_ln2_bias, grad_ffn_in_bias, grad_ffn_out_bias, grad_up_bias,
    )
    small = lax.psum(jnp.concatenate(small_parts), ("dp", "seq"))
    cuts = np.cumsum([part.shape[0] for part in small_parts])[:-1].tolist()
    (
        sum_pool_bias, sum_ln1_gain, sum_ln1_bias, sum_content, sum_pos,
        sum_ln2_gain, sum_ln2_bias, sum_in_bias, sum_out_bias, sum_up_bias,
    ) = jnp.split(small, cuts)
    sum_in, sum_out, sum_up, sum_mix = (grad.astype(F32) for grad in early)
    sum_pool, sum_q, sum_k, sum_v, sum_p = (grad.astype(F32) for grad in late)
    return (
        outputs, input_grad, sum_pool, sum_pool_bias, sum_ln1_gain, sum_ln1_bias, sum_q, sum_k, sum_v,
        sum_mix, sum_p, sum_content, sum_pos, sum_ln2_gain, sum_ln2_bias, sum_in, sum_in_bias,
        sum_out, sum_out_bias, sum_up, sum_up_bias,
    )


EARLY_ROWS, LATE_ROWS = 6144, 3584
EARLY_CHUNKS = ((0, 2048, False), (2048, 2048, True), (4096, 2048, False))
LATE_CHUNKS = ((3072, 512, False), (1536, 1024, False), (2560, 512, True), (0, 1024, False), (1024, 512, True))
QKV_SUMS, POOL_SUMS = slice(4, 6), slice(6, None)
SMALL_ROWS = 16
TILE = 768
OVER_ROWS = ((0,), (0,))
OVER_COLUMNS = ((1,), (1,))


class Reduction:
    def __init__(self, buffer, start, rows, by_z, bufs, sems, free, small=None):
        self.buffer, self.sems, self.free, self.small = buffer, sems, free, small
        core, chip = lax.axis_index("dp"), lax.axis_index("seq")
        self.core, self.chip = core, chip
        x, y, z = chip % 2, (chip // 2) % 2, chip // 4
        first_x = core == 0
        self.peer_x, self.peer_y = (core, chip + 1 - 2 * x), (core, chip + 2 - 4 * y)
        self.z_peers = [(core, chip + ((z + away) % 4 - z) * 4) for away in (1, 2, 3)]
        self.z = z

        def pair(bit, peer_core, peer_chip):
            return (bit, [(1 - bit, peer_core, peer_chip)])

        one = pair(jnp.where(first_x, x, y), core, jnp.where(first_x, self.peer_x[1], self.peer_y[1]))
        two = pair(jnp.where(first_x, y, x), core, jnp.where(first_x, self.peer_y[1], self.peer_x[1]))
        stages = [pair(core, 1 - core, chip)]
        if by_z:
            low, high = z % 2, z // 2
            stages += [pair(low, core, chip + 4 - 8 * low), one, two, pair(high, core, chip + 8 - 16 * high)]
        else:
            stages += [one, two, (z, [((z + away) % 4, core, self.z_peers[away - 1][1]) for away in (1, 2, 3)])]
        self.stages = []
        at, size, first = start, rows, 0
        for buf, (own, others) in zip(bufs, stages):
            ways = len(others) + 1
            self.stages.append((at, size, size // ways, own, others, buf, first))
            at, size, first = at + own * (size // ways), size // ways, first + len(others)
        self.back = first
        self.last = 2 * len(stages)

    def rows(self, start, size):
        return self.buffer.at[pl.ds(pl.multiple_of(start, 16), size)]

    def copy(self, index, source, target, core, chip):
        return pltpu.make_async_remote_copy(
            source, target, self.sems.at[0, index], self.sems.at[1, index],
            device_id=(core, chip), device_id_type=MESH,
        )

    def done(self, index, source):
        copy = self.copy(index, source, source, 1 - self.core, self.chip)
        copy.wait_send()
        copy.wait_recv()

    def add(self, start, size, part_start, buf):
        chunk = min(size, 128)
        while size % chunk:
            chunk -= 16

        def one(step, carry):
            at = pl.ds(pl.multiple_of(start + step * chunk, 16), chunk)
            here = pl.ds(pl.multiple_of(part_start + step * chunk, 16), chunk)
            total = self.buffer[at].astype(F32)
            for part in range(buf.shape[0]):
                total = total + buf[part, here].astype(F32)
            self.buffer[at] = total.astype(BF16)
            return carry

        lax.fori_loop(0, size // chunk, one, 0)

    def send_parts(self, number):
        at, _, part, _, others, buf, first = self.stages[number]
        for place, (other, core, chip) in enumerate(others):
            self.copy(first + place, self.rows(at + other * part, part), buf.at[place], core, chip).start()

    def send_back(self, number):
        at, _, part, own, others, _, first = self.stages[number]
        pl.semaphore_wait(self.free.at[number], len(others))
        mine = self.rows(at + own * part, part)
        for place, (_, core, chip) in enumerate(others):
            self.copy(self.back + first + place, mine, mine, core, chip).start()

    def step(self, number):
        count = len(self.stages)
        if number == 0:
            self.send_parts(0)
        elif number <= count:
            at, _, part, own, others, buf, first = self.stages[number - 1]
            for place, (_, core, chip) in enumerate(others):
                self.done(first + place, buf.at[place])
            for _, core, chip in others:
                pl.semaphore_signal(self.free.at[number - 1], inc=1, device_id=(core, chip), device_id_type=MESH)
            kept = at + own * part
            if number < count:
                _, _, next_part, next_own, next_others, _, _ = self.stages[number]
                for other, _, _ in next_others:
                    self.add(kept + other * next_part, next_part, other * next_part, buf)
                self.send_parts(number)
                self.add(kept + next_own * next_part, next_part, next_own * next_part, buf)
            else:
                self.add(kept, part, 0, buf)
                self.send_back(count - 1)
        else:
            stage = 2 * count - number
            at, _, part, own, others, _, first = self.stages[stage]
            for place in range(len(others)):
                self.done(self.back + first + place, self.rows(at + own * part, part))
            if stage > 0:
                self.send_back(stage - 1)
        if self.small is not None:
            self.small_step(number)

    def small_step(self, number):
        own, taken = self.small
        first = 2 * self.back
        if number in (1, 2, 3):
            self.done(first + number - 1, own)
            own[...] = own[...] + taken[number - 1]
        if number < 3:
            core, chip = ((1 - self.core, self.chip), self.peer_x, self.peer_y)[number]
            self.copy(first + number, own, taken.at[number], core, chip).start()
        if number == 3:
            taken[3 + self.z] = own[...]
            for place, (core, chip) in enumerate(self.z_peers):
                self.copy(first + 3 + place, own, taken.at[3 + self.z], core, chip).start()
        if number == 4:
            for place in range(3):
                self.done(first + 3 + place, own)
            own[...] = (taken[3] + taken[4]) + (taken[5] + taken[6])


REDUCTION_SEMS = 18


def reduction_scratch(rows, by_z):
    shapes = [(1, rows // 2), (1, rows // 4), (1, rows // 8)]
    shapes += [(1, rows // 16), (1, rows // 32)] if by_z else [(3, rows // 32)]
    return [pltpu.VMEM(shape + (512,), BF16) for shape in shapes]


def gelu_pair(value):
    falling = jnp.exp(value * value * -0.5)
    turn = 1.0 / (1.0 + 0.3275911 * 0.7071067811865476 * jnp.abs(value))
    series = turn * (
        0.254829592
        + turn * (-0.284496736 + turn * (1.421413741 + turn * (-1.453152027 + turn * 1.061405429)))
    )
    tail = 0.5 * series * falling
    share = jnp.where(value >= 0, 1.0 - tail, tail)
    return value * share, share + value * falling * 0.3989422804014327


def norm_parts(hidden):
    average = jnp.mean(hidden, -1, keepdims=True)
    centred = hidden - average
    inverse = lax.rsqrt(jnp.mean(centred * centred, -1, keepdims=True) + epsilon)
    return centred * inverse, inverse


def norm_grad(grad_out, normed, inverse, gain):
    scaled = grad_out * gain
    return inverse * (
        scaled
        - jnp.mean(scaled, -1, keepdims=True)
        - normed * jnp.mean(scaled * normed, -1, keepdims=True)
    )


def column_sum(value):
    return jnp.sum(value, 0, keepdims=True)


def most_tiles(turn, length):
    return ((2 * turn + 2) * length + TILE - 1) // TILE


def layer_kernel(n, length, layout, *refs):
    taken = iter(refs)
    given, vectors, outs, scratch = ({name: next(taken) for name in part} for part in layout)
    r = types.SimpleNamespace(**vectors, **outs, **scratch)
    group = 2
    rounds = n // group
    tile = TILE
    width = 512
    scale = HEAD**-0.5
    core, chip, row, head, member = whereabouts(group)
    count = 2 * n
    me = core * n + chip

    loads = {}
    chunk_refs = list(refs[len(refs) - sum(5 if cut[2] else 4 for cut in EARLY_CHUNKS + LATE_CHUNKS) :])

    def reduction(buffer, index, cut, small=None):
        bufs = [chunk_refs.pop(0) for _ in range(5 if cut[2] else 4)]
        return Reduction(buffer, *cut, bufs, r.sum_sem.at[index], r.sum_free.at[index], small)

    for index, (name, source) in enumerate(given.items()):
        loads[name] = pltpu.make_async_copy(source, scratch[name], r.load_sem.at[index])
        loads[name].start()

    def ready(*which):
        for ref in which:
            next(loads[name] for name in given if scratch[name] is ref).wait()

    r.up_b[...] = r.up_flat[...].reshape(1, 3 * width)

    barrier = pltpu.get_barrier_semaphore()

    def greet(step, carry):
        other = (me + step) % count
        pl.semaphore_signal(barrier, inc=1, device_id=(other // n, other % n), device_id_type=MESH)
        return carry

    lax.fori_loop(1, count, greet, 0)

    low_bound, high_bound = r.bounds[0, 0], r.bounds[0, 1]
    r.edges[core, :8] = jnp.full((8, 128), low_bound, jnp.int32)
    r.edges[core, 8:] = jnp.full((8, 128), high_bound, jnp.int32)

    def tokens_of(source, target):
        for block in range(width // 128):
            r.mixing[block] = source[:, block * 128 : (block + 1) * 128].astype(F32)
            for part in range(3):
                every = r.mixing[block, pl.ds(part, length, stride=3), :]
                start = part * width + block * 128
                target[:, start : start + 128] = every.astype(BF16)

    ready(r.x_bytes, r.pool_w)
    tokens_of(r.x_bytes, r.x3)
    own = dot(r.x3[:, :width], r.pool_w[2 * width :])
    before = dot(r.x3[:, width:], r.pool_w[: 2 * width])
    pl.semaphore_wait(barrier, count - 1)

    def edge_copy():
        return pltpu.make_async_remote_copy(
            r.edges.at[core], r.edges.at[core], r.side_sem.at[0], r.side_sem.at[1],
            device_id=(1 - core, chip), device_id_type=MESH,
        )

    def rim_copy():
        return pltpu.make_async_remote_copy(
            r.x3.at[length - 16 :, width:], r.rim, r.side_sem.at[2], r.side_sem.at[3],
            device_id=(core, (chip + 1) % n), device_id_type=MESH,
        )

    edge_copy().start()

    @pl.when(chip < n - 1)
    def _():
        rim_copy().start()

    @pl.when(chip == 0)
    def _():
        r.rim[...] = jnp.zeros_like(r.rim)

    @pl.when(chip > 0)
    def _():
        rim_copy().wait_recv()

    rim_sum = dot(r.rim[...], r.pool_w[: 2 * width])
    at_row = lax.broadcasted_iota(jnp.int32, (length, width), 0)
    before = jnp.where(at_row == 0, rim_sum[15:16], pltpu.roll(before, 1, 0))
    pooled = own + before + r.pool_b[...]
    r.pooled[...] = pooled
    plain, _ = norm_parts(pooled)
    attn_in = (plain * r.ln1_g[...] + r.ln1_b[...]).astype(BF16)
    r.attn_in[...] = attn_in
    ready(r.q_w, r.k_w, r.v_w)
    query = dot(attn_in, r.q_w[...])
    keys = dot(attn_in, r.k_w[...])
    values = dot(attn_in, r.v_w[...])
    for h in range(HEADS):
        at = slice(h * HEAD, (h + 1) * HEAD)
        r.q_out[h] = packed(query[:, at]).astype(BF16)
        r.kv_out[h] = jnp.concatenate([keys[:, at], values[:, at]], 1).astype(BF16)
    turn_to, spot_to = place_of(chip, group)

    def q_jobs(array, out, sem, recv):
        jobs = []
        for h in range(HEADS):
            to_chip, to_core = chip_of(core, h, spot_to, group)
            jobs.append((array.at[h], out.at[turn_to], (sem, recv.at[turn_to]), to_core, to_chip))
        return jobs

    def rows_in(block):
        return pl.ds(pl.multiple_of(block * length, length), length)

    kv_jobs = []
    for h in range(HEADS):
        to_chip, _ = chip_of(core, h, 0, group)
        sems = (r.send_sem.at[1], r.kv_sem.at[chip])
        kv_jobs.append((r.kv_out.at[h], r.kv.at[rows_in(chip)], sems, chip % 2, to_chip))
    query_jobs = q_jobs(r.q_out, r.q, r.send_sem.at[0], r.q_sem)
    for job in kv_jobs + query_jobs:
        send(*job)

    ready(r.ct_bytes, r.up_w, r.ffn_out)
    tokens_of(r.ct_bytes, r.ct3)
    grad_final = dot(r.ct3[...], r.up_w[...], OVER_COLUMNS)
    r.grad_final[...] = grad_final
    first_jobs = kv_jobs + query_jobs
    grad_branch = grad_final.astype(BF16)
    r.grad_branch[...] = grad_branch
    for part in range(4):
        at = slice(part * width, (part + 1) * width)
        r.grad_act[:, at] = dot(grad_branch, r.ffn_out[at], OVER_COLUMNS)
    small = r.small
    small[...] = jnp.zeros_like(small)
    small[11:12] = column_sum(grad_branch.astype(F32))
    for part in range(3):
        at = slice(part * width, (part + 1) * width)
        small[12 + part : 13 + part] = column_sum(r.ct3[:, at].astype(F32))

    ready(r.pos_w, r.table)
    odd = head % 2 == 1
    pair_at = pl.ds(pl.multiple_of((head // 2) * PAIR, PAIR), PAIR)

    def of_head(ref):
        both = ref[:, pair_at].astype(F32)
        return jnp.where(odd, both[:, HEAD:], both[:, :HEAD])

    r.head_w[...] = of_head(r.pos_w).astype(BF16)
    content_bias, pos_bias = of_head(r.content), of_head(r.pos)
    edge_copy().wait_send()
    edge_copy().wait_recv()
    low_edge = r.edges[row, 0:1, 0:1]
    high_edge = r.edges[row, 8:9, 0:1]
    half = width // 2
    lanes = lax.broadcasted_iota(jnp.int32, (length, tile), 1)

    def rows_of(start):
        return pl.ds(pl.multiple_of(start, 64), tile)

    def tiles_to(block):
        return ((block + 1) * length + tile - 1) // tile

    def kept_at(turn):
        return sum(jnp.where(turn > before, most_tiles(before, length), 0) for before in range(rounds - 1))

    def forward(turn):
        at = turn * group + core
        return pltpu.make_async_remote_copy(
            r.kv.at[rows_in(at)], r.kv.at[rows_in(at)], r.send_sem.at[6], r.kv_sem.at[at], device_id=(1 - core, chip), device_id_type=MESH
        )

    def pass_on(turn):
        at = turn * group + core
        arrived(r.kv.at[rows_in(at)], r.kv_sem.at[at])
        forward(turn).start()

    def met(turn):
        other = turn * group + 1 - core
        arrived(r.kv.at[rows_in(other)], r.kv_sem.at[other])

    rising = row == 0
    pass_on(0)
    pass_on(1)

    @pl.when(jnp.logical_not(rising))
    def _():
        lax.fori_loop(2, rounds, lambda turn, carry: (pass_on(turn), carry)[1], 0)

    met(0)

    @pl.when(jnp.logical_not(rising))
    def _():
        lax.fori_loop(1, rounds, lambda turn, carry: (met(turn), carry)[1], 0)

    def attend(index, carry):
        turn = jnp.where(rising, index, rounds - 1 - index)
        block = block_of(turn, member, group)

        @pl.when(jnp.logical_and(rising, index < rounds - 2))
        def _():
            pass_on(index + 2)

        @pl.when(jnp.logical_and(rising, index < rounds - 1))
        def _():
            met(index + 1)

        arrived(r.q.at[turn], r.q_sem.at[turn])
        query_u, _, turned = query_parts(
            r.q[turn], content_bias, pos_bias, r.head_w[...], r.sines[...], r.cosines[...]
        )
        head_part = (query_u.astype(F32) * scale).astype(BF16)
        r.extra[:, :PAIR] = jnp.concatenate([head_part, jnp.zeros_like(head_part)], 1)
        r.extra[:, PAIR:] = (turned * scale).astype(BF16)
        places = block * length + lax.broadcasted_iota(jnp.int32, (length, 1), 0)
        opening = jnp.where(places >= high_edge, high_edge, jnp.where(places >= low_edge, low_edge, 0))

        def score_step(step, top):
            pair = r.kv[rows_of(step * tile), :]
            waves = r.table[rows_of((n - 1 - block) * length + step * tile), :]
            score = dot(r.extra[:, :PAIR], pair, OVER_COLUMNS) + dot(r.extra[:, PAIR:], waves, OVER_COLUMNS)
            at = lanes + step * tile
            allowed = jnp.logical_and(at <= places, at >= opening)
            score = jnp.where(allowed, score, masked_score)
            r.score[step] = score
            for part in range(tile // 128):
                top = jnp.maximum(top, score[:, part * 128 : (part + 1) * 128])
            return top

        kept, tiles = kept_at(turn), tiles_to(block)
        top = lax.fori_loop(0, tiles, score_step, jnp.full((length, 128), masked_score, F32))
        top = jnp.max(top, 1, keepdims=True)

        def value_step(step, state):
            total, summed = state
            weight = jnp.exp(r.score[step] - top)
            for part in range(tile // 128):
                total = total + weight[:, part * 128 : (part + 1) * 128]
            low = weight.astype(BF16)
            r.keep[kept + step] = low
            pair = r.kv[rows_of(step * tile), :]
            return total, summed + dot(low, pair)

        total, summed = lax.fori_loop(
            0, tiles, value_step, (jnp.zeros((length, 128), F32), jnp.zeros((length, PAIR), F32))
        )
        inverse = 1.0 / jnp.sum(total, 1, keepdims=True)
        attended = summed[:, HEAD:] * inverse
        r.att[turn] = jnp.concatenate([jnp.broadcast_to(inverse, (length, HEAD)), attended], 1)
        r.att_out[turn] = packed(attended).astype(BF16)
        send(
            r.att_out.at[turn], r.att_in.at[head], (r.send_sem.at[2], r.att_sem.at[0]), row, block
        )
        return carry

    lax.fori_loop(0, rounds, attend, 0)
    for source, _, sems, to_core, to_chip in first_jobs:
        sent(source, sems[0], to_core, to_chip)
    for turn in range(rounds):
        forward(turn).wait_send()

    def joined(get):
        parts = [get(h) for h in range(HEADS)]
        upper = jnp.concatenate([part[:, :HEAD] for part in parts], 1)
        lower = jnp.concatenate([part[:, HEAD:] for part in parts], 1)
        return jnp.concatenate([upper, lower], 0)

    arrived(r.att_in, r.att_sem.at[0])
    ready(r.out_w, r.ffn_in)
    att_low = joined(lambda h: r.att_in[h].astype(F32)).astype(BF16)
    r.att_low[...] = att_low
    mixed = r.pooled[...] + dot(att_low, r.out_w[...])
    r.mixed[...] = mixed
    plain_two, inverse_two = norm_parts(mixed)
    ffn_input = (plain_two * r.ln2_g[...] + r.ln2_b[...]).astype(BF16)
    r.ffn_input[...] = ffn_input
    grad_normed = jnp.zeros((length, width), F32)
    for part in range(4):
        at = slice(part * width, (part + 1) * width)
        pre_act = dot(ffn_input, r.ffn_in[:, at]) + r.ffn_in_b[:, at]
        act, slope = gelu_pair(pre_act)
        r.act_low[:, at] = act.astype(BF16)
        grad_pre = (r.grad_act[:, at] * slope).astype(BF16)
        r.grad_pre[:, at] = grad_pre
        small[7 + part : 8 + part] = column_sum(grad_pre.astype(F32))
        grad_normed = grad_normed + dot(grad_pre, r.ffn_in[:, at], OVER_COLUMNS)
    small[5:6] = column_sum(grad_normed * plain_two)
    small[6:7] = column_sum(grad_normed)
    grad_mixed = r.grad_final[...] + norm_grad(grad_normed, plain_two, inverse_two, r.ln2_g[...])
    r.grad_final[...] = grad_mixed
    grad_mixed_low = grad_mixed.astype(BF16)
    grad_att = dot(grad_mixed_low, r.out_w[...], OVER_COLUMNS)
    for h in range(HEADS):
        r.q_out[h] = packed(grad_att[:, h * HEAD : (h + 1) * HEAD]).astype(BF16)
    second_jobs = q_jobs(r.q_out, r.grad, r.send_sem.at[3], r.grad_sem)
    for job in second_jobs:
        send(*job)

    early, late = r.early, r.late
    count_early, count_late = len(EARLY_CHUNKS), len(LATE_CHUNKS)
    sums = [reduction(early, index, cut) for index, cut in enumerate(EARLY_CHUNKS)]
    for index, cut in enumerate(LATE_CHUNKS):
        small_pair = (small, r.small_in) if index == count_late - 1 else None
        sums.append(reduction(late, count_early + index, cut, small_pair))

    def leave(index):
        cut = (EARLY_CHUNKS + LATE_CHUNKS)[index]
        buffer, target = (early, r.early_o) if index < count_early else (late, r.late_o)
        at = pl.ds(cut[0], cut[1])
        return pltpu.make_async_copy(buffer.at[at], target.at[at], r.leave_sem.at[index])

    def steps_at(moment):
        for index, number in SCHEDULE.get(moment, ()):
            sums[index].step(number)
            if number == sums[index].last:
                leave(index).start()

    for part in range(4):
        at = slice(part * width, (part + 1) * width)
        early[at] = dot(r.ffn_input[...], r.grad_pre[:, at], OVER_ROWS).astype(BF16)
    sums[0].step(0)
    steps_at(-4)
    for part in range(4):
        at = slice(part * width, (part + 1) * width)
        early[2048 + part * width : 2048 + (part + 1) * width] = dot(
            r.act_low[:, at], r.grad_branch[...], OVER_ROWS
        ).astype(BF16)
    sums[1].step(0)
    steps_at(-3)
    early[5632:] = dot(r.att_low[...], grad_mixed_low, OVER_ROWS).astype(BF16)
    final_low = (r.mixed[...] + dot(r.act_low[...], r.ffn_out[...]) + r.ffn_out_b[...]).astype(BF16)
    for part in range(3):
        at = slice(part * width, (part + 1) * width)
        early[4096 + part * width : 4096 + (part + 1) * width] = dot(final_low, r.ct3[:, at], OVER_ROWS).astype(BF16)
    sums[2].step(0)
    steps_at(-2)
    for part in range(3):
        at = slice(part * width, (part + 1) * width)
        lifted = dot(final_low, r.up_w[:, at]) + r.up_b[:, at]
        r.out3[:, at] = (r.x3[:, at].astype(F32) + lifted).astype(BF16)

    steps_at(-1)

    r.dkv[...] = jnp.zeros_like(r.dkv)
    r.dhead[...] = jnp.zeros_like(r.dhead)
    r.dbias[...] = jnp.zeros_like(r.dbias)

    def give_over(turn):
        return pltpu.make_async_remote_copy(
            r.dkv_out.at[turn * group + 1 - core], r.dkv_other.at[turn], r.send_sem.at[7], r.other_sem.at[turn],
            device_id=(1 - core, chip), device_id_type=MESH,
        )

    def hand_in(turn):
        at = turn * group + core
        give_over(turn).wait_recv()
        total = r.dkv[pl.ds(pl.multiple_of(at * length, length), length)] + r.dkv_other[turn].astype(F32)
        r.dkv_out[at] = total.astype(BF16)
        send(r.dkv_out.at[at], r.dkv_in.at[head], (r.send_sem.at[4], r.dkv_sem.at[0]), row, at)

    def back(index, carry):
        turn = rounds - 1 - index
        block = block_of(turn, member, group)
        arrived(r.grad.at[turn], r.grad_sem.at[turn])
        query = unpacked(r.q[turn].astype(F32))
        query_u = ((query + content_bias).astype(BF16).astype(F32) * scale).astype(BF16)
        query_v = (query + pos_bias).astype(BF16)
        grad = unpacked(r.grad[turn].astype(F32))
        inverse = r.att[turn][:, :HEAD]
        grad_part = grad * inverse
        delta = jnp.sum(grad_part * r.att[turn][:, HEAD:], 1, keepdims=True)
        nothing = jnp.zeros((length, HEAD), F32)
        r.extra[:, :PAIR] = jnp.concatenate([nothing, grad_part], 1).astype(BF16)
        r.extra[:, PAIR : 2 * PAIR] = jnp.concatenate([query_u.astype(F32), nothing], 1).astype(BF16)
        r.near[...] = jnp.zeros_like(r.near)
        r.far[...] = jnp.zeros_like(r.far)

        def step_over(step, inner):
            pair = r.kv[rows_of(step * tile), :]
            waves = r.table[rows_of((n - 1 - block) * length + step * tile), :]
            weight = r.keep[kept + step]
            grad_weight = dot(r.extra[:, :PAIR], pair, OVER_COLUMNS)
            grad_score = (weight.astype(F32) * (grad_weight - delta)).astype(BF16)
            r.near[...] += dot(grad_score, pair)
            r.far[...] += dot(grad_score, waves)
            at = pl.ds(pl.multiple_of(step * tile, tile), tile)
            r.dkv[at] += dot(grad_score, r.extra[:, PAIR : 2 * PAIR], OVER_ROWS) + dot(
                weight, r.extra[:, :PAIR], OVER_ROWS
            )
            return inner

        kept = kept_at(turn)
        lax.fori_loop(0, tiles_to(block), step_over, 0)
        give = turn * group + 1 - core
        r.dkv_out[give] = r.dkv[pl.ds(pl.multiple_of(give * length, length), length)].astype(BF16)
        give_over(turn).start()

        @pl.when(index > 0)
        def _():
            hand_in(turn + 1)

        grad_u = r.near[:, :HEAD] * scale
        turn_sin, turn_cos = r.sines[...], r.cosines[...]
        on_sin, on_cos = r.far[:, :half] * scale, r.far[:, half:] * scale
        lift = on_cos * turn_sin - on_sin * turn_cos
        rest = on_cos * turn_cos + on_sin * turn_sin
        spread = jnp.concatenate([lift, rest], 1).astype(BF16)
        grad_v = dot(spread, r.head_w[...])
        r.dhead[...] += dot(spread, query_v, OVER_ROWS)
        r.dbias[0:1] += column_sum(grad_u)
        r.dbias[1:2] += column_sum(grad_v)
        r.dq_out[turn] = packed(grad_u + grad_v).astype(BF16)
        send(r.dq_out.at[turn], r.dq_in.at[head], (r.send_sem.at[5], r.dq_sem.at[0]), row, block)
        for when in range(rounds):
            if when in SCHEDULE:

                @pl.when(index == when)
                def _(when=when):
                    steps_at(when)

        return carry

    lax.fori_loop(0, rounds, back, 0)
    hand_in(0)

    late[2048 + 1024 :] = jnp.zeros((512, 512), BF16)
    dhead = r.dhead[...]
    nothing = jnp.zeros_like(dhead)
    late[3072:, pair_at] = jnp.where(
        odd, jnp.concatenate([nothing, dhead], 1), jnp.concatenate([dhead, nothing], 1)
    ).astype(BF16)
    nothing = jnp.zeros((2, HEAD), F32)
    dbias = r.dbias[...][:2]
    small[3:5, pair_at] = jnp.where(
        odd, jnp.concatenate([nothing, dbias], 1), jnp.concatenate([dbias, nothing], 1)
    )
    sums[3].step(0)
    steps_at(8)
    for source, _, sems, to_core, to_chip in second_jobs:
        sent(source, sems[0], to_core, to_chip)
    for turn in range(rounds):
        block = block_of(jnp.int32(turn), member, group)
        sent(r.att_out.at[turn], r.send_sem.at[2], row, block)
        sent(r.dq_out.at[turn], r.send_sem.at[5], row, block)
    for turn in range(rounds):
        sent(r.dkv_out.at[turn * group + core], r.send_sem.at[4], row, turn * group + core)
        give_over(turn).wait_send()
    arrived(r.dq_in, r.dq_sem.at[0])
    arrived(r.dkv_in, r.dkv_sem.at[0])
    grad_query = joined(lambda h: r.dq_in[h].astype(F32)).astype(BF16)
    both = [r.dkv_in[h].astype(F32) for h in range(HEADS)]
    grad_keys = jnp.concatenate([part[:, :HEAD] for part in both], 1).astype(BF16)
    grad_values = jnp.concatenate([part[:, HEAD:] for part in both], 1).astype(BF16)
    steps_at(9)
    attn_in = r.attn_in[...]
    grad_normed = (
        dot(grad_query, r.q_w[...], OVER_COLUMNS)
        + dot(grad_keys, r.k_w[...], OVER_COLUMNS)
        + dot(grad_values, r.v_w[...], OVER_COLUMNS)
    )
    plain, inverse = norm_parts(r.pooled[...])
    small[1:2] = column_sum(grad_normed * plain)
    small[2:3] = column_sum(grad_normed)
    grad_pooled = (r.grad_final[...] + norm_grad(grad_normed, plain, inverse, r.ln1_g[...])).astype(BF16)
    r.grad_pooled[...] = grad_pooled
    grad_pooled_wide = grad_pooled.astype(F32)
    steps_at(10)
    small[0:1] = column_sum(grad_pooled_wide)

    def back_rim_copy():
        return pltpu.make_async_remote_copy(
            r.grad_pooled.at[:16], r.back_rim, r.side_sem.at[4], r.side_sem.at[5],
            device_id=(core, (chip + n - 1) % n), device_id_type=MESH,
        )

    @pl.when(chip > 0)
    def _():
        back_rim_copy().start()

    late[1024:1536] = dot(r.x3[:, :width], grad_pooled, OVER_ROWS).astype(BF16)
    follow = pltpu.roll(grad_pooled_wide, length - 1, 0)
    within = jnp.where(at_row == length - 1, 0.0, follow).astype(BF16)
    at_rim = lax.broadcasted_iota(jnp.int32, (16, width), 0)
    rim_row = jnp.where(at_rim == 15, jnp.broadcast_to(grad_pooled_wide[:1], (16, width)), 0.0).astype(BF16)
    late[:1024] = (
        dot(r.x3[:, width:], within, OVER_ROWS) + dot(r.rim[...], rim_row, OVER_ROWS)
    ).astype(BF16)
    for later in sums[POOL_SUMS]:
        later.step(0)
    steps_at(11)
    late[1536:2048] = dot(attn_in, grad_query, OVER_ROWS).astype(BF16)
    late[2048:2560] = dot(attn_in, grad_keys, OVER_ROWS).astype(BF16)
    late[2560:3072] = dot(attn_in, grad_values, OVER_ROWS).astype(BF16)
    for later in sums[QKV_SUMS]:
        later.step(0)
    steps_at(12)

    @pl.when(chip == n - 1)
    def _():
        r.back_rim[...] = jnp.zeros_like(r.back_rim)

    @pl.when(chip < n - 1)
    def _():
        back_rim_copy().wait_recv()

    next_row = r.back_rim[...].astype(F32)[:1]
    follow = jnp.where(at_row == length - 1, next_row, follow).astype(BF16)
    first_part = r.ct3[:, :width].astype(F32) + dot(grad_pooled, r.pool_w[2 * width :], OVER_COLUMNS)
    r.grad3[:, :width] = first_part.astype(BF16)
    other_part = r.ct3[:, width:].astype(F32) + dot(follow, r.pool_w[: 2 * width], OVER_COLUMNS)
    r.grad3[:, width:] = other_part.astype(BF16)

    @pl.when(chip < n - 1)
    def _():
        rim_copy().wait_send()

    @pl.when(chip > 0)
    def _():
        back_rim_copy().wait_send()

    steps_at(13)
    for index in range(len(sums)):
        leave(index).wait()


SCHEDULE = {
    -2: ((1, 1),),
    -1: ((0, 1),),
    1: ((0, 2),),
    2: ((1, 2), (2, 1), (0, 3),),
    8: ((2, 2), (1, 3), (0, 4), (3, 1),),
    10: ((1, 4),),
    11: ((2, 3),),
    12: ((3, 2), (0, 5), (7, 1), (4, 1), (3, 3), (1, 5), (5, 1), (6, 1),),
    13: (
        (7, 2), (2, 4), (4, 2), (1, 6), (6, 2), (3, 4), (5, 2), (7, 3), (0, 6), (4, 3), (1, 7), (5, 3), (6, 3),
        (2, 5), (3, 5), (5, 4), (7, 4), (4, 4), (5, 5), (6, 4), (7, 5), (1, 8), (3, 6), (2, 6), (5, 6), (7, 6),
        (4, 5), (0, 7), (7, 7), (3, 7), (6, 5), (0, 8), (5, 7), (3, 8), (7, 8), (4, 6), (6, 6), (5, 8), (1, 9),
        (2, 7), (7, 9), (4, 7), (5, 9), (1, 10), (6, 7), (7, 10), (4, 8), (2, 8), (5, 10), (6, 8),
    ),
}


WIDENED = (
    (0, 4, True), (2048, 4, False), (4096, 3, True), (5632, 1, False),
    (0, 3, False), (1536, 1, False), (2048, 1, False), (2560, 1, False), (3072, 1, False),
)
NARROW = ((0, 1), (1, 1), (2, 1), (3, 1), (4, 1), (5, 1), (6, 1), (7, 4), (11, 1), (12, 3))


def last_kernel(*refs):
    early, late, out3, grad3, small = refs[:5]
    wide_outs, narrow_outs, byte_outs = refs[5:14], refs[14:24], refs[24:26]
    loaded, staging, mixing, bytes_low, load_sems, sems = refs[26:]
    blocks = []
    for index, (out, (start, count, across)) in enumerate(zip(wide_outs, WIDENED)):
        for block in range(count):
            first = start + block * 512
            at = slice(block * 512, (block + 1) * 512)
            source = (early if index < 4 else late).at[first : first + 512]
            blocks.append((source, out.at[:, at] if across else out.at[at]))
    loads = [
        pltpu.make_async_copy(source, loaded.at[slot], load_sems.at[slot]) for slot, (source, _) in enumerate(blocks)
    ]
    stores = [
        pltpu.make_async_copy(staging.at[slot], target, sems.at[slot]) for slot, (_, target) in enumerate(blocks)
    ]
    for load in loads:
        load.start()
    for out, (start, count) in zip(narrow_outs, NARROW):
        if count == 3:
            out[...] = jnp.concatenate([small[start + block : start + block + 1] for block in range(count)], 1).reshape(-1)
        else:
            for block in range(count):
                out[:, block * 512 : (block + 1) * 512] = small[start + block : start + block + 1]

    def widen(slot):
        loads[slot].wait()

        def rows(step, carry):
            here = pl.ds(pl.multiple_of(step * 128, 128), 128)
            staging[slot, here] = loaded[slot, here].astype(F32)
            return carry

        lax.fori_loop(0, 4, rows, 0)
        stores[slot].start()

    some = len(blocks) // 2
    for slot in range(some):
        widen(slot)
    for index, (out, tokens) in enumerate(zip(byte_outs, (out3, grad3))):
        length, width = out.shape[0] // 3, out.shape[1]
        for block in range(width // 128):
            for part in range(3):
                start = part * width + block * 128
                mixing[block, pl.ds(part, length, stride=3), :] = tokens[:, start : start + 128].astype(F32)
            bytes_low[index, :, block * 128 : (block + 1) * 128] = mixing[block].astype(BF16)
        store = pltpu.make_async_copy(bytes_low.at[index], out, sems.at[len(blocks) + index])
        store.start()
        stores.append(store)
    for slot in range(some, len(blocks)):
        widen(slot)
    for store in stores:
        store.wait()


def finished(early, late, out3, grad3, small):
    length, width = out3.shape[0], out3.shape[1] // 3
    vmem = pl.BlockSpec(memory_space=pltpu.VMEM)
    shapes = [(512, 512 * blocks) if across else (512 * blocks, 512) for _, blocks, across in WIDENED]
    narrow = [(512 * blocks,) if blocks == 3 else (1, 512 * blocks) for _, blocks in NARROW]
    count = sum(blocks for _, blocks, _ in WIDENED)
    outs = pl.pallas_call(
        last_kernel,
        in_specs=[pl.BlockSpec(memory_space=pl.ANY)] * 2 + [vmem] * 3,
        out_specs=[pl.BlockSpec(memory_space=pl.ANY)] * len(shapes)
        + [vmem] * len(narrow)
        + [pl.BlockSpec(memory_space=pl.ANY)] * 2,
        out_shape=[jax.ShapeDtypeStruct(shape, F32) for shape in shapes + narrow]
        + [jax.ShapeDtypeStruct((3 * length, width), BF16)] * 2,
        scratch_shapes=[
            pltpu.VMEM((count, 512, 512), BF16), pltpu.VMEM((count, 512, 512), F32), pltpu.VMEM((width // 128, 3 * length, 128), F32),
            pltpu.VMEM((2, 3 * length, width), BF16), pltpu.SemaphoreType.DMA((count,)), pltpu.SemaphoreType.DMA((count + 2,)),
        ],
        compiler_params=pltpu.CompilerParams(vmem_limit_bytes=56 * 2**20),
    )(early, late, out3, grad3, small)
    return outs[: len(shapes)], [out if out.ndim == 1 else out[0] for out in outs[len(shapes) : -2]], outs[-2:]


def fused_body(
    inputs, doc_bounds, pool_weight, pool_bias, ln1_gain, ln1_bias, query_weight, key_weight,
    value_weight, out_weight, pos_weight, content_bias, pos_bias, ln2_gain, ln2_bias, ffn_in,
    ffn_in_bias, ffn_out, ffn_out_bias, up_weight, up_bias, cotangent,
):
    _, bytes_here, width = inputs.shape
    length = bytes_here // 3
    n = lax.axis_size("seq")
    tokens = n * length
    rounds = n // 2
    table, sines, cosines = wave_tables(tokens, length, width, TILE)
    given = dict(
        x_bytes=inputs[0], pool_w=pool_weight, q_w=query_weight, k_w=key_weight, v_w=value_weight,
        ct_bytes=cotangent[0], up_w=up_weight, ffn_out=ffn_out, pos_w=pos_weight, table=table,
        out_w=out_weight, ffn_in=ffn_in,
    )
    vectors = dict(
        pool_b=pool_bias, ln1_g=ln1_gain, ln1_b=ln1_bias, content=content_bias, pos=pos_bias, ln2_g=ln2_gain,
        ln2_b=ln2_bias, ffn_in_b=ffn_in_bias, ffn_out_b=ffn_out_bias,
    )
    vectors = {name: vector[None] for name, vector in vectors.items()} | dict(up_flat=up_bias, sines=sines, cosines=cosines)
    vmem = pl.BlockSpec(memory_space=pltpu.VMEM)
    outs = dict(
        out3=((length, 3 * width), BF16), grad3=((length, 3 * width), BF16), small=((SMALL_ROWS, 512), F32),
        early_o=((EARLY_ROWS, 512), BF16), late_o=((LATE_ROWS, 512), BF16),
    )
    pair_half = (length // 2, PAIR)
    block, wide = (length, width), (length, 4 * width)
    dma, signal = pltpu.SemaphoreType.DMA, pltpu.SemaphoreType.REGULAR
    scratch = {name: pltpu.VMEM(array.shape, array.dtype) for name, array in given.items()}
    low = dict(
        x3=(length, 3 * width), ct3=(length, 3 * width), rim=(16, 2 * width), back_rim=(16, width), attn_in=block, q_out=(HEADS,) + pair_half,
        kv_out=(HEADS, length, PAIR), q=(rounds,) + pair_half, kv=(tokens, PAIR), grad_branch=block,
        head_w=(width, HEAD), extra=(length, PAIR + width), keep=(sum(most_tiles(turn, length) for turn in range(rounds)), length, TILE),
        att_out=(rounds,) + pair_half, att_in=(HEADS,) + pair_half, att_low=block, ffn_input=block, act_low=wide,
        grad_pre=wide, grad=(rounds,) + pair_half, dkv_out=(n, length, PAIR), dkv_in=(HEADS, length, PAIR),
        dkv_other=(rounds, length, PAIR), dq_out=(rounds,) + pair_half, dq_in=(HEADS,) + pair_half, grad_pooled=block, early=(EARLY_ROWS, 512), late=(LATE_ROWS, 512),
    )
    full = dict(
        mixing=(width // 128, 3 * length, 128), pooled=block, grad_final=block, grad_act=wide, score=(tokens // TILE, length, TILE), att=(rounds, length, PAIR),
        mixed=block, dkv=(tokens, PAIR), dhead=(width, HEAD), dbias=(8, HEAD), near=(length, PAIR), far=block,
        small_in=(7, SMALL_ROWS, 512), up_b=(1, 3 * width),
    )
    scratch |= {name: pltpu.VMEM(shape, BF16) for name, shape in low.items()}
    scratch |= {name: pltpu.VMEM(shape, F32) for name, shape in full.items()}
    scratch |= dict(
        edges=pltpu.VMEM((2, 16, 128), jnp.int32), load_sem=dma((len(given),)), side_sem=dma((6,)), send_sem=dma((8,)), other_sem=dma((rounds,)),

        q_sem=dma((rounds,)), kv_sem=dma((n,)), att_sem=dma((1,)), grad_sem=dma((rounds,)), dkv_sem=dma((1,)),
        dq_sem=dma((1,)), sum_sem=dma((len(EARLY_CHUNKS + LATE_CHUNKS), 2, REDUCTION_SEMS)),
        sum_free=signal((len(EARLY_CHUNKS + LATE_CHUNKS), 5)), leave_sem=dma((len(EARLY_CHUNKS + LATE_CHUNKS),)),
    )
    layout = (list(given), list(vectors) + ["bounds"], list(outs), list(scratch))
    out3, grad3, small, early, late = pl.pallas_call(
        functools.partial(layer_kernel, n, length, layout),
        in_specs=[pl.BlockSpec(memory_space=pl.ANY)] * len(given)
        + [vmem] * len(vectors)
        + [pl.BlockSpec(memory_space=pltpu.SMEM)],
        out_specs=[vmem] * 3 + [pl.BlockSpec(memory_space=pl.ANY)] * 2,
        out_shape=[jax.ShapeDtypeStruct(*out) for out in outs.values()],
        scratch_shapes=list(scratch.values())
        + sum((reduction_scratch(*cut[1:]) for cut in EARLY_CHUNKS + LATE_CHUNKS), []),
        compiler_params=pltpu.CompilerParams(
            collective_id=0, has_side_effects=True, vmem_limit_bytes=62 * 2**20
        ),
    )(*given.values(), *vectors.values(), doc_bounds)
    wide, narrow, both = finished(early, late, out3, grad3, small)
    sum_in, sum_out, sum_up, sum_mix, sum_pool, sum_q, sum_k, sum_v, sum_p = wide
    pool_b, ln1_g, ln1_b, content, pos, ln2_g, ln2_b, in_b, out_b, up_b = narrow
    return (
        both[0][None], both[1][None], sum_pool, pool_b, ln1_g, ln1_b, sum_q, sum_k, sum_v, sum_mix, sum_p,
        content, pos, ln2_g, ln2_b, sum_in, in_b, sum_out, out_b, sum_up, up_b,
    )


def solution(mesh):
    split = P("dp", "seq", None)
    fits = mesh.shape["seq"] == 16
    return jax.shard_map(
        fused_body if fits else body,
        mesh=mesh,
        in_specs=(split, P("dp", None)) + (P(),) * 19 + (split,),
        out_specs=(split, split) + (P(),) * 19,
        check_vma=False,
    )
```

```python
import functools
import types

import jax
import jax.numpy as jnp
import numpy as np
from jax import lax
from jax.experimental import pallas as pl
from jax.experimental.pallas import tpu as pltpu
from jax.sharding import PartitionSpec as P

HEADS = 8
ROWS = 2
HEAD = 64
PAIR = 2 * HEAD
MESH = pl.DeviceIdType.MESH
F32 = jnp.float32
BF16 = jnp.bfloat16

epsilon = 1e-05
masked_score = -1e30


def dot(left, right, dims=((1,), (0,))):
    return lax.dot_general(left, right, (dims, ((), ())), preferred_element_type=F32)


def passed_along(value, axis, steps):
    count = lax.axis_size(axis)
    first, last = (max(0, -steps), min(count, count - steps))
    return lax.ppermute(value, axis, [(source, source + steps) for source in range(first, last)])


def place_of(block, group):
    turn, spot = block // group, block % group
    return turn, jnp.where((turn + turn // 4) % 2 == 0, spot, group - 1 - spot)


def block_of(turn, member, group):
    return turn * group + jnp.where((turn + turn // 4) % 2 == 0, member, group - 1 - member)


def whereabouts(group):
    core, chip = lax.axis_index("dp"), lax.axis_index("seq")
    chips = group // 2
    unit = chip // chips
    member = (chip % chips) * 2 + core
    return core, chip, unit // HEADS, unit % HEADS, member


def chip_of(row, head, member, group):
    return (row * HEADS + head) * (group // 2) + member // 2, member % 2


def meet(n, group, to_units):
    core, chip, row, head, member = whereabouts(group)
    barrier = pltpu.get_barrier_semaphore()

    def greet(row_or_core, chip_at):
        away = jnp.logical_or(row_or_core != core, chip_at != chip)

        @pl.when(away)
        def _():
            pl.semaphore_signal(
                barrier, inc=1, device_id=(row_or_core, chip_at), device_id_type=MESH
            )

        return away.astype(jnp.int32)

    own_row = row == core
    if to_units:
        for s in range(n):
            greet(row, jnp.int32(s))
        mine = jnp.logical_and(chip // (HEADS * (group // 2)) == core, True)
        pl.semaphore_wait(barrier, HEADS * group - mine.astype(jnp.int32))
    else:
        for h in range(HEADS):
            for g in range(group):
                c, k = chip_of(core, h, g, group)
                greet(jnp.int32(k), c)
        pl.semaphore_wait(barrier, n - own_row.astype(jnp.int32))


def send(source, target, sems, core, chip):
    here_core, here_chip = lax.axis_index("dp"), lax.axis_index("seq")
    here = jnp.logical_and(core == here_core, chip == here_chip)

    @pl.when(here)
    def _():
        pltpu.make_async_copy(source, target, sems[1]).start()

    @pl.when(jnp.logical_not(here))
    def _():
        pltpu.make_async_remote_copy(
            source, target, sems[0], sems[1], device_id=(core, chip), device_id_type=MESH
        ).start()


def sent(source, sem, core, chip):
    here_core, here_chip = lax.axis_index("dp"), lax.axis_index("seq")
    here = jnp.logical_and(core == here_core, chip == here_chip)

    @pl.when(jnp.logical_not(here))
    def _():
        pltpu.make_async_copy(source, source, sem).wait()


def arrived(whole, sem):
    pltpu.make_async_copy(whole, whole, sem).wait()


def to_units_kernel(n, group, *refs):
    count = len(refs) - 2
    arrays, outs = refs[: count // 2], refs[count // 2 : count]
    send_sem, recv_sem = refs[count:]
    core, chip, row, head, member = whereabouts(group)
    turn, spot = place_of(chip, group)
    meet(n, group, True)
    jobs = []
    for h in range(HEADS):
        for index, (array, out) in enumerate(zip(arrays, outs)):
            sems = (send_sem.at[index], recv_sem.at[index])
            if index == 0:
                to_chip, to_core = chip_of(core, h, spot, group)
                jobs.append((array.at[h], out.at[turn], sems, to_core, to_chip))
            else:
                for g in range(group):
                    to_chip, to_core = chip_of(core, h, g, group)
                    jobs.append((array.at[h], out.at[chip], sems, jnp.int32(to_core), to_chip))
    for job in jobs:
        send(*job)
    for source, _, sems, to_core, to_chip in jobs:
        sent(source, sems[0], to_core, to_chip)
    for index, out in enumerate(outs):
        arrived(out, recv_sem.at[index])


def to_owners_kernel(n, group, *refs):
    count = len(refs) - 2
    arrays, outs = refs[: count // 2], refs[count // 2 : count]
    send_sem, recv_sem = refs[count:]
    core, chip, row, head, member = whereabouts(group)
    meet(n, group, False)
    jobs = []
    for turn in range(n // group):
        block = block_of(jnp.int32(turn), member, group)
        sems = (send_sem.at[0], recv_sem.at[0])
        jobs.append((arrays[0].at[turn], outs[0].at[head], sems, row, block))
    if len(arrays) > 1:
        for block in range(n):
            sems = (send_sem.at[1], recv_sem.at[1])
            jobs.append((arrays[1].at[block], outs[1].at[member, head], sems, row, jnp.int32(block)))
    for job in jobs:
        send(*job)
    for source, _, sems, to_core, to_chip in jobs:
        sent(source, sems[0], to_core, to_chip)
    for index, out in enumerate(outs):
        arrived(out, recv_sem.at[index])


def exchange(kernel, n, group, arrays, shapes, ident):
    vmem = pl.BlockSpec(memory_space=pltpu.VMEM)
    return pl.pallas_call(
        functools.partial(kernel, n, group),
        out_shape=[jax.ShapeDtypeStruct(shape, array.dtype) for shape, array in zip(shapes, arrays)],
        in_specs=[vmem] * len(arrays),
        out_specs=[vmem] * len(arrays),
        scratch_shapes=[
            pltpu.SemaphoreType.DMA((len(arrays),)),
            pltpu.SemaphoreType.DMA((len(arrays),)),
        ],
        compiler_params=pltpu.CompilerParams(
            collective_id=ident, has_side_effects=True, vmem_limit_bytes=48 * 2**20
        ),
    )(*arrays)


def unpacked(pair):
    return jnp.concatenate([pair[:, :HEAD], pair[:, HEAD:]], 0)


def packed(block):
    half = block.shape[0] // 2
    return jnp.concatenate([block[:half], block[half:]], 1)


def query_parts(q_pair, content_bias, pos_bias, pos_weight, turn_sin, turn_cos):
    query = unpacked(q_pair.astype(F32))
    query_u = (query + content_bias).astype(BF16)
    query_v = (query + pos_bias).astype(BF16)
    spread = dot(query_v, pos_weight, ((1,), (1,)))
    half = turn_sin.shape[1]
    lift, rest = spread[:, :half], spread[:, half:]
    on_sin = rest * turn_sin - lift * turn_cos
    on_cos = lift * turn_sin + rest * turn_cos
    turned = jnp.concatenate([on_sin, on_cos], 1)
    return query_u, query_v, turned


def attend_kernel(
    n, group, tile, q_ref, kv_ref, table_ref, sin_ref, cos_ref, weight_ref, cb_ref, pb_ref, bounds_ref,
    att_ref, low_ref, total_ref, keep_ref, score_ref, extra_ref,
):
    turn = pl.program_id(0)
    member = whereabouts(group)[4]
    block = block_of(turn, member, group)
    length = sin_ref.shape[0]
    tokens = n * length
    query_u, _, turned = query_parts(
        q_ref[...], cb_ref[...], pb_ref[...], weight_ref[...], sin_ref[...], cos_ref[...]
    )
    scale = HEAD**-0.5
    head_part = (query_u.astype(F32) * scale).astype(BF16)
    extra_ref[:, :HEAD] = head_part
    extra_ref[:, HEAD:PAIR] = jnp.zeros_like(head_part)
    extra_ref[:, PAIR:] = (turned * scale).astype(BF16)
    first = block * length
    tiles = (first + length + tile - 1) // tile
    low_bound, high_bound = bounds_ref[0], bounds_ref[1]
    places = first + lax.broadcasted_iota(jnp.int32, (length, 1), 0)
    opening = jnp.where(
        places >= high_bound, high_bound, jnp.where(places >= low_bound, low_bound, 0)
    )
    lanes = lax.broadcasted_iota(jnp.int32, (length, tile), 1)

    def score_step(step, top):
        start = pl.multiple_of(step * tile, tile)
        keys = kv_ref[pl.ds(start, tile), :]
        waves = table_ref[pl.ds(pl.multiple_of((n - 1 - block) * length + start, length), tile), :]
        score = dot(extra_ref[:, :PAIR], keys, ((1,), (1,))) + dot(
            extra_ref[:, PAIR:], waves, ((1,), (1,))
        )
        at = lanes + start
        allowed = jnp.logical_and(at <= places, at >= opening)
        score = jnp.where(allowed, score, masked_score)
        score_ref[:, pl.ds(start, tile)] = score
        for part in range(tile // 128):
            top = jnp.maximum(top, score[:, part * 128 : (part + 1) * 128])
        return top

    top = lax.fori_loop(0, tiles, score_step, jnp.full((length, 128), masked_score, F32))
    top = jnp.max(top, 1, keepdims=True)

    def value_step(step, state):
        total, summed = state
        start = pl.multiple_of(step * tile, tile)
        weight = jnp.exp(score_ref[:, pl.ds(start, tile)] - top)
        for part in range(tile // 128):
            total = total + weight[:, part * 128 : (part + 1) * 128]
        low = weight.astype(BF16)
        keep_ref[:, pl.ds(start, tile)] = low
        return total, summed + dot(low, kv_ref[pl.ds(start, tile), :])

    total, summed = lax.fori_loop(
        0, tiles, value_step, (jnp.zeros((length, 128), F32), jnp.zeros((length, PAIR), F32))
    )
    total = jnp.sum(total, 1, keepdims=True)
    attended = summed[:, HEAD:] / total
    att_ref[...] = attended
    total_ref[...] = jnp.broadcast_to(total, (length, 128))
    low_ref[...] = packed(attended).astype(BF16)


def back_kernel(
    n, group, tile, q_ref, kv_ref, table_ref, sin_ref, cos_ref, weight_ref, cb_ref, pb_ref,
    att_ref, total_ref, keep_ref, grad_ref,
    dq_ref, dkv_ref, dweight_ref, dcb_ref, dpb_ref, dkv_acc,
):
    turn = pl.program_id(0)
    member = whereabouts(group)[4]
    block = block_of(turn, member, group)
    length = sin_ref.shape[0]
    scale = HEAD**-0.5

    @pl.when(turn == 0)
    def _():
        dkv_acc[...] = jnp.zeros_like(dkv_acc)
        dweight_ref[...] = jnp.zeros_like(dweight_ref)
        dcb_ref[...] = jnp.zeros_like(dcb_ref)
        dpb_ref[...] = jnp.zeros_like(dpb_ref)

    query_u, query_v, _ = query_parts(
        q_ref[...], cb_ref[...], pb_ref[...], weight_ref[...], sin_ref[...], cos_ref[...]
    )
    head_part = (query_u.astype(F32) * scale).astype(BF16)
    grad = unpacked(grad_ref[...].astype(F32))
    inverse = 1.0 / total_ref[:, :1]
    delta = jnp.sum(grad * att_ref[...], 1, keepdims=True) * inverse
    grad_low = (grad * inverse).astype(BF16)
    nothing = jnp.zeros_like(grad_low)
    grad_wide = jnp.concatenate([nothing, grad_low], 1)
    query_wide = jnp.concatenate([head_part, nothing], 1)
    tiles = (block * length + length + tile - 1) // tile

    def step_over(step, state):
        near, far = state
        start = pl.multiple_of(step * tile, tile)
        keys = kv_ref[pl.ds(start, tile), :]
        waves = table_ref[pl.ds(pl.multiple_of((n - 1 - block) * length + start, length), tile), :]
        weight = keep_ref[:, pl.ds(start, tile)]
        grad_weight = dot(grad_wide, keys, ((1,), (1,)))
        grad_score = (weight.astype(F32) * (grad_weight - delta)).astype(BF16)
        near = near + dot(grad_score, keys)
        far = far + dot(grad_score, waves)
        dkv_acc[pl.ds(start, tile), :] += dot(grad_score, query_wide, ((0,), (0,))) + dot(
            weight, grad_wide, ((0,), (0,))
        )
        return near, far

    near, far = lax.fori_loop(
        0,
        tiles,
        step_over,
        (jnp.zeros((length, PAIR), F32), jnp.zeros((length, table_ref.shape[1]), F32)),
    )
    grad_u = near[:, :HEAD] * scale
    half = sin_ref.shape[1]
    turn_sin, turn_cos = sin_ref[...], cos_ref[...]
    on_sin, on_cos = far[:, :half] * scale, far[:, half:] * scale
    lift = on_cos * turn_sin - on_sin * turn_cos
    rest = on_cos * turn_cos + on_sin * turn_sin
    spread = jnp.concatenate([lift, rest], 1).astype(BF16)
    grad_v = dot(spread, weight_ref[...])
    dweight_ref[...] += dot(spread, query_v, ((0,), (0,)))
    dcb_ref[...] += jnp.sum(grad_u, 0, keepdims=True)
    dpb_ref[...] += jnp.sum(grad_v, 0, keepdims=True)
    dq_ref[...] = packed(grad_u + grad_v).astype(BF16)

    @pl.when(turn == pl.num_programs(0) - 1)
    def _():
        dkv_ref[...] = dkv_acc[...].astype(BF16)


def wave_tables(tokens, length, width, more=0):
    rates = 10000.0 ** (-2.0 * np.arange(width // 2, dtype=np.float64) / width)
    far = (np.arange(tokens + max(length, more), dtype=np.float64) - (tokens - length))[:, None] * rates
    near = np.arange(length, dtype=np.float64)[:, None] * rates
    table = np.concatenate([np.sin(far), np.cos(far)], 1)
    return (
        jnp.asarray(table, dtype=BF16),
        jnp.asarray(np.sin(near), dtype=F32),
        jnp.asarray(np.cos(near), dtype=F32),
    )


def whole_spec(shape):
    return pl.BlockSpec(shape, lambda turn: (0,) * len(shape))


def turn_spec(shape):
    return pl.BlockSpec((None,) + shape, lambda turn: (turn,) + (0,) * len(shape))


def layer_norm(hidden, gain, bias):
    average = jnp.mean(hidden, -1, keepdims=True)
    centred = hidden - average
    inverse = lax.rsqrt(jnp.mean(centred * centred, -1, keepdims=True) + epsilon)
    normed = centred * inverse
    return (normed * gain + bias, normed, inverse)


def norm_back(grad_out, normed, inverse, gain):
    scaled = grad_out * gain
    grad_in = inverse * (
        scaled
        - jnp.mean(scaled, -1, keepdims=True)
        - normed * jnp.mean(scaled * normed, -1, keepdims=True)
    )
    return (grad_in, jnp.sum(grad_out * normed, axis=0), jnp.sum(grad_out, axis=0))


def exact_gelu(value):
    return jax.nn.gelu(value, approximate=False)


def heads_packed(array):
    length = array.shape[0]
    split = array.reshape(2, length // 2, HEADS, HEAD)
    return jnp.transpose(split, (2, 1, 0, 3)).reshape(HEADS, length // 2, PAIR)


def heads_unpacked(array):
    half = array.shape[1]
    split = array.reshape(HEADS, half, 2, HEAD)
    return jnp.transpose(split, (2, 1, 0, 3)).reshape(2 * half, HEADS * HEAD)


def body(
    inputs, doc_bounds, pool_weight, pool_bias, ln1_gain, ln1_bias, query_weight, key_weight,
    value_weight, out_weight, pos_weight, content_bias, pos_bias, ln2_gain, ln2_bias, ffn_in,
    ffn_in_bias, ffn_out, ffn_out_bias, up_weight, up_bias, cotangent,
):
    _, bytes_here, width = inputs.shape
    length = bytes_here // 3
    n = lax.axis_size("seq")
    tokens = n * length
    group = 2 * n // (ROWS * HEADS)
    rounds = n // group
    tile = 2 * length
    row, head, member = whereabouts(group)[2:]

    all_bounds = lax.all_gather(doc_bounds, "dp", axis=0, tiled=True)
    bounds = lax.dynamic_slice(all_bounds, (row, 0), (1, 2))[0]
    table, turn_sin, turn_cos = wave_tables(tokens, length, width)
    head_weight = lax.dynamic_slice(pos_weight, (0, head * HEAD), (width, HEAD))
    head_cb = lax.dynamic_slice(content_bias, (head * HEAD,), (HEAD,))[None]
    head_pb = lax.dynamic_slice(pos_bias, (head * HEAD,), (HEAD,))[None]

    rim = passed_along(inputs[:, bytes_here - 2 :, :], "seq", 1)
    shifted = jnp.concatenate([rim, inputs[:, : bytes_here - 2, :]], 1)
    pooled_in = shifted.reshape(length, 3 * width)
    pooled = dot(pooled_in, pool_weight) + pool_bias
    normed_one, plain_one, inverse_one = layer_norm(pooled, ln1_gain, ln1_bias)
    attn_in = normed_one.astype(BF16)
    query = dot(attn_in, query_weight).astype(BF16)
    keys = dot(attn_in, key_weight).astype(BF16).reshape(length, HEADS, HEAD)
    values = dot(attn_in, value_weight).astype(BF16).reshape(length, HEADS, HEAD)
    q_out = heads_packed(query)
    kv_out = jnp.transpose(jnp.concatenate([keys, values], 2), (1, 0, 2))

    q_in, kv_in = exchange(
        to_units_kernel, n, group, (q_out, kv_out),
        ((rounds, length // 2, PAIR), (n, length, PAIR)), 0,
    )
    kv_in = kv_in.reshape(tokens, PAIR)

    common_specs = [
        turn_spec((length // 2, PAIR)),
        whole_spec((tokens, PAIR)),
        whole_spec(table.shape),
        whole_spec(turn_sin.shape),
        whole_spec(turn_cos.shape),
        whole_spec(head_weight.shape),
        whole_spec((1, HEAD)),
        whole_spec((1, HEAD)),
    ]
    common = (q_in, kv_in, table, turn_sin, turn_cos, head_weight, head_cb, head_pb)
    attended, att_low, total, keep = pl.pallas_call(
        functools.partial(attend_kernel, n, group, tile),
        grid=(rounds,),
        in_specs=common_specs + [pl.BlockSpec(memory_space=pltpu.SMEM)],
        out_specs=[
            turn_spec((length, HEAD)),
            turn_spec((length // 2, PAIR)),
            turn_spec((length, 128)),
            turn_spec((length, tokens)),
        ],
        out_shape=[
            jax.ShapeDtypeStruct((rounds, length, HEAD), F32),
            jax.ShapeDtypeStruct((rounds, length // 2, PAIR), BF16),
            jax.ShapeDtypeStruct((rounds, length, 128), F32),
            jax.ShapeDtypeStruct((rounds, length, tokens), BF16),
        ],
        scratch_shapes=[
            pltpu.VMEM((length, tokens), F32),
            pltpu.VMEM((length, PAIR + width), BF16),
        ],
        compiler_params=pltpu.CompilerParams(vmem_limit_bytes=56 * 2**20),
    )(*common, bounds)

    (att_back,) = exchange(
        to_owners_kernel, n, group, (att_low,), ((HEADS, length // 2, PAIR),), 1
    )
    attended_low = heads_unpacked(att_back)

    mixed = pooled + dot(attended_low, out_weight)
    normed_two, plain_two, inverse_two = layer_norm(mixed, ln2_gain, ln2_bias)
    ffn_input = normed_two.astype(BF16)
    pre_act = dot(ffn_input, ffn_in) + ffn_in_bias
    activated, gelu_pull = jax.vjp(exact_gelu, pre_act)
    act_low = activated.astype(BF16)
    final = mixed + dot(act_low, ffn_out) + ffn_out_bias
    final_low = final.astype(BF16)
    upsampled = dot(final_low, up_weight) + up_bias
    outputs = (inputs.astype(F32) + upsampled.reshape(1, bytes_here, width)).astype(BF16)
    grad_up = cotangent.reshape(length, 3 * width)
    over_rows = ((0,), (0,))
    over_columns = ((1,), (1,))
    grad_up_weight = dot(final_low, grad_up, over_rows)
    grad_up_bias = jnp.sum(grad_up.astype(F32), axis=0)
    grad_final = dot(grad_up, up_weight, over_columns)
    grad_branch = grad_final.astype(BF16)
    grad_ffn_out = dot(act_low, grad_branch, over_rows)
    grad_ffn_out_bias = jnp.sum(grad_branch.astype(F32), axis=0)
    grad_act = dot(grad_branch, ffn_out, over_columns)
    grad_pre = gelu_pull(grad_act)[0].astype(BF16)
    grad_ffn_in = dot(ffn_input, grad_pre, over_rows)
    grad_ffn_in_bias = jnp.sum(grad_pre.astype(F32), axis=0)
    grad_normed_two = dot(grad_pre, ffn_in, over_columns)
    grad_from_two, grad_ln2_gain, grad_ln2_bias = norm_back(
        grad_normed_two, plain_two, inverse_two, ln2_gain
    )
    grad_mixed = grad_final + grad_from_two
    grad_attn_branch = grad_mixed.astype(BF16)
    grad_out_weight = dot(attended_low, grad_attn_branch, over_rows)
    grad_attended = dot(grad_attn_branch, out_weight, over_columns).astype(BF16)

    early = lax.psum(
        tuple(
            grad.astype(BF16) for grad in (grad_ffn_in, grad_ffn_out, grad_up_weight, grad_out_weight)
        ),
        ("dp", "seq"),
    )

    (grad_in,) = exchange(
        to_units_kernel, n, group, (heads_packed(grad_attended),), ((rounds, length // 2, PAIR),), 2
    )
    dq_out, dkv_out, grad_head_weight, grad_head_cb, grad_head_pb = pl.pallas_call(
        functools.partial(back_kernel, n, group, tile),
        grid=(rounds,),
        in_specs=common_specs
        + [
            turn_spec((length, HEAD)),
            turn_spec((length, 128)),
            turn_spec((length, tokens)),
            turn_spec((length // 2, PAIR)),
        ],
        out_specs=[
            turn_spec((length // 2, PAIR)),
            whole_spec((tokens, PAIR)),
            whole_spec((width, HEAD)),
            whole_spec((1, HEAD)),
            whole_spec((1, HEAD)),
        ],
        out_shape=[
            jax.ShapeDtypeStruct((rounds, length // 2, PAIR), BF16),
            jax.ShapeDtypeStruct((tokens, PAIR), BF16),
            jax.ShapeDtypeStruct((width, HEAD), F32),
            jax.ShapeDtypeStruct((1, HEAD), F32),
            jax.ShapeDtypeStruct((1, HEAD), F32),
        ],
        scratch_shapes=[pltpu.VMEM((tokens, PAIR), F32)],
        compiler_params=pltpu.CompilerParams(vmem_limit_bytes=56 * 2**20),
    )(*common, attended, total, keep, grad_in)
    dq_back, dkv_back = exchange(
        to_owners_kernel, n, group, (dq_out, dkv_out.reshape(n, length, PAIR)),
        ((HEADS, length // 2, PAIR), (group, HEADS, length, PAIR)), 3,
    )
    grad_query = heads_unpacked(dq_back)
    dkv_back = jnp.transpose(jnp.sum(dkv_back.astype(F32), 0), (1, 0, 2)).astype(BF16)
    grad_key_low = dkv_back[:, :, :HEAD].reshape(length, width)
    grad_value_low = dkv_back[:, :, HEAD:].reshape(length, width)

    def at_head(part, shape):
        return lax.dynamic_update_slice(
            jnp.zeros(shape, F32), part.reshape(shape[:-1] + (HEAD,)), (0,) * (len(shape) - 1) + (head * HEAD,)
        )

    grad_pos_weight = at_head(grad_head_weight, (width, width))
    grad_content_bias = at_head(grad_head_cb, (width,))
    grad_pos_bias = at_head(grad_head_pb, (width,))
    grad_query_weight = dot(attn_in, grad_query, over_rows)
    grad_key_weight = dot(attn_in, grad_key_low, over_rows)
    grad_value_weight = dot(attn_in, grad_value_low, over_rows)
    grad_normed_one = (
        dot(grad_query, query_weight, over_columns)
        + dot(grad_key_low, key_weight, over_columns)
        + dot(grad_value_low, value_weight, over_columns)
    )
    grad_from_one, grad_ln1_gain, grad_ln1_bias = norm_back(
        grad_normed_one, plain_one, inverse_one, ln1_gain
    )
    grad_pooled = (grad_mixed + grad_from_one).astype(BF16)
    grad_pool_weight = dot(pooled_in, grad_pooled, over_rows)
    grad_pool_bias = jnp.sum(grad_pooled.astype(F32), axis=0)
    grad_shifted = dot(grad_pooled, pool_weight, over_columns).reshape(1, bytes_here, width)
    incoming = passed_along(grad_shifted[:, :2, :], "seq", -1)
    input_grad = (
        cotangent.astype(F32) + jnp.concatenate([grad_shifted[:, 2:, :], incoming], 1)
    ).astype(BF16)
    late = lax.psum(
        tuple(
            grad.astype(BF16)
            for grad in (
                grad_pool_weight, grad_query_weight, grad_key_weight, grad_value_weight, grad_pos_weight,
            )
        ),
        ("dp", "seq"),
    )
    small_parts = (
        grad_pool_bias, grad_ln1_gain, grad_ln1_bias, grad_content_bias, grad_pos_bias,
        grad_ln2_gain, grad_ln2_bias, grad_ffn_in_bias, grad_ffn_out_bias, grad_up_bias,
    )
    small = lax.psum(jnp.concatenate(small_parts), ("dp", "seq"))
    cuts = np.cumsum([part.shape[0] for part in small_parts])[:-1].tolist()
    (
        sum_pool_bias, sum_ln1_gain, sum_ln1_bias, sum_content, sum_pos,
        sum_ln2_gain, sum_ln2_bias, sum_in_bias, sum_out_bias, sum_up_bias,
    ) = jnp.split(small, cuts)
    sum_in, sum_out, sum_up, sum_mix = (grad.astype(F32) for grad in early)
    sum_pool, sum_q, sum_k, sum_v, sum_p = (grad.astype(F32) for grad in late)
    return (
        outputs, input_grad, sum_pool, sum_pool_bias, sum_ln1_gain, sum_ln1_bias, sum_q, sum_k, sum_v,
        sum_mix, sum_p, sum_content, sum_pos, sum_ln2_gain, sum_ln2_bias, sum_in, sum_in_bias,
        sum_out, sum_out_bias, sum_up, sum_up_bias,
    )


EARLY_ROWS, LATE_ROWS = 6144, 3584
EARLY_CHUNKS = ((0, 2048, False), (2048, 2048, True), (4096, 2048, False))
LATE_CHUNKS = ((3072, 512, False), (1536, 1024, False), (2560, 512, True), (0, 1024, False), (1024, 512, True))
QKV_SUMS, POOL_SUMS = slice(4, 6), slice(6, None)
SMALL_ROWS = 16
TILE = 768
OVER_ROWS = ((0,), (0,))
OVER_COLUMNS = ((1,), (1,))


class Reduction:
    def __init__(self, buffer, start, rows, by_z, bufs, sems, free, small=None):
        self.buffer, self.sems, self.free, self.small = buffer, sems, free, small
        core, chip = lax.axis_index("dp"), lax.axis_index("seq")
        self.core, self.chip = core, chip
        x, y, z = chip % 2, (chip // 2) % 2, chip // 4
        first_x = core == 0
        self.peer_x, self.peer_y = (core, chip + 1 - 2 * x), (core, chip + 2 - 4 * y)
        self.z_peers = [(core, chip + ((z + away) % 4 - z) * 4) for away in (1, 2, 3)]
        self.z = z

        def pair(bit, peer_core, peer_chip):
            return (bit, [(1 - bit, peer_core, peer_chip)])

        one = pair(jnp.where(first_x, x, y), core, jnp.where(first_x, self.peer_x[1], self.peer_y[1]))
        two = pair(jnp.where(first_x, y, x), core, jnp.where(first_x, self.peer_y[1], self.peer_x[1]))
        stages = [pair(core, 1 - core, chip)]
        if by_z:
            low, high = z % 2, z // 2
            stages += [pair(low, core, chip + 4 - 8 * low), one, two, pair(high, core, chip + 8 - 16 * high)]
        else:
            stages += [one, two, (z, [((z + away) % 4, core, self.z_peers[away - 1][1]) for away in (1, 2, 3)])]
        self.stages = []
        at, size, first = start, rows, 0
        for buf, (own, others) in zip(bufs, stages):
            ways = len(others) + 1
            self.stages.append((at, size, size // ways, own, others, buf, first))
            at, size, first = at + own * (size // ways), size // ways, first + len(others)
        self.back = first
        self.last = 2 * len(stages)

    def rows(self, start, size):
        return self.buffer.at[pl.ds(pl.multiple_of(start, 16), size)]

    def copy(self, index, source, target, core, chip):
        return pltpu.make_async_remote_copy(
            source, target, self.sems.at[0, index], self.sems.at[1, index],
            device_id=(core, chip), device_id_type=MESH,
        )

    def done(self, index, source):
        copy = self.copy(index, source, source, 1 - self.core, self.chip)
        copy.wait_send()
        copy.wait_recv()

    def add(self, start, size, part_start, buf):
        chunk = min(size, 128)
        while size % chunk:
            chunk -= 16

        def one(step, carry):
            at = pl.ds(pl.multiple_of(start + step * chunk, 16), chunk)
            here = pl.ds(pl.multiple_of(part_start + step * chunk, 16), chunk)
            total = self.buffer[at].astype(F32)
            for part in range(buf.shape[0]):
                total = total + buf[part, here].astype(F32)
            self.buffer[at] = total.astype(BF16)
            return carry

        lax.fori_loop(0, size // chunk, one, 0)

    def send_parts(self, number):
        at, _, part, _, others, buf, first = self.stages[number]
        for place, (other, core, chip) in enumerate(others):
            self.copy(first + place, self.rows(at + other * part, part), buf.at[place], core, chip).start()

    def send_back(self, number):
        at, _, part, own, others, _, first = self.stages[number]
        pl.semaphore_wait(self.free.at[number], len(others))
        mine = self.rows(at + own * part, part)
        for place, (_, core, chip) in enumerate(others):
            self.copy(self.back + first + place, mine, mine, core, chip).start()

    def step(self, number):
        count = len(self.stages)
        if number == 0:
            self.send_parts(0)
        elif number <= count:
            at, _, part, own, others, buf, first = self.stages[number - 1]
            for place, (_, core, chip) in enumerate(others):
                self.done(first + place, buf.at[place])
            for _, core, chip in others:
                pl.semaphore_signal(self.free.at[number - 1], inc=1, device_id=(core, chip), device_id_type=MESH)
            kept = at + own * part
            if number < count:
                _, _, next_part, next_own, next_others, _, _ = self.stages[number]
                for other, _, _ in next_others:
                    self.add(kept + other * next_part, next_part, other * next_part, buf)
                self.send_parts(number)
                self.add(kept + next_own * next_part, next_part, next_own * next_part, buf)
            else:
                self.add(kept, part, 0, buf)
                self.send_back(count - 1)
        else:
            stage = 2 * count - number
            at, _, part, own, others, _, first = self.stages[stage]
            for place in range(len(others)):
                self.done(self.back + first + place, self.rows(at + own * part, part))
            if stage > 0:
                self.send_back(stage - 1)
        if self.small is not None:
            self.small_step(number)

    def small_step(self, number):
        own, taken = self.small
        first = 2 * self.back
        if number in (1, 2, 3):
            self.done(first + number - 1, own)
            own[...] = own[...] + taken[number - 1]
        if number < 3:
            core, chip = ((1 - self.core, self.chip), self.peer_x, self.peer_y)[number]
            self.copy(first + number, own, taken.at[number], core, chip).start()
        if number == 3:
            taken[3 + self.z] = own[...]
            for place, (core, chip) in enumerate(self.z_peers):
                self.copy(first + 3 + place, own, taken.at[3 + self.z], core, chip).start()
        if number == 4:
            for place in range(3):
                self.done(first + 3 + place, own)
            own[...] = (taken[3] + taken[4]) + (taken[5] + taken[6])


REDUCTION_SEMS = 18


def reduction_scratch(rows, by_z):
    shapes = [(1, rows // 2), (1, rows // 4), (1, rows // 8)]
    shapes += [(1, rows // 16), (1, rows // 32)] if by_z else [(3, rows // 32)]
    return [pltpu.VMEM(shape + (512,), BF16) for shape in shapes]


def gelu_pair(value):
    falling = jnp.exp(value * value * -0.5)
    turn = 1.0 / (1.0 + 0.3275911 * 0.7071067811865476 * jnp.abs(value))
    series = turn * (
        0.254829592
        + turn * (-0.284496736 + turn * (1.421413741 + turn * (-1.453152027 + turn * 1.061405429)))
    )
    tail = 0.5 * series * falling
    share = jnp.where(value >= 0, 1.0 - tail, tail)
    return value * share, share + value * falling * 0.3989422804014327


def norm_parts(hidden):
    average = jnp.mean(hidden, -1, keepdims=True)
    centred = hidden - average
    inverse = lax.rsqrt(jnp.mean(centred * centred, -1, keepdims=True) + epsilon)
    return centred * inverse, inverse


def norm_grad(grad_out, normed, inverse, gain):
    scaled = grad_out * gain
    return inverse * (
        scaled
        - jnp.mean(scaled, -1, keepdims=True)
        - normed * jnp.mean(scaled * normed, -1, keepdims=True)
    )


def column_sum(value):
    return jnp.sum(value, 0, keepdims=True)


def most_tiles(turn, length):
    return ((2 * turn + 2) * length + TILE - 1) // TILE


def layer_kernel(n, length, layout, *refs):
    taken = iter(refs)
    given, vectors, outs, scratch = ({name: next(taken) for name in part} for part in layout)
    r = types.SimpleNamespace(**vectors, **outs, **scratch)
    group = 2
    rounds = n // group
    tile = TILE
    width = 512
    scale = HEAD**-0.5
    core, chip, row, head, member = whereabouts(group)
    count = 2 * n
    me = core * n + chip

    loads = {}
    chunk_refs = list(refs[len(refs) - sum(5 if cut[2] else 4 for cut in EARLY_CHUNKS + LATE_CHUNKS) :])

    def reduction(buffer, index, cut, small=None):
        bufs = [chunk_refs.pop(0) for _ in range(5 if cut[2] else 4)]
        return Reduction(buffer, *cut, bufs, r.sum_sem.at[index], r.sum_free.at[index], small)

    for index, (name, source) in enumerate(given.items()):
        loads[name] = pltpu.make_async_copy(source, scratch[name], r.load_sem.at[index])
        loads[name].start()

    def ready(*which):
        for ref in which:
            next(loads[name] for name in given if scratch[name] is ref).wait()

    r.up_b[...] = r.up_flat[...].reshape(1, 3 * width)

    barrier = pltpu.get_barrier_semaphore()

    def greet(step, carry):
        other = (me + step) % count
        pl.semaphore_signal(barrier, inc=1, device_id=(other // n, other % n), device_id_type=MESH)
        return carry

    lax.fori_loop(1, count, greet, 0)

    low_bound, high_bound = r.bounds[0, 0], r.bounds[0, 1]
    r.edges[core, :8] = jnp.full((8, 128), low_bound, jnp.int32)
    r.edges[core, 8:] = jnp.full((8, 128), high_bound, jnp.int32)

    def tokens_of(source, target):
        for block in range(width // 128):
            r.mixing[block] = source[:, block * 128 : (block + 1) * 128].astype(F32)
            for part in range(3):
                every = r.mixing[block, pl.ds(part, length, stride=3), :]
                start = part * width + block * 128
                target[:, start : start + 128] = every.astype(BF16)

    ready(r.x_bytes, r.pool_w)
    tokens_of(r.x_bytes, r.x3)
    own = dot(r.x3[:, :width], r.pool_w[2 * width :])
    before = dot(r.x3[:, width:], r.pool_w[: 2 * width])
    pl.semaphore_wait(barrier, count - 1)

    def edge_copy():
        return pltpu.make_async_remote_copy(
            r.edges.at[core], r.edges.at[core], r.side_sem.at[0], r.side_sem.at[1],
            device_id=(1 - core, chip), device_id_type=MESH,
        )

    def rim_copy():
        return pltpu.make_async_remote_copy(
            r.x3.at[length - 16 :, width:], r.rim, r.side_sem.at[2], r.side_sem.at[3],
            device_id=(core, (chip + 1) % n), device_id_type=MESH,
        )

    edge_copy().start()

    @pl.when(chip < n - 1)
    def _():
        rim_copy().start()

    @pl.when(chip == 0)
    def _():
        r.rim[...] = jnp.zeros_like(r.rim)

    @pl.when(chip > 0)
    def _():
        rim_copy().wait_recv()

    rim_sum = dot(r.rim[...], r.pool_w[: 2 * width])
    at_row = lax.broadcasted_iota(jnp.int32, (length, width), 0)
    before = jnp.where(at_row == 0, rim_sum[15:16], pltpu.roll(before, 1, 0))
    pooled = own + before + r.pool_b[...]
    r.pooled[...] = pooled
    plain, _ = norm_parts(pooled)
    attn_in = (plain * r.ln1_g[...] + r.ln1_b[...]).astype(BF16)
    r.attn_in[...] = attn_in
    ready(r.q_w, r.k_w, r.v_w)
    query = dot(attn_in, r.q_w[...])
    keys = dot(attn_in, r.k_w[...])
    values = dot(attn_in, r.v_w[...])
    for h in range(HEADS):
        at = slice(h * HEAD, (h + 1) * HEAD)
        r.q_out[h] = packed(query[:, at]).astype(BF16)
        r.kv_out[h] = jnp.concatenate([keys[:, at], values[:, at]], 1).astype(BF16)
    turn_to, spot_to = place_of(chip, group)

    def q_jobs(array, out, sem, recv):
        jobs = []
        for h in range(HEADS):
            to_chip, to_core = chip_of(core, h, spot_to, group)
            jobs.append((array.at[h], out.at[turn_to], (sem, recv.at[turn_to]), to_core, to_chip))
        return jobs

    def rows_in(block):
        return pl.ds(pl.multiple_of(block * length, length), length)

    kv_jobs = []
    for h in range(HEADS):
        to_chip, _ = chip_of(core, h, 0, group)
        sems = (r.send_sem.at[1], r.kv_sem.at[chip])
        kv_jobs.append((r.kv_out.at[h], r.kv.at[rows_in(chip)], sems, chip % 2, to_chip))
    query_jobs = q_jobs(r.q_out, r.q, r.send_sem.at[0], r.q_sem)
    for job in kv_jobs + query_jobs:
        send(*job)

    ready(r.ct_bytes, r.up_w, r.ffn_out)
    tokens_of(r.ct_bytes, r.ct3)
    grad_final = dot(r.ct3[...], r.up_w[...], OVER_COLUMNS)
    r.grad_final[...] = grad_final
    first_jobs = kv_jobs + query_jobs
    grad_branch = grad_final.astype(BF16)
    r.grad_branch[...] = grad_branch
    for part in range(4):
        at = slice(part * width, (part + 1) * width)
        r.grad_act[:, at] = dot(grad_branch, r.ffn_out[at], OVER_COLUMNS)
    small = r.small
    small[...] = jnp.zeros_like(small)
    small[11:12] = column_sum(grad_branch.astype(F32))
    for part in range(3):
        at = slice(part * width, (part + 1) * width)
        small[12 + part : 13 + part] = column_sum(r.ct3[:, at].astype(F32))

    ready(r.pos_w, r.table)
    odd = head % 2 == 1
    pair_at = pl.ds(pl.multiple_of((head // 2) * PAIR, PAIR), PAIR)

    def of_head(ref):
        both = ref[:, pair_at].astype(F32)
        return jnp.where(odd, both[:, HEAD:], both[:, :HEAD])

    r.head_w[...] = of_head(r.pos_w).astype(BF16)
    content_bias, pos_bias = of_head(r.content), of_head(r.pos)
    edge_copy().wait_send()
    edge_copy().wait_recv()
    low_edge = r.edges[row, 0:1, 0:1]
    high_edge = r.edges[row, 8:9, 0:1]
    half = width // 2
    lanes = lax.broadcasted_iota(jnp.int32, (length, tile), 1)

    def rows_of(start):
        return pl.ds(pl.multiple_of(start, 64), tile)

    def tiles_to(block):
        return ((block + 1) * length + tile - 1) // tile

    def kept_at(turn):
        return sum(jnp.where(turn > before, most_tiles(before, length), 0) for before in range(rounds - 1))

    def forward(turn):
        at = turn * group + core
        return pltpu.make_async_remote_copy(
            r.kv.at[rows_in(at)], r.kv.at[rows_in(at)], r.send_sem.at[6], r.kv_sem.at[at], device_id=(1 - core, chip), device_id_type=MESH
        )

    def pass_on(turn):
        at = turn * group + core
        arrived(r.kv.at[rows_in(at)], r.kv_sem.at[at])
        forward(turn).start()

    def met(turn):
        other = turn * group + 1 - core
        arrived(r.kv.at[rows_in(other)], r.kv_sem.at[other])

    rising = row == 0
    pass_on(0)
    pass_on(1)

    @pl.when(jnp.logical_not(rising))
    def _():
        lax.fori_loop(2, rounds, lambda turn, carry: (pass_on(turn), carry)[1], 0)

    met(0)

    @pl.when(jnp.logical_not(rising))
    def _():
        lax.fori_loop(1, rounds, lambda turn, carry: (met(turn), carry)[1], 0)

    def attend(index, carry):
        turn = jnp.where(rising, index, rounds - 1 - index)
        block = block_of(turn, member, group)

        @pl.when(jnp.logical_and(rising, index < rounds - 2))
        def _():
            pass_on(index + 2)

        @pl.when(jnp.logical_and(rising, index < rounds - 1))
        def _():
            met(index + 1)

        arrived(r.q.at[turn], r.q_sem.at[turn])
        query_u, _, turned = query_parts(
            r.q[turn], content_bias, pos_bias, r.head_w[...], r.sines[...], r.cosines[...]
        )
        head_part = (query_u.astype(F32) * scale).astype(BF16)
        r.extra[:, :PAIR] = jnp.concatenate([head_part, jnp.zeros_like(head_part)], 1)
        r.extra[:, PAIR:] = (turned * scale).astype(BF16)
        places = block * length + lax.broadcasted_iota(jnp.int32, (length, 1), 0)
        opening = jnp.where(places >= high_edge, high_edge, jnp.where(places >= low_edge, low_edge, 0))

        def score_step(step, top):
            pair = r.kv[rows_of(step * tile), :]
            waves = r.table[rows_of((n - 1 - block) * length + step * tile), :]
            score = dot(r.extra[:, :PAIR], pair, OVER_COLUMNS) + dot(r.extra[:, PAIR:], waves, OVER_COLUMNS)
            at = lanes + step * tile
            allowed = jnp.logical_and(at <= places, at >= opening)
            score = jnp.where(allowed, score, masked_score)
            r.score[step] = score
            for part in range(tile // 128):
                top = jnp.maximum(top, score[:, part * 128 : (part + 1) * 128])
            return top

        kept, tiles = kept_at(turn), tiles_to(block)
        top = lax.fori_loop(0, tiles, score_step, jnp.full((length, 128), masked_score, F32))
        top = jnp.max(top, 1, keepdims=True)

        def value_step(step, state):
            total, summed = state
            weight = jnp.exp(r.score[step] - top)
            for part in range(tile // 128):
                total = total + weight[:, part * 128 : (part + 1) * 128]
            low = weight.astype(BF16)
            r.keep[kept + step] = low
            pair = r.kv[rows_of(step * tile), :]
            return total, summed + dot(low, pair)

        total, summed = lax.fori_loop(
            0, tiles, value_step, (jnp.zeros((length, 128), F32), jnp.zeros((length, PAIR), F32))
        )
        inverse = 1.0 / jnp.sum(total, 1, keepdims=True)
        attended = summed[:, HEAD:] * inverse
        r.att[turn] = jnp.concatenate([jnp.broadcast_to(inverse, (length, HEAD)), attended], 1)
        r.att_out[turn] = packed(attended).astype(BF16)
        send(
            r.att_out.at[turn], r.att_in.at[head], (r.send_sem.at[2], r.att_sem.at[0]), row, block
        )
        return carry

    lax.fori_loop(0, rounds, attend, 0)
    for source, _, sems, to_core, to_chip in first_jobs:
        sent(source, sems[0], to_core, to_chip)
    for turn in range(rounds):
        forward(turn).wait_send()

    def joined(get):
        parts = [get(h) for h in range(HEADS)]
        upper = jnp.concatenate([part[:, :HEAD] for part in parts], 1)
        lower = jnp.concatenate([part[:, HEAD:] for part in parts], 1)
        return jnp.concatenate([upper, lower], 0)

    arrived(r.att_in, r.att_sem.at[0])
    ready(r.out_w, r.ffn_in)
    att_low = joined(lambda h: r.att_in[h].astype(F32)).astype(BF16)
    r.att_low[...] = att_low
    mixed = r.pooled[...] + dot(att_low, r.out_w[...])
    r.mixed[...] = mixed
    plain_two, inverse_two = norm_parts(mixed)
    ffn_input = (plain_two * r.ln2_g[...] + r.ln2_b[...]).astype(BF16)
    r.ffn_input[...] = ffn_input
    grad_normed = jnp.zeros((length, width), F32)
    for part in range(4):
        at = slice(part * width, (part + 1) * width)
        pre_act = dot(ffn_input, r.ffn_in[:, at]) + r.ffn_in_b[:, at]
        act, slope = gelu_pair(pre_act)
        r.act_low[:, at] = act.astype(BF16)
        grad_pre = (r.grad_act[:, at] * slope).astype(BF16)
        r.grad_pre[:, at] = grad_pre
        small[7 + part : 8 + part] = column_sum(grad_pre.astype(F32))
        grad_normed = grad_normed + dot(grad_pre, r.ffn_in[:, at], OVER_COLUMNS)
    small[5:6] = column_sum(grad_normed * plain_two)
    small[6:7] = column_sum(grad_normed)
    grad_mixed = r.grad_final[...] + norm_grad(grad_normed, plain_two, inverse_two, r.ln2_g[...])
    r.grad_final[...] = grad_mixed
    grad_mixed_low = grad_mixed.astype(BF16)
    grad_att = dot(grad_mixed_low, r.out_w[...], OVER_COLUMNS)
    for h in range(HEADS):
        r.q_out[h] = packed(grad_att[:, h * HEAD : (h + 1) * HEAD]).astype(BF16)
    second_jobs = q_jobs(r.q_out, r.grad, r.send_sem.at[3], r.grad_sem)
    for job in second_jobs:
        send(*job)

    early, late = r.early, r.late
    count_early, count_late = len(EARLY_CHUNKS), len(LATE_CHUNKS)
    sums = [reduction(early, index, cut) for index, cut in enumerate(EARLY_CHUNKS)]
    for index, cut in enumerate(LATE_CHUNKS):
        small_pair = (small, r.small_in) if index == count_late - 1 else None
        sums.append(reduction(late, count_early + index, cut, small_pair))

    def leave(index):
        cut = (EARLY_CHUNKS + LATE_CHUNKS)[index]
        buffer, target = (early, r.early_o) if index < count_early else (late, r.late_o)
        at = pl.ds(cut[0], cut[1])
        return pltpu.make_async_copy(buffer.at[at], target.at[at], r.leave_sem.at[index])

    def steps_at(moment):
        for index, number in SCHEDULE.get(moment, ()):
            sums[index].step(number)
            if number == sums[index].last:
                leave(index).start()

    for part in range(4):
        at = slice(part * width, (part + 1) * width)
        early[at] = dot(r.ffn_input[...], r.grad_pre[:, at], OVER_ROWS).astype(BF16)
    sums[0].step(0)
    steps_at(-4)
    for part in range(4):
        at = slice(part * width, (part + 1) * width)
        early[2048 + part * width : 2048 + (part + 1) * width] = dot(
            r.act_low[:, at], r.grad_branch[...], OVER_ROWS
        ).astype(BF16)
    sums[1].step(0)
    steps_at(-3)
    early[5632:] = dot(r.att_low[...], grad_mixed_low, OVER_ROWS).astype(BF16)
    final_low = (r.mixed[...] + dot(r.act_low[...], r.ffn_out[...]) + r.ffn_out_b[...]).astype(BF16)
    for part in range(3):
        at = slice(part * width, (part + 1) * width)
        early[4096 + part * width : 4096 + (part + 1) * width] = dot(final_low, r.ct3[:, at], OVER_ROWS).astype(BF16)
    sums[2].step(0)
    steps_at(-2)
    r.att_low[...] = final_low

    steps_at(-1)

    r.dkv[...] = jnp.zeros_like(r.dkv)
    r.dhead[...] = jnp.zeros_like(r.dhead)
    r.dbias[...] = jnp.zeros_like(r.dbias)

    def give_over(turn):
        return pltpu.make_async_remote_copy(
            r.dkv_out.at[turn * group + 1 - core], r.dkv_other.at[turn], r.send_sem.at[7], r.other_sem.at[turn],
            device_id=(1 - core, chip), device_id_type=MESH,
        )

    def hand_in(turn):
        at = turn * group + core
        give_over(turn).wait_recv()
        total = r.dkv[pl.ds(pl.multiple_of(at * length, length), length)] + r.dkv_other[turn].astype(F32)
        r.dkv_out[at] = total.astype(BF16)
        send(r.dkv_out.at[at], r.dkv_in.at[head], (r.send_sem.at[4], r.dkv_sem.at[0]), row, at)

    def back(index, carry):
        turn = rounds - 1 - index
        block = block_of(turn, member, group)
        arrived(r.grad.at[turn], r.grad_sem.at[turn])
        query = unpacked(r.q[turn].astype(F32))
        query_u = ((query + content_bias).astype(BF16).astype(F32) * scale).astype(BF16)
        query_v = (query + pos_bias).astype(BF16)
        grad = unpacked(r.grad[turn].astype(F32))
        inverse = r.att[turn][:, :HEAD]
        grad_part = grad * inverse
        delta = jnp.sum(grad_part * r.att[turn][:, HEAD:], 1, keepdims=True)
        nothing = jnp.zeros((length, HEAD), F32)
        r.extra[:, :PAIR] = jnp.concatenate([nothing, grad_part], 1).astype(BF16)
        r.extra[:, PAIR : 2 * PAIR] = jnp.concatenate([query_u.astype(F32), nothing], 1).astype(BF16)
        r.near[...] = jnp.zeros_like(r.near)
        r.far[...] = jnp.zeros_like(r.far)

        def step_over(step, inner):
            pair = r.kv[rows_of(step * tile), :]
            waves = r.table[rows_of((n - 1 - block) * length + step * tile), :]
            weight = r.keep[kept + step]
            grad_weight = dot(r.extra[:, :PAIR], pair, OVER_COLUMNS)
            grad_score = (weight.astype(F32) * (grad_weight - delta)).astype(BF16)
            r.near[...] += dot(grad_score, pair)
            r.far[...] += dot(grad_score, waves)
            at = pl.ds(pl.multiple_of(step * tile, tile), tile)
            r.dkv[at] += dot(grad_score, r.extra[:, PAIR : 2 * PAIR], OVER_ROWS) + dot(
                weight, r.extra[:, :PAIR], OVER_ROWS
            )
            return inner

        kept = kept_at(turn)
        lax.fori_loop(0, tiles_to(block), step_over, 0)
        give = turn * group + 1 - core
        r.dkv_out[give] = r.dkv[pl.ds(pl.multiple_of(give * length, length), length)].astype(BF16)
        give_over(turn).start()

        @pl.when(index > 0)
        def _():
            hand_in(turn + 1)

        grad_u = r.near[:, :HEAD] * scale
        turn_sin, turn_cos = r.sines[...], r.cosines[...]
        on_sin, on_cos = r.far[:, :half] * scale, r.far[:, half:] * scale
        lift = on_cos * turn_sin - on_sin * turn_cos
        rest = on_cos * turn_cos + on_sin * turn_sin
        spread = jnp.concatenate([lift, rest], 1).astype(BF16)
        grad_v = dot(spread, r.head_w[...])
        r.dhead[...] += dot(spread, query_v, OVER_ROWS)
        r.dbias[0:1] += column_sum(grad_u)
        r.dbias[1:2] += column_sum(grad_v)
        r.dq_out[turn] = packed(grad_u + grad_v).astype(BF16)
        send(r.dq_out.at[turn], r.dq_in.at[head], (r.send_sem.at[5], r.dq_sem.at[0]), row, block)
        for when in range(rounds):
            if when in SCHEDULE:

                @pl.when(index == when)
                def _(when=when):
                    steps_at(when)

        return carry

    lax.fori_loop(0, rounds, back, 0)
    hand_in(0)

    late[2048 + 1024 :] = jnp.zeros((512, 512), BF16)
    dhead = r.dhead[...]
    nothing = jnp.zeros_like(dhead)
    late[3072:, pair_at] = jnp.where(
        odd, jnp.concatenate([nothing, dhead], 1), jnp.concatenate([dhead, nothing], 1)
    ).astype(BF16)
    nothing = jnp.zeros((2, HEAD), F32)
    dbias = r.dbias[...][:2]
    small[3:5, pair_at] = jnp.where(
        odd, jnp.concatenate([nothing, dbias], 1), jnp.concatenate([dbias, nothing], 1)
    )
    sums[3].step(0)
    steps_at(8)
    for source, _, sems, to_core, to_chip in second_jobs:
        sent(source, sems[0], to_core, to_chip)
    for turn in range(rounds):
        block = block_of(jnp.int32(turn), member, group)
        sent(r.att_out.at[turn], r.send_sem.at[2], row, block)
        sent(r.dq_out.at[turn], r.send_sem.at[5], row, block)
    for turn in range(rounds):
        sent(r.dkv_out.at[turn * group + core], r.send_sem.at[4], row, turn * group + core)
        give_over(turn).wait_send()
    for part in range(3):
        at = slice(part * width, (part + 1) * width)
        lifted = dot(r.att_low[...], r.up_w[:, at]) + r.up_b[:, at]
        r.out3[:, at] = (r.x3[:, at].astype(F32) + lifted).astype(BF16)
    arrived(r.dq_in, r.dq_sem.at[0])
    arrived(r.dkv_in, r.dkv_sem.at[0])
    grad_query = joined(lambda h: r.dq_in[h].astype(F32)).astype(BF16)
    both = [r.dkv_in[h].astype(F32) for h in range(HEADS)]
    grad_keys = jnp.concatenate([part[:, :HEAD] for part in both], 1).astype(BF16)
    grad_values = jnp.concatenate([part[:, HEAD:] for part in both], 1).astype(BF16)
    steps_at(9)
    attn_in = r.attn_in[...]
    grad_normed = (
        dot(grad_query, r.q_w[...], OVER_COLUMNS)
        + dot(grad_keys, r.k_w[...], OVER_COLUMNS)
        + dot(grad_values, r.v_w[...], OVER_COLUMNS)
    )
    plain, inverse = norm_parts(r.pooled[...])
    small[1:2] = column_sum(grad_normed * plain)
    small[2:3] = column_sum(grad_normed)
    grad_pooled = (r.grad_final[...] + norm_grad(grad_normed, plain, inverse, r.ln1_g[...])).astype(BF16)
    r.grad_pooled[...] = grad_pooled
    grad_pooled_wide = grad_pooled.astype(F32)
    steps_at(10)
    small[0:1] = column_sum(grad_pooled_wide)

    def back_rim_copy():
        return pltpu.make_async_remote_copy(
            r.grad_pooled.at[:16], r.back_rim, r.side_sem.at[4], r.side_sem.at[5],
            device_id=(core, (chip + n - 1) % n), device_id_type=MESH,
        )

    @pl.when(chip > 0)
    def _():
        back_rim_copy().start()

    late[1024:1536] = dot(r.x3[:, :width], grad_pooled, OVER_ROWS).astype(BF16)
    follow = pltpu.roll(grad_pooled_wide, length - 1, 0)
    within = jnp.where(at_row == length - 1, 0.0, follow).astype(BF16)
    at_rim = lax.broadcasted_iota(jnp.int32, (16, width), 0)
    rim_row = jnp.where(at_rim == 15, jnp.broadcast_to(grad_pooled_wide[:1], (16, width)), 0.0).astype(BF16)
    late[:1024] = (
        dot(r.x3[:, width:], within, OVER_ROWS) + dot(r.rim[...], rim_row, OVER_ROWS)
    ).astype(BF16)
    for later in sums[POOL_SUMS]:
        later.step(0)
    steps_at(11)
    late[1536:2048] = dot(attn_in, grad_query, OVER_ROWS).astype(BF16)
    late[2048:2560] = dot(attn_in, grad_keys, OVER_ROWS).astype(BF16)
    late[2560:3072] = dot(attn_in, grad_values, OVER_ROWS).astype(BF16)
    for later in sums[QKV_SUMS]:
        later.step(0)
    steps_at(12)

    @pl.when(chip == n - 1)
    def _():
        r.back_rim[...] = jnp.zeros_like(r.back_rim)

    @pl.when(chip < n - 1)
    def _():
        back_rim_copy().wait_recv()

    next_row = r.back_rim[...].astype(F32)[:1]
    follow = jnp.where(at_row == length - 1, next_row, follow).astype(BF16)
    first_part = r.ct3[:, :width].astype(F32) + dot(grad_pooled, r.pool_w[2 * width :], OVER_COLUMNS)
    r.grad3[:, :width] = first_part.astype(BF16)
    other_part = r.ct3[:, width:].astype(F32) + dot(follow, r.pool_w[: 2 * width], OVER_COLUMNS)
    r.grad3[:, width:] = other_part.astype(BF16)

    @pl.when(chip < n - 1)
    def _():
        rim_copy().wait_send()

    @pl.when(chip > 0)
    def _():
        back_rim_copy().wait_send()

    steps_at(13)
    for index in range(len(sums)):
        leave(index).wait()


SCHEDULE = {
    -2: ((1, 1),),
    -1: ((0, 1),),
    1: ((0, 2),),
    2: ((1, 2), (2, 1), (0, 3),),
    8: ((2, 2), (1, 3), (0, 4), (3, 1),),
    10: ((1, 4),),
    11: ((2, 3),),
    12: ((3, 2), (0, 5), (7, 1), (4, 1), (3, 3), (1, 5), (5, 1), (6, 1),),
    13: (
        (7, 2), (2, 4), (4, 2), (1, 6), (6, 2), (3, 4), (5, 2), (7, 3), (0, 6), (4, 3), (1, 7), (5, 3), (6, 3),
        (2, 5), (3, 5), (5, 4), (7, 4), (4, 4), (5, 5), (6, 4), (7, 5), (1, 8), (3, 6), (2, 6), (5, 6), (7, 6),
        (4, 5), (0, 7), (7, 7), (3, 7), (6, 5), (0, 8), (5, 7), (3, 8), (7, 8), (4, 6), (6, 6), (5, 8), (1, 9),
        (2, 7), (7, 9), (4, 7), (5, 9), (1, 10), (6, 7), (7, 10), (4, 8), (2, 8), (5, 10), (6, 8),
    ),
}


WIDENED = (
    (0, 4, True), (2048, 4, False), (4096, 3, True), (5632, 1, False),
    (0, 3, False), (1536, 1, False), (2048, 1, False), (2560, 1, False), (3072, 1, False),
)
NARROW = ((0, 1), (1, 1), (2, 1), (3, 1), (4, 1), (5, 1), (6, 1), (7, 4), (11, 1), (12, 3))


def last_kernel(*refs):
    early, late, out3, grad3, small = refs[:5]
    wide_outs, narrow_outs, byte_outs = refs[5:14], refs[14:24], refs[24:26]
    loaded, staging, mixing, bytes_low, load_sems, sems = refs[26:]
    blocks = []
    for index, (out, (start, count, across)) in enumerate(zip(wide_outs, WIDENED)):
        for block in range(count):
            first = start + block * 512
            at = slice(block * 512, (block + 1) * 512)
            source = (early if index < 4 else late).at[first : first + 512]
            blocks.append((source, out.at[:, at] if across else out.at[at]))
    loads = [
        pltpu.make_async_copy(source, loaded.at[slot], load_sems.at[slot]) for slot, (source, _) in enumerate(blocks)
    ]
    stores = [
        pltpu.make_async_copy(staging.at[slot], target, sems.at[slot]) for slot, (_, target) in enumerate(blocks)
    ]
    for load in loads:
        load.start()
    for out, (start, count) in zip(narrow_outs, NARROW):
        if count == 3:
            out[...] = jnp.concatenate([small[start + block : start + block + 1] for block in range(count)], 1).reshape(-1)
        else:
            for block in range(count):
                out[:, block * 512 : (block + 1) * 512] = small[start + block : start + block + 1]

    def widen(slot):
        loads[slot].wait()

        def rows(step, carry):
            here = pl.ds(pl.multiple_of(step * 128, 128), 128)
            staging[slot, here] = loaded[slot, here].astype(F32)
            return carry

        lax.fori_loop(0, 4, rows, 0)
        stores[slot].start()

    some = len(blocks) // 2
    for slot in range(some):
        widen(slot)
    for index, (out, tokens) in enumerate(zip(byte_outs, (out3, grad3))):
        length, width = out.shape[0] // 3, out.shape[1]
        for block in range(width // 128):
            for part in range(3):
                start = part * width + block * 128
                mixing[block, pl.ds(part, length, stride=3), :] = tokens[:, start : start + 128].astype(F32)
            bytes_low[index, :, block * 128 : (block + 1) * 128] = mixing[block].astype(BF16)
        store = pltpu.make_async_copy(bytes_low.at[index], out, sems.at[len(blocks) + index])
        store.start()
        stores.append(store)
    for slot in range(some, len(blocks)):
        widen(slot)
    for store in stores:
        store.wait()


def finished(early, late, out3, grad3, small):
    length, width = out3.shape[0], out3.shape[1] // 3
    vmem = pl.BlockSpec(memory_space=pltpu.VMEM)
    shapes = [(512, 512 * blocks) if across else (512 * blocks, 512) for _, blocks, across in WIDENED]
    narrow = [(512 * blocks,) if blocks == 3 else (1, 512 * blocks) for _, blocks in NARROW]
    count = sum(blocks for _, blocks, _ in WIDENED)
    outs = pl.pallas_call(
        last_kernel,
        in_specs=[pl.BlockSpec(memory_space=pl.ANY)] * 2 + [vmem] * 3,
        out_specs=[pl.BlockSpec(memory_space=pl.ANY)] * len(shapes)
        + [vmem] * len(narrow)
        + [pl.BlockSpec(memory_space=pl.ANY)] * 2,
        out_shape=[jax.ShapeDtypeStruct(shape, F32) for shape in shapes + narrow]
        + [jax.ShapeDtypeStruct((3 * length, width), BF16)] * 2,
        scratch_shapes=[
            pltpu.VMEM((count, 512, 512), BF16), pltpu.VMEM((count, 512, 512), F32), pltpu.VMEM((width // 128, 3 * length, 128), F32),
            pltpu.VMEM((2, 3 * length, width), BF16), pltpu.SemaphoreType.DMA((count,)), pltpu.SemaphoreType.DMA((count + 2,)),
        ],
        compiler_params=pltpu.CompilerParams(vmem_limit_bytes=56 * 2**20),
    )(early, late, out3, grad3, small)
    return outs[: len(shapes)], [out if out.ndim == 1 else out[0] for out in outs[len(shapes) : -2]], outs[-2:]


def fused_body(
    inputs, doc_bounds, pool_weight, pool_bias, ln1_gain, ln1_bias, query_weight, key_weight,
    value_weight, out_weight, pos_weight, content_bias, pos_bias, ln2_gain, ln2_bias, ffn_in,
    ffn_in_bias, ffn_out, ffn_out_bias, up_weight, up_bias, cotangent,
):
    _, bytes_here, width = inputs.shape
    length = bytes_here // 3
    n = lax.axis_size("seq")
    tokens = n * length
    rounds = n // 2
    table, sines, cosines = wave_tables(tokens, length, width, TILE)
    given = dict(
        x_bytes=inputs[0], pool_w=pool_weight, q_w=query_weight, k_w=key_weight, v_w=value_weight,
        ct_bytes=cotangent[0], up_w=up_weight, ffn_out=ffn_out, pos_w=pos_weight, table=table,
        out_w=out_weight, ffn_in=ffn_in,
    )
    vectors = dict(
        pool_b=pool_bias, ln1_g=ln1_gain, ln1_b=ln1_bias, content=content_bias, pos=pos_bias, ln2_g=ln2_gain,
        ln2_b=ln2_bias, ffn_in_b=ffn_in_bias, ffn_out_b=ffn_out_bias,
    )
    vectors = {name: vector[None] for name, vector in vectors.items()} | dict(up_flat=up_bias, sines=sines, cosines=cosines)
    vmem = pl.BlockSpec(memory_space=pltpu.VMEM)
    outs = dict(
        out3=((length, 3 * width), BF16), grad3=((length, 3 * width), BF16), small=((SMALL_ROWS, 512), F32),
        early_o=((EARLY_ROWS, 512), BF16), late_o=((LATE_ROWS, 512), BF16),
    )
    pair_half = (length // 2, PAIR)
    block, wide = (length, width), (length, 4 * width)
    dma, signal = pltpu.SemaphoreType.DMA, pltpu.SemaphoreType.REGULAR
    scratch = {name: pltpu.VMEM(array.shape, array.dtype) for name, array in given.items()}
    low = dict(
        x3=(length, 3 * width), ct3=(length, 3 * width), rim=(16, 2 * width), back_rim=(16, width), attn_in=block, q_out=(HEADS,) + pair_half,
        kv_out=(HEADS, length, PAIR), q=(rounds,) + pair_half, kv=(tokens, PAIR), grad_branch=block,
        head_w=(width, HEAD), extra=(length, PAIR + width), keep=(sum(most_tiles(turn, length) for turn in range(rounds)), length, TILE),
        att_out=(rounds,) + pair_half, att_in=(HEADS,) + pair_half, att_low=block, ffn_input=block, act_low=wide,
        grad_pre=wide, grad=(rounds,) + pair_half, dkv_out=(n, length, PAIR), dkv_in=(HEADS, length, PAIR),
        dkv_other=(rounds, length, PAIR), dq_out=(rounds,) + pair_half, dq_in=(HEADS,) + pair_half, grad_pooled=block, early=(EARLY_ROWS, 512), late=(LATE_ROWS, 512),
    )
    full = dict(
        mixing=(width // 128, 3 * length, 128), pooled=block, grad_final=block, grad_act=wide, score=(tokens // TILE, length, TILE), att=(rounds, length, PAIR),
        mixed=block, dkv=(tokens, PAIR), dhead=(width, HEAD), dbias=(8, HEAD), near=(length, PAIR), far=block,
        small_in=(7, SMALL_ROWS, 512), up_b=(1, 3 * width),
    )
    scratch |= {name: pltpu.VMEM(shape, BF16) for name, shape in low.items()}
    scratch |= {name: pltpu.VMEM(shape, F32) for name, shape in full.items()}
    scratch |= dict(
        edges=pltpu.VMEM((2, 16, 128), jnp.int32), load_sem=dma((len(given),)), side_sem=dma((6,)), send_sem=dma((8,)), other_sem=dma((rounds,)),

        q_sem=dma((rounds,)), kv_sem=dma((n,)), att_sem=dma((1,)), grad_sem=dma((rounds,)), dkv_sem=dma((1,)),
        dq_sem=dma((1,)), sum_sem=dma((len(EARLY_CHUNKS + LATE_CHUNKS), 2, REDUCTION_SEMS)),
        sum_free=signal((len(EARLY_CHUNKS + LATE_CHUNKS), 5)), leave_sem=dma((len(EARLY_CHUNKS + LATE_CHUNKS),)),
    )
    layout = (list(given), list(vectors) + ["bounds"], list(outs), list(scratch))
    out3, grad3, small, early, late = pl.pallas_call(
        functools.partial(layer_kernel, n, length, layout),
        in_specs=[pl.BlockSpec(memory_space=pl.ANY)] * len(given)
        + [vmem] * len(vectors)
        + [pl.BlockSpec(memory_space=pltpu.SMEM)],
        out_specs=[vmem] * 3 + [pl.BlockSpec(memory_space=pl.ANY)] * 2,
        out_shape=[jax.ShapeDtypeStruct(*out) for out in outs.values()],
        scratch_shapes=list(scratch.values())
        + sum((reduction_scratch(*cut[1:]) for cut in EARLY_CHUNKS + LATE_CHUNKS), []),
        compiler_params=pltpu.CompilerParams(
            collective_id=0, has_side_effects=True, vmem_limit_bytes=62 * 2**20
        ),
    )(*given.values(), *vectors.values(), doc_bounds)
    wide, narrow, both = finished(early, late, out3, grad3, small)
    sum_in, sum_out, sum_up, sum_mix, sum_pool, sum_q, sum_k, sum_v, sum_p = wide
    pool_b, ln1_g, ln1_b, content, pos, ln2_g, ln2_b, in_b, out_b, up_b = narrow
    return (
        both[0][None], both[1][None], sum_pool, pool_b, ln1_g, ln1_b, sum_q, sum_k, sum_v, sum_mix, sum_p,
        content, pos, ln2_g, ln2_b, sum_in, in_b, sum_out, out_b, sum_up, up_b,
    )


def solution(mesh):
    split = P("dp", "seq", None)
    fits = mesh.shape["seq"] == 16
    return jax.shard_map(
        fused_body if fits else body,
        mesh=mesh,
        in_specs=(split, P("dp", None)) + (P(),) * 19 + (split,),
        out_specs=(split, split) + (P(),) * 19,
        check_vma=False,
    )
```
